32 devices in a mesh: lat: 8 (over z, y), fld: 4 (over x, core).
Axes of the slice: x: 2, y: 2, z: 4, core: 2. Of those that a mesh axis runs over, the one named last changes fastest.
Arguments:
- grid: bfloat16 [20, 8, 2, 5248], P('fld', 'lat'), may hold values from -6 to 6
- row_lengths: int32 [8], replicated, may hold values from 20 to 5136, as said below
- band_map: int32 [8], replicated, may hold values from 0 to 7, each once
- fold_map: int32 [32, 40], replicated, may hold values from 0 to 1279, as said below
- legendre: float32 [640, 1281, 8], P(('lat', 'fld')), may hold values from -1.5 to 1.5
- to_modes: float32 [20, 20], replicated, may hold values from -1.25 to 1.25
- back_modes: float32 [20, 20], replicated, may hold values from -1.25 to 1.25
- mode_rates: float32 [20], replicated, may hold values from 0.1 to 30
Outputs:
- spectral: float32 [20, 2, 640, 1281], P(None, None, ('lat', 'fld'))
- grid_out: bfloat16 [20, 8, 2, 5248], P('fld', 'lat')
The draws below stay inside these ranges and needn't reach their ends.
Inputs may be any that keep to these rules, and one draw needn't show every extreme that they name: `row_lengths`: entry j is 20 + 4 i for an octahedral row index i with j * S <= i < (j + 1) * S, S = 160; entry 0 is 20 and the last entry is 5136; every entry is a multiple of 4. `fold_map`: every wavenumber 0 to 1279 stands exactly once; in every row, entries 2 s and 2 s + 1 are m and 1279 - m with m < 640. Row d lists the wavenumbers of the device with joined index d of lat+fld (lat index times the size of fld plus fld index). `band_map`: A permutation.
All inputs are finite; a program needn't handle non-finite values.
Results may differ from the reference program's by a relative error of at most 0.006.
Values sent between devices are 32-bit elements; how exact they have to be, the bound alone decides.
No kernel may reach another device: no remote copies, remote signals or barrier semaphores. Data moves between devices by JAX's collectives and lax.ppermute only.
A program may use at most 128 MiB of HBM per device.

```python
import math
import jax
import jax.numpy as jnp
from jax import lax

TRUNC = 1279
FL = 20
NSP = 1281
NPAIRS = 640
MDEV = 40
BANDS = 8
NLATH = 8
ROWS = 2
GRIDW = 5248
N_LAT = 8


def draw_row_lengths(key, part):
    key = jax.random.fold_in(key, 11)
    stride = (TRUNC + 1) // NLATH
    base = jnp.arange(NLATH, dtype=jnp.int32) * stride
    step = jax.random.randint(key, (NLATH,), 0, stride, dtype=jnp.int32)
    index = base + step
    index = index.at[0].set(0).at[NLATH - 1].set(TRUNC)
    return (20 + 4 * index).astype(jnp.int32)


def draw_fold_map(key, part):
    key = jax.random.fold_in(key, 23)
    order = jax.random.permutation(key, NPAIRS).astype(jnp.int32)
    paired = jnp.stack([order, TRUNC - order], axis=1)
    return paired.reshape(-1, MDEV).astype(jnp.int32)


def block_levels(own_key, dims, split, least, top_value):
    gain, own = 1.0, jax.random.fold_in(own_key, 6)
    for dim, blocks in split:
        steps = jnp.exp(jax.random.uniform(jax.random.fold_in(own, dim), (blocks,), jnp.float32, least / len(split), top_value / len(split)))
        gain = gain * jnp.repeat(steps, dims[dim] // blocks).reshape([-1 if axis == dim else 1 for axis in range(len(dims))])
    return gain


def noise(key, dims, deviation, reach, cuts=(), held_as=jnp.bfloat16):
    level = block_levels(key, dims, cuts, -0.22, 0.18) if cuts else 1.0
    drawn = jax.random.normal(key, dims, jnp.float32) * deviation * level
    return jnp.minimum(jnp.maximum(drawn, -reach), reach).astype(held_as)


def setup_inputs(seed: int = 0) -> dict:
    streams_of = jax.random.split(jax.random.key(seed), 9)
    return {
        "grid": noise(streams_of[0], (FL, BANDS, ROWS, GRIDW), 1.0, 6.0, ((0, 4), (1, 8))),
        "row_lengths": draw_row_lengths(jax.random.fold_in(streams_of[8], 71), 0),
        "band_map": jax.random.permutation(streams_of[2], N_LAT).astype(jnp.int32),
        "fold_map": draw_fold_map(jax.random.fold_in(streams_of[8], 71), 0),
        "legendre": noise(streams_of[4], (NPAIRS, NSP, NLATH), (2 * NLATH) ** -0.5, 1.5, ((0, 32),), jnp.float32),
        "to_modes": noise(streams_of[5], (FL, FL), FL ** -0.5, 1.25, (), jnp.float32),
        "back_modes": noise(streams_of[6], (FL, FL), FL ** -0.5, 1.25, (), jnp.float32),
        "mode_rates": jnp.clip(jnp.exp(jax.random.uniform(streams_of[7], (FL,), jnp.float32, math.log(0.1), math.log(30.0))), 0.1, 30.0),
    }


HIGH = lax.Precision.HIGHEST
TWO_PI = 2.0 * math.pi

def row_tables(length, quarter_pad, cut_off):
    quarter = length // 4
    top = jnp.minimum(cut_off, (length - 1) // 2)
    across = jnp.arange(quarter_pad, dtype=jnp.int32)[:, None]
    wave = jnp.arange(cut_off + 1, dtype=jnp.int32)[None, :]
    keep = (across < quarter) & (wave <= top)
    inner = (across * wave % quarter).astype(jnp.float32) * (TWO_PI / quarter.astype(jnp.float32))
    cos_table = jnp.where(keep, jnp.cos(inner), 0.0).astype(jnp.bfloat16)
    sin_table = jnp.where(keep, jnp.sin(inner), 0.0).astype(jnp.bfloat16)
    phase = jnp.arange(4, dtype=jnp.int32)[:, None]
    twist = (phase * wave % length).astype(jnp.float32) * (TWO_PI / length.astype(jnp.float32))
    weight = jnp.where(wave == 0, 1.0, 2.0) * (wave <= top).astype(jnp.float32)
    scale = 1.0 / jnp.sqrt(length.astype(jnp.float32))
    return (cos_table, sin_table, jnp.cos(twist), jnp.sin(twist), weight, scale)

def forward_row(values, length, cut_off):
    cos_table, sin_table, cos_twist, sin_twist, weight, scale = row_tables(length, values.shape[1], cut_off)
    wide = values.astype(jnp.float32)
    real_part = jnp.einsum('fab,am->bfm', wide, cos_table.astype(jnp.float32), precision=HIGH)
    imag_part = -jnp.einsum('fab,am->bfm', wide, sin_table.astype(jnp.float32), precision=HIGH)
    cos_b = cos_twist[:, None, :]
    sin_b = sin_twist[:, None, :]
    four_re = scale * lax.optimization_barrier(jnp.sum(cos_b * real_part + sin_b * imag_part, axis=0))
    four_im = scale * lax.optimization_barrier(jnp.sum(cos_b * imag_part - sin_b * real_part, axis=0))
    return jnp.stack([four_re, four_im], axis=1)

def inverse_row(four, length, quarter_pad, cut_off):
    cos_table, sin_table, cos_twist, sin_twist, weight, scale = row_tables(length, quarter_pad, cut_off)
    fields = four.shape[0]
    cos_b = cos_twist[:, None, :]
    sin_b = sin_twist[:, None, :]
    four_re = (four[:, 0] * weight)[None]
    four_im = (four[:, 1] * weight)[None]
    twisted_re = (cos_b * four_re - sin_b * four_im).astype(jnp.bfloat16)
    twisted_im = (sin_b * four_re + cos_b * four_im).astype(jnp.bfloat16)
    total = jnp.einsum('bfm,am->fab', twisted_re.astype(jnp.float32), cos_table.astype(jnp.float32), precision=HIGH)
    total = total - jnp.einsum('bfm,am->fab', twisted_im.astype(jnp.float32), sin_table.astype(jnp.float32), precision=HIGH)
    return (scale * total).reshape(fields, quarter_pad * 4).astype(jnp.bfloat16)

def pair_layout(first, cut_off):
    place = jnp.arange(cut_off + 2, dtype=jnp.int32)[None, :]
    start = first[:, None]
    second = cut_off - start
    partner = place > second
    degree = jnp.where(partner, place - 1, start + place)
    wave = jnp.where(partner, second, start)
    odd = (degree + wave) % 2 == 1
    return (partner, odd, degree)

def direct_legendre(sym, asym, table, partner, odd):
    nlat, fields, two, slots = sym.shape
    pairs = slots // 2
    both = jnp.stack([sym, asym], axis=1).reshape(nlat, 2, fields, 2, pairs, 2)
    stacked = jnp.transpose(both, (4, 0, 5, 1, 2, 3)).reshape(pairs, nlat, 8 * fields)
    raw = jnp.einsum('pqj,pjx->pqx', table, stacked, precision=HIGH)
    raw = raw.reshape(pairs, table.shape[1], 2, 2, fields, 2)
    pick = jnp.where(partner[:, :, None, None, None], raw[:, :, 1], raw[:, :, 0])
    pick = jnp.where(odd[:, :, None, None], pick[:, :, 1], pick[:, :, 0])
    return jnp.transpose(pick, (2, 3, 0, 1))

def inverse_legendre(spectral, table, partner, odd):
    fields = spectral.shape[0]
    pairs, places, nlat = table.shape
    coef = jnp.transpose(spectral, (2, 3, 0, 1))
    parts = []
    for chosen in (jnp.logical_not(partner), partner):
        for parity in (jnp.logical_not(odd), odd):
            parts.append(jnp.where((chosen & parity)[:, :, None, None], coef, 0.0))
    spread = jnp.stack(parts, axis=2).reshape(pairs, places, 8 * fields)
    sums = jnp.einsum('pqj,pqx->pjx', table, spread, precision=HIGH).reshape(pairs, nlat, 2, 2, fields, 2)
    north = sums[:, :, :, 0] + sums[:, :, :, 1]
    south = sums[:, :, :, 0] - sums[:, :, :, 1]
    north = jnp.transpose(north, (1, 3, 4, 0, 2)).reshape(nlat, fields, 2, 2 * pairs)
    south = jnp.transpose(south, (1, 3, 4, 0, 2)).reshape(nlat, fields, 2, 2 * pairs)
    return (north, south)

def implicit_solve(raw, degree, cut_off, to_modes, back_modes, mode_rates):
    modes = jnp.einsum('kf,fcpq->kcpq', to_modes, raw, precision=HIGH)
    tau = (degree * (degree + 1)).astype(jnp.float32) / float(cut_off * (cut_off + 1))
    damped = modes / (1.0 + tau[None, None] * mode_rates[:, None, None, None])
    return jnp.einsum('gk,kcpq->gcpq', back_modes, damped, precision=HIGH)

def reference(grid, row_lengths, band_map, fold_map, legendre, to_modes, back_modes, mode_rates):
    fields, bands, rows, width = grid.shape
    lat_dev = rows // 2
    quarter_pad = width // 4
    pairs_all, places, nlat = legendre.shape
    cut_off = places - 2
    band_rows = band_map[:, None] * lat_dev + jnp.arange(rows, dtype=jnp.int32)[None, :] % lat_dev
    lengths = row_lengths[band_rows].reshape(-1)
    values = jnp.transpose(grid.reshape(fields, bands * rows, quarter_pad, 4), (1, 0, 2, 3))
    four = lax.map(lambda item: forward_row(item[0], item[1], cut_off), (values, lengths))
    by_band = four.reshape(bands, rows, fields, 2, cut_off + 1)[jnp.argsort(band_map)]
    north = by_band[:, :lat_dev].reshape(nlat, fields, 2, cut_off + 1)
    south = by_band[:, lat_dev:].reshape(nlat, fields, 2, cut_off + 1)
    order = fold_map.reshape(-1)
    sym = (north + south)[..., order]
    asym = (north - south)[..., order]
    partner, odd, degree = pair_layout(order[0::2], cut_off)
    raw = direct_legendre(sym, asym, legendre, partner, odd)
    spectral = implicit_solve(raw, degree, cut_off, to_modes, back_modes, mode_rates)
    north_back, south_back = inverse_legendre(spectral, legendre, partner, odd)
    empty = jnp.zeros((nlat, fields, 2, cut_off + 1), jnp.float32)
    north_back = empty.at[..., order].set(north_back)
    south_back = empty.at[..., order].set(south_back)
    rows_back = jnp.concatenate([north_back.reshape(bands, lat_dev, fields, 2, cut_off + 1), south_back.reshape(bands, lat_dev, fields, 2, cut_off + 1)], axis=1)[band_map]
    outgoing = lax.map(lambda item: inverse_row(item[0], item[1], quarter_pad, cut_off), (rows_back.reshape(bands * rows, fields, 2, cut_off + 1), lengths))
    grid_out = jnp.transpose(outgoing.reshape(bands, rows, fields, width), (2, 0, 1, 3))
    return (spectral, grid_out)
```

```python
import functools
import math

import jax
import jax.numpy as jnp
from jax import lax
from jax.experimental import pallas as pl
from jax.experimental.pallas import tpu as pltpu
from jax.sharding import PartitionSpec as P

LANES = 128
KPAD = 24
FPAD = 64
F32 = jnp.float32
BF16 = jnp.bfloat16
NT_DIMS = (((1,), (1,)), ((), ()))
SIN_POLY = (
    6.283185302447051,
    -41.34170038368319,
    81.60513023312113,
    -76.70299324464969,
    42.02573766814694,
    -14.899106966102595,
    3.237062655726421,
)
COS_POLY = (
    0.9999999889083757,
    -19.739204448887243,
    64.93911476570418,
    -85.45008785413638,
    60.167188450194914,
    -25.9658703083255,
    6.526145851512229,
)


def dot(a, b):
    return jnp.dot(a, b, preferred_element_type=F32)


def dot_nt(a, b):
    return lax.dot_general(a, b, NT_DIMS, preferred_element_type=F32)


def split(x):
    high = x.astype(BF16)
    return high, (x - high.astype(F32)).astype(BF16)


def horner(coefs, z):
    total = coefs[-1] * z + coefs[-2]
    for coef in coefs[-3::-1]:
        total = total * z + coef
    return total


def turn(steps, period, inverse):
    rest = steps - period * jnp.floor(steps * inverse + 0.5)
    part = rest * inverse
    z = part * part
    return horner(COS_POLY, z), part * horner(SIN_POLY, z)


def lane_iota(shape):
    return lax.broadcasted_iota(jnp.int32, shape, len(shape) - 1)


def row_iota(shape):
    return lax.broadcasted_iota(jnp.int32, shape, len(shape) - 2)


def spread_matrix():
    shape = (4 * LANES, LANES)
    picks = []
    for phase in range(4):
        picks.append(jnp.where(row_iota(shape) == 4 * lane_iota(shape) + phase, 1.0, 0.0))
    return jnp.concatenate(picks, axis=1).astype(BF16)


def forward_kernel(
    cut_off, groups, len_ref, band_ref, fold_ref, grid_ref,
    msg_ref, cos_ref, sin_ref, k1_ref, k2_ref, fold_s, mb, cb, sb, xs, xq, ys,
):
    fields, _, rows, width = grid_ref.shape
    owners, per_owner = fold_ref.shape
    slots, across = cos_ref.shape
    chunks = across // LANES
    padded = groups * 8
    unit = rows * fields * 2
    length = len_ref[band_ref[lax.axis_index("lat")]]
    top = jnp.minimum(cut_off, (length - 1) // 2)

    fold_s[...] = jnp.full(fold_s.shape, -1.0, F32)
    fold_s[0:owners, 0:per_owner] = fold_ref[...].astype(F32)
    waves = jnp.transpose(fold_s[...])[0:padded]
    small = waves.shape
    period = jnp.full(small, length // 4, jnp.int32).astype(F32)
    step_c, step_s = turn(waves * float(LANES), period, 1.0 / period)
    for owner in range(owners):
        put = pl.ds(owner * padded, padded)
        wide = (padded, LANES)
        mb[put, :] = jnp.broadcast_to(waves[:, owner:owner + 1], wide)
        cb[put, :] = jnp.broadcast_to(step_c[:, owner:owner + 1], wide)
        sb[put, :] = jnp.broadcast_to(step_s[:, owner:owner + 1], wide)

    xs[...] = jnp.zeros(xs.shape, F32)
    inside = lane_iota((rows, width)) < length
    for field in range(fields):
        points = grid_ref[field, 0].astype(F32)
        xs[rows * field:rows * (field + 1), 0:width] = jnp.where(inside, points, 0.0)
    stacked = jnp.concatenate(
        [xs[:, 4 * LANES * c:4 * LANES * (c + 1)] for c in range(chunks)], axis=0
    ).astype(BF16)
    phases = dot(stacked, spread_matrix()).astype(BF16)
    for c in range(chunks):
        for phase in range(4):
            piece = phases[16 * c:16 * (c + 1), LANES * phase:LANES * (phase + 1)]
            for half in (0, 64):
                xq[half + 16 * phase:half + 16 * (phase + 1), LANES * c:LANES * (c + 1)] = piece

    block = 32
    shape = (block, LANES)
    lane = lane_iota(shape)
    lane_f = lane.astype(F32)
    phase_f = ((lane % 64) // 16).astype(F32)
    quarter_v = jnp.full(shape, length // 4, jnp.int32).astype(F32)
    quarter_i = 1.0 / quarter_v
    length_v = jnp.full(shape, length, jnp.int32).astype(F32)
    length_i = 1.0 / length_v
    top_v = jnp.full(shape, top, jnp.int32).astype(F32)

    def table_block(i, carry):
        at = pl.ds(pl.multiple_of(i * block, block), block)
        wave = mb[at, :]
        c1 = cb[at, :]
        s1 = sb[at, :]
        c_old, s_old = turn(wave * lane_f, quarter_v, quarter_i)
        c_now = c_old * c1 - s_old * s1
        s_now = s_old * c1 + c_old * s1
        twice = c1 + c1
        cos_ref[at, 0:LANES] = c_old.astype(BF16)
        sin_ref[at, 0:LANES] = s_old.astype(BF16)
        for c in range(1, chunks):
            cos_ref[at, LANES * c:LANES * (c + 1)] = c_now.astype(BF16)
            sin_ref[at, LANES * c:LANES * (c + 1)] = s_now.astype(BF16)
            c_old, c_now = c_now, twice * c_now - c_old
            s_old, s_now = s_now, twice * s_now - s_old
        co, si = turn(wave * phase_f, length_v, length_i)
        weight = jnp.where(wave == 0.0, 1.0, 2.0)
        weight = jnp.where((wave >= 0.0) & (wave <= top_v), weight, 0.0)
        upper = lane >= 64
        k1_ref[at, :] = jnp.where(upper, -si, co) * weight
        k2_ref[at, :] = jnp.where(upper, co, si) * weight
        return carry

    lax.fori_loop(0, slots // block, table_block, 0)

    big = 256
    values = xq[...]

    def dot_block(i, carry):
        at = pl.ds(pl.multiple_of(i * big, big), big)
        both = jnp.concatenate([cos_ref[at, :], sin_ref[at, :]], axis=0)
        inner = dot_nt(both, values)
        fix = jnp.where(mb[at, :] == 0.0, 1.0, 0.5)
        ys[at, :] = (inner[0:big] * k1_ref[at, :] - inner[big:2 * big] * k2_ref[at, :]) * fix
        return carry

    lax.fori_loop(0, slots // big, dot_block, 0)

    turned = ys[...].reshape(owners, groups, 8, LANES)
    shape = (LANES, LANES)
    source = row_iota(shape)
    target = lane_iota(shape)
    vec = source % 16
    base = (vec % rows) * (fields * 2) + (vec // rows) * 2 + source // 64
    total = jnp.zeros((owners * 8, LANES), F32)
    for t in range(groups):
        place = jnp.where((vec < rows * fields) & (target == base + unit * t), 1.0, 0.0).astype(BF16)
        high, low = split(turned[:, t].reshape(owners * 8, LANES))
        total = total + dot(
            jnp.concatenate([high, low], axis=1), jnp.concatenate([place, place], axis=0)
        )
    scale = 1.0 / jnp.sqrt(jnp.full((owners * 8, LANES), length, jnp.int32).astype(F32))
    msg_ref[...] = (total * scale).reshape(owners, 8, LANES)


def inverse_kernel(
    groups, len_ref, band_ref, msg_ref, cos_ref, sin_ref, k1_ref, k2_ref, grid_ref, zs, os,
):
    fields, _, rows, width = grid_ref.shape
    owners = msg_ref.shape[0]
    slots, across = cos_ref.shape
    chunks = across // LANES
    unit = rows * fields * 2
    length = len_ref[band_ref[lax.axis_index("lat")]]
    high, low = split(msg_ref[...].reshape(owners * 8, LANES))
    pieces = jnp.concatenate([high, low], axis=1)
    shape = (LANES, 2 * LANES)
    source = row_iota(shape)
    target = lane_iota(shape)
    vec = target % 16
    upper = (target % LANES) >= 64
    imag = target >= LANES
    base = (vec % rows) * (fields * 2) + (vec // rows) * 2 + jnp.where(imag, 1, 0)
    sign = jnp.where(upper != imag, -1.0, 1.0)
    factor_a = k1_ref[...].reshape(owners, groups, 8, LANES)
    factor_b = k2_ref[...].reshape(owners, groups, 8, LANES)
    for t in range(groups):
        place = jnp.where((vec < rows * fields) & (source == base + unit * t), sign, 0.0).astype(BF16)
        both = dot(pieces, jnp.concatenate([place, place], axis=0))
        z = (
            both[:, 0:LANES] * factor_a[:, t].reshape(owners * 8, LANES)
            + both[:, LANES:] * factor_b[:, t].reshape(owners * 8, LANES)
        )
        zs[:, t] = z.reshape(owners, 8, LANES)
    turned = jnp.transpose(zs[...].reshape(slots, LANES)).astype(BF16)
    real = turned[0:64]
    imag_part = turned[64:128]
    scale = 1.0 / jnp.sqrt(jnp.full((64, 2 * LANES), length, jnp.int32).astype(F32))
    for start in range(0, across, 2 * LANES):
        size = min(2 * LANES, across - start)
        total = dot(real, cos_ref[:, start:start + size]) - dot(imag_part, sin_ref[:, start:start + size])
        out = total * scale[:, 0:size]
        for phase in range(4):
            for sub in range(size // LANES):
                c = start // LANES + sub
                os[16 * c:16 * (c + 1), LANES * phase:LANES * (phase + 1)] = out[
                    16 * phase:16 * (phase + 1), LANES * sub:LANES * (sub + 1)
                ].astype(BF16)
    merged = dot_nt(os[...], spread_matrix())
    for c in range(chunks):
        begin = 4 * LANES * c
        size = min(4 * LANES, width - begin)
        if size <= 0:
            continue
        inside = begin + lane_iota((16, size)) < length
        piece = jnp.where(inside, merged[16 * c:16 * (c + 1), 0:size], 0.0)
        for field in range(fields):
            grid_ref[field, 0, :, begin:begin + size] = piece[
                rows * field:rows * (field + 1)
            ].astype(BF16)


def spectral_kernel(
    cut_off, pairs, fields, rows, band_ref, fold_ref, rates_ref, msg_ref, leg_ref, tm_ref, bm_ref,
    spec_ref, out_ref, vs, fq, bk, pad_s, eh, sq, cs,
):
    everyone = tm_ref.shape[0]
    quad, lats, places = leg_ref.shape
    holders = band_ref.shape[0]
    groups_f = everyone // fields
    groups = fq.shape[0] // (4 * KPAD)
    wf = fields * 2
    unit = rows * wf
    span = eh.shape[1]
    step = pl.program_id(0)
    owner = lax.axis_index("lat") * groups_f + lax.axis_index("fld")
    eight = 8 * lats

    @pl.when(step == 0)
    def _():
        for holder in range(holders):
            lat = band_ref[holder]
            for g in range(groups_f):
                vs[pl.ds(pl.multiple_of((g * lats + lat) * 8, 8), 8), :] = msg_ref[holder * groups_f + g]
        tall = []
        for i8 in range(8):
            tall.append(
                jnp.concatenate(
                    [vs[pl.ds(g * lats * 8 + i8, lats, stride=8), :] for g in range(groups_f)], axis=1
                )
            )
        v_high, v_low = split(jnp.concatenate(tall, axis=0))
        pad_s[...] = jnp.zeros(pad_s.shape, F32)
        pad_s[0:everyone, 0:everyone] = tm_ref[...]
        m_high, m_low = split(pad_s[...])
        shape = (LANES, LANES)
        level = (lane_iota(shape) % wf) // 2
        wide_h, wide_l = [], []
        for g in range(groups_f):
            pick = jnp.where(row_iota(shape) == fields * g + level, 1.0, 0.0).astype(BF16)
            wide_h.append(dot(m_high, pick))
            wide_l.append(dot(m_low, pick))
        wide_h = jnp.concatenate(wide_h, axis=1)
        wide_l = jnp.concatenate(wide_l, axis=1)
        lane = lane_iota(wide_h.shape) % LANES
        total_h, total_l = [], []
        for t in range(groups):
            for r in range(rows):
                for c in range(2):
                    keep = (lane // wf == t * rows + r) & (lane % 2 == c)
                    total_h.append(jnp.where(keep, wide_h, 0.0))
                    total_l.append(jnp.where(keep, wide_l, 0.0))
        mix_h = jnp.concatenate(total_h, axis=0).astype(BF16)
        mix_l = jnp.concatenate(total_l, axis=0).astype(BF16)
        fq[...] = dot_nt(mix_h, v_high) + dot_nt(mix_l, v_high) + dot_nt(mix_h, v_low)

        pad_s[...] = jnp.zeros(pad_s.shape, F32)
        pad_s[0:everyone, 0:everyone] = bm_ref[...]
        b_high, b_low = split(pad_s[...])
        shape = (FPAD, KPAD)
        expand = jnp.where(row_iota(shape) // 2 == lane_iota(shape), 1.0, 0.0).astype(BF16)
        shape = (LANES, 8 * KPAD)
        repeat = jnp.where(row_iota(shape) == lane_iota(shape) % KPAD, 1.0, 0.0).astype(BF16)
        shape = (FPAD, 8 * KPAD)
        same = row_iota(shape) % 2 == (lane_iota(shape) // KPAD) % 2
        pair_of = lane_iota(shape) // (2 * KPAD)
        for part, piece in enumerate((b_high, b_low)):
            full = dot(dot(expand, piece).astype(BF16), repeat)
            for pp in range(4):
                bk[(4 * part + pp) * FPAD:(4 * part + pp + 1) * FPAD, :] = jnp.where(
                    same & (pair_of == pp), full, 0.0
                ).astype(BF16)

    whole = places // LANES * LANES
    waves, seconds, lasts = [], [], []
    for pp in range(4):
        pair = 4 * step + pp
        there = pair < pairs
        wave = fold_ref[owner, 2 * jnp.minimum(pair, pairs - 1)]
        waves.append(wave)
        seconds.append(jnp.where(there, cut_off - wave, -1))
        lasts.append(jnp.where(there, places - 1, -1))
    shape = (lats, span)
    place = lane_iota(shape)
    for pp in range(4):
        leg = jnp.concatenate(
            [
                leg_ref[pp, :, 0:whole],
                jnp.broadcast_to(leg_ref[pp, :, whole:places], (lats, span - whole)),
            ],
            axis=1,
        )
        first = place <= seconds[pp]
        second = (place > seconds[pp]) & (place <= lasts[pp])
        odd = ((place + jnp.where(first, 0, waves[pp])) & 1) == 1
        signed = jnp.where(odd, -leg, leg)
        for r, rowset in enumerate((leg, signed)):
            start = r * eight + 2 * pp * lats
            eh[start:start + 2 * lats, :] = jnp.concatenate(
                [jnp.where(first, rowset, 0.0), jnp.where(second, rowset, 0.0)], axis=0
            ).astype(BF16)

    mixed = fq[pl.ds(pl.multiple_of(step * 4 * KPAD, 8), 4 * KPAD), :]
    mixed = jnp.concatenate([mixed[0:2 * KPAD], mixed[2 * KPAD:4 * KPAD]], axis=1)
    slot_pair = (lane_iota(mixed.shape) % eight) // (2 * lats)
    left = jnp.concatenate([jnp.where(slot_pair == pp, mixed, 0.0) for pp in range(4)], axis=0)
    left_h, left_l = split(left)
    left = jnp.concatenate([left_h, left_l], axis=0)
    tall_rows = 8 * KPAD

    rate_shape = (KPAD, 2 * LANES)
    rate_row = row_iota(rate_shape)
    rate = jnp.zeros(rate_shape, F32)
    for k in range(everyone):
        rate = jnp.where(rate_row == k, rates_ref[k], rate)

    for start in range(0, span, 2 * LANES):
        size = min(2 * LANES, span - start)
        modes = dot(left, eh[:, start:start + size])
        modes = modes[0:tall_rows] + modes[tall_rows:]
        place = start + lane_iota((1, size))
        damped = []
        for pp in range(4):
            degree = jnp.where(place > seconds[pp], place - 1, place + waves[pp])
            tau = (degree * (degree + 1)).astype(F32) * (1.0 / float(cut_off * (cut_off + 1)))
            factor = 1.0 / (1.0 + tau * rate[:, 0:size])
            at = 2 * pp * KPAD
            damped.append(modes[at:at + KPAD] * factor)
            damped.append(modes[at + KPAD:at + 2 * KPAD] * factor)
        damped = jnp.concatenate(damped, axis=0).astype(BF16)
        spec = dot(bk[...], damped)
        spec = spec[0:4 * FPAD] + spec[4 * FPAD:]
        sq[:, start:start + size] = spec.astype(BF16)
        kept = min(size, places - start)
        for pp in range(4):
            for f in range(everyone):
                at = pp * FPAD + 2 * f
                spec_ref[f, pp, :, start:start + kept] = spec[at:at + 2, 0:kept]

    sums = dot_nt(eh[...], sq[...])
    for r in range(rows):
        for i8 in range(8):
            at = (r * 8 + i8) * lats
            pp = i8 // 2
            tile = sums[at:at + lats, LANES * (pp // 2):LANES * (pp // 2 + 1)]
            if pp % 2:
                tile = pltpu.roll(tile, 64, 1)
            cs[pl.ds(pl.multiple_of(step * 2 * eight + at, 8), lats), :] = tile

    @pl.when(step == groups - 1)
    def _():
        lane = lane_iota((8, LANES))
        for holder in range(holders):
            lat = band_ref[holder]
            tiles = [jnp.zeros((8, LANES), F32) for _ in range(groups_f)]
            for t in range(groups):
                for r in range(rows):
                    put = unit * t + wf * r
                    piece = cs[pl.ds((t * rows + r) * eight + lat, 8, stride=lats), :]
                    keep = (lane >= put) & (lane < put + wf)
                    for g in range(groups_f):
                        moved = pltpu.roll(piece, (put - wf * g) % LANES, 1)
                        tiles[g] = jnp.where(keep, moved, tiles[g])
            for g in range(groups_f):
                out_ref[holder * groups_f + g] = tiles[g]


def per_device(grid, row_lengths, band_map, fold_map, legendre, to_modes, back_modes, mode_rates):
    fields, single, rows, width = grid.shape
    pairs, places, lats = legendre.shape
    cut_off = places - 2
    everyone = to_modes.shape[0]
    owners, per_owner = fold_map.shape
    groups = -(-per_owner // 8)
    slots = owners * groups * 8
    chunks = -(-(width // 4) // LANES)
    across = chunks * LANES
    span = -(-places // LANES) * LANES
    smem = pl.BlockSpec(memory_space=pltpu.SMEM)
    vmem = pl.BlockSpec(memory_space=pltpu.VMEM)
    room = pltpu.CompilerParams(vmem_limit_bytes=48 * 1024 * 1024)
    message = jax.ShapeDtypeStruct((owners, 8, LANES), F32)

    sending, cos_table, sin_table, first_factor, second_factor = pl.pallas_call(
        functools.partial(forward_kernel, cut_off, groups),
        out_shape=(
            message,
            jax.ShapeDtypeStruct((slots, across), BF16),
            jax.ShapeDtypeStruct((slots, across), BF16),
            jax.ShapeDtypeStruct((slots, LANES), F32),
            jax.ShapeDtypeStruct((slots, LANES), F32),
        ),
        in_specs=[smem, smem, vmem, vmem],
        out_specs=(vmem,) * 5,
        scratch_shapes=[
            pltpu.VMEM((LANES, LANES), F32),
            pltpu.VMEM((slots, LANES), F32),
            pltpu.VMEM((slots, LANES), F32),
            pltpu.VMEM((slots, LANES), F32),
            pltpu.VMEM((16, 4 * across), F32),
            pltpu.VMEM((LANES, across), BF16),
            pltpu.VMEM((slots, LANES), F32),
        ],
        compiler_params=room,
        name="forward_rows",
    )(row_lengths, band_map, fold_map, grid)

    arrived = lax.all_to_all(sending, ("lat", "fld"), split_axis=0, concat_axis=0, tiled=True)

    spectral, leaving = pl.pallas_call(
        functools.partial(spectral_kernel, cut_off, pairs, fields, rows),
        grid=(groups,),
        out_shape=(jax.ShapeDtypeStruct((everyone, pairs, 2, places), F32), message),
        in_specs=[
            smem,
            smem,
            smem,
            pl.BlockSpec((owners, 8, LANES), lambda t: (0, 0, 0)),
            pl.BlockSpec((4, lats, places), lambda t: (t, 0, 0)),
            pl.BlockSpec((everyone, everyone), lambda t: (0, 0)),
            pl.BlockSpec((everyone, everyone), lambda t: (0, 0)),
        ],
        out_specs=(
            pl.BlockSpec((everyone, 4, 2, places), lambda t: (0, t, 0, 0)),
            pl.BlockSpec((owners, 8, LANES), lambda t: (0, 0, 0)),
        ),
        scratch_shapes=[
            pltpu.VMEM((owners * 8, LANES), F32),
            pltpu.VMEM((groups * 4 * KPAD, 8 * lats), F32),
            pltpu.VMEM((8 * FPAD, 8 * KPAD), BF16),
            pltpu.VMEM((KPAD, LANES), F32),
            pltpu.VMEM((16 * lats, span), BF16),
            pltpu.VMEM((4 * FPAD, span), BF16),
            pltpu.VMEM((groups * 16 * lats, LANES), F32),
        ],
        compiler_params=pltpu.CompilerParams(
            dimension_semantics=("arbitrary",), vmem_limit_bytes=48 * 1024 * 1024
        ),
        name="spectral_solve",
    )(band_map, fold_map, mode_rates, arrived, jnp.transpose(legendre, (0, 2, 1)), to_modes, back_modes)

    returned = lax.all_to_all(leaving, ("lat", "fld"), split_axis=0, concat_axis=0, tiled=True)

    grid_out = pl.pallas_call(
        functools.partial(inverse_kernel, groups),
        out_shape=jax.ShapeDtypeStruct(grid.shape, BF16),
        in_specs=[smem, smem, vmem, vmem, vmem, vmem, vmem],
        out_specs=vmem,
        scratch_shapes=[
            pltpu.VMEM((owners, groups, 8, LANES), F32),
            pltpu.VMEM((16 * chunks, 4 * LANES), BF16),
        ],
        compiler_params=room,
        name="inverse_rows",
    )(row_lengths, band_map, returned, cos_table, sin_table, first_factor, second_factor)
    return (jnp.transpose(spectral, (0, 2, 1, 3)), grid_out)


def solution(mesh):
    placed = (
        P("fld", "lat", None, None),
        P(),
        P(),
        P(),
        P(("lat", "fld"), None, None),
        P(),
        P(),
        P(),
    )
    return jax.shard_map(
        per_device,
        mesh=mesh,
        in_specs=placed,
        out_specs=(P(None, None, ("lat", "fld"), None), P("fld", "lat", None, None)),
        check_vma=False,
    )
```

```python
import functools
import math

import jax
import jax.numpy as jnp
from jax import lax
from jax.experimental import pallas as pl
from jax.experimental.pallas import tpu as pltpu
from jax.sharding import PartitionSpec as P

LANES = 128
KPAD = 24
FPAD = 64
ROOM = 24 * 1024 * 1024
F32 = jnp.float32
BF16 = jnp.bfloat16
NT_DIMS = (((1,), (1,)), ((), ()))
SIN_POLY = (
    6.283185302447051,
    -41.34170038368319,
    81.60513023312113,
    -76.70299324464969,
    42.02573766814694,
    -14.899106966102595,
    3.237062655726421,
)
COS_POLY = (
    0.9999999889083757,
    -19.739204448887243,
    64.93911476570418,
    -85.45008785413638,
    60.167188450194914,
    -25.9658703083255,
    6.526145851512229,
)


def dot(a, b):
    return jnp.dot(a, b, preferred_element_type=F32)


def dot_nt(a, b):
    return lax.dot_general(a, b, NT_DIMS, preferred_element_type=F32)


def split(x):
    high = x.astype(BF16)
    return high, (x - high.astype(F32)).astype(BF16)


def horner(coefs, z):
    total = coefs[-1] * z + coefs[-2]
    for coef in coefs[-3::-1]:
        total = total * z + coef
    return total


def turn(steps, period, inverse):
    rest = steps - period * jnp.floor(steps * inverse + 0.5)
    part = rest * inverse
    z = part * part
    return horner(COS_POLY, z), part * horner(SIN_POLY, z)


def fetch_all(sources, targets, sems):
    copies = [
        pltpu.make_async_copy(source, target, sems.at[i])
        for i, (source, target) in enumerate(zip(sources, targets))
    ]
    for copy in copies:
        copy.start()
    for copy in copies:
        copy.wait()


def lane_iota(shape):
    return lax.broadcasted_iota(jnp.int32, shape, len(shape) - 1)


def row_iota(shape):
    return lax.broadcasted_iota(jnp.int32, shape, len(shape) - 2)


def spread_matrix():
    shape = (4 * LANES, LANES)
    picks = []
    for phase in range(4):
        picks.append(jnp.where(row_iota(shape) == 4 * lane_iota(shape) + phase, 1.0, 0.0))
    return jnp.concatenate(picks, axis=1).astype(BF16)


def forward_kernel(
    cut_off, groups, len_hbm, band_hbm, fold_hbm, grid_hbm,
    msg_ref, cos_ref, sin_ref, k1_ref, k2_ref,
    len_ref, band_ref, fold_ref, grid_ref, sems, fold_s, mb, cb, sb, xs, xq, ys,
):
    fetch_all(
        (len_hbm, band_hbm, fold_hbm, grid_hbm), (len_ref, band_ref, fold_ref, grid_ref), sems
    )
    fields, _, rows, width = grid_ref.shape
    owners, per_owner = fold_ref.shape
    slots, across = cos_ref.shape
    chunks = across // LANES
    padded = groups * 8
    unit = rows * fields * 2
    length = len_ref[band_ref[lax.axis_index("lat")]]
    top = jnp.minimum(cut_off, (length - 1) // 2)

    fold_s[...] = jnp.full(fold_s.shape, -1.0, F32)
    fold_s[0:owners, 0:per_owner] = fold_ref[...].astype(F32)
    waves = jnp.transpose(fold_s[...])[0:padded]
    small = waves.shape
    period = jnp.full(small, length // 4, jnp.int32).astype(F32)
    step_c, step_s = turn(waves * float(LANES), period, 1.0 / period)
    for owner in range(owners):
        put = pl.ds(owner * padded, padded)
        wide = (padded, LANES)
        mb[put, :] = jnp.broadcast_to(waves[:, owner:owner + 1], wide)
        cb[put, :] = jnp.broadcast_to(step_c[:, owner:owner + 1], wide)
        sb[put, :] = jnp.broadcast_to(step_s[:, owner:owner + 1], wide)

    xs[...] = jnp.zeros(xs.shape, F32)
    inside = lane_iota((rows, width)) < length
    for field in range(fields):
        points = grid_ref[field, 0].astype(F32)
        xs[rows * field:rows * (field + 1), 0:width] = jnp.where(inside, points, 0.0)
    stacked = jnp.concatenate(
        [xs[:, 4 * LANES * c:4 * LANES * (c + 1)] for c in range(chunks)], axis=0
    ).astype(BF16)
    phases = dot(stacked, spread_matrix()).astype(BF16)
    for c in range(chunks):
        for phase in range(4):
            piece = phases[16 * c:16 * (c + 1), LANES * phase:LANES * (phase + 1)]
            for half in (0, 64):
                xq[half + 16 * phase:half + 16 * (phase + 1), LANES * c:LANES * (c + 1)] = piece

    block = 32
    shape = (block, LANES)
    lane = lane_iota(shape)
    lane_f = lane.astype(F32)
    phase_f = ((lane % 64) // 16).astype(F32)
    quarter_v = jnp.full(shape, length // 4, jnp.int32).astype(F32)
    quarter_i = 1.0 / quarter_v
    length_v = jnp.full(shape, length, jnp.int32).astype(F32)
    length_i = 1.0 / length_v
    top_v = jnp.full(shape, top, jnp.int32).astype(F32)

    def table_block(i, carry):
        at = pl.ds(pl.multiple_of(i * block, block), block)
        wave = mb[at, :]
        c1 = cb[at, :]
        s1 = sb[at, :]
        c_old, s_old = turn(wave * lane_f, quarter_v, quarter_i)
        c_now = c_old * c1 - s_old * s1
        s_now = s_old * c1 + c_old * s1
        twice = c1 + c1
        cos_ref[at, 0:LANES] = c_old.astype(BF16)
        sin_ref[at, 0:LANES] = s_old.astype(BF16)
        for c in range(1, chunks):
            cos_ref[at, LANES * c:LANES * (c + 1)] = c_now.astype(BF16)
            sin_ref[at, LANES * c:LANES * (c + 1)] = s_now.astype(BF16)
            c_old, c_now = c_now, twice * c_now - c_old
            s_old, s_now = s_now, twice * s_now - s_old
        co, si = turn(wave * phase_f, length_v, length_i)
        weight = jnp.where(wave == 0.0, 1.0, 2.0)
        weight = jnp.where((wave >= 0.0) & (wave <= top_v), weight, 0.0)
        upper = lane >= 64
        k1_ref[at, :] = jnp.where(upper, -si, co) * weight
        k2_ref[at, :] = jnp.where(upper, co, si) * weight
        return carry

    lax.fori_loop(0, slots // block, table_block, 0)

    big = 256
    values = xq[...]

    def dot_block(i, carry):
        at = pl.ds(pl.multiple_of(i * big, big), big)
        both = jnp.concatenate([cos_ref[at, :], sin_ref[at, :]], axis=0)
        inner = dot_nt(both, values)
        fix = jnp.where(mb[at, :] == 0.0, 1.0, 0.5)
        ys[at, :] = (inner[0:big] * k1_ref[at, :] - inner[big:2 * big] * k2_ref[at, :]) * fix
        return carry

    lax.fori_loop(0, slots // big, dot_block, 0)

    turned = ys[...].reshape(owners, groups, 8, LANES)
    shape = (LANES, LANES)
    source = row_iota(shape)
    target = lane_iota(shape)
    vec = source % 16
    base = (vec % rows) * (fields * 2) + (vec // rows) * 2 + source // 64
    total = jnp.zeros((owners * 8, LANES), F32)
    for t in range(groups):
        place = jnp.where((vec < rows * fields) & (target == base + unit * t), 1.0, 0.0).astype(BF16)
        high, low = split(turned[:, t].reshape(owners * 8, LANES))
        total = total + dot(
            jnp.concatenate([high, low], axis=1), jnp.concatenate([place, place], axis=0)
        )
    scale = 1.0 / jnp.sqrt(jnp.full((owners * 8, LANES), length, jnp.int32).astype(F32))
    msg_ref[...] = (total * scale).reshape(owners, 8, LANES)


def inverse_kernel(
    groups, len_hbm, band_hbm, msg_ref, cos_ref, sin_ref, k1_ref, k2_ref, grid_ref,
    len_ref, band_ref, sems, zs, os,
):
    fetch_all((len_hbm, band_hbm), (len_ref, band_ref), sems)
    fields, _, rows, width = grid_ref.shape
    owners = msg_ref.shape[0]
    slots, across = cos_ref.shape
    chunks = across // LANES
    unit = rows * fields * 2
    length = len_ref[band_ref[lax.axis_index("lat")]]
    high, low = split(msg_ref[...].reshape(owners * 8, LANES))
    pieces = jnp.concatenate([high, low], axis=1)
    shape = (LANES, 2 * LANES)
    source = row_iota(shape)
    target = lane_iota(shape)
    vec = target % 16
    upper = (target % LANES) >= 64
    imag = target >= LANES
    base = (vec % rows) * (fields * 2) + (vec // rows) * 2 + jnp.where(imag, 1, 0)
    sign = jnp.where(upper != imag, -1.0, 1.0)
    factor_a = k1_ref[...].reshape(owners, groups, 8, LANES)
    factor_b = k2_ref[...].reshape(owners, groups, 8, LANES)
    for t in range(groups):
        place = jnp.where((vec < rows * fields) & (source == base + unit * t), sign, 0.0).astype(BF16)
        both = dot(pieces, jnp.concatenate([place, place], axis=0))
        z = (
            both[:, 0:LANES] * factor_a[:, t].reshape(owners * 8, LANES)
            + both[:, LANES:] * factor_b[:, t].reshape(owners * 8, LANES)
        )
        zs[:, t] = z.reshape(owners, 8, LANES)
    turned = jnp.transpose(zs[...].reshape(slots, LANES)).astype(BF16)
    real = turned[0:64]
    imag_part = turned[64:128]
    scale = 1.0 / jnp.sqrt(jnp.full((64, 2 * LANES), length, jnp.int32).astype(F32))
    for start in range(0, across, 2 * LANES):
        size = min(2 * LANES, across - start)
        total = dot(real, cos_ref[:, start:start + size]) - dot(imag_part, sin_ref[:, start:start + size])
        out = total * scale[:, 0:size]
        for phase in range(4):
            for sub in range(size // LANES):
                c = start // LANES + sub
                os[16 * c:16 * (c + 1), LANES * phase:LANES * (phase + 1)] = out[
                    16 * phase:16 * (phase + 1), LANES * sub:LANES * (sub + 1)
                ].astype(BF16)
    merged = dot_nt(os[...], spread_matrix())
    for c in range(chunks):
        begin = 4 * LANES * c
        size = min(4 * LANES, width - begin)
        if size <= 0:
            continue
        inside = begin + lane_iota((16, size)) < length
        piece = jnp.where(inside, merged[16 * c:16 * (c + 1), 0:size], 0.0)
        for field in range(fields):
            grid_ref[field, 0, :, begin:begin + size] = piece[
                rows * field:rows * (field + 1)
            ].astype(BF16)


def prepare_kernel(
    cut_off, pairs, fields, rows, fold_hbm, rates_hbm, leg_hbm, tm_hbm, bm_hbm,
    eh_ref, factor_ref, mix_ref, back_ref,
    fold_ref, rates_ref, leg_ref, tm_ref, bm_ref, sems, pad_s,
):
    fetch_all(
        (fold_hbm, rates_hbm, leg_hbm, tm_hbm, bm_hbm),
        (fold_ref, rates_ref, leg_ref, tm_ref, bm_ref),
        sems,
    )
    everyone = tm_ref.shape[0]
    _, lats, places = leg_ref.shape
    groups_f = everyone // fields
    wf = fields * 2
    span = eh_ref.shape[1]
    eight = 8 * lats
    groups = eh_ref.shape[0] // (2 * eight)
    owner = lax.axis_index("lat") * groups_f + lax.axis_index("fld")

    pad_s[...] = jnp.zeros(pad_s.shape, F32)
    pad_s[0:everyone, 0:everyone] = tm_ref[...]
    m_high, m_low = split(pad_s[...])
    shape = (LANES, LANES)
    level = (lane_iota(shape) % wf) // 2
    wide = []
    for piece in (m_high, m_low):
        parts = []
        for g in range(groups_f):
            pick = jnp.where(row_iota(shape) == fields * g + level, 1.0, 0.0).astype(BF16)
            parts.append(dot(piece, pick))
        wide.append(jnp.concatenate(parts, axis=1))
    lane = lane_iota(wide[0].shape) % LANES
    for part, piece in enumerate(wide):
        for t in range(groups):
            total = []
            for r in range(rows):
                for c in range(2):
                    keep = (lane // wf == t * rows + r) & (lane % 2 == c)
                    total.append(jnp.where(keep, piece, 0.0))
            at = (part * groups + t) * 4 * KPAD
            mix_ref[at:at + 4 * KPAD, :] = jnp.concatenate(total, axis=0).astype(BF16)

    pad_s[...] = jnp.zeros(pad_s.shape, F32)
    pad_s[0:everyone, 0:everyone] = bm_ref[...]
    shape = (FPAD, KPAD)
    expand = jnp.where(row_iota(shape) // 2 == lane_iota(shape), 1.0, 0.0).astype(BF16)
    shape = (LANES, 8 * KPAD)
    repeat = jnp.where(row_iota(shape) == lane_iota(shape) % KPAD, 1.0, 0.0).astype(BF16)
    shape = (FPAD, 8 * KPAD)
    same = row_iota(shape) % 2 == (lane_iota(shape) // KPAD) % 2
    for part, piece in enumerate(split(pad_s[...])):
        full = dot(dot(expand, piece).astype(BF16), repeat)
        back_ref[part * FPAD:(part + 1) * FPAD, :] = jnp.where(same, full, 0.0).astype(BF16)

    rate_row = row_iota((KPAD, LANES))
    rate = jnp.zeros((KPAD, LANES), F32)
    for k in range(everyone):
        rate = jnp.where(rate_row == k, rates_ref[k], rate)
    rate = jnp.concatenate([rate] * (span // LANES), axis=1)

    whole = places // LANES * LANES
    shape = (lats, span)
    place = lane_iota(shape)

    def pair_block(pair, carry):
        there = pair < pairs
        index = jnp.minimum(pair, pairs - 1)
        wave = fold_ref[owner, 2 * index]
        limit = jnp.where(there, cut_off - wave, -1)
        last = jnp.where(there, places - 1, -1)
        leg = jnp.concatenate(
            [
                leg_ref[index, :, 0:whole],
                jnp.broadcast_to(leg_ref[index, :, whole:places], (lats, span - whole)),
            ],
            axis=1,
        )
        first = place <= limit
        second = (place > limit) & (place <= last)
        odd = ((place + jnp.where(first, 0, wave)) & 1) == 1
        signed = jnp.where(odd, -leg, leg)
        base = (pair // 4) * 2 * eight + (pair % 4) * 2 * lats
        for r, rowset in enumerate((leg, signed)):
            eh_ref[pl.ds(pl.multiple_of(base + r * eight, 16), 2 * lats), :] = jnp.concatenate(
                [jnp.where(first, rowset, 0.0), jnp.where(second, rowset, 0.0)], axis=0
            ).astype(BF16)
        row = lane_iota((1, span))
        degree = jnp.where(row > limit, row - 1, row + wave)
        tau = (degree * (degree + 1)).astype(F32) * (1.0 / float(cut_off * (cut_off + 1)))
        factor_ref[pl.ds(pl.multiple_of(pair * KPAD, 8), KPAD), :] = 1.0 / (1.0 + tau * rate)
        return carry

    lax.fori_loop(0, 4 * groups, pair_block, 0)


def solve_kernel(
    fields, rows, band_hbm, msg_ref, eh_ref, factor_ref, mix_ref, back_ref,
    damped_ref, out_ref,
    band_ref, sems, vs, fq, sums, cs,
):
    fetch_all((band_hbm,), (band_ref,), sems)
    holders = band_ref.shape[0]
    groups_f = msg_ref.shape[0] // holders
    lats = holders
    groups = fq.shape[0] // (4 * KPAD)
    wf = fields * 2
    unit = rows * wf
    span = eh_ref.shape[1]
    eight = 8 * lats
    for holder in range(holders):
        lat = band_ref[holder]
        for g in range(groups_f):
            vs[pl.ds(pl.multiple_of((g * lats + lat) * 8, 8), 8), :] = msg_ref[holder * groups_f + g]
    tall = []
    for i8 in range(8):
        tall.append(
            jnp.concatenate(
                [vs[pl.ds(g * lats * 8 + i8, lats, stride=8), :] for g in range(groups_f)], axis=1
            )
        )
    v_high, v_low = split(jnp.concatenate(tall, axis=0))
    half = mix_ref.shape[0] // 2
    mix_h = mix_ref[0:half, :]
    fq[...] = dot_nt(mix_h, v_high) + dot_nt(mix_ref[half:, :], v_high) + dot_nt(mix_h, v_low)
    tall_rows = 8 * KPAD

    def quad_block(t, carry):
        mixed = fq[pl.ds(pl.multiple_of(t * 4 * KPAD, 8), 4 * KPAD), :]
        mixed = jnp.concatenate([mixed[0:2 * KPAD], mixed[2 * KPAD:4 * KPAD]], axis=1)
        slot_pair = (lane_iota(mixed.shape) % eight) // (2 * lats)
        left = jnp.concatenate([jnp.where(slot_pair == pp, mixed, 0.0) for pp in range(4)], axis=0)
        left = jnp.concatenate(split(left), axis=0)
        legs = pl.ds(pl.multiple_of(t * 2 * eight, 16), 2 * eight)
        deep = pl.ds(pl.multiple_of(t * tall_rows, 16), tall_rows)
        factor_at = pl.multiple_of(t * 4 * KPAD, 8)
        for start in range(0, span, 2 * LANES):
            size = min(2 * LANES, span - start)
            modes = dot(left, eh_ref[legs, start:start + size])
            modes = modes[0:tall_rows] + modes[tall_rows:]
            damped = []
            for pp in range(4):
                factor = factor_ref[pl.ds(factor_at + pp * KPAD, KPAD), start:start + size]
                at = 2 * pp * KPAD
                damped.append(modes[at:at + KPAD] * factor)
                damped.append(modes[at + KPAD:at + 2 * KPAD] * factor)
            damped_ref[deep, start:start + size] = jnp.concatenate(damped, axis=0).astype(BF16)
        sums[legs, :] = dot_nt(eh_ref[legs, :], damped_ref[deep, :])
        return carry

    lax.fori_loop(0, groups, quad_block, 0)

    everything = sums[...]
    own = (row_iota(everything.shape) // lats) % 8 // 2 == lane_iota(everything.shape) // (2 * KPAD)
    own_h, own_l = split(jnp.where(own, everything, 0.0))
    back_h = back_ref[0:FPAD, :]
    cs[:, 0:FPAD] = dot_nt(own_h, back_h) + dot_nt(own_l, back_h) + dot_nt(own_h, back_ref[FPAD:, :])

    lane = lane_iota((8, LANES))
    for holder in range(holders):
        lat = band_ref[holder]
        tiles = [jnp.zeros((8, LANES), F32) for _ in range(groups_f)]
        for t in range(groups):
            for r in range(rows):
                put = unit * t + wf * r
                piece = cs[pl.ds((t * rows + r) * eight + lat, 8, stride=lats), :]
                keep = (lane >= put) & (lane < put + wf)
                for g in range(groups_f):
                    moved = pltpu.roll(piece, (put - wf * g) % LANES, 1)
                    tiles[g] = jnp.where(keep, moved, tiles[g])
        for g in range(groups_f):
            out_ref[holder * groups_f + g] = tiles[g]


def output_kernel(damped_ref, back_ref, spec_ref, bk):
    everyone, quad, _, places = spec_ref.shape
    span = damped_ref.shape[1]

    @pl.when(pl.program_id(0) == 0)
    def _():
        shape = (FPAD, 8 * KPAD)
        pair_of = lane_iota(shape) // (2 * KPAD)
        for part in range(2):
            full = back_ref[part * FPAD:(part + 1) * FPAD, :].astype(F32)
            for pp in range(4):
                at = (4 * part + pp) * FPAD
                bk[at:at + FPAD, :] = jnp.where(pair_of == pp, full, 0.0).astype(BF16)

    for start in range(0, span, 2 * LANES):
        size = min(2 * LANES, span - start)
        spec = dot(bk[...], damped_ref[:, start:start + size])
        spec = spec[0:4 * FPAD] + spec[4 * FPAD:]
        kept = min(size, places - start)
        for pp in range(4):
            for f in range(everyone):
                at = pp * FPAD + 2 * f
                spec_ref[f, pp, :, start:start + kept] = spec[at:at + 2, 0:kept]


def per_device(grid, row_lengths, band_map, fold_map, legendre, to_modes, back_modes, mode_rates):
    fields, single, rows, width = grid.shape
    pairs, places, lats = legendre.shape
    cut_off = places - 2
    everyone = to_modes.shape[0]
    owners, per_owner = fold_map.shape
    groups = -(-per_owner // 8)
    slots = owners * groups * 8
    chunks = -(-(width // 4) // LANES)
    across = chunks * LANES
    span = -(-places // LANES) * LANES
    hbm = pl.BlockSpec(memory_space=pltpu.HBM)
    vmem = pl.BlockSpec(memory_space=pltpu.VMEM)
    room = pltpu.CompilerParams(vmem_limit_bytes=ROOM)
    message = jax.ShapeDtypeStruct((owners, 8, LANES), F32)
    holders = band_map.shape[0]
    groups_f = everyone // fields
    dma = pltpu.SemaphoreType.DMA

    sending, cos_table, sin_table, first_factor, second_factor = pl.pallas_call(
        functools.partial(forward_kernel, cut_off, groups),
        out_shape=(
            message,
            jax.ShapeDtypeStruct((slots, across), BF16),
            jax.ShapeDtypeStruct((slots, across), BF16),
            jax.ShapeDtypeStruct((slots, LANES), F32),
            jax.ShapeDtypeStruct((slots, LANES), F32),
        ),
        in_specs=[hbm] * 4,
        out_specs=(vmem,) * 5,
        scratch_shapes=[
            pltpu.SMEM(row_lengths.shape, jnp.int32),
            pltpu.SMEM(band_map.shape, jnp.int32),
            pltpu.VMEM(fold_map.shape, jnp.int32),
            pltpu.VMEM(grid.shape, BF16),
            dma((4,)),
            pltpu.VMEM((LANES, LANES), F32),
            pltpu.VMEM((slots, LANES), F32),
            pltpu.VMEM((slots, LANES), F32),
            pltpu.VMEM((slots, LANES), F32),
            pltpu.VMEM((16, 4 * across), F32),
            pltpu.VMEM((LANES, across), BF16),
            pltpu.VMEM((slots, LANES), F32),
        ],
        compiler_params=room,
        name="forward_rows",
    )(row_lengths, band_map, fold_map, grid)

    arrived = lax.all_to_all(sending, ("lat", "fld"), split_axis=0, concat_axis=0, tiled=True)

    legs, factors, mix, back = pl.pallas_call(
        functools.partial(prepare_kernel, cut_off, pairs, fields, rows),
        out_shape=(
            jax.ShapeDtypeStruct((groups * 16 * lats, span), BF16),
            jax.ShapeDtypeStruct((groups * 4 * KPAD, span), F32),
            jax.ShapeDtypeStruct((2 * groups * 4 * KPAD, groups_f * LANES), BF16),
            jax.ShapeDtypeStruct((2 * FPAD, 8 * KPAD), BF16),
        ),
        in_specs=[hbm] * 5,
        out_specs=(vmem,) * 4,
        scratch_shapes=[
            pltpu.SMEM(fold_map.shape, jnp.int32),
            pltpu.SMEM(mode_rates.shape, F32),
            pltpu.VMEM((pairs, lats, places), F32),
            pltpu.VMEM(to_modes.shape, F32),
            pltpu.VMEM(back_modes.shape, F32),
            dma((5,)),
            pltpu.VMEM((KPAD, LANES), F32),
        ],
        compiler_params=room,
        cost_estimate=pl.CostEstimate(flops=10**8, bytes_accessed=8 * 10**6, transcendentals=0),
        name="prepare",
    )(fold_map, mode_rates, jnp.transpose(legendre, (0, 2, 1)), to_modes, back_modes)

    damped, leaving = pl.pallas_call(
        functools.partial(solve_kernel, fields, rows),
        out_shape=(jax.ShapeDtypeStruct((groups * 8 * KPAD, span), BF16), message),
        in_specs=[hbm] + [vmem] * 5,
        out_specs=(vmem,) * 2,
        scratch_shapes=[
            pltpu.SMEM(band_map.shape, jnp.int32),
            dma((1,)),
            pltpu.VMEM((owners * 8, LANES), F32),
            pltpu.VMEM((groups * 4 * KPAD, 8 * lats), F32),
            pltpu.VMEM((groups * 16 * lats, 8 * KPAD), F32),
            pltpu.VMEM((groups * 16 * lats, LANES), F32),
        ],
        compiler_params=room,
        name="solve",
    )(band_map, arrived, legs, factors, mix, back)

    returned = lax.all_to_all(leaving, ("lat", "fld"), split_axis=0, concat_axis=0, tiled=True)

    spectral = pl.pallas_call(
        output_kernel,
        grid=(groups,),
        out_shape=jax.ShapeDtypeStruct((everyone, pairs, 2, places), F32),
        in_specs=[
            pl.BlockSpec((8 * KPAD, span), lambda t: (t, 0)),
            pl.BlockSpec((2 * FPAD, 8 * KPAD), lambda t: (0, 0)),
        ],
        out_specs=pl.BlockSpec((everyone, 4, 2, places), lambda t: (0, t, 0, 0)),
        scratch_shapes=[pltpu.VMEM((8 * FPAD, 8 * KPAD), BF16)],
        compiler_params=pltpu.CompilerParams(
            dimension_semantics=("arbitrary",), vmem_limit_bytes=ROOM
        ),
        cost_estimate=pl.CostEstimate(flops=10**8, bytes_accessed=8 * 10**6, transcendentals=0),
        name="spectral_output",
    )(damped, back)

    grid_out = pl.pallas_call(
        functools.partial(inverse_kernel, groups),
        out_shape=jax.ShapeDtypeStruct(grid.shape, BF16),
        in_specs=[hbm, hbm] + [vmem] * 5,
        out_specs=vmem,
        scratch_shapes=[
            pltpu.SMEM(row_lengths.shape, jnp.int32),
            pltpu.SMEM(band_map.shape, jnp.int32),
            dma((2,)),
            pltpu.VMEM((owners, groups, 8, LANES), F32),
            pltpu.VMEM((16 * chunks, 4 * LANES), BF16),
        ],
        compiler_params=room,
        name="inverse_rows",
    )(row_lengths, band_map, returned, cos_table, sin_table, first_factor, second_factor)
    return (jnp.transpose(spectral, (0, 2, 1, 3)), grid_out)


def solution(mesh):
    placed = (
        P("fld", "lat", None, None),
        P(),
        P(),
        P(),
        P(("lat", "fld"), None, None),
        P(),
        P(),
        P(),
    )
    return jax.shard_map(
        per_device,
        mesh=mesh,
        in_specs=placed,
        out_specs=(P(None, None, ("lat", "fld"), None), P("fld", "lat", None, None)),
        check_vma=False,
    )
```

```python
import functools
import math

import jax
import jax.numpy as jnp
from jax import lax
from jax.experimental import pallas as pl
from jax.experimental.pallas import tpu as pltpu
from jax.sharding import PartitionSpec as P

LANES = 128
KPAD = 24
FPAD = 64
ROOM = 24 * 1024 * 1024
F32 = jnp.float32
BF16 = jnp.bfloat16
NT_DIMS = (((1,), (1,)), ((), ()))
SIN_POLY = (
    6.283185302447051,
    -41.34170038368319,
    81.60513023312113,
    -76.70299324464969,
    42.02573766814694,
    -14.899106966102595,
    3.237062655726421,
)
COS_POLY = (
    0.9999999889083757,
    -19.739204448887243,
    64.93911476570418,
    -85.45008785413638,
    60.167188450194914,
    -25.9658703083255,
    6.526145851512229,
)


def dot(a, b):
    return jnp.dot(a, b, preferred_element_type=F32)


def dot_nt(a, b):
    return lax.dot_general(a, b, NT_DIMS, preferred_element_type=F32)


def split(x):
    high = x.astype(BF16)
    return high, (x - high.astype(F32)).astype(BF16)


def horner(coefs, z):
    total = coefs[-1] * z + coefs[-2]
    for coef in coefs[-3::-1]:
        total = total * z + coef
    return total


def turn(steps, period, inverse):
    rest = steps - period * jnp.floor(steps * inverse + 0.5)
    part = rest * inverse
    z = part * part
    return horner(COS_POLY, z), part * horner(SIN_POLY, z)


def fetch_all(sources, targets, sems):
    copies = [
        pltpu.make_async_copy(source, target, sems.at[i])
        for i, (source, target) in enumerate(zip(sources, targets))
    ]
    for copy in copies:
        copy.start()
    for copy in copies:
        copy.wait()


def lane_iota(shape):
    return lax.broadcasted_iota(jnp.int32, shape, len(shape) - 1)


def row_iota(shape):
    return lax.broadcasted_iota(jnp.int32, shape, len(shape) - 2)


def spread_matrix():
    shape = (4 * LANES, LANES)
    picks = []
    for phase in range(4):
        picks.append(jnp.where(row_iota(shape) == 4 * lane_iota(shape) + phase, 1.0, 0.0))
    return jnp.concatenate(picks, axis=1).astype(BF16)


def forward_kernel(
    cut_off, groups, len_hbm, band_hbm, fold_hbm, grid_hbm,
    msg_ref, cos_ref, sin_ref, k1_ref, k2_ref,
    len_ref, band_ref, fold_ref, grid_ref, sems, fold_s, mb, cb, sb, xs, xq, ys,
):
    fetch_all(
        (len_hbm, band_hbm, fold_hbm, grid_hbm), (len_ref, band_ref, fold_ref, grid_ref), sems
    )
    fields, _, rows, width = grid_ref.shape
    owners, per_owner = fold_ref.shape
    slots, across = cos_ref.shape
    chunks = across // LANES
    padded = groups * 8
    unit = rows * fields * 2
    length = len_ref[band_ref[lax.axis_index("lat")]]
    top = jnp.minimum(cut_off, (length - 1) // 2)

    fold_s[...] = jnp.full(fold_s.shape, -1.0, F32)
    fold_s[0:owners, 0:per_owner] = fold_ref[...].astype(F32)
    waves = jnp.transpose(fold_s[...])[0:padded]
    small = waves.shape
    period = jnp.full(small, length // 4, jnp.int32).astype(F32)
    step_c, step_s = turn(waves * float(LANES), period, 1.0 / period)
    for owner in range(owners):
        put = pl.ds(owner * padded, padded)
        wide = (padded, LANES)
        mb[put, :] = jnp.broadcast_to(waves[:, owner:owner + 1], wide)
        cb[put, :] = jnp.broadcast_to(step_c[:, owner:owner + 1], wide)
        sb[put, :] = jnp.broadcast_to(step_s[:, owner:owner + 1], wide)

    xs[...] = jnp.zeros(xs.shape, F32)
    inside = lane_iota((rows, width)) < length
    for field in range(fields):
        points = grid_ref[field, 0].astype(F32)
        xs[rows * field:rows * (field + 1), 0:width] = jnp.where(inside, points, 0.0)
    stacked = jnp.concatenate(
        [xs[:, 4 * LANES * c:4 * LANES * (c + 1)] for c in range(chunks)], axis=0
    ).astype(BF16)
    phases = dot(stacked, spread_matrix()).astype(BF16)
    for c in range(chunks):
        for phase in range(4):
            piece = phases[16 * c:16 * (c + 1), LANES * phase:LANES * (phase + 1)]
            for half in (0, 64):
                xq[half + 16 * phase:half + 16 * (phase + 1), LANES * c:LANES * (c + 1)] = piece

    block = 32
    shape = (block, LANES)
    lane = lane_iota(shape)
    lane_f = lane.astype(F32)
    phase_f = ((lane % 64) // 16).astype(F32)
    quarter_v = jnp.full(shape, length // 4, jnp.int32).astype(F32)
    quarter_i = 1.0 / quarter_v
    length_v = jnp.full(shape, length, jnp.int32).astype(F32)
    length_i = 1.0 / length_v
    top_v = jnp.full(shape, top, jnp.int32).astype(F32)

    def table_block(i, carry):
        at = pl.ds(pl.multiple_of(i * block, block), block)
        wave = mb[at, :]
        c1 = cb[at, :]
        s1 = sb[at, :]
        c_old, s_old = turn(wave * lane_f, quarter_v, quarter_i)
        c_now = c_old * c1 - s_old * s1
        s_now = s_old * c1 + c_old * s1
        twice = c1 + c1
        cos_ref[at, 0:LANES] = c_old.astype(BF16)
        sin_ref[at, 0:LANES] = s_old.astype(BF16)
        for c in range(1, chunks):
            cos_ref[at, LANES * c:LANES * (c + 1)] = c_now.astype(BF16)
            sin_ref[at, LANES * c:LANES * (c + 1)] = s_now.astype(BF16)
            c_old, c_now = c_now, twice * c_now - c_old
            s_old, s_now = s_now, twice * s_now - s_old
        co, si = turn(wave * phase_f, length_v, length_i)
        weight = jnp.where(wave == 0.0, 1.0, 2.0)
        weight = jnp.where((wave >= 0.0) & (wave <= top_v), weight, 0.0)
        upper = lane >= 64
        k1_ref[at, :] = jnp.where(upper, -si, co) * weight
        k2_ref[at, :] = jnp.where(upper, co, si) * weight
        return carry

    lax.fori_loop(0, slots // block, table_block, 0)

    big = 256
    values = xq[...]

    def dot_block(i, carry):
        at = pl.ds(pl.multiple_of(i * big, big), big)
        both = jnp.concatenate([cos_ref[at, :], sin_ref[at, :]], axis=0)
        inner = dot_nt(both, values)
        fix = jnp.where(mb[at, :] == 0.0, 1.0, 0.5)
        ys[at, :] = (inner[0:big] * k1_ref[at, :] - inner[big:2 * big] * k2_ref[at, :]) * fix
        return carry

    lax.fori_loop(0, slots // big, dot_block, 0)

    turned = ys[...].reshape(owners, groups, 8, LANES)
    shape = (LANES, LANES)
    source = row_iota(shape)
    target = lane_iota(shape)
    vec = source % 16
    base = (vec % rows) * (fields * 2) + (vec // rows) * 2 + source // 64
    total = jnp.zeros((owners * 8, LANES), F32)
    for t in range(groups):
        place = jnp.where((vec < rows * fields) & (target == base + unit * t), 1.0, 0.0).astype(BF16)
        high, low = split(turned[:, t].reshape(owners * 8, LANES))
        total = total + dot(
            jnp.concatenate([high, low], axis=1), jnp.concatenate([place, place], axis=0)
        )
    scale = 1.0 / jnp.sqrt(jnp.full((owners * 8, LANES), length, jnp.int32).astype(F32))
    msg_ref[...] = (total * scale).reshape(owners, 8, LANES)


def inverse_kernel(
    groups, len_hbm, band_hbm, msg_ref, cos_ref, sin_ref, k1_ref, k2_ref, grid_ref,
    len_ref, band_ref, sems, zs, os,
):
    fetch_all((len_hbm, band_hbm), (len_ref, band_ref), sems)
    fields, _, rows, width = grid_ref.shape
    owners = msg_ref.shape[0]
    slots, across = cos_ref.shape
    chunks = across // LANES
    unit = rows * fields * 2
    length = len_ref[band_ref[lax.axis_index("lat")]]
    high, low = split(msg_ref[...].reshape(owners * 8, LANES))
    pieces = jnp.concatenate([high, low], axis=1)
    shape = (LANES, 2 * LANES)
    source = row_iota(shape)
    target = lane_iota(shape)
    vec = target % 16
    upper = (target % LANES) >= 64
    imag = target >= LANES
    base = (vec % rows) * (fields * 2) + (vec // rows) * 2 + jnp.where(imag, 1, 0)
    sign = jnp.where(upper != imag, -1.0, 1.0)
    factor_a = k1_ref[...].reshape(owners, groups, 8, LANES)
    factor_b = k2_ref[...].reshape(owners, groups, 8, LANES)
    for t in range(groups):
        place = jnp.where((vec < rows * fields) & (source == base + unit * t), sign, 0.0).astype(BF16)
        both = dot(pieces, jnp.concatenate([place, place], axis=0))
        z = (
            both[:, 0:LANES] * factor_a[:, t].reshape(owners * 8, LANES)
            + both[:, LANES:] * factor_b[:, t].reshape(owners * 8, LANES)
        )
        zs[:, t] = z.reshape(owners, 8, LANES)
    turned = jnp.transpose(zs[...].reshape(slots, LANES)).astype(BF16)
    real = turned[0:64]
    imag_part = turned[64:128]
    scale = 1.0 / jnp.sqrt(jnp.full((64, 2 * LANES), length, jnp.int32).astype(F32))
    for start in range(0, across, 2 * LANES):
        size = min(2 * LANES, across - start)
        total = dot(real, cos_ref[:, start:start + size]) - dot(imag_part, sin_ref[:, start:start + size])
        out = total * scale[:, 0:size]
        for phase in range(4):
            for sub in range(size // LANES):
                c = start // LANES + sub
                os[16 * c:16 * (c + 1), LANES * phase:LANES * (phase + 1)] = out[
                    16 * phase:16 * (phase + 1), LANES * sub:LANES * (sub + 1)
                ].astype(BF16)
    merged = dot_nt(os[...], spread_matrix())
    for c in range(chunks):
        begin = 4 * LANES * c
        size = min(4 * LANES, width - begin)
        if size <= 0:
            continue
        inside = begin + lane_iota((16, size)) < length
        piece = jnp.where(inside, merged[16 * c:16 * (c + 1), 0:size], 0.0)
        for field in range(fields):
            grid_ref[field, 0, :, begin:begin + size] = piece[
                rows * field:rows * (field + 1)
            ].astype(BF16)


def prepare_kernel(
    cut_off, pairs, fields, rows, fold_hbm, rates_hbm, leg_hbm, tm_hbm, bm_hbm,
    eh_ref, factor_ref, mix_ref, back_ref,
    fold_ref, rates_ref, leg_ref, tm_ref, bm_ref, sems, pad_s,
):
    fetch_all(
        (fold_hbm, rates_hbm, leg_hbm, tm_hbm, bm_hbm),
        (fold_ref, rates_ref, leg_ref, tm_ref, bm_ref),
        sems,
    )
    everyone = tm_ref.shape[0]
    _, lats, places = leg_ref.shape
    groups_f = everyone // fields
    wf = fields * 2
    span = eh_ref.shape[1]
    eight = 8 * lats
    groups = eh_ref.shape[0] // (2 * eight)
    owner = lax.axis_index("lat") * groups_f + lax.axis_index("fld")

    pad_s[...] = jnp.zeros(pad_s.shape, F32)
    pad_s[0:everyone, 0:everyone] = tm_ref[...]
    m_high, m_low = split(pad_s[...])
    shape = (LANES, LANES)
    level = (lane_iota(shape) % wf) // 2
    wide = []
    for piece in (m_high, m_low):
        parts = []
        for g in range(groups_f):
            pick = jnp.where(row_iota(shape) == fields * g + level, 1.0, 0.0).astype(BF16)
            parts.append(dot(piece, pick))
        wide.append(jnp.concatenate(parts, axis=1))
    lane = lane_iota(wide[0].shape) % LANES
    for part, piece in enumerate(wide):
        for t in range(groups):
            total = []
            for r in range(rows):
                for c in range(2):
                    keep = (lane // wf == t * rows + r) & (lane % 2 == c)
                    total.append(jnp.where(keep, piece, 0.0))
            at = (part * groups + t) * 4 * KPAD
            mix_ref[at:at + 4 * KPAD, :] = jnp.concatenate(total, axis=0).astype(BF16)

    pad_s[...] = jnp.zeros(pad_s.shape, F32)
    pad_s[0:everyone, 0:everyone] = bm_ref[...]
    shape = (FPAD, KPAD)
    expand = jnp.where(row_iota(shape) // 2 == lane_iota(shape), 1.0, 0.0).astype(BF16)
    shape = (LANES, 8 * KPAD)
    repeat = jnp.where(row_iota(shape) == lane_iota(shape) % KPAD, 1.0, 0.0).astype(BF16)
    shape = (FPAD, 8 * KPAD)
    same = row_iota(shape) % 2 == (lane_iota(shape) // KPAD) % 2
    for part, piece in enumerate(split(pad_s[...])):
        full = dot(dot(expand, piece).astype(BF16), repeat)
        back_ref[part * FPAD:(part + 1) * FPAD, :] = jnp.where(same, full, 0.0).astype(BF16)

    rate_row = row_iota((KPAD, LANES))
    rate = jnp.zeros((KPAD, LANES), F32)
    for k in range(everyone):
        rate = jnp.where(rate_row == k, rates_ref[k], rate)
    rate = jnp.concatenate([rate] * (span // LANES), axis=1)

    whole = places // LANES * LANES
    shape = (lats, span)
    place = lane_iota(shape)

    def pair_block(pair, carry):
        there = pair < pairs
        index = jnp.minimum(pair, pairs - 1)
        wave = fold_ref[owner, 2 * index]
        limit = jnp.where(there, cut_off - wave, -1)
        last = jnp.where(there, places - 1, -1)
        leg = jnp.concatenate(
            [
                leg_ref[index, :, 0:whole],
                jnp.broadcast_to(leg_ref[index, :, whole:places], (lats, span - whole)),
            ],
            axis=1,
        )
        first = place <= limit
        second = (place > limit) & (place <= last)
        odd = ((place + jnp.where(first, 0, wave)) & 1) == 1
        signed = jnp.where(odd, -leg, leg)
        base = (pair // 4) * 2 * eight + (pair % 4) * 2 * lats
        for r, rowset in enumerate((leg, signed)):
            eh_ref[pl.ds(pl.multiple_of(base + r * eight, 16), 2 * lats), :] = jnp.concatenate(
                [jnp.where(first, rowset, 0.0), jnp.where(second, rowset, 0.0)], axis=0
            ).astype(BF16)
        row = lane_iota((1, span))
        degree = jnp.where(row > limit, row - 1, row + wave)
        tau = (degree * (degree + 1)).astype(F32) * (1.0 / float(cut_off * (cut_off + 1)))
        factor_ref[pl.ds(pl.multiple_of(pair * KPAD, 8), KPAD), :] = 1.0 / (1.0 + tau * rate)
        return carry

    lax.fori_loop(0, 4 * groups, pair_block, 0)


def solve_kernel(
    fields, rows, band_hbm, msg_ref, eh_ref, factor_ref, mix_ref, back_ref,
    damped_ref, out_ref,
    band_ref, sems, vs, fq, sums, cs,
):
    fetch_all((band_hbm,), (band_ref,), sems)
    holders = band_ref.shape[0]
    groups_f = msg_ref.shape[0] // holders
    lats = holders
    groups = fq.shape[0] // (4 * KPAD)
    wf = fields * 2
    unit = rows * wf
    span = eh_ref.shape[1]
    eight = 8 * lats
    for holder in range(holders):
        lat = band_ref[holder]
        for g in range(groups_f):
            vs[pl.ds(pl.multiple_of((g * lats + lat) * 8, 8), 8), :] = msg_ref[holder * groups_f + g]
    tall = []
    for i8 in range(8):
        tall.append(
            jnp.concatenate(
                [vs[pl.ds(g * lats * 8 + i8, lats, stride=8), :] for g in range(groups_f)], axis=1
            )
        )
    v_high, v_low = split(jnp.concatenate(tall, axis=0))
    half = mix_ref.shape[0] // 2
    mix_h = mix_ref[0:half, :]
    fq[...] = dot_nt(mix_h, v_high) + dot_nt(mix_ref[half:, :], v_high) + dot_nt(mix_h, v_low)
    tall_rows = 8 * KPAD

    def quad_block(t, carry):
        mixed = fq[pl.ds(pl.multiple_of(t * 4 * KPAD, 8), 4 * KPAD), :]
        mixed = jnp.concatenate([mixed[0:2 * KPAD], mixed[2 * KPAD:4 * KPAD]], axis=1)
        slot_pair = (lane_iota(mixed.shape) % eight) // (2 * lats)
        left = jnp.concatenate([jnp.where(slot_pair == pp, mixed, 0.0) for pp in range(4)], axis=0)
        left = jnp.concatenate(split(left), axis=0)
        legs = pl.ds(pl.multiple_of(t * 2 * eight, 16), 2 * eight)
        deep = pl.ds(pl.multiple_of(t * tall_rows, 16), tall_rows)
        factor_at = pl.multiple_of(t * 4 * KPAD, 8)
        for start in range(0, span, 2 * LANES):
            size = min(2 * LANES, span - start)
            modes = dot(left, eh_ref[legs, start:start + size])
            modes = modes[0:tall_rows] + modes[tall_rows:]
            damped = []
            for pp in range(4):
                factor = factor_ref[pl.ds(factor_at + pp * KPAD, KPAD), start:start + size]
                at = 2 * pp * KPAD
                damped.append(modes[at:at + KPAD] * factor)
                damped.append(modes[at + KPAD:at + 2 * KPAD] * factor)
            damped_ref[deep, start:start + size] = jnp.concatenate(damped, axis=0).astype(BF16)
        sums[legs, :] = dot_nt(eh_ref[legs, :], damped_ref[deep, :])
        return carry

    lax.fori_loop(0, groups, quad_block, 0)

    everything = sums[...]
    own = (row_iota(everything.shape) // lats) % 8 // 2 == lane_iota(everything.shape) // (2 * KPAD)
    own_h, own_l = split(jnp.where(own, everything, 0.0))
    back_h = back_ref[0:FPAD, :]
    cs[:, 0:FPAD] = dot_nt(own_h, back_h) + dot_nt(own_l, back_h) + dot_nt(own_h, back_ref[FPAD:, :])

    lane = lane_iota((8, LANES))
    for holder in range(holders):
        lat = band_ref[holder]
        tiles = [jnp.zeros((8, LANES), F32) for _ in range(groups_f)]
        for t in range(groups):
            for r in range(rows):
                put = unit * t + wf * r
                piece = cs[pl.ds((t * rows + r) * eight + lat, 8, stride=lats), :]
                keep = (lane >= put) & (lane < put + wf)
                for g in range(groups_f):
                    moved = pltpu.roll(piece, (put - wf * g) % LANES, 1)
                    tiles[g] = jnp.where(keep, moved, tiles[g])
        for g in range(groups_f):
            out_ref[holder * groups_f + g] = tiles[g]


def output_kernel(damped_ref, back_ref, spec_ref, bk):
    everyone, quad, _, places = spec_ref.shape
    span = damped_ref.shape[1]

    @pl.when(pl.program_id(0) == 0)
    def _():
        shape = (FPAD, 8 * KPAD)
        pair_of = lane_iota(shape) // (2 * KPAD)
        for part in range(2):
            full = back_ref[part * FPAD:(part + 1) * FPAD, :].astype(F32)
            for pp in range(4):
                at = (4 * part + pp) * FPAD
                bk[at:at + FPAD, :] = jnp.where(pair_of == pp, full, 0.0).astype(BF16)

    for start in range(0, span, 2 * LANES):
        size = min(2 * LANES, span - start)
        spec = dot(bk[...], damped_ref[:, start:start + size])
        spec = spec[0:4 * FPAD] + spec[4 * FPAD:]
        kept = min(size, places - start)
        for pp in range(4):
            for f in range(everyone):
                at = pp * FPAD + 2 * f
                spec_ref[f, pp, :, start:start + kept] = spec[at:at + 2, 0:kept]


def per_device(grid, row_lengths, band_map, fold_map, legendre, to_modes, back_modes, mode_rates):
    fields, single, rows, width = grid.shape
    pairs, places, lats = legendre.shape
    cut_off = places - 2
    everyone = to_modes.shape[0]
    owners, per_owner = fold_map.shape
    groups = -(-per_owner // 8)
    slots = owners * groups * 8
    chunks = -(-(width // 4) // LANES)
    across = chunks * LANES
    span = -(-places // LANES) * LANES
    hbm = pl.BlockSpec(memory_space=pltpu.HBM)
    vmem = pl.BlockSpec(memory_space=pltpu.VMEM)
    room = pltpu.CompilerParams(vmem_limit_bytes=ROOM)
    message = pltpu.HBM((owners, 8, LANES), F32)
    holders = band_map.shape[0]
    groups_f = everyone // fields
    dma = pltpu.SemaphoreType.DMA
    row_lengths, band_map, fold_map, to_modes, back_modes, mode_rates, grid = (
        pltpu.with_memory_space_constraint(x, pltpu.HBM)
        for x in (row_lengths, band_map, fold_map, to_modes, back_modes, mode_rates, grid)
    )
    legendre = pltpu.with_memory_space_constraint(jnp.transpose(legendre, (0, 2, 1)), pltpu.HBM)

    sending, cos_table, sin_table, first_factor, second_factor = pl.pallas_call(
        functools.partial(forward_kernel, cut_off, groups),
        out_shape=(
            message,
            pltpu.VMEM((slots, across), BF16),
            pltpu.VMEM((slots, across), BF16),
            pltpu.VMEM((slots, LANES), F32),
            pltpu.VMEM((slots, LANES), F32),
        ),
        in_specs=[hbm] * 4,
        out_specs=(vmem,) * 5,
        scratch_shapes=[
            pltpu.SMEM(row_lengths.shape, jnp.int32),
            pltpu.SMEM(band_map.shape, jnp.int32),
            pltpu.VMEM(fold_map.shape, jnp.int32),
            pltpu.VMEM(grid.shape, BF16),
            dma((4,)),
            pltpu.VMEM((LANES, LANES), F32),
            pltpu.VMEM((slots, LANES), F32),
            pltpu.VMEM((slots, LANES), F32),
            pltpu.VMEM((slots, LANES), F32),
            pltpu.VMEM((16, 4 * across), F32),
            pltpu.VMEM((LANES, across), BF16),
            pltpu.VMEM((slots, LANES), F32),
        ],
        compiler_params=room,
        name="forward_rows",
    )(row_lengths, band_map, fold_map, grid)

    cos_table, sin_table, first_factor, second_factor = (
        pltpu.with_memory_space_constraint(x, pltpu.VMEM)
        for x in (cos_table, sin_table, first_factor, second_factor)
    )
    arrived = lax.all_to_all(sending, ("lat", "fld"), split_axis=0, concat_axis=0, tiled=True)

    legs, factors, mix, back = pl.pallas_call(
        functools.partial(prepare_kernel, cut_off, pairs, fields, rows),
        out_shape=(
            pltpu.VMEM((groups * 16 * lats, span), BF16),
            pltpu.VMEM((groups * 4 * KPAD, span), F32),
            pltpu.VMEM((2 * groups * 4 * KPAD, groups_f * LANES), BF16),
            pltpu.VMEM((2 * FPAD, 8 * KPAD), BF16),
        ),
        in_specs=[hbm] * 5,
        out_specs=(vmem,) * 4,
        scratch_shapes=[
            pltpu.SMEM(fold_map.shape, jnp.int32),
            pltpu.SMEM(mode_rates.shape, F32),
            pltpu.VMEM((pairs, lats, places), F32),
            pltpu.VMEM(to_modes.shape, F32),
            pltpu.VMEM(back_modes.shape, F32),
            dma((5,)),
            pltpu.VMEM((KPAD, LANES), F32),
        ],
        compiler_params=room,
        cost_estimate=pl.CostEstimate(flops=10**8, bytes_accessed=8 * 10**6, transcendentals=0),
        name="prepare",
    )(fold_map, mode_rates, legendre, to_modes, back_modes)

    legs, factors, mix, back = (
        pltpu.with_memory_space_constraint(x, pltpu.VMEM) for x in (legs, factors, mix, back)
    )
    damped, leaving = pl.pallas_call(
        functools.partial(solve_kernel, fields, rows),
        out_shape=(pltpu.VMEM((groups * 8 * KPAD, span), BF16), message),
        in_specs=[hbm] + [vmem] * 5,
        out_specs=(vmem,) * 2,
        scratch_shapes=[
            pltpu.SMEM(band_map.shape, jnp.int32),
            dma((1,)),
            pltpu.VMEM((owners * 8, LANES), F32),
            pltpu.VMEM((groups * 4 * KPAD, 8 * lats), F32),
            pltpu.VMEM((groups * 16 * lats, 8 * KPAD), F32),
            pltpu.VMEM((groups * 16 * lats, LANES), F32),
        ],
        compiler_params=room,
        name="solve",
    )(band_map, arrived, legs, factors, mix, back)

    returned = lax.all_to_all(leaving, ("lat", "fld"), split_axis=0, concat_axis=0, tiled=True)

    damped = pltpu.with_memory_space_constraint(damped, pltpu.VMEM)
    spectral = pl.pallas_call(
        output_kernel,
        grid=(groups,),
        out_shape=jax.ShapeDtypeStruct((everyone, pairs, 2, places), F32),
        in_specs=[
            pl.BlockSpec((8 * KPAD, span), lambda t: (t, 0)),
            pl.BlockSpec((2 * FPAD, 8 * KPAD), lambda t: (0, 0)),
        ],
        out_specs=pl.BlockSpec((everyone, 4, 2, places), lambda t: (0, t, 0, 0)),
        scratch_shapes=[pltpu.VMEM((8 * FPAD, 8 * KPAD), BF16)],
        compiler_params=pltpu.CompilerParams(
            dimension_semantics=("arbitrary",), vmem_limit_bytes=ROOM
        ),
        cost_estimate=pl.CostEstimate(flops=10**8, bytes_accessed=8 * 10**6, transcendentals=0),
        name="spectral_output",
    )(damped, back)

    grid_out = pl.pallas_call(
        functools.partial(inverse_kernel, groups),
        out_shape=jax.ShapeDtypeStruct(grid.shape, BF16),
        in_specs=[hbm, hbm] + [vmem] * 5,
        out_specs=vmem,
        scratch_shapes=[
            pltpu.SMEM(row_lengths.shape, jnp.int32),
            pltpu.SMEM(band_map.shape, jnp.int32),
            dma((2,)),
            pltpu.VMEM((owners, groups, 8, LANES), F32),
            pltpu.VMEM((16 * chunks, 4 * LANES), BF16),
        ],
        compiler_params=room,
        name="inverse_rows",
    )(row_lengths, band_map, returned, cos_table, sin_table, first_factor, second_factor)
    return (jnp.transpose(spectral, (0, 2, 1, 3)), grid_out)


def solution(mesh):
    placed = (
        P("fld", "lat", None, None),
        P(),
        P(),
        P(),
        P(("lat", "fld"), None, None),
        P(),
        P(),
        P(),
    )
    return jax.shard_map(
        per_device,
        mesh=mesh,
        in_specs=placed,
        out_specs=(P(None, None, ("lat", "fld"), None), P("fld", "lat", None, None)),
        check_vma=False,
    )
```

```python
import functools
import math

import jax
import jax.numpy as jnp
from jax import lax
from jax.experimental import pallas as pl
from jax.experimental.pallas import tpu as pltpu
from jax.sharding import PartitionSpec as P

LANES = 128
KPAD = 24
FPAD = 64
DEEP = 256
ROOM = 24 * 1024 * 1024
F32 = jnp.float32
BF16 = jnp.bfloat16
NT_DIMS = (((1,), (1,)), ((), ()))
SIN_POLY = (
    6.283185302447051,
    -41.34170038368319,
    81.60513023312113,
    -76.70299324464969,
    42.02573766814694,
    -14.899106966102595,
    3.237062655726421,
)
COS_POLY = (
    0.9999999889083757,
    -19.739204448887243,
    64.93911476570418,
    -85.45008785413638,
    60.167188450194914,
    -25.9658703083255,
    6.526145851512229,
)


def dot(a, b):
    return jnp.dot(a, b, preferred_element_type=F32)


def dot_nt(a, b):
    return lax.dot_general(a, b, NT_DIMS, preferred_element_type=F32)


def split(x):
    high = x.astype(BF16)
    return high, (x - high.astype(F32)).astype(BF16)


def horner(coefs, z):
    total = coefs[-1] * z + coefs[-2]
    for coef in coefs[-3::-1]:
        total = total * z + coef
    return total


def turn(steps, period, inverse):
    rest = steps - period * jnp.floor(steps * inverse + 0.5)
    part = rest * inverse
    z = part * part
    return horner(COS_POLY, z), part * horner(SIN_POLY, z)


def fetch_all(sources, targets, sems):
    copies = [
        pltpu.make_async_copy(source, target, sems.at[i])
        for i, (source, target) in enumerate(zip(sources, targets))
    ]
    for copy in copies:
        copy.start()
    for copy in copies:
        copy.wait()


def lane_iota(shape):
    return lax.broadcasted_iota(jnp.int32, shape, len(shape) - 1)


def row_iota(shape):
    return lax.broadcasted_iota(jnp.int32, shape, len(shape) - 2)


def spread_matrix():
    shape = (4 * LANES, LANES)
    picks = []
    for phase in range(4):
        picks.append(jnp.where(row_iota(shape) == 4 * lane_iota(shape) + phase, 1.0, 0.0))
    return jnp.concatenate(picks, axis=1).astype(BF16)


def phases_of(groups, wave, length, lanes):
    shape = (groups + 16, lanes)
    row = row_iota(shape)
    steps = jnp.where(row < groups, (row // 4) * (4 * DEEP) + row % 4, 4 * (row - groups))
    steps = jnp.where(row >= groups + 8, 32 << jnp.maximum(row - groups - 8, 0), steps)
    period = jnp.full(shape, length, jnp.int32).astype(F32)
    return turn(steps.astype(F32) * wave, period, 1.0 / period)


def forward_kernel(
    cut_off, groups, len_hbm, band_hbm, fold_hbm, grid_hbm,
    msg_ref, tc_hbm, ts_hbm, fc_hbm, fs_hbm,
    len_ref, band_ref, fold_ref, grid_ref, sems, fold_s, wave_s, xs, xq, tc, ts, fc, fs, xt, ys,
):
    fetch_all(
        (len_hbm, band_hbm, fold_hbm, grid_hbm), (len_ref, band_ref, fold_ref, grid_ref), sems
    )
    fields, _, rows, width = grid_ref.shape
    owners, per_owner = fold_ref.shape
    slots = tc.shape[1]
    pieces = xq.shape[0] // 64
    padded = groups * 8
    unit = rows * fields * 2
    length = len_ref[band_ref[lax.axis_index("lat")]]
    top = jnp.minimum(cut_off, (length - 1) // 2)

    fold_s[...] = jnp.full(fold_s.shape, -1.0, F32)
    fold_s[0:owners, 0:per_owner] = fold_ref[...].astype(F32)
    lane = lane_iota((1, LANES))
    tiles = [jnp.full((1, LANES), -1.0, F32) for _ in range(slots // LANES)]
    for owner in range(owners):
        at, off = divmod(owner * padded, LANES)
        line = fold_s[owner:owner + 1, :]
        if off:
            line = pltpu.roll(line, off, 1)
        tiles[at] = jnp.where((lane >= off) & (lane < off + padded), line, tiles[at])
        if off + padded > LANES:
            tiles[at + 1] = jnp.where(lane < off + padded - LANES, line, tiles[at + 1])
    wave_s[...] = jnp.broadcast_to(jnp.concatenate(tiles, axis=1), wave_s.shape)

    xs[...] = jnp.zeros(xs.shape, F32)
    inside = lane_iota((rows, width)) < length
    for field in range(fields):
        points = grid_ref[field, 0].astype(F32)
        xs[rows * field:rows * (field + 1), 0:width] = jnp.where(inside, points, 0.0)
    stacked = jnp.concatenate(
        [xs[:, 4 * LANES * c:4 * LANES * (c + 1)] for c in range(2 * pieces)], axis=0
    ).astype(BF16)
    spread = dot(stacked, spread_matrix()).astype(BF16)
    for c in range(2 * pieces):
        for phase in range(4):
            at = (4 * (c // 2) + phase) * 16
            off = LANES * (c % 2)
            xq[at:at + 16, off:off + LANES] = spread[
                16 * c:16 * (c + 1), LANES * phase:LANES * (phase + 1)
            ]

    turns = 4 * pieces
    block = 2 * LANES
    xt[64:128, :] = jnp.zeros((64, slots), F32)
    values = xq[...]

    def lane_block(i, carry):
        at = pl.ds(pl.multiple_of(i * block, block), block)
        wave = wave_s[:, at]
        wave = jnp.concatenate([wave] * ((turns + 16) // 8), axis=0)
        co, si = phases_of(turns, wave, length, block)
        one = wave[0:1]
        weight = jnp.where(one == 0.0, 1.0, 2.0)
        weight = jnp.where((one >= 0.0) & (one <= jnp.full(one.shape, top, jnp.int32).astype(F32)), weight, 0.0)
        fc[:, at] = co[0:turns] * weight
        fs[:, at] = si[0:turns] * weight
        c_all = co[turns:turns + 8]
        s_all = si[turns:turns + 8]
        size, step = 8, turns + 8
        while size < DEEP:
            c1 = co[step:step + 1]
            s1 = si[step:step + 1]
            c_new = c_all * c1 - s_all * s1
            s_new = s_all * c1 + c_all * s1
            c_all = jnp.concatenate([c_all, c_new], axis=0)
            s_all = jnp.concatenate([s_all, s_new], axis=0)
            size, step = 2 * size, step + 1
        c_all = c_all.astype(BF16)
        s_all = s_all.astype(BF16)
        tc[:, at] = c_all
        ts[:, at] = s_all
        inner_c = dot(values, c_all)
        inner_s = dot(values, s_all)
        real = jnp.zeros((16, block), F32)
        imag = jnp.zeros((16, block), F32)
        for g in range(turns):
            c1 = fc[g:g + 1, at]
            s1 = fs[g:g + 1, at]
            part_c = inner_c[16 * g:16 * (g + 1)]
            part_s = inner_s[16 * g:16 * (g + 1)]
            real = real + (c1 * part_c - s1 * part_s)
            imag = imag - (c1 * part_s + s1 * part_c)
        both = jnp.concatenate([real, imag], axis=0) * jnp.where(one == 0.0, 1.0, 0.5)
        high = both.astype(BF16).astype(F32)
        xt[0:32, at] = high
        xt[32:64, at] = both - high
        return carry

    lax.fori_loop(0, slots // block, lane_block, 0)
    keeps = [
        pltpu.make_async_copy(source, target, sems.at[i])
        for i, (source, target) in enumerate(
            ((tc, tc_hbm), (ts, ts_hbm), (fc, fc_hbm), (fs, fs_hbm))
        )
    ]
    for keep in keeps:
        keep.start()

    for c in range(slots // LANES):
        ys[LANES * c:LANES * (c + 1), :] = jnp.transpose(xt[:, LANES * c:LANES * (c + 1)])
    turned = ys[...].reshape(owners, groups, 8, LANES)
    shape = (LANES, LANES)
    source = row_iota(shape)
    target = lane_iota(shape)
    vec = source % 16
    base = (vec % rows) * (fields * 2) + (vec // rows) * 2 + (source // 16) % 2
    used = (vec < rows * fields) & (source < 64)
    total = jnp.zeros((owners * 8, LANES), F32)
    for t in range(groups):
        place = jnp.where(used & (target == base + unit * t), 1.0, 0.0).astype(BF16)
        total = total + dot(turned[:, t].reshape(owners * 8, LANES).astype(BF16), place)
    scale = 1.0 / jnp.sqrt(jnp.full((owners * 8, LANES), length, jnp.int32).astype(F32))
    msg_ref[...] = (total * scale).reshape(owners, 8, LANES)
    for keep in keeps:
        keep.wait()


def inverse_kernel(
    groups, len_hbm, band_hbm, fc_hbm, fs_hbm, tc_hbm, ts_hbm, msg_ref, grid_ref,
    len_ref, band_ref, fc, fs, tc, ts, sems, zs, xt, zr, zi, os,
):
    copies = [
        pltpu.make_async_copy(source, target, sems.at[i])
        for i, (source, target) in enumerate(
            (
                (len_hbm, len_ref), (band_hbm, band_ref), (fc_hbm, fc),
                (fs_hbm, fs), (tc_hbm, tc), (ts_hbm, ts),
            )
        )
    ]
    for copy in copies:
        copy.start()
    fields, _, rows, width = grid_ref.shape
    owners = msg_ref.shape[0]
    slots = tc.shape[1]
    turns = fc.shape[0]
    unit = rows * fields * 2
    high, low = split(msg_ref[...].reshape(owners * 8, LANES))
    pieces = jnp.concatenate([high, low], axis=1)
    shape = (LANES, LANES)
    source = row_iota(shape)
    target = lane_iota(shape)
    vec = target % 16
    base = (vec % rows) * (fields * 2) + (vec // rows) * 2 + target // 16
    used = (vec < rows * fields) & (target < 32)
    for t in range(groups):
        place = jnp.where(used & (source == base + unit * t), 1.0, 0.0).astype(BF16)
        zs[:, t] = dot(pieces, jnp.concatenate([place, place], axis=0)).reshape(owners, 8, LANES)
    turned = zs[...].reshape(slots, LANES)
    for c in range(slots // LANES):
        xt[:, LANES * c:LANES * (c + 1)] = jnp.transpose(turned[LANES * c:LANES * (c + 1)])[0:32]
    for copy in copies[0:4]:
        copy.wait()
    length = len_ref[band_ref[lax.axis_index("lat")]]
    block = 2 * LANES

    def lane_block(i, carry):
        at = pl.ds(pl.multiple_of(i * block, block), block)
        real = xt[0:16, at]
        imag = xt[16:32, at]
        for g in range(turns):
            c1 = fc[g:g + 1, at]
            s1 = fs[g:g + 1, at]
            zr[16 * g:16 * (g + 1), at] = (c1 * real - s1 * imag).astype(BF16)
            zi[16 * g:16 * (g + 1), at] = (s1 * real + c1 * imag).astype(BF16)
        return carry

    lax.fori_loop(0, slots // block, lane_block, 0)
    for copy in copies[4:]:
        copy.wait()
    out = dot_nt(zr[...], tc[...]) - dot_nt(zi[...], ts[...])
    out = out * (1.0 / jnp.sqrt(jnp.full((16 * turns, DEEP), length, jnp.int32).astype(F32)))
    chunks = os.shape[0] // 16
    for c in range(chunks):
        for phase in range(4):
            at = (4 * (c // 2) + phase) * 16
            off = LANES * (c % 2)
            os[16 * c:16 * (c + 1), LANES * phase:LANES * (phase + 1)] = out[
                at:at + 16, off:off + LANES
            ].astype(BF16)
    merged = dot_nt(os[...], spread_matrix())
    for c in range(chunks):
        begin = 4 * LANES * c
        size = min(4 * LANES, width - begin)
        if size <= 0:
            continue
        inside = begin + lane_iota((16, size)) < length
        piece = jnp.where(inside, merged[16 * c:16 * (c + 1), 0:size], 0.0)
        for field in range(fields):
            grid_ref[field, 0, :, begin:begin + size] = piece[
                rows * field:rows * (field + 1)
            ].astype(BF16)


def prepare_kernel(
    cut_off, pairs, fields, rows, fold_hbm, rates_hbm, leg_hbm, tm_hbm, bm_hbm,
    eh_hbm, factor_hbm, mix_hbm, back_ref,
    fold_ref, rates_ref, leg_ref, tm_ref, bm_ref, sems, pad_s,
    eh_ref, factor_ref, mix_ref, out_sems, mix_sem,
):
    fetch_all(
        (fold_hbm, rates_hbm, leg_hbm, tm_hbm, bm_hbm),
        (fold_ref, rates_ref, leg_ref, tm_ref, bm_ref),
        sems,
    )
    everyone = tm_ref.shape[0]
    _, lats, places = leg_ref.shape
    groups_f = everyone // fields
    wf = fields * 2
    span = eh_ref.shape[1]
    eight = 8 * lats
    groups = eh_ref.shape[0] // (2 * eight)
    owner = lax.axis_index("lat") * groups_f + lax.axis_index("fld")

    pad_s[...] = jnp.zeros(pad_s.shape, F32)
    pad_s[0:everyone, 0:everyone] = tm_ref[...]
    m_high, m_low = split(pad_s[...])
    shape = (LANES, LANES)
    level = (lane_iota(shape) % wf) // 2
    wide = []
    for piece in (m_high, m_low):
        parts = []
        for g in range(groups_f):
            pick = jnp.where(row_iota(shape) == fields * g + level, 1.0, 0.0).astype(BF16)
            parts.append(dot(piece, pick))
        wide.append(jnp.concatenate(parts, axis=1))
    lane = lane_iota(wide[0].shape) % LANES
    for part, piece in enumerate(wide):
        for t in range(groups):
            total = []
            for r in range(rows):
                for c in range(2):
                    keep = (lane // wf == t * rows + r) & (lane % 2 == c)
                    total.append(jnp.where(keep, piece, 0.0))
            at = (part * groups + t) * 4 * KPAD
            mix_ref[at:at + 4 * KPAD, :] = jnp.concatenate(total, axis=0).astype(BF16)
    keeps = [pltpu.make_async_copy(mix_ref, mix_hbm, mix_sem)]
    keeps[0].start()

    pad_s[...] = jnp.zeros(pad_s.shape, F32)
    pad_s[0:everyone, 0:everyone] = bm_ref[...]
    shape = (FPAD, KPAD)
    expand = jnp.where(row_iota(shape) // 2 == lane_iota(shape), 1.0, 0.0).astype(BF16)
    shape = (LANES, 8 * KPAD)
    repeat = jnp.where(row_iota(shape) == lane_iota(shape) % KPAD, 1.0, 0.0).astype(BF16)
    shape = (FPAD, 8 * KPAD)
    same = row_iota(shape) % 2 == (lane_iota(shape) // KPAD) % 2
    for part, piece in enumerate(split(pad_s[...])):
        full = dot(dot(expand, piece).astype(BF16), repeat)
        back_ref[part * FPAD:(part + 1) * FPAD, :] = jnp.where(same, full, 0.0).astype(BF16)

    rate_row = row_iota((KPAD, LANES))
    rate = jnp.zeros((KPAD, LANES), F32)
    for k in range(everyone):
        rate = jnp.where(rate_row == k, rates_ref[k], rate)
    rate = jnp.concatenate([rate] * (span // LANES), axis=1)

    whole = places // LANES * LANES
    shape = (lats, span)
    place = lane_iota(shape)

    def pair_block(pair, carry):
        there = pair < pairs
        index = jnp.minimum(pair, pairs - 1)
        wave = fold_ref[owner, 2 * index]
        limit = jnp.where(there, cut_off - wave, -1)
        last = jnp.where(there, places - 1, -1)
        leg = jnp.concatenate(
            [
                leg_ref[index, :, 0:whole],
                jnp.broadcast_to(leg_ref[index, :, whole:places], (lats, span - whole)),
            ],
            axis=1,
        )
        first = place <= limit
        second = (place > limit) & (place <= last)
        odd = ((place + jnp.where(first, 0, wave)) & 1) == 1
        signed = jnp.where(odd, -leg, leg)
        base = (pair // 4) * 2 * eight + (pair % 4) * 2 * lats
        for r, rowset in enumerate((leg, signed)):
            eh_ref[pl.ds(pl.multiple_of(base + r * eight, 16), 2 * lats), :] = jnp.concatenate(
                [jnp.where(first, rowset, 0.0), jnp.where(second, rowset, 0.0)], axis=0
            ).astype(BF16)
        row = lane_iota((1, span))
        degree = jnp.where(row > limit, row - 1, row + wave)
        tau = (degree * (degree + 1)).astype(F32) * (1.0 / float(cut_off * (cut_off + 1)))
        factor_ref[pl.ds(pl.multiple_of(pair * KPAD, 8), KPAD), :] = 1.0 / (1.0 + tau * rate)
        return carry

    for t in range(groups):
        lax.fori_loop(4 * t, 4 * t + 4, pair_block, 0)
        part = pl.ds(4 * KPAD * t, 4 * KPAD)
        legs = pl.ds(2 * eight * t, 2 * eight)
        for keep in (
            pltpu.make_async_copy(factor_ref.at[part], factor_hbm.at[part], out_sems.at[0, t]),
            pltpu.make_async_copy(eh_ref.at[legs], eh_hbm.at[legs], out_sems.at[1, t]),
        ):
            keep.start()
            keeps.append(keep)
    for keep in keeps:
        keep.wait()


def solve_kernel(
    fields, rows, band_hbm, factor_hbm, eh_hbm, mix_hbm, msg_ref, back_ref,
    damped_ref, out_ref,
    band_ref, sems, vs, fq, sums, cs, factor_ref, eh_ref, mix_ref, in_sems,
):
    first = [
        pltpu.make_async_copy(band_hbm, band_ref, sems.at[0]),
        pltpu.make_async_copy(mix_hbm, mix_ref, sems.at[1]),
    ]
    for copy in first:
        copy.start()
    later = []
    legs_rows = 16 * band_ref.shape[0]
    for t in range(fq.shape[0] // (4 * KPAD)):
        part = pl.ds(4 * KPAD * t, 4 * KPAD)
        legs = pl.ds(legs_rows * t, legs_rows)
        later.append(
            (
                pltpu.make_async_copy(eh_hbm.at[legs], eh_ref.at[legs], in_sems.at[0, t]),
                pltpu.make_async_copy(factor_hbm.at[part], factor_ref.at[part], in_sems.at[1, t]),
            )
        )
        for copy in later[-1]:
            copy.start()
    first[0].wait()
    holders = band_ref.shape[0]
    groups_f = msg_ref.shape[0] // holders
    lats = holders
    groups = fq.shape[0] // (4 * KPAD)
    wf = fields * 2
    unit = rows * wf
    span = eh_ref.shape[1]
    eight = 8 * lats
    for holder in range(holders):
        lat = band_ref[holder]
        for g in range(groups_f):
            vs[pl.ds(pl.multiple_of((g * lats + lat) * 8, 8), 8), :] = msg_ref[holder * groups_f + g]
    tall = []
    for i8 in range(8):
        tall.append(
            jnp.concatenate(
                [vs[pl.ds(g * lats * 8 + i8, lats, stride=8), :] for g in range(groups_f)], axis=1
            )
        )
    v_high, v_low = split(jnp.concatenate(tall, axis=0))
    first[1].wait()
    half = mix_ref.shape[0] // 2
    mix_h = mix_ref[0:half, :]
    fq[...] = dot_nt(mix_h, v_high) + dot_nt(mix_ref[half:, :], v_high) + dot_nt(mix_h, v_low)
    tall_rows = 8 * KPAD

    def quad_block(t, carry):
        mixed = fq[pl.ds(pl.multiple_of(t * 4 * KPAD, 8), 4 * KPAD), :]
        mixed = jnp.concatenate([mixed[0:2 * KPAD], mixed[2 * KPAD:4 * KPAD]], axis=1)
        slot_pair = (lane_iota(mixed.shape) % eight) // (2 * lats)
        left = jnp.concatenate([jnp.where(slot_pair == pp, mixed, 0.0) for pp in range(4)], axis=0)
        left = jnp.concatenate(split(left), axis=0)
        legs = pl.ds(pl.multiple_of(t * 2 * eight, 16), 2 * eight)
        deep = pl.ds(pl.multiple_of(t * tall_rows, 16), tall_rows)
        factor_at = pl.multiple_of(t * 4 * KPAD, 8)
        for start in range(0, span, 2 * LANES):
            size = min(2 * LANES, span - start)
            modes = dot(left, eh_ref[legs, start:start + size])
            modes = modes[0:tall_rows] + modes[tall_rows:]
            damped = []
            for pp in range(4):
                factor = factor_ref[pl.ds(factor_at + pp * KPAD, KPAD), start:start + size]
                at = 2 * pp * KPAD
                damped.append(modes[at:at + KPAD] * factor)
                damped.append(modes[at + KPAD:at + 2 * KPAD] * factor)
            damped_ref[deep, start:start + size] = jnp.concatenate(damped, axis=0).astype(BF16)
        sums[legs, :] = dot_nt(eh_ref[legs, :], damped_ref[deep, :])
        return carry

    for t in range(groups):
        for copy in later[t]:
            copy.wait()
        quad_block(t, 0)

    everything = sums[...]
    own = (row_iota(everything.shape) // lats) % 8 // 2 == lane_iota(everything.shape) // (2 * KPAD)
    own_h, own_l = split(jnp.where(own, everything, 0.0))
    back_h = back_ref[0:FPAD, :]
    cs[:, 0:FPAD] = dot_nt(own_h, back_h) + dot_nt(own_l, back_h) + dot_nt(own_h, back_ref[FPAD:, :])

    lane = lane_iota((8, LANES))
    for holder in range(holders):
        lat = band_ref[holder]
        tiles = [jnp.zeros((8, LANES), F32) for _ in range(groups_f)]
        for t in range(groups):
            for r in range(rows):
                put = unit * t + wf * r
                piece = cs[pl.ds((t * rows + r) * eight + lat, 8, stride=lats), :]
                keep = (lane >= put) & (lane < put + wf)
                for g in range(groups_f):
                    moved = pltpu.roll(piece, (put - wf * g) % LANES, 1)
                    tiles[g] = jnp.where(keep, moved, tiles[g])
        for g in range(groups_f):
            out_ref[holder * groups_f + g] = tiles[g]


def output_kernel(damped_ref, back_ref, spec_ref, bk):
    everyone, quad, _, places = spec_ref.shape
    span = damped_ref.shape[1]

    @pl.when(pl.program_id(0) == 0)
    def _():
        shape = (FPAD, 8 * KPAD)
        pair_of = lane_iota(shape) // (2 * KPAD)
        for part in range(2):
            full = back_ref[part * FPAD:(part + 1) * FPAD, :].astype(F32)
            for pp in range(4):
                at = (4 * part + pp) * FPAD
                bk[at:at + FPAD, :] = jnp.where(pair_of == pp, full, 0.0).astype(BF16)

    for start in range(0, span, 2 * LANES):
        size = min(2 * LANES, span - start)
        spec = dot(bk[...], damped_ref[:, start:start + size])
        spec = spec[0:4 * FPAD] + spec[4 * FPAD:]
        kept = min(size, places - start)
        for pp in range(4):
            for f in range(everyone):
                at = pp * FPAD + 2 * f
                spec_ref[f, pp, :, start:start + kept] = spec[at:at + 2, 0:kept]


def per_device(grid, row_lengths, band_map, fold_map, legendre, to_modes, back_modes, mode_rates):
    fields, single, rows, width = grid.shape
    pairs, places, lats = legendre.shape
    cut_off = places - 2
    everyone = to_modes.shape[0]
    owners, per_owner = fold_map.shape
    groups = -(-per_owner // 8)
    slots = owners * groups * 8
    pieces = -(-(width // 4) // DEEP)
    turns = 4 * pieces
    span = -(-places // LANES) * LANES
    hbm = pl.BlockSpec(memory_space=pltpu.HBM)
    vmem = pl.BlockSpec(memory_space=pltpu.VMEM)
    room = pltpu.CompilerParams(vmem_limit_bytes=ROOM)
    message = pltpu.HBM((owners, 8, LANES), F32)
    holders = band_map.shape[0]
    groups_f = everyone // fields
    dma = pltpu.SemaphoreType.DMA
    row_lengths, band_map, fold_map, to_modes, back_modes, mode_rates, grid = (
        pltpu.with_memory_space_constraint(x, pltpu.HBM)
        for x in (row_lengths, band_map, fold_map, to_modes, back_modes, mode_rates, grid)
    )
    legendre = pltpu.with_memory_space_constraint(jnp.transpose(legendre, (0, 2, 1)), pltpu.HBM)

    sending, cos_table, sin_table, cos_turn, sin_turn = pl.pallas_call(
        functools.partial(forward_kernel, cut_off, groups),
        out_shape=(
            message,
            pltpu.HBM((DEEP, slots), BF16),
            pltpu.HBM((DEEP, slots), BF16),
            pltpu.HBM((turns, slots), F32),
            pltpu.HBM((turns, slots), F32),
        ),
        in_specs=[hbm] * 4,
        out_specs=(vmem,) + (hbm,) * 4,
        scratch_shapes=[
            pltpu.SMEM(row_lengths.shape, jnp.int32),
            pltpu.SMEM(band_map.shape, jnp.int32),
            pltpu.VMEM(fold_map.shape, jnp.int32),
            pltpu.VMEM(grid.shape, BF16),
            dma((4,)),
            pltpu.VMEM((max(owners, 8), LANES), F32),
            pltpu.VMEM((8, slots), F32),
            pltpu.VMEM((16, 4 * DEEP * pieces), F32),
            pltpu.VMEM((16 * turns, DEEP), BF16),
            pltpu.VMEM((DEEP, slots), BF16),
            pltpu.VMEM((DEEP, slots), BF16),
            pltpu.VMEM((turns, slots), F32),
            pltpu.VMEM((turns, slots), F32),
            pltpu.VMEM((LANES, slots), F32),
            pltpu.VMEM((slots, LANES), F32),
        ],
        compiler_params=room,
        name="forward_rows",
    )(row_lengths, band_map, fold_map, grid)
    tables = [
        pltpu.with_memory_space_constraint(x, pltpu.HBM)
        for x in (cos_turn, sin_turn, cos_table, sin_table)
    ]
    arrived = lax.all_to_all(sending, ("lat", "fld"), split_axis=0, concat_axis=0, tiled=True)

    legs, factors, mix, back = pl.pallas_call(
        functools.partial(prepare_kernel, cut_off, pairs, fields, rows),
        out_shape=(
            pltpu.HBM((groups * 16 * lats, span), BF16),
            pltpu.HBM((groups * 4 * KPAD, span), F32),
            pltpu.HBM((2 * groups * 4 * KPAD, groups_f * LANES), BF16),
            pltpu.VMEM((2 * FPAD, 8 * KPAD), BF16),
        ),
        in_specs=[hbm] * 5,
        out_specs=(hbm, hbm, hbm, vmem),
        scratch_shapes=[
            pltpu.SMEM(fold_map.shape, jnp.int32),
            pltpu.SMEM(mode_rates.shape, F32),
            pltpu.VMEM((pairs, lats, places), F32),
            pltpu.VMEM(to_modes.shape, F32),
            pltpu.VMEM(back_modes.shape, F32),
            dma((5,)),
            pltpu.VMEM((KPAD, LANES), F32),
            pltpu.VMEM((groups * 16 * lats, span), BF16),
            pltpu.VMEM((groups * 4 * KPAD, span), F32),
            pltpu.VMEM((2 * groups * 4 * KPAD, groups_f * LANES), BF16),
            dma((2, groups)),
            dma,
        ],
        compiler_params=room,
        cost_estimate=pl.CostEstimate(flops=10**8, bytes_accessed=8 * 10**6, transcendentals=0),
        name="prepare",
    )(fold_map, mode_rates, legendre, to_modes, back_modes)

    legs, factors, mix = (
        pltpu.with_memory_space_constraint(x, pltpu.HBM) for x in (legs, factors, mix)
    )
    back = pltpu.with_memory_space_constraint(back, pltpu.VMEM)
    damped, leaving = pl.pallas_call(
        functools.partial(solve_kernel, fields, rows),
        out_shape=(pltpu.VMEM((groups * 8 * KPAD, span), BF16), message),
        in_specs=[hbm] * 4 + [vmem] * 2,
        out_specs=(vmem,) * 2,
        scratch_shapes=[
            pltpu.SMEM(band_map.shape, jnp.int32),
            dma((2,)),
            pltpu.VMEM((owners * 8, LANES), F32),
            pltpu.VMEM((groups * 4 * KPAD, 8 * lats), F32),
            pltpu.VMEM((groups * 16 * lats, 8 * KPAD), F32),
            pltpu.VMEM((groups * 16 * lats, LANES), F32),
            pltpu.VMEM((groups * 4 * KPAD, span), F32),
            pltpu.VMEM((groups * 16 * lats, span), BF16),
            pltpu.VMEM((2 * groups * 4 * KPAD, groups_f * LANES), BF16),
            dma((2, groups)),
        ],
        compiler_params=room,
        name="solve",
    )(band_map, factors, legs, mix, arrived, back)

    returned = lax.all_to_all(leaving, ("lat", "fld"), split_axis=0, concat_axis=0, tiled=True)

    damped = pltpu.with_memory_space_constraint(damped, pltpu.VMEM)
    spectral = pl.pallas_call(
        output_kernel,
        grid=(groups,),
        out_shape=jax.ShapeDtypeStruct((everyone, pairs, 2, places), F32),
        in_specs=[
            pl.BlockSpec((8 * KPAD, span), lambda t: (t, 0)),
            pl.BlockSpec((2 * FPAD, 8 * KPAD), lambda t: (0, 0)),
        ],
        out_specs=pl.BlockSpec((everyone, 4, 2, places), lambda t: (0, t, 0, 0)),
        scratch_shapes=[pltpu.VMEM((8 * FPAD, 8 * KPAD), BF16)],
        compiler_params=pltpu.CompilerParams(
            dimension_semantics=("arbitrary",), vmem_limit_bytes=ROOM
        ),
        cost_estimate=pl.CostEstimate(flops=10**8, bytes_accessed=8 * 10**6, transcendentals=0),
        name="spectral_output",
    )(damped, back)

    grid_out = pl.pallas_call(
        functools.partial(inverse_kernel, groups),
        out_shape=jax.ShapeDtypeStruct(grid.shape, BF16),
        in_specs=[hbm] * 6 + [vmem],
        out_specs=vmem,
        scratch_shapes=[
            pltpu.SMEM(row_lengths.shape, jnp.int32),
            pltpu.SMEM(band_map.shape, jnp.int32),
            pltpu.VMEM((turns, slots), F32),
            pltpu.VMEM((turns, slots), F32),
            pltpu.VMEM((DEEP, slots), BF16),
            pltpu.VMEM((DEEP, slots), BF16),
            dma((6,)),
            pltpu.VMEM((owners, groups, 8, LANES), F32),
            pltpu.VMEM((32, slots), F32),
            pltpu.VMEM((16 * turns, slots), BF16),
            pltpu.VMEM((16 * turns, slots), BF16),
            pltpu.VMEM((32 * pieces, 4 * LANES), BF16),
        ],
        compiler_params=room,
        name="inverse_rows",
    )(row_lengths, band_map, *tables, returned)
    return (jnp.transpose(spectral, (0, 2, 1, 3)), grid_out)


def solution(mesh):
    placed = (
        P("fld", "lat", None, None),
        P(),
        P(),
        P(),
        P(("lat", "fld"), None, None),
        P(),
        P(),
        P(),
    )
    return jax.shard_map(
        per_device,
        mesh=mesh,
        in_specs=placed,
        out_specs=(P(None, None, ("lat", "fld"), None), P("fld", "lat", None, None)),
        check_vma=False,
    )
```

```python
import functools
import math

import jax
import jax.numpy as jnp
from jax import lax
from jax.experimental import pallas as pl
from jax.experimental.pallas import tpu as pltpu
from jax.sharding import PartitionSpec as P

LANES = 128
KPAD = 24
FPAD = 64
DEEP = 256
ROOM = 24 * 1024 * 1024
F32 = jnp.float32
BF16 = jnp.bfloat16
NT_DIMS = (((1,), (1,)), ((), ()))
SIN_POLY = (
    6.283185302447051,
    -41.34170038368319,
    81.60513023312113,
    -76.70299324464969,
    42.02573766814694,
    -14.899106966102595,
    3.237062655726421,
)
COS_POLY = (
    0.9999999889083757,
    -19.739204448887243,
    64.93911476570418,
    -85.45008785413638,
    60.167188450194914,
    -25.9658703083255,
    6.526145851512229,
)


def dot(a, b):
    return jnp.dot(a, b, preferred_element_type=F32)


def dot_nt(a, b):
    return lax.dot_general(a, b, NT_DIMS, preferred_element_type=F32)


def split(x):
    high = x.astype(BF16)
    return high, (x - high.astype(F32)).astype(BF16)


def horner(coefs, z):
    total = coefs[-1] * z + coefs[-2]
    for coef in coefs[-3::-1]:
        total = total * z + coef
    return total


def turn(steps, period, inverse):
    rest = steps - period * jnp.floor(steps * inverse + 0.5)
    part = rest * inverse
    z = part * part
    return horner(COS_POLY, z), part * horner(SIN_POLY, z)


def fetch_all(sources, targets, sems):
    copies = [
        pltpu.make_async_copy(source, target, sems.at[i])
        for i, (source, target) in enumerate(zip(sources, targets))
    ]
    for copy in copies:
        copy.start()
    for copy in copies:
        copy.wait()


def lane_iota(shape):
    return lax.broadcasted_iota(jnp.int32, shape, len(shape) - 1)


def row_iota(shape):
    return lax.broadcasted_iota(jnp.int32, shape, len(shape) - 2)


def spread_matrix():
    shape = (4 * LANES, LANES)
    picks = []
    for phase in range(4):
        picks.append(jnp.where(row_iota(shape) == 4 * lane_iota(shape) + phase, 1.0, 0.0))
    return jnp.concatenate(picks, axis=1).astype(BF16)


def phases_of(groups, wave, length, lanes):
    shape = (groups + 16, lanes)
    row = row_iota(shape)
    steps = jnp.where(row < groups, (row // 4) * (4 * DEEP) + row % 4, 4 * (row - groups))
    steps = jnp.where(row >= groups + 8, 32 << jnp.maximum(row - groups - 8, 0), steps)
    period = jnp.full(shape, length, jnp.int32).astype(F32)
    return turn(steps.astype(F32) * wave, period, 1.0 / period)


def forward_kernel(
    cut_off, groups, len_hbm, band_hbm, fold_hbm, grid_hbm,
    msg_ref, tc_hbm, ts_hbm, fc_hbm, fs_hbm,
    len_ref, band_ref, fold_ref, grid_ref, sems, fold_s, wave_s, xs, xq, tc, ts, fc, fs, xt, ys,
):
    fetch_all(
        (len_hbm, band_hbm, fold_hbm, grid_hbm), (len_ref, band_ref, fold_ref, grid_ref), sems
    )
    fields, _, rows, width = grid_ref.shape
    owners, per_owner = fold_ref.shape
    slots = tc.shape[1]
    pieces = xq.shape[0] // 64
    padded = groups * 8
    unit = rows * fields * 2
    length = len_ref[band_ref[lax.axis_index("lat")]]
    top = jnp.minimum(cut_off, (length - 1) // 2)

    fold_s[...] = jnp.full(fold_s.shape, -1.0, F32)
    fold_s[0:owners, 0:per_owner] = fold_ref[...].astype(F32)
    lane = lane_iota((1, LANES))
    tiles = [jnp.full((1, LANES), -1.0, F32) for _ in range(slots // LANES)]
    for owner in range(owners):
        at, off = divmod(owner * padded, LANES)
        line = fold_s[owner:owner + 1, :]
        if off:
            line = pltpu.roll(line, off, 1)
        tiles[at] = jnp.where((lane >= off) & (lane < off + padded), line, tiles[at])
        if off + padded > LANES:
            tiles[at + 1] = jnp.where(lane < off + padded - LANES, line, tiles[at + 1])
    wave_s[...] = jnp.broadcast_to(jnp.concatenate(tiles, axis=1), wave_s.shape)

    xs[...] = jnp.zeros(xs.shape, F32)
    inside = lane_iota((rows, width)) < length
    for field in range(fields):
        points = grid_ref[field, 0].astype(F32)
        xs[rows * field:rows * (field + 1), 0:width] = jnp.where(inside, points, 0.0)
    stacked = jnp.concatenate(
        [xs[:, 4 * LANES * c:4 * LANES * (c + 1)] for c in range(2 * pieces)], axis=0
    ).astype(BF16)
    spread = dot(stacked, spread_matrix()).astype(BF16)
    for c in range(2 * pieces):
        for phase in range(4):
            at = (4 * (c // 2) + phase) * 16
            off = LANES * (c % 2)
            xq[at:at + 16, off:off + LANES] = spread[
                16 * c:16 * (c + 1), LANES * phase:LANES * (phase + 1)
            ]

    turns = 4 * pieces
    block = 2 * LANES
    xt[64:128, :] = jnp.zeros((64, slots), F32)
    values = xq[...]

    def lane_block(i, carry):
        at = pl.ds(pl.multiple_of(i * block, block), block)
        wave = wave_s[:, at]
        wave = jnp.concatenate([wave] * ((turns + 16) // 8), axis=0)
        co, si = phases_of(turns, wave, length, block)
        one = wave[0:1]
        weight = jnp.where(one == 0.0, 1.0, 2.0)
        weight = jnp.where((one >= 0.0) & (one <= jnp.full(one.shape, top, jnp.int32).astype(F32)), weight, 0.0)
        fc[:, at] = co[0:turns] * weight
        fs[:, at] = si[0:turns] * weight
        c_all = co[turns:turns + 8]
        s_all = si[turns:turns + 8]
        size, step = 8, turns + 8
        while size < DEEP:
            c1 = co[step:step + 1]
            s1 = si[step:step + 1]
            c_new = c_all * c1 - s_all * s1
            s_new = s_all * c1 + c_all * s1
            c_all = jnp.concatenate([c_all, c_new], axis=0)
            s_all = jnp.concatenate([s_all, s_new], axis=0)
            size, step = 2 * size, step + 1
        c_all = c_all.astype(BF16)
        s_all = s_all.astype(BF16)
        tc[:, at] = c_all
        ts[:, at] = s_all
        inner_c = dot(values, c_all)
        inner_s = dot(values, s_all)
        real = jnp.zeros((16, block), F32)
        imag = jnp.zeros((16, block), F32)
        for g in range(turns):
            c1 = fc[g:g + 1, at]
            s1 = fs[g:g + 1, at]
            part_c = inner_c[16 * g:16 * (g + 1)]
            part_s = inner_s[16 * g:16 * (g + 1)]
            real = real + (c1 * part_c - s1 * part_s)
            imag = imag - (c1 * part_s + s1 * part_c)
        both = jnp.concatenate([real, imag], axis=0) * jnp.where(one == 0.0, 1.0, 0.5)
        high = both.astype(BF16).astype(F32)
        xt[0:32, at] = high
        xt[32:64, at] = both - high
        return carry

    lax.fori_loop(0, slots // block, lane_block, 0)
    keeps = [
        pltpu.make_async_copy(source, target, sems.at[i])
        for i, (source, target) in enumerate(
            ((tc, tc_hbm), (ts, ts_hbm), (fc, fc_hbm), (fs, fs_hbm))
        )
    ]
    for keep in keeps:
        keep.start()

    for c in range(slots // LANES):
        ys[LANES * c:LANES * (c + 1), :] = jnp.transpose(xt[:, LANES * c:LANES * (c + 1)])
    turned = ys[...].reshape(owners, groups, 8, LANES)
    shape = (LANES, LANES)
    source = row_iota(shape)
    target = lane_iota(shape)
    vec = source % 16
    base = (vec % rows) * (fields * 2) + (vec // rows) * 2 + (source // 16) % 2
    mine = lax.axis_index("fld")
    used = (vec < rows * fields) & (source < 64)
    total = jnp.zeros((owners * 8, LANES), F32)
    for t in range(groups):
        place = jnp.where(used & (target == (base + unit * (t + mine)) % LANES), 1.0, 0.0).astype(BF16)
        total = total + dot(turned[:, t].reshape(owners * 8, LANES).astype(BF16), place)
    scale = 1.0 / jnp.sqrt(jnp.full((owners * 8, LANES), length, jnp.int32).astype(F32))
    msg_ref[...] = (total * scale).reshape(owners, 8, LANES)
    for keep in keeps:
        keep.wait()


def inverse_kernel(
    groups, len_hbm, band_hbm, fc_hbm, fs_hbm, tc_hbm, ts_hbm, msg_ref, grid_ref,
    len_ref, band_ref, fc, fs, tc, ts, sems, zs, xt, zr, zi, os,
):
    copies = [
        pltpu.make_async_copy(source, target, sems.at[i])
        for i, (source, target) in enumerate(
            (
                (len_hbm, len_ref), (band_hbm, band_ref), (fc_hbm, fc),
                (fs_hbm, fs), (tc_hbm, tc), (ts_hbm, ts),
            )
        )
    ]
    for copy in copies:
        copy.start()
    fields, _, rows, width = grid_ref.shape
    owners = msg_ref.shape[0]
    slots = tc.shape[1]
    turns = fc.shape[0]
    unit = rows * fields * 2
    high, low = split(msg_ref[...].reshape(owners * 8, LANES))
    pieces = jnp.concatenate([high, low], axis=1)
    shape = (LANES, LANES)
    source = row_iota(shape)
    target = lane_iota(shape)
    vec = target % 16
    base = (vec % rows + lax.axis_index("fld")) * (fields * 2) + (vec // rows) * 2 + target // 16
    used = (vec < rows * fields) & (target < 32)
    for t in range(groups):
        place = jnp.where(used & (source == (base + unit * t) % LANES), 1.0, 0.0).astype(BF16)
        zs[:, t] = dot(pieces, jnp.concatenate([place, place], axis=0)).reshape(owners, 8, LANES)
    turned = zs[...].reshape(slots, LANES)
    for c in range(slots // LANES):
        xt[:, LANES * c:LANES * (c + 1)] = jnp.transpose(turned[LANES * c:LANES * (c + 1)])[0:32]
    for copy in copies[0:4]:
        copy.wait()
    length = len_ref[band_ref[lax.axis_index("lat")]]
    block = 2 * LANES

    def lane_block(i, carry):
        at = pl.ds(pl.multiple_of(i * block, block), block)
        real = xt[0:16, at]
        imag = xt[16:32, at]
        for g in range(turns):
            c1 = fc[g:g + 1, at]
            s1 = fs[g:g + 1, at]
            zr[16 * g:16 * (g + 1), at] = (c1 * real - s1 * imag).astype(BF16)
            zi[16 * g:16 * (g + 1), at] = (s1 * real + c1 * imag).astype(BF16)
        return carry

    lax.fori_loop(0, slots // block, lane_block, 0)
    for copy in copies[4:]:
        copy.wait()
    out = dot_nt(zr[...], tc[...]) - dot_nt(zi[...], ts[...])
    out = out * (1.0 / jnp.sqrt(jnp.full((16 * turns, DEEP), length, jnp.int32).astype(F32)))
    chunks = os.shape[0] // 16
    for c in range(chunks):
        for phase in range(4):
            at = (4 * (c // 2) + phase) * 16
            off = LANES * (c % 2)
            os[16 * c:16 * (c + 1), LANES * phase:LANES * (phase + 1)] = out[
                at:at + 16, off:off + LANES
            ].astype(BF16)
    merged = dot_nt(os[...], spread_matrix())
    for c in range(chunks):
        begin = 4 * LANES * c
        size = min(4 * LANES, width - begin)
        if size <= 0:
            continue
        inside = begin + lane_iota((16, size)) < length
        piece = jnp.where(inside, merged[16 * c:16 * (c + 1), 0:size], 0.0)
        for field in range(fields):
            grid_ref[field, 0, :, begin:begin + size] = piece[
                rows * field:rows * (field + 1)
            ].astype(BF16)


def prepare_kernel(
    cut_off, pairs, fields, rows, fold_hbm, leg_hbm, tm_hbm, bm_hbm,
    eh_hbm, mix_ref, back_ref, turn_ref,
    fold_ref, leg_ref, tm_ref, bm_ref, sems, pad_s, eh_ref, out_sems,
):
    fetch_all(
        (fold_hbm, leg_hbm, tm_hbm, bm_hbm), (fold_ref, leg_ref, tm_ref, bm_ref), sems
    )
    everyone = tm_ref.shape[0]
    _, lats, places = leg_ref.shape
    groups_f = everyone // fields
    wf = fields * 2
    unit = rows * wf
    span = eh_ref.shape[1]
    eight = 8 * lats
    groups = eh_ref.shape[0] // (2 * eight)
    owner = lax.axis_index("lat") * groups_f + lax.axis_index("fld")

    pad_s[...] = jnp.zeros(pad_s.shape, F32)
    pad_s[0:everyone, 0:everyone] = tm_ref[...]
    shape = (LANES, LANES)
    level = (lane_iota(shape) // unit) * fields + (lane_iota(shape) % wf) // 2
    pick = jnp.where(row_iota(shape) == level, 1.0, 0.0).astype(BF16)
    lane = lane_iota((KPAD, LANES))
    parts = []
    for piece in split(pad_s[...]):
        wide = dot(piece, pick)
        total = []
        for r in range(rows):
            for c in range(2):
                keep = ((lane % unit) // wf == r) & (lane % 2 == c) & (lane < unit * groups_f)
                total.append(jnp.where(keep, wide, 0.0))
        parts.append(jnp.concatenate(total, axis=0).astype(BF16))
    mix_ref[...] = jnp.concatenate([parts[0], parts[1], parts[0]], axis=1)

    pad_s[...] = jnp.zeros(pad_s.shape, F32)
    pad_s[0:everyone, 0:everyone] = bm_ref[...]
    shape = (FPAD, KPAD)
    expand = jnp.where(row_iota(shape) // 2 == lane_iota(shape), 1.0, 0.0).astype(BF16)
    shape = (LANES, 2 * LANES)
    repeat = jnp.where(row_iota(shape) == lane_iota(shape) % KPAD, 1.0, 0.0).astype(BF16)
    shape = (FPAD, 2 * LANES)
    same = row_iota(shape) % 2 == (lane_iota(shape) // KPAD) % 2
    half = lane_iota((FPAD, LANES)) < 64
    narrow = lane_iota((FPAD, LANES)) < 2 * KPAD
    fulls = []
    for part, piece in enumerate(split(pad_s[...])):
        full = jnp.where(same, dot(dot(expand, piece).astype(BF16), repeat), 0.0)
        back_ref[part * FPAD:(part + 1) * FPAD, :] = full[:, 0:8 * KPAD].astype(BF16)
        fulls.append(jnp.where(narrow, full[:, 0:LANES], 0.0))
    turn_ref[...] = jnp.concatenate(
        [jnp.where(half, fulls[0], pltpu.roll(fulls[0], 64, 1)), fulls[1]], axis=1
    ).astype(BF16)

    whole = places // LANES * LANES
    shape = (lats, span)
    place = lane_iota(shape)

    def pair_block(pair, carry):
        there = pair < pairs
        index = jnp.minimum(pair, pairs - 1)
        wave = fold_ref[owner, 2 * index]
        limit = jnp.where(there, cut_off - wave, -1)
        last = jnp.where(there, places - 1, -1)
        leg = jnp.concatenate(
            [
                leg_ref[index, :, 0:whole],
                jnp.broadcast_to(leg_ref[index, :, whole:places], (lats, span - whole)),
            ],
            axis=1,
        )
        first = place <= limit
        second = (place > limit) & (place <= last)
        odd = ((place + jnp.where(first, 0, wave)) & 1) == 1
        signed = jnp.where(odd, -leg, leg)
        base = (pair // 4) * 2 * eight + (pair % 4) * 2 * lats
        for r, rowset in enumerate((leg, signed)):
            eh_ref[pl.ds(pl.multiple_of(base + r * eight, 16), 2 * lats), :] = jnp.concatenate(
                [jnp.where(first, rowset, 0.0), jnp.where(second, rowset, 0.0)], axis=0
            ).astype(BF16)
        return carry

    keeps = []
    for t in range(groups):
        lax.fori_loop(4 * t, 4 * t + 4, pair_block, 0)
        part = pl.ds(2 * eight * t, 2 * eight)
        keeps.append(pltpu.make_async_copy(eh_ref.at[part], eh_hbm.at[part], out_sems.at[t]))
        keeps[-1].start()
    for keep in keeps:
        keep.wait()


def solve_kernel(
    cut_off, pairs, fields, rows, band_hbm, fold_hbm, rates_hbm, eh_hbm, msg_ref, mix_ref, turn_ref,
    damped_ref, out_ref,
    band_ref, fold_ref, rates_ref, sems, vs, cs, eh_ref, in_sems,
):
    later = []
    for t in range(in_sems.shape[0]):
        size = eh_ref.shape[0] // in_sems.shape[0]
        part = pl.ds(size * t, size)
        later.append(pltpu.make_async_copy(eh_hbm.at[part], eh_ref.at[part], in_sems.at[t]))
        later[-1].start()
    fetch_all((band_hbm, fold_hbm, rates_hbm), (band_ref, fold_ref, rates_ref), sems)
    everyone = rates_ref.shape[0]
    lats = band_ref.shape[0]
    groups_f = msg_ref.shape[0] // lats
    wf = fields * 2
    unit = rows * wf
    span = eh_ref.shape[1]
    eight = 8 * lats
    groups = eh_ref.shape[0] // (2 * eight)
    deep = 8 * KPAD
    owner = lax.axis_index("lat") * groups_f + lax.axis_index("fld")
    for holder in range(lats):
        lat = band_ref[holder]
        for g in range(groups_f):
            vs[pl.ds(pl.multiple_of((g * lats + lat) * 8, 8), 8), :] = msg_ref[holder * groups_f + g]
    lane = lane_iota((lats, LANES))
    tiles = [
        [vs[pl.ds(g * eight + i8, lats, stride=8), :] for g in range(groups_f)] for i8 in range(8)
    ]
    tall = []
    for t in range(groups):
        for i8 in range(8):
            line = tiles[i8][0]
            for g in range(1, groups_f):
                here = (lane - unit * (t + g)) % LANES < unit
                line = jnp.where(here, tiles[i8][g], line)
            if t:
                line = pltpu.roll(line, LANES - unit * t, 1)
            tall.append(line)
    v_high, v_low = split(jnp.concatenate(tall, axis=0))
    mixed = dot_nt(mix_ref[...], jnp.concatenate([v_high, v_high, v_low], axis=1))

    rate_row = row_iota((KPAD, 2 * LANES))
    rate = jnp.zeros((KPAD, 2 * LANES), F32)
    for k in range(everyone):
        rate = jnp.where(rate_row == k, rates_ref[k], rate)
    slot_pair = (lane_iota((2 * KPAD, 2 * eight)) % eight) // (2 * lats)
    blank = jnp.zeros((64 - 2 * KPAD, span), BF16)
    front = lane_iota((lats, LANES)) < 64

    for t in range(groups):
        mine = mixed[:, eight * t:eight * (t + 1)]
        mine = jnp.concatenate([mine[0:2 * KPAD], mine[2 * KPAD:4 * KPAD]], axis=1)
        left = jnp.concatenate([jnp.where(slot_pair == pp, mine, 0.0) for pp in range(4)], axis=0)
        left = jnp.concatenate(split(left), axis=1)
        legs = pl.ds(2 * eight * t, 2 * eight)
        later[t].wait()
        waves, limits = [], []
        for pp in range(4):
            wave = fold_ref[owner, 2 * min(4 * t + pp, pairs - 1)]
            waves.append(wave)
            limits.append(cut_off - wave)
        for start in range(0, span, 2 * LANES):
            size = min(2 * LANES, span - start)
            right = eh_ref[legs, start:start + size]
            modes = dot(left, jnp.concatenate([right, right], axis=0))
            place = start + lane_iota((1, size))
            damped = []
            for pp in range(4):
                degree = jnp.where(place > limits[pp], place - 1, place + waves[pp])
                tau = (degree * (degree + 1)).astype(F32) * (1.0 / float(cut_off * (cut_off + 1)))
                below = 1.0 + tau * rate[:, 0:size]
                factor = pl.reciprocal(below, approx=True)
                factor = factor * (2.0 - below * factor)
                at = 2 * pp * KPAD
                damped.append(modes[at:at + KPAD] * factor)
                damped.append(modes[at + KPAD:at + 2 * KPAD] * factor)
            damped_ref[deep * t:deep * (t + 1), start:start + size] = jnp.concatenate(
                damped, axis=0
            ).astype(BF16)
        pieces = []
        for pp in range(4):
            at = deep * t + 2 * KPAD * pp
            pieces += [damped_ref[at:at + 2 * KPAD, :], blank]
        sums = dot_nt(eh_ref[legs, :], jnp.concatenate(pieces, axis=0))
        highs, lows = [], []
        for r in range(rows):
            for i8 in range(8):
                at = (r * 8 + i8) * lats
                pp = i8 // 2
                tile = sums[at:at + lats, LANES * (pp // 2):LANES * (pp // 2 + 1)]
                if pp % 2:
                    tile = pltpu.roll(tile, 64, 1)
                high = tile.astype(BF16).astype(F32)
                low = pltpu.roll(tile - high, 64, 1)
                highs.append(jnp.where(front, high, low))
                lows.append(jnp.where(front, high, 0.0))
        own = jnp.concatenate(
            [jnp.concatenate(highs, axis=0), jnp.concatenate(lows, axis=0)], axis=1
        ).astype(BF16)
        cs[2 * eight * t:2 * eight * (t + 1), 0:FPAD] = dot_nt(own, turn_ref[...])

    lane = lane_iota((8, LANES))
    for holder in range(lats):
        lat = band_ref[holder]
        tiles = [jnp.zeros((8, LANES), F32) for _ in range(groups_f)]
        for t in range(groups):
            for r in range(rows):
                put = wf * (rows * t + r)
                piece = cs[pl.ds((t * rows + r) * eight + lat, 8, stride=lats), :]
                if put:
                    piece = pltpu.roll(piece, put, 1)
                for g in range(groups_f):
                    here = (lane - (put + wf * g)) % LANES < wf
                    tiles[g] = jnp.where(here, piece, tiles[g])
        for g in range(groups_f):
            out_ref[holder * groups_f + g] = tiles[g]


def output_kernel(damped_ref, back_ref, spec_ref, bk):
    everyone, quad, _, places = spec_ref.shape
    span = damped_ref.shape[1]

    @pl.when(pl.program_id(0) == 0)
    def _():
        shape = (FPAD, 8 * KPAD)
        pair_of = lane_iota(shape) // (2 * KPAD)
        for part in range(2):
            full = back_ref[part * FPAD:(part + 1) * FPAD, :].astype(F32)
            for pp in range(4):
                at = (4 * part + pp) * FPAD
                bk[at:at + FPAD, :] = jnp.where(pair_of == pp, full, 0.0).astype(BF16)

    for start in range(0, span, 2 * LANES):
        size = min(2 * LANES, span - start)
        spec = dot(bk[...], damped_ref[:, start:start + size])
        spec = spec[0:4 * FPAD] + spec[4 * FPAD:]
        kept = min(size, places - start)
        for pp in range(4):
            for f in range(everyone):
                at = pp * FPAD + 2 * f
                spec_ref[f, pp, :, start:start + kept] = spec[at:at + 2, 0:kept]


def per_device(grid, row_lengths, band_map, fold_map, legendre, to_modes, back_modes, mode_rates):
    fields, single, rows, width = grid.shape
    pairs, places, lats = legendre.shape
    cut_off = places - 2
    everyone = to_modes.shape[0]
    owners, per_owner = fold_map.shape
    groups = -(-per_owner // 8)
    slots = owners * groups * 8
    pieces = -(-(width // 4) // DEEP)
    turns = 4 * pieces
    span = -(-places // LANES) * LANES
    hbm = pl.BlockSpec(memory_space=pltpu.HBM)
    vmem = pl.BlockSpec(memory_space=pltpu.VMEM)
    room = pltpu.CompilerParams(vmem_limit_bytes=ROOM)
    message = pltpu.HBM((owners, 8, LANES), F32)
    holders = band_map.shape[0]
    groups_f = everyone // fields
    dma = pltpu.SemaphoreType.DMA
    row_lengths, band_map, fold_map, to_modes, back_modes, mode_rates, grid = (
        pltpu.with_memory_space_constraint(x, pltpu.HBM)
        for x in (row_lengths, band_map, fold_map, to_modes, back_modes, mode_rates, grid)
    )
    legendre = pltpu.with_memory_space_constraint(jnp.transpose(legendre, (0, 2, 1)), pltpu.HBM)

    sending, cos_table, sin_table, cos_turn, sin_turn = pl.pallas_call(
        functools.partial(forward_kernel, cut_off, groups),
        out_shape=(
            message,
            pltpu.HBM((DEEP, slots), BF16),
            pltpu.HBM((DEEP, slots), BF16),
            pltpu.HBM((turns, slots), F32),
            pltpu.HBM((turns, slots), F32),
        ),
        in_specs=[hbm] * 4,
        out_specs=(vmem,) + (hbm,) * 4,
        scratch_shapes=[
            pltpu.SMEM(row_lengths.shape, jnp.int32),
            pltpu.SMEM(band_map.shape, jnp.int32),
            pltpu.VMEM(fold_map.shape, jnp.int32),
            pltpu.VMEM(grid.shape, BF16),
            dma((4,)),
            pltpu.VMEM((max(owners, 8), LANES), F32),
            pltpu.VMEM((8, slots), F32),
            pltpu.VMEM((16, 4 * DEEP * pieces), F32),
            pltpu.VMEM((16 * turns, DEEP), BF16),
            pltpu.VMEM((DEEP, slots), BF16),
            pltpu.VMEM((DEEP, slots), BF16),
            pltpu.VMEM((turns, slots), F32),
            pltpu.VMEM((turns, slots), F32),
            pltpu.VMEM((LANES, slots), F32),
            pltpu.VMEM((slots, LANES), F32),
        ],
        compiler_params=room,
        name="forward_rows",
    )(row_lengths, band_map, fold_map, grid)
    tables = [
        pltpu.with_memory_space_constraint(x, pltpu.HBM)
        for x in (cos_turn, sin_turn, cos_table, sin_table)
    ]
    arrived = lax.all_to_all(sending, ("lat", "fld"), split_axis=0, concat_axis=0, tiled=True)

    legs, mix, back, turn_back = pl.pallas_call(
        functools.partial(prepare_kernel, cut_off, pairs, fields, rows),
        out_shape=(
            pltpu.HBM((groups * 16 * lats, span), BF16),
            pltpu.VMEM((2 * rows * KPAD, 3 * LANES), BF16),
            pltpu.VMEM((2 * FPAD, 8 * KPAD), BF16),
            pltpu.VMEM((FPAD, 2 * LANES), BF16),
        ),
        in_specs=[hbm] * 4,
        out_specs=(hbm,) + (vmem,) * 3,
        scratch_shapes=[
            pltpu.SMEM(fold_map.shape, jnp.int32),
            pltpu.VMEM((pairs, lats, places), F32),
            pltpu.VMEM(to_modes.shape, F32),
            pltpu.VMEM(back_modes.shape, F32),
            dma((4,)),
            pltpu.VMEM((KPAD, LANES), F32),
            pltpu.VMEM((groups * 16 * lats, span), BF16),
            dma((groups,)),
        ],
        compiler_params=room,
        cost_estimate=pl.CostEstimate(flops=10**8, bytes_accessed=8 * 10**6, transcendentals=0),
        name="prepare",
    )(fold_map, legendre, to_modes, back_modes)
    legs = pltpu.with_memory_space_constraint(legs, pltpu.HBM)
    mix, back, turn_back = (
        pltpu.with_memory_space_constraint(x, pltpu.VMEM) for x in (mix, back, turn_back)
    )

    damped, leaving = pl.pallas_call(
        functools.partial(solve_kernel, cut_off, pairs, fields, rows),
        out_shape=(pltpu.VMEM((groups * 8 * KPAD, span), BF16), message),
        in_specs=[hbm] * 4 + [vmem] * 3,
        out_specs=(vmem,) * 2,
        scratch_shapes=[
            pltpu.SMEM(band_map.shape, jnp.int32),
            pltpu.SMEM(fold_map.shape, jnp.int32),
            pltpu.SMEM(mode_rates.shape, F32),
            dma((3,)),
            pltpu.VMEM((owners * 8, LANES), F32),
            pltpu.VMEM((groups * 16 * lats, LANES), F32),
            pltpu.VMEM((groups * 16 * lats, span), BF16),
            dma((groups,)),
        ],
        compiler_params=room,
        name="solve",
    )(band_map, fold_map, mode_rates, legs, arrived, mix, turn_back)

    returned = lax.all_to_all(leaving, ("lat", "fld"), split_axis=0, concat_axis=0, tiled=True)

    damped = pltpu.with_memory_space_constraint(damped, pltpu.VMEM)
    spectral = pl.pallas_call(
        output_kernel,
        grid=(groups,),
        out_shape=jax.ShapeDtypeStruct((everyone, pairs, 2, places), F32),
        in_specs=[
            pl.BlockSpec((8 * KPAD, span), lambda t: (t, 0)),
            pl.BlockSpec((2 * FPAD, 8 * KPAD), lambda t: (0, 0)),
        ],
        out_specs=pl.BlockSpec((everyone, 4, 2, places), lambda t: (0, t, 0, 0)),
        scratch_shapes=[pltpu.VMEM((8 * FPAD, 8 * KPAD), BF16)],
        compiler_params=pltpu.CompilerParams(
            dimension_semantics=("arbitrary",), vmem_limit_bytes=ROOM
        ),
        cost_estimate=pl.CostEstimate(flops=10**8, bytes_accessed=8 * 10**6, transcendentals=0),
        name="spectral_output",
    )(damped, back)

    grid_out = pl.pallas_call(
        functools.partial(inverse_kernel, groups),
        out_shape=jax.ShapeDtypeStruct(grid.shape, BF16),
        in_specs=[hbm] * 6 + [vmem],
        out_specs=vmem,
        scratch_shapes=[
            pltpu.SMEM(row_lengths.shape, jnp.int32),
            pltpu.SMEM(band_map.shape, jnp.int32),
            pltpu.VMEM((turns, slots), F32),
            pltpu.VMEM((turns, slots), F32),
            pltpu.VMEM((DEEP, slots), BF16),
            pltpu.VMEM((DEEP, slots), BF16),
            dma((6,)),
            pltpu.VMEM((owners, groups, 8, LANES), F32),
            pltpu.VMEM((32, slots), F32),
            pltpu.VMEM((16 * turns, slots), BF16),
            pltpu.VMEM((16 * turns, slots), BF16),
            pltpu.VMEM((32 * pieces, 4 * LANES), BF16),
        ],
        compiler_params=room,
        name="inverse_rows",
    )(row_lengths, band_map, *tables, returned)
    return (jnp.transpose(spectral, (0, 2, 1, 3)), grid_out)


def solution(mesh):
    placed = (
        P("fld", "lat", None, None),
        P(),
        P(),
        P(),
        P(("lat", "fld"), None, None),
        P(),
        P(),
        P(),
    )
    return jax.shard_map(
        per_device,
        mesh=mesh,
        in_specs=placed,
        out_specs=(P(None, None, ("lat", "fld"), None), P("fld", "lat", None, None)),
        check_vma=False,
    )
```

```python
import functools
import math

import jax
import jax.numpy as jnp
from jax import lax
from jax.experimental import pallas as pl
from jax.experimental.pallas import tpu as pltpu
from jax.sharding import PartitionSpec as P

LANES = 128
KPAD = 24
FPAD = 64
DEEP = 256
ROOM = 24 * 1024 * 1024
F32 = jnp.float32
BF16 = jnp.bfloat16
NT_DIMS = (((1,), (1,)), ((), ()))
SIN_POLY = (
    6.283185302447051,
    -41.34170038368319,
    81.60513023312113,
    -76.70299324464969,
    42.02573766814694,
    -14.899106966102595,
    3.237062655726421,
)
COS_POLY = (
    0.9999999889083757,
    -19.739204448887243,
    64.93911476570418,
    -85.45008785413638,
    60.167188450194914,
    -25.9658703083255,
    6.526145851512229,
)


def dot(a, b):
    return jnp.dot(a, b, preferred_element_type=F32)


def dot_nt(a, b):
    return lax.dot_general(a, b, NT_DIMS, preferred_element_type=F32)


def split(x):
    high = x.astype(BF16)
    return high, (x - high.astype(F32)).astype(BF16)


def horner(coefs, z):
    total = coefs[-1] * z + coefs[-2]
    for coef in coefs[-3::-1]:
        total = total * z + coef
    return total


def turn(steps, period, inverse):
    rest = steps - period * jnp.floor(steps * inverse + 0.5)
    part = rest * inverse
    z = part * part
    return horner(COS_POLY, z), part * horner(SIN_POLY, z)


def fetch_all(sources, targets, sems):
    copies = [
        pltpu.make_async_copy(source, target, sems.at[i])
        for i, (source, target) in enumerate(zip(sources, targets))
    ]
    for copy in copies:
        copy.start()
    for copy in copies:
        copy.wait()


def lane_iota(shape):
    return lax.broadcasted_iota(jnp.int32, shape, len(shape) - 1)


def row_iota(shape):
    return lax.broadcasted_iota(jnp.int32, shape, len(shape) - 2)


def lanes_within(lane, start, size):
    start %= LANES
    if start + size <= LANES:
        return (lane >= start) & (lane < start + size)
    return (lane >= start) | (lane < start + size - LANES)


def spread_matrix():
    shape = (4 * LANES, LANES)
    picks = []
    for phase in range(4):
        picks.append(jnp.where(row_iota(shape) == 4 * lane_iota(shape) + phase, 1.0, 0.0))
    return jnp.concatenate(picks, axis=1).astype(BF16)


def phases_of(groups, wave, length, lanes):
    shape = (groups + 16, lanes)
    row = row_iota(shape)
    steps = jnp.where(row < groups, (row // 4) * (4 * DEEP) + row % 4, 4 * (row - groups))
    steps = jnp.where(row >= groups + 8, 32 << jnp.maximum(row - groups - 8, 0), steps)
    period = jnp.full(shape, length, jnp.int32).astype(F32)
    return turn(steps.astype(F32) * wave, period, 1.0 / period)


def forward_kernel(
    cut_off, groups, len_hbm, band_hbm, fold_hbm, grid_hbm,
    msg_ref, tc_hbm, ts_hbm, fc, fs,
    len_ref, band_ref, fold_ref, grid_ref, sems, fold_s, wave_s, xs, xq, tc, ts, xt,
):
    fetch_all(
        (len_hbm, band_hbm, fold_hbm, grid_hbm), (len_ref, band_ref, fold_ref, grid_ref), sems
    )
    fields, _, rows, width = grid_ref.shape
    owners, per_owner = fold_ref.shape
    slots = tc.shape[1]
    pieces = xq.shape[0] // 64
    unit = rows * fields * 2
    length = len_ref[band_ref[lax.axis_index("lat")]]
    top = jnp.minimum(cut_off, (length - 1) // 2)

    fold_s[...] = jnp.full(fold_s.shape, -1.0, F32)
    fold_s[0:owners, 0:per_owner] = fold_ref[...].astype(F32)
    eights = jnp.floor(fold_s[...] * 0.125)
    parts = jnp.concatenate([eights, fold_s[...] - 8.0 * eights], axis=1).astype(BF16)
    shape = (owners * 8, fold_s.shape[0])
    repeat = jnp.where(row_iota(shape) // 8 == lane_iota(shape), 1.0, 0.0).astype(BF16)
    repeated = dot(repeat, parts)
    lane = lane_iota(repeated.shape)
    place = lane % LANES - row_iota(repeated.shape) % 8
    weigh = jnp.where(lane_iota((8, 2 * LANES)) < LANES, 8.0, 1.0).astype(BF16)
    for t in range(groups):
        chosen = jnp.where(place == 8 * t, repeated, 0.0).astype(BF16)
        wave_s[:, owners * 8 * t:owners * 8 * (t + 1)] = dot_nt(weigh, chosen)

    xs[...] = jnp.zeros(xs.shape, F32)
    inside = lane_iota((rows, width)) < length
    for field in range(fields):
        points = grid_ref[field, 0].astype(F32)
        xs[rows * field:rows * (field + 1), 0:width] = jnp.where(inside, points, 0.0)
    stacked = jnp.concatenate(
        [xs[:, 4 * LANES * c:4 * LANES * (c + 1)] for c in range(2 * pieces)], axis=0
    ).astype(BF16)
    spread = dot(stacked, spread_matrix()).astype(BF16)
    for c in range(2 * pieces):
        for phase in range(4):
            at = (4 * (c // 2) + phase) * 16
            off = LANES * (c % 2)
            xq[at:at + 16, off:off + LANES] = spread[
                16 * c:16 * (c + 1), LANES * phase:LANES * (phase + 1)
            ]

    turns = 4 * pieces
    block = 2 * LANES
    values = xq[...]
    for i in range(slots // block):
        at = pl.ds(i * block, block)
        wave = wave_s[:, at]
        wave = jnp.concatenate([wave] * ((turns + 16) // 8), axis=0)
        co, si = phases_of(turns, wave, length, block)
        one = wave[0:1]
        weight = jnp.where(one == 0.0, 1.0, 2.0)
        weight = jnp.where((one >= 0.0) & (one <= jnp.full(one.shape, top, jnp.int32).astype(F32)), weight, 0.0)
        fc[:, at] = co[0:turns] * weight
        fs[:, at] = si[0:turns] * weight
        c_all = co[turns:turns + 8]
        s_all = si[turns:turns + 8]
        size, step = 8, turns + 8
        while size < DEEP:
            c1 = co[step:step + 1]
            s1 = si[step:step + 1]
            c_new = c_all * c1 - s_all * s1
            s_new = s_all * c1 + c_all * s1
            c_all = jnp.concatenate([c_all, c_new], axis=0)
            s_all = jnp.concatenate([s_all, s_new], axis=0)
            size, step = 2 * size, step + 1
        c_all = c_all.astype(BF16)
        s_all = s_all.astype(BF16)
        tc[:, at] = c_all
        ts[:, at] = s_all
        inner_c = dot(values, c_all)
        inner_s = dot(values, s_all)
        real = jnp.zeros((16, block), F32)
        imag = jnp.zeros((16, block), F32)
        for g in range(turns):
            c1 = fc[g:g + 1, at]
            s1 = fs[g:g + 1, at]
            part_c = inner_c[16 * g:16 * (g + 1)]
            part_s = inner_s[16 * g:16 * (g + 1)]
            real = real + (c1 * part_c - s1 * part_s)
            imag = imag - (c1 * part_s + s1 * part_c)
        both = jnp.concatenate([real, imag], axis=0) * jnp.where(one == 0.0, 1.0, 0.5)
        xt[:, at] = jnp.concatenate(split(both), axis=0)
    keeps = [
        pltpu.make_async_copy(source, target, sems.at[i])
        for i, (source, target) in enumerate(
            ((tc, tc_hbm), (ts, ts_hbm))
        )
    ]
    for keep in keeps:
        keep.start()

    turned = jnp.concatenate(
        [xt[:, owners * 8 * t:owners * 8 * (t + 1)] for t in range(groups)], axis=0
    )
    shape = (LANES, 64 * groups)
    source = lane_iota(shape)
    vec = source % 16
    base = (vec % rows) * (fields * 2) + (vec // rows) * 2 + (source // 16) % 2
    target = (base + unit * (source // 64 + lax.axis_index("fld"))) % LANES
    place = jnp.where((vec < rows * fields) & (row_iota(shape) == target), 1.0, 0.0).astype(BF16)
    total = dot(place, turned)
    scale = 1.0 / jnp.sqrt(jnp.full(total.shape, length, jnp.int32).astype(F32))
    msg_ref[...] = jnp.transpose(total * scale).reshape(owners, 8, LANES)
    for keep in keeps:
        keep.wait()


def inverse_kernel(
    groups, len_hbm, band_hbm, tc_hbm, ts_hbm, fc, fs, msg_ref, grid_ref,
    len_ref, band_ref, tc, ts, sems, os,
):
    copies = [
        pltpu.make_async_copy(source, target, sems.at[i])
        for i, (source, target) in enumerate(
            ((len_hbm, len_ref), (band_hbm, band_ref), (tc_hbm, tc), (ts_hbm, ts))
        )
    ]
    for copy in copies:
        copy.start()
    fields, _, rows, width = grid_ref.shape
    owners = msg_ref.shape[0]
    slots = tc.shape[1]
    turns = fc.shape[0]
    unit = rows * fields * 2
    high, low = split(msg_ref[...].reshape(owners * 8, LANES))
    pieces = jnp.concatenate([high, low], axis=1)
    shape = (32 * groups, 2 * LANES)
    target = row_iota(shape) % 32
    vec = target % 16
    base = (vec % rows) * (fields * 2) + (vec // rows) * 2 + target // 16
    source = (base + unit * (row_iota(shape) // 32) + lax.axis_index("fld") * (fields * 2)) % LANES
    place = jnp.where(
        (vec < rows * fields) & (lane_iota(shape) % LANES == source), 1.0, 0.0
    ).astype(BF16)
    turned = dot_nt(place, pieces)
    block = 2 * LANES
    for copy in copies:
        copy.wait()
    length = len_ref[band_ref[lax.axis_index("lat")]]
    out = jnp.zeros((16 * turns, DEEP), F32)
    for i in range(slots // block):
        t, off = divmod(i * block, owners * 8)
        real = turned[32 * t:32 * t + 16, off:off + block]
        imag = turned[32 * t + 16:32 * t + 32, off:off + block]
        at = pl.ds(i * block, block)
        reals, imags = [], []
        for g in range(turns):
            c1 = fc[g:g + 1, at]
            s1 = fs[g:g + 1, at]
            reals.append(c1 * real - s1 * imag)
            imags.append(s1 * real + c1 * imag)
        reals = jnp.concatenate(reals, axis=0).astype(BF16)
        imags = jnp.concatenate(imags, axis=0).astype(BF16)
        out = out + (dot_nt(reals, tc[:, at]) - dot_nt(imags, ts[:, at]))
    out = out * (1.0 / jnp.sqrt(jnp.full((16 * turns, DEEP), length, jnp.int32).astype(F32)))
    chunks = os.shape[0] // 16
    for c in range(chunks):
        for phase in range(4):
            at = (4 * (c // 2) + phase) * 16
            off = LANES * (c % 2)
            os[16 * c:16 * (c + 1), LANES * phase:LANES * (phase + 1)] = out[
                at:at + 16, off:off + LANES
            ].astype(BF16)
    merged = dot_nt(os[...], spread_matrix())
    for c in range(chunks):
        begin = 4 * LANES * c
        size = min(4 * LANES, width - begin)
        if size <= 0:
            continue
        inside = begin + lane_iota((16, size)) < length
        piece = jnp.where(inside, merged[16 * c:16 * (c + 1), 0:size], 0.0)
        for field in range(fields):
            grid_ref[field, 0, :, begin:begin + size] = piece[
                rows * field:rows * (field + 1)
            ].astype(BF16)


def prepare_kernel(
    cut_off, pairs, fields, rows, fold_hbm, band_hbm, rates_hbm, leg_hbm, tm_hbm, bm_hbm,
    eh_hbm, mix_ref, back_ref, turn_ref, tau_ref, rate_ref,
    fold_ref, band_ref, rates_ref, leg_ref, tm_ref, bm_ref, sems, pad_s, eh_ref, out_sems,
):
    fetch_all(
        (fold_hbm, band_hbm, rates_hbm, leg_hbm, tm_hbm, bm_hbm),
        (fold_ref, band_ref, rates_ref, leg_ref, tm_ref, bm_ref),
        sems,
    )
    everyone = tm_ref.shape[0]
    _, lats, places = leg_ref.shape
    groups_f = everyone // fields
    wf = fields * 2
    unit = rows * wf
    span = eh_ref.shape[1]
    eight = 8 * lats
    groups = eh_ref.shape[0] // (2 * eight)
    owner = lax.axis_index("lat") * groups_f + lax.axis_index("fld")

    pad_s[...] = jnp.zeros(pad_s.shape, F32)
    pad_s[0:everyone, 0:everyone] = tm_ref[...]
    shape = (LANES, LANES)
    level = (lane_iota(shape) // unit) * fields + (lane_iota(shape) % wf) // 2
    pick = jnp.where(row_iota(shape) == level, 1.0, 0.0).astype(BF16)
    lane = lane_iota((KPAD, LANES))
    parts = []
    for piece in split(pad_s[...]):
        wide = dot(piece, pick)
        total = []
        for r in range(rows):
            for c in range(2):
                keep = ((lane % unit) // wf == r) & (lane % 2 == c) & (lane < unit * groups_f)
                total.append(jnp.where(keep, wide, 0.0))
        parts.append(jnp.concatenate(total, axis=0).astype(BF16))
    mix_ref[...] = jnp.concatenate([parts[0], parts[1], parts[0]], axis=1)

    pad_s[...] = jnp.zeros(pad_s.shape, F32)
    pad_s[0:everyone, 0:everyone] = bm_ref[...]
    shape = (FPAD, KPAD)
    expand = jnp.where(row_iota(shape) // 2 == lane_iota(shape), 1.0, 0.0).astype(BF16)
    shape = (LANES, 2 * LANES)
    repeat = jnp.where(row_iota(shape) == lane_iota(shape) % KPAD, 1.0, 0.0).astype(BF16)
    shape = (FPAD, 2 * LANES)
    same = row_iota(shape) % 2 == (lane_iota(shape) // KPAD) % 2
    half = lane_iota((FPAD, LANES)) < 64
    narrow = lane_iota((FPAD, LANES)) < 2 * KPAD
    fulls = []
    for part, piece in enumerate(split(pad_s[...])):
        full = jnp.where(same, dot(dot(expand, piece).astype(BF16), repeat), 0.0)
        back_ref[part * FPAD:(part + 1) * FPAD, :] = full[:, 0:8 * KPAD].astype(BF16)
        fulls.append(jnp.where(narrow, full[:, 0:LANES], 0.0))
    turn_ref[...] = jnp.concatenate(
        [jnp.where(half, fulls[0], pltpu.roll(fulls[0], 64, 1)), fulls[1]], axis=1
    ).astype(BF16)

    row = row_iota((KPAD, 2 * LANES))
    rate = jnp.zeros((KPAD, 2 * LANES), F32)
    for k in range(everyone):
        rate = jnp.where(row == k, rates_ref[k], rate)
    rate_ref[...] = rate
    line = lane_iota((1, span))
    for pair in range(4 * groups):
        wave = fold_ref[owner, 2 * min(pair, pairs - 1)]
        degree = jnp.where(line > cut_off - wave, line - 1, line + wave)
        tau_ref[pair:pair + 1, :] = (degree * (degree + 1)).astype(F32) * (
            1.0 / float(cut_off * (cut_off + 1))
        )

    shape = (2 * eight, 2 * eight)
    band = jnp.zeros(shape, jnp.int32)
    for holder in range(lats):
        band = jnp.where(row_iota(shape) % lats == holder, band_ref[holder], band)
    order = jnp.where(
        (row_iota(shape) // lats == lane_iota(shape) // lats) & (lane_iota(shape) % lats == band),
        1.0,
        0.0,
    ).astype(BF16)

    whole = places // LANES * LANES
    shape = (lats, span)
    place = lane_iota(shape)

    def pair_block(pair, carry):
        there = pair < pairs
        index = jnp.minimum(pair, pairs - 1)
        wave = fold_ref[owner, 2 * index]
        limit = jnp.where(there, cut_off - wave, -1)
        last = jnp.where(there, places - 1, -1)
        leg = jnp.concatenate(
            [
                leg_ref[index, :, 0:whole],
                jnp.broadcast_to(leg_ref[index, :, whole:places], (lats, span - whole)),
            ],
            axis=1,
        )
        first = place <= limit
        second = (place > limit) & (place <= last)
        odd = ((place + jnp.where(first, 0, wave)) & 1) == 1
        signed = jnp.where(odd, -leg, leg)
        base = (pair // 4) * 2 * eight + (pair % 4) * 2 * lats
        for r, rowset in enumerate((leg, signed)):
            eh_ref[pl.ds(pl.multiple_of(base + r * eight, 16), 2 * lats), :] = jnp.concatenate(
                [jnp.where(first, rowset, 0.0), jnp.where(second, rowset, 0.0)], axis=0
            ).astype(BF16)
        return carry

    keeps = []
    for t in range(groups):
        lax.fori_loop(4 * t, 4 * t + 4, pair_block, 0)
        part = pl.ds(2 * eight * t, 2 * eight)
        eh_ref[part, :] = dot(order, eh_ref[part, :]).astype(BF16)
        keeps.append(pltpu.make_async_copy(eh_ref.at[part], eh_hbm.at[part], out_sems.at[t]))
        keeps[-1].start()
    for keep in keeps:
        keep.wait()


def solve_kernel(
    fields, rows, lats, eh_hbm, msg_ref, mix_ref, turn_ref, tau_ref, rate_ref,
    damped_ref, out_ref, cs, eh_ref, in_sems,
):
    groups = in_sems.shape[0]
    eight = 8 * lats
    later = []
    for t in range(groups):
        part = pl.ds(2 * eight * t, 2 * eight)
        later.append(pltpu.make_async_copy(eh_hbm.at[part], eh_ref.at[part], in_sems.at[t]))
        later[-1].start()
    groups_f = msg_ref.shape[0] // eight
    wf = fields * 2
    unit = rows * wf
    span = eh_ref.shape[1]
    deep = 8 * KPAD
    lane = lane_iota((lats, LANES))
    tiles = [
        [msg_ref[pl.ds(8 * g + i8, lats, stride=8 * groups_f), :] for g in range(groups_f)]
        for i8 in range(8)
    ]
    tall = []
    for t in range(groups):
        here = [lanes_within(lane, unit * (t + g), unit) for g in range(groups_f)]
        for i8 in range(8):
            line = tiles[i8][0]
            for g in range(1, groups_f):
                line = jnp.where(here[g], tiles[i8][g], line)
            if t:
                line = pltpu.roll(line, LANES - unit * t, 1)
            tall.append(line)
    v_high, v_low = split(jnp.concatenate(tall, axis=0))
    mixed = dot_nt(mix_ref[...], jnp.concatenate([v_high, v_high, v_low], axis=1))

    rate = rate_ref[...]
    slot_pair = (lane_iota((2 * KPAD, 2 * eight)) % eight) // (2 * lats)
    blank = jnp.zeros((64 - 2 * KPAD, span), BF16)
    front = lane_iota((lats, LANES)) < 64

    for t in range(groups):
        mine = mixed[:, eight * t:eight * (t + 1)]
        mine = jnp.concatenate([mine[0:2 * KPAD], mine[2 * KPAD:4 * KPAD]], axis=1)
        left = jnp.concatenate([jnp.where(slot_pair == pp, mine, 0.0) for pp in range(4)], axis=0)
        left = jnp.concatenate(split(left), axis=1)
        legs = pl.ds(2 * eight * t, 2 * eight)
        later[t].wait()
        for start in range(0, span, 2 * LANES):
            size = min(2 * LANES, span - start)
            right = eh_ref[legs, start:start + size]
            modes = dot(left, jnp.concatenate([right, right], axis=0))
            damped = []
            for pp in range(4):
                tau = tau_ref[4 * t + pp:4 * t + pp + 1, start:start + size]
                below = 1.0 + tau * rate[:, 0:size]
                factor = pl.reciprocal(below, approx=True)
                factor = factor * (2.0 - below * factor)
                at = 2 * pp * KPAD
                damped.append(modes[at:at + KPAD] * factor)
                damped.append(modes[at + KPAD:at + 2 * KPAD] * factor)
            damped_ref[deep * t:deep * (t + 1), start:start + size] = jnp.concatenate(
                damped, axis=0
            ).astype(BF16)
        pieces = []
        for pp in range(4):
            at = deep * t + 2 * KPAD * pp
            pieces += [damped_ref[at:at + 2 * KPAD, :], blank]
        sums = dot_nt(eh_ref[legs, :], jnp.concatenate(pieces, axis=0))
        highs, lows = [], []
        for r in range(rows):
            for i8 in range(8):
                at = (r * 8 + i8) * lats
                pp = i8 // 2
                tile = sums[at:at + lats, LANES * (pp // 2):LANES * (pp // 2 + 1)]
                if pp % 2:
                    tile = pltpu.roll(tile, 64, 1)
                high = tile.astype(BF16).astype(F32)
                low = pltpu.roll(tile - high, 64, 1)
                highs.append(jnp.where(front, high, low))
                lows.append(jnp.where(front, high, 0.0))
        own = jnp.concatenate(
            [jnp.concatenate(highs, axis=0), jnp.concatenate(lows, axis=0)], axis=1
        ).astype(BF16)
        cs[2 * eight * t:2 * eight * (t + 1), 0:FPAD] = dot_nt(own, turn_ref[...])

    lane = lane_iota((8, LANES))
    here = [
        lanes_within(lane, wf * u, wf) for u in range(rows * groups + groups_f - 1)
    ]
    for holder in range(lats):
        tiles = [jnp.zeros((8, LANES), F32) for _ in range(groups_f)]
        for u in range(rows * groups):
            piece = cs[pl.ds(u * eight + holder, 8, stride=lats), :]
            if u:
                piece = pltpu.roll(piece, wf * u, 1)
            for g in range(groups_f):
                tiles[g] = jnp.where(here[u + g], piece, tiles[g])
        for g in range(groups_f):
            at = (holder * groups_f + g) * 8
            out_ref[at:at + 8, :] = tiles[g]


def output_kernel(damped_ref, back_ref, spec_ref, bk):
    everyone, quad, _, places = spec_ref.shape
    span = damped_ref.shape[1]

    @pl.when(pl.program_id(0) == 0)
    def _():
        shape = (FPAD, 8 * KPAD)
        pair_of = lane_iota(shape) // (2 * KPAD)
        for part in range(2):
            full = back_ref[part * FPAD:(part + 1) * FPAD, :].astype(F32)
            for pp in range(4):
                at = (4 * part + pp) * FPAD
                bk[at:at + FPAD, :] = jnp.where(pair_of == pp, full, 0.0).astype(BF16)

    for start in range(0, span, 2 * LANES):
        size = min(2 * LANES, span - start)
        spec = dot(bk[...], damped_ref[:, start:start + size])
        spec = spec[0:4 * FPAD] + spec[4 * FPAD:]
        kept = min(size, places - start)
        for pp in range(4):
            for f in range(everyone):
                at = pp * FPAD + 2 * f
                spec_ref[f, pp, :, start:start + kept] = spec[at:at + 2, 0:kept]


def per_device(grid, row_lengths, band_map, fold_map, legendre, to_modes, back_modes, mode_rates):
    fields, single, rows, width = grid.shape
    pairs, places, lats = legendre.shape
    cut_off = places - 2
    everyone = to_modes.shape[0]
    owners, per_owner = fold_map.shape
    groups = -(-per_owner // 8)
    slots = owners * groups * 8
    pieces = -(-(width // 4) // DEEP)
    turns = 4 * pieces
    span = -(-places // LANES) * LANES
    hbm = pl.BlockSpec(memory_space=pltpu.HBM)
    vmem = pl.BlockSpec(memory_space=pltpu.VMEM)
    room = pltpu.CompilerParams(vmem_limit_bytes=ROOM)
    message = pltpu.HBM((owners, 8, LANES), F32)
    holders = band_map.shape[0]
    groups_f = everyone // fields
    dma = pltpu.SemaphoreType.DMA
    row_lengths, band_map, fold_map, to_modes, back_modes, mode_rates, grid = (
        pltpu.with_memory_space_constraint(x, pltpu.HBM)
        for x in (row_lengths, band_map, fold_map, to_modes, back_modes, mode_rates, grid)
    )
    legendre = pltpu.with_memory_space_constraint(jnp.transpose(legendre, (0, 2, 1)), pltpu.HBM)

    sending, cos_table, sin_table, cos_turn, sin_turn = pl.pallas_call(
        functools.partial(forward_kernel, cut_off, groups),
        out_shape=(
            message,
            pltpu.HBM((DEEP, slots), BF16),
            pltpu.HBM((DEEP, slots), BF16),
            pltpu.VMEM((turns, slots), F32),
            pltpu.VMEM((turns, slots), F32),
        ),
        in_specs=[hbm] * 4,
        out_specs=(vmem, hbm, hbm, vmem, vmem),
        scratch_shapes=[
            pltpu.SMEM(row_lengths.shape, jnp.int32),
            pltpu.SMEM(band_map.shape, jnp.int32),
            pltpu.VMEM(fold_map.shape, jnp.int32),
            pltpu.VMEM(grid.shape, BF16),
            dma((4,)),
            pltpu.VMEM((LANES, LANES), F32),
            pltpu.VMEM((8, slots), F32),
            pltpu.VMEM((16, 4 * DEEP * pieces), F32),
            pltpu.VMEM((16 * turns, DEEP), BF16),
            pltpu.VMEM((DEEP, slots), BF16),
            pltpu.VMEM((DEEP, slots), BF16),
            pltpu.VMEM((64, slots), BF16),
        ],
        compiler_params=room,
        name="forward_rows",
    )(row_lengths, band_map, fold_map, grid)
    tables = [
        pltpu.with_memory_space_constraint(x, pltpu.HBM) for x in (cos_table, sin_table)
    ] + [pltpu.with_memory_space_constraint(x, pltpu.VMEM) for x in (cos_turn, sin_turn)]
    arrived = lax.all_to_all(sending, ("lat", "fld"), split_axis=0, concat_axis=0, tiled=True)

    legs, mix, back, turn_back, tau, rate = pl.pallas_call(
        functools.partial(prepare_kernel, cut_off, pairs, fields, rows),
        out_shape=(
            pltpu.HBM((groups * 16 * lats, span), BF16),
            pltpu.VMEM((2 * rows * KPAD, 3 * LANES), BF16),
            pltpu.VMEM((2 * FPAD, 8 * KPAD), BF16),
            pltpu.VMEM((FPAD, 2 * LANES), BF16),
            pltpu.VMEM((groups * 4, span), F32),
            pltpu.VMEM((KPAD, 2 * LANES), F32),
        ),
        in_specs=[hbm] * 6,
        out_specs=(hbm,) + (vmem,) * 5,
        scratch_shapes=[
            pltpu.SMEM(fold_map.shape, jnp.int32),
            pltpu.SMEM(band_map.shape, jnp.int32),
            pltpu.SMEM(mode_rates.shape, F32),
            pltpu.VMEM((pairs, lats, places), F32),
            pltpu.VMEM(to_modes.shape, F32),
            pltpu.VMEM(back_modes.shape, F32),
            dma((6,)),
            pltpu.VMEM((KPAD, LANES), F32),
            pltpu.VMEM((groups * 16 * lats, span), BF16),
            dma((groups,)),
        ],
        compiler_params=room,
        cost_estimate=pl.CostEstimate(flops=10**8, bytes_accessed=8 * 10**6, transcendentals=0),
        name="prepare",
    )(fold_map, band_map, mode_rates, legendre, to_modes, back_modes)
    legs = pltpu.with_memory_space_constraint(legs, pltpu.HBM)
    mix, back, turn_back, tau, rate = (
        pltpu.with_memory_space_constraint(x, pltpu.VMEM)
        for x in (mix, back, turn_back, tau, rate)
    )

    damped, leaving = pl.pallas_call(
        functools.partial(solve_kernel, fields, rows, lats),
        out_shape=(
            pltpu.VMEM((groups * 8 * KPAD, span), BF16),
            pltpu.HBM((owners * 8, LANES), F32),
        ),
        in_specs=[hbm] + [vmem] * 5,
        out_specs=(vmem,) * 2,
        scratch_shapes=[
            pltpu.VMEM((groups * 16 * lats, LANES), F32),
            pltpu.VMEM((groups * 16 * lats, span), BF16),
            dma((groups,)),
        ],
        compiler_params=room,
        name="solve",
    )(legs, arrived.reshape(owners * 8, LANES), mix, turn_back, tau, rate)
    leaving = leaving.reshape(owners, 8, LANES)

    returned = lax.all_to_all(leaving, ("lat", "fld"), split_axis=0, concat_axis=0, tiled=True)

    damped = pltpu.with_memory_space_constraint(damped, pltpu.VMEM)
    spectral = pl.pallas_call(
        output_kernel,
        grid=(groups,),
        out_shape=jax.ShapeDtypeStruct((everyone, pairs, 2, places), F32),
        in_specs=[
            pl.BlockSpec((8 * KPAD, span), lambda t: (t, 0)),
            pl.BlockSpec((2 * FPAD, 8 * KPAD), lambda t: (0, 0)),
        ],
        out_specs=pl.BlockSpec((everyone, 4, 2, places), lambda t: (0, t, 0, 0)),
        scratch_shapes=[pltpu.VMEM((8 * FPAD, 8 * KPAD), BF16)],
        compiler_params=pltpu.CompilerParams(
            dimension_semantics=("arbitrary",), vmem_limit_bytes=ROOM
        ),
        cost_estimate=pl.CostEstimate(flops=10**8, bytes_accessed=8 * 10**6, transcendentals=0),
        name="spectral_output",
    )(damped, back)

    grid_out = pl.pallas_call(
        functools.partial(inverse_kernel, groups),
        out_shape=jax.ShapeDtypeStruct(grid.shape, BF16),
        in_specs=[hbm] * 4 + [vmem] * 3,
        out_specs=vmem,
        scratch_shapes=[
            pltpu.SMEM(row_lengths.shape, jnp.int32),
            pltpu.SMEM(band_map.shape, jnp.int32),
            pltpu.VMEM((DEEP, slots), BF16),
            pltpu.VMEM((DEEP, slots), BF16),
            dma((4,)),
            pltpu.VMEM((32 * pieces, 4 * LANES), BF16),
        ],
        compiler_params=room,
        name="inverse_rows",
    )(row_lengths, band_map, *tables, returned)
    return (jnp.transpose(spectral, (0, 2, 1, 3)), grid_out)


def solution(mesh):
    placed = (
        P("fld", "lat", None, None),
        P(),
        P(),
        P(),
        P(("lat", "fld"), None, None),
        P(),
        P(),
        P(),
    )
    return jax.shard_map(
        per_device,
        mesh=mesh,
        in_specs=placed,
        out_specs=(P(None, None, ("lat", "fld"), None), P("fld", "lat", None, None)),
        check_vma=False,
    )
```

```python
import functools
import math

import jax
import jax.numpy as jnp
from jax import lax
from jax.experimental import pallas as pl
from jax.experimental.pallas import tpu as pltpu
from jax.sharding import PartitionSpec as P

LANES = 128
KPAD = 24
FPAD = 64
DEEP = 256
ROOM = 24 * 1024 * 1024
F32 = jnp.float32
BF16 = jnp.bfloat16
NT_DIMS = (((1,), (1,)), ((), ()))
SIN_POLY = (
    6.283185302447051,
    -41.34170038368319,
    81.60513023312113,
    -76.70299324464969,
    42.02573766814694,
    -14.899106966102595,
    3.237062655726421,
)
COS_POLY = (
    0.9999999889083757,
    -19.739204448887243,
    64.93911476570418,
    -85.45008785413638,
    60.167188450194914,
    -25.9658703083255,
    6.526145851512229,
)


def dot(a, b):
    return jnp.dot(a, b, preferred_element_type=F32)


def dot_nt(a, b):
    return lax.dot_general(a, b, NT_DIMS, preferred_element_type=F32)


def split(x):
    high = x.astype(BF16)
    return high, (x - high.astype(F32)).astype(BF16)


def horner(coefs, z):
    total = coefs[-1] * z + coefs[-2]
    for coef in coefs[-3::-1]:
        total = total * z + coef
    return total


def turn(steps, period, inverse):
    rest = steps - period * jnp.floor(steps * inverse + 0.5)
    part = rest * inverse
    z = part * part
    return horner(COS_POLY, z), part * horner(SIN_POLY, z)


def start_all(sources, targets, sems):
    copies = [
        pltpu.make_async_copy(source, target, sems.at[i])
        for i, (source, target) in enumerate(zip(sources, targets))
    ]
    for copy in copies:
        copy.start()
    return copies


def wait_all(copies):
    for copy in copies:
        copy.wait()


def lane_iota(shape):
    return lax.broadcasted_iota(jnp.int32, shape, len(shape) - 1)


def row_iota(shape):
    return lax.broadcasted_iota(jnp.int32, shape, len(shape) - 2)


def lanes_within(lane, start, size):
    start %= LANES
    if start + size <= LANES:
        return (lane >= start) & (lane < start + size)
    return (lane >= start) | (lane < start + size - LANES)


def spread_matrix():
    shape = (4 * LANES, LANES)
    picks = []
    for phase in range(4):
        picks.append(jnp.where(row_iota(shape) == 4 * lane_iota(shape) + phase, 1.0, 0.0))
    return jnp.concatenate(picks, axis=1).astype(BF16)


def phases_of(groups, wave, length, lanes):
    shape = (groups + 16, lanes)
    row = row_iota(shape)
    steps = jnp.where(row < groups, (row // 4) * (4 * DEEP) + row % 4, 4 * (row - groups))
    steps = jnp.where(row >= groups + 8, 32 << jnp.maximum(row - groups - 8, 0), steps)
    period = jnp.full(shape, length, jnp.int32).astype(F32)
    return turn(steps.astype(F32) * wave, period, 1.0 / period)


def forward_kernel(
    cut_off, groups, len_hbm, band_hbm, fold_hbm, grid_hbm,
    msg_ref, tc, ts, fc, fs,
    len_ref, band_ref, fold_ref, grid_ref, sems, fold_s, wave_s, xs, xq, xt,
):
    copies = start_all(
        (len_hbm, band_hbm, fold_hbm, grid_hbm), (len_ref, band_ref, fold_ref, grid_ref), sems
    )
    fields, _, rows, width = grid_ref.shape
    owners, per_owner = fold_ref.shape
    slots = tc.shape[1]
    pieces = xq.shape[0] // 64
    unit = rows * fields * 2
    spread_s = spread_matrix()
    shape = (owners * 8, fold_s.shape[0])
    repeat = jnp.where(row_iota(shape) // 8 == lane_iota(shape), 1.0, 0.0).astype(BF16)
    weigh = jnp.where(lane_iota((8, 2 * LANES)) < LANES, 8.0, 1.0).astype(BF16)
    shape = (LANES, 64 * groups)
    source = lane_iota(shape)
    vec = source % 16
    base = (vec % rows) * (fields * 2) + (vec // rows) * 2 + (source // 16) % 2
    target = (base + unit * (source // 64 + lax.axis_index("fld"))) % LANES
    packing = jnp.where((vec < rows * fields) & (row_iota(shape) == target), 1.0, 0.0).astype(BF16)
    fold_s[...] = jnp.full(fold_s.shape, -1.0, F32)
    xs[...] = jnp.zeros(xs.shape, F32)
    wait_all(copies)
    length = len_ref[band_ref[lax.axis_index("lat")]]
    top = jnp.minimum(cut_off, (length - 1) // 2)

    fold_s[0:owners, 0:per_owner] = fold_ref[...].astype(F32)
    eights = jnp.floor(fold_s[...] * 0.125)
    parts = jnp.concatenate([eights, fold_s[...] - 8.0 * eights], axis=1).astype(BF16)
    repeated = dot(repeat, parts)
    lane = lane_iota(repeated.shape)
    place = lane % LANES - row_iota(repeated.shape) % 8
    for t in range(groups):
        chosen = jnp.where(place == 8 * t, repeated, 0.0).astype(BF16)
        wave_s[:, owners * 8 * t:owners * 8 * (t + 1)] = dot_nt(weigh, chosen)

    for field in range(fields):
        xs[rows * field:rows * (field + 1), 0:width] = grid_ref[field, 0].astype(F32)
    stacked = jnp.concatenate(
        [xs[:, 4 * LANES * c:4 * LANES * (c + 1)] for c in range(2 * pieces)], axis=0
    ).astype(BF16)
    spread = dot(stacked, spread_s)
    across = (row_iota(spread.shape) // 16) * LANES + lane_iota(spread.shape) % LANES
    spread = jnp.where(across < length // 4, spread, 0.0).astype(BF16)
    for c in range(2 * pieces):
        for phase in range(4):
            at = (4 * (c // 2) + phase) * 16
            off = LANES * (c % 2)
            xq[at:at + 16, off:off + LANES] = spread[
                16 * c:16 * (c + 1), LANES * phase:LANES * (phase + 1)
            ]

    turns = 4 * pieces
    block = 2 * LANES
    values = xq[...]
    for i in range(slots // block):
        at = pl.ds(i * block, block)
        wave = wave_s[:, at]
        wave = jnp.concatenate([wave] * ((turns + 16) // 8), axis=0)
        co, si = phases_of(turns, wave, length, block)
        one = wave[0:1]
        weight = jnp.where(one == 0.0, 1.0, 2.0)
        weight = jnp.where((one >= 0.0) & (one <= jnp.full(one.shape, top, jnp.int32).astype(F32)), weight, 0.0)
        fc[:, at] = co[0:turns] * weight
        fs[:, at] = si[0:turns] * weight
        c_all = co[turns:turns + 8]
        s_all = si[turns:turns + 8]
        size, step = 8, turns + 8
        while size < DEEP:
            c1 = co[step:step + 1]
            s1 = si[step:step + 1]
            c_new = c_all * c1 - s_all * s1
            s_new = s_all * c1 + c_all * s1
            c_all = jnp.concatenate([c_all, c_new], axis=0)
            s_all = jnp.concatenate([s_all, s_new], axis=0)
            size, step = 2 * size, step + 1
        c_all = c_all.astype(BF16)
        s_all = s_all.astype(BF16)
        tc[:, at] = c_all
        ts[:, at] = s_all
        inner_c = dot(values, c_all)
        inner_s = dot(values, s_all)
        real = jnp.zeros((16, block), F32)
        imag = jnp.zeros((16, block), F32)
        for g in range(turns):
            c1 = fc[g:g + 1, at]
            s1 = fs[g:g + 1, at]
            part_c = inner_c[16 * g:16 * (g + 1)]
            part_s = inner_s[16 * g:16 * (g + 1)]
            real = real + (c1 * part_c - s1 * part_s)
            imag = imag - (c1 * part_s + s1 * part_c)
        both = jnp.concatenate([real, imag], axis=0) * jnp.where(one == 0.0, 1.0, 0.5)
        xt[:, at] = jnp.concatenate(split(both), axis=0)
    turned = jnp.concatenate(
        [xt[:, owners * 8 * t:owners * 8 * (t + 1)] for t in range(groups)], axis=0
    )
    total = dot(packing, turned)
    scale = 1.0 / jnp.sqrt(jnp.full(total.shape, length, jnp.int32).astype(F32))
    msg_ref[...] = jnp.transpose(total * scale).reshape(owners, 8, LANES)


def inverse_kernel(
    groups, len_hbm, band_hbm, tc, ts, fc, fs, msg_ref, grid_ref,
    len_ref, band_ref, sems, os,
):
    copies = start_all((len_hbm, band_hbm), (len_ref, band_ref), sems)
    spread_s = spread_matrix()
    fields, _, rows, width = grid_ref.shape
    owners = msg_ref.shape[0]
    slots = tc.shape[1]
    turns = fc.shape[0]
    unit = rows * fields * 2
    high, low = split(msg_ref[...].reshape(owners * 8, LANES))
    pieces = jnp.concatenate([high, low], axis=1)
    shape = (32 * groups, 2 * LANES)
    target = row_iota(shape) % 32
    vec = target % 16
    base = (vec % rows) * (fields * 2) + (vec // rows) * 2 + target // 16
    source = (base + unit * (row_iota(shape) // 32) + lax.axis_index("fld") * (fields * 2)) % LANES
    place = jnp.where(
        (vec < rows * fields) & (lane_iota(shape) % LANES == source), 1.0, 0.0
    ).astype(BF16)
    turned = dot_nt(place, pieces)
    block = 2 * LANES
    out = jnp.zeros((16 * turns, DEEP), F32)
    for i in range(slots // block):
        t, off = divmod(i * block, owners * 8)
        real = turned[32 * t:32 * t + 16, off:off + block]
        imag = turned[32 * t + 16:32 * t + 32, off:off + block]
        at = pl.ds(i * block, block)
        reals, imags = [], []
        for g in range(turns):
            c1 = fc[g:g + 1, at]
            s1 = fs[g:g + 1, at]
            reals.append(c1 * real - s1 * imag)
            imags.append(s1 * real + c1 * imag)
        reals = jnp.concatenate(reals, axis=0).astype(BF16)
        imags = jnp.concatenate(imags, axis=0).astype(BF16)
        out = out + (dot_nt(reals, tc[:, at]) - dot_nt(imags, ts[:, at]))
    wait_all(copies)
    length = len_ref[band_ref[lax.axis_index("lat")]]
    out = out * (1.0 / jnp.sqrt(jnp.full((16 * turns, DEEP), length, jnp.int32).astype(F32)))
    chunks = os.shape[0] // 16
    for c in range(chunks):
        for phase in range(4):
            at = (4 * (c // 2) + phase) * 16
            off = LANES * (c % 2)
            os[16 * c:16 * (c + 1), LANES * phase:LANES * (phase + 1)] = out[
                at:at + 16, off:off + LANES
            ].astype(BF16)
    merged = dot_nt(os[...], spread_s)
    for c in range(chunks):
        begin = 4 * LANES * c
        size = min(4 * LANES, width - begin)
        if size <= 0:
            continue
        inside = begin + lane_iota((16, size)) < length
        piece = jnp.where(inside, merged[16 * c:16 * (c + 1), 0:size], 0.0)
        for field in range(fields):
            grid_ref[field, 0, :, begin:begin + size] = piece[
                rows * field:rows * (field + 1)
            ].astype(BF16)


def prepare_kernel(
    cut_off, pairs, fields, rows, fold_hbm, band_hbm, rates_hbm, leg_hbm, tm_hbm, bm_hbm,
    eh_hbm, mix_ref, back_ref, turn_ref, tau_ref, rate_ref,
    fold_ref, band_ref, rates_ref, leg_ref, tm_ref, bm_ref, sems, pad_s, eh_ref, out_sems,
):
    copies = start_all(
        (fold_hbm, band_hbm, rates_hbm, tm_hbm, bm_hbm, leg_hbm),
        (fold_ref, band_ref, rates_ref, tm_ref, bm_ref, leg_ref),
        sems,
    )
    wait_all(copies[:-1])
    everyone = tm_ref.shape[0]
    _, lats, places = leg_ref.shape
    groups_f = everyone // fields
    wf = fields * 2
    unit = rows * wf
    span = eh_ref.shape[1]
    eight = 8 * lats
    groups = eh_ref.shape[0] // (2 * eight)
    owner = lax.axis_index("lat") * groups_f + lax.axis_index("fld")

    pad_s[...] = jnp.zeros(pad_s.shape, F32)
    pad_s[0:everyone, 0:everyone] = tm_ref[...]
    shape = (LANES, LANES)
    level = (lane_iota(shape) // unit) * fields + (lane_iota(shape) % wf) // 2
    pick = jnp.where(row_iota(shape) == level, 1.0, 0.0).astype(BF16)
    lane = lane_iota((KPAD, LANES))
    parts = []
    for piece in split(pad_s[...]):
        wide = dot(piece, pick)
        total = []
        for r in range(rows):
            for c in range(2):
                keep = ((lane % unit) // wf == r) & (lane % 2 == c) & (lane < unit * groups_f)
                total.append(jnp.where(keep, wide, 0.0))
        parts.append(jnp.concatenate(total, axis=0).astype(BF16))
    mix_ref[...] = jnp.concatenate([parts[0], parts[1], parts[0]], axis=1)

    pad_s[...] = jnp.zeros(pad_s.shape, F32)
    pad_s[0:everyone, 0:everyone] = bm_ref[...]
    shape = (FPAD, KPAD)
    expand = jnp.where(row_iota(shape) // 2 == lane_iota(shape), 1.0, 0.0).astype(BF16)
    shape = (LANES, 2 * LANES)
    repeat = jnp.where(row_iota(shape) == lane_iota(shape) % KPAD, 1.0, 0.0).astype(BF16)
    shape = (FPAD, 2 * LANES)
    same = row_iota(shape) % 2 == (lane_iota(shape) // KPAD) % 2
    half = lane_iota((FPAD, LANES)) < 64
    narrow = lane_iota((FPAD, LANES)) < 2 * KPAD
    fulls = []
    for part, piece in enumerate(split(pad_s[...])):
        full = jnp.where(same, dot(dot(expand, piece).astype(BF16), repeat), 0.0)
        back_ref[part * FPAD:(part + 1) * FPAD, :] = full[:, 0:8 * KPAD].astype(BF16)
        fulls.append(jnp.where(narrow, full[:, 0:LANES], 0.0))
    turn_ref[...] = jnp.concatenate(
        [jnp.where(half, fulls[0], pltpu.roll(fulls[0], 64, 1)), fulls[1]], axis=1
    ).astype(BF16)

    row = row_iota((KPAD, 2 * LANES))
    rate = jnp.zeros((KPAD, 2 * LANES), F32)
    for k in range(everyone):
        rate = jnp.where(row == k, rates_ref[k], rate)
    rate_ref[...] = rate
    paired = tau_ref.shape[0]
    row = row_iota((paired, LANES))
    waves = []
    wave = jnp.zeros((paired, LANES), jnp.int32)
    for pair in range(4 * groups):
        waves.append(fold_ref[owner, 2 * min(pair, pairs - 1)])
        wave = jnp.where(row == pair, waves[pair], wave)
    wave = jnp.concatenate([wave] * (span // LANES), axis=1)
    line = lane_iota((paired, span))
    degree = jnp.where(line > cut_off - wave, line - 1, line + wave)
    tau_ref[...] = (degree * (degree + 1)).astype(F32) * (1.0 / float(cut_off * (cut_off + 1)))

    quad_rows = 4 * lats
    shape = (quad_rows, quad_rows)
    band = jnp.zeros(shape, jnp.int32)
    for holder in range(lats):
        band = jnp.where(row_iota(shape) % lats == holder, band_ref[holder], band)
    order = jnp.where(
        (row_iota(shape) // lats == lane_iota(shape) // lats) & (lane_iota(shape) % lats == band),
        1.0,
        0.0,
    ).astype(BF16)

    whole = places // LANES * LANES
    line = lane_iota((quad_rows, span))
    row = row_iota((quad_rows, LANES)) // lats
    copies[-1].wait()
    keeps = []
    for t in range(groups):
        wave = jnp.zeros((quad_rows, LANES), jnp.int32)
        last = jnp.zeros((quad_rows, LANES), jnp.int32)
        stack = []
        for pp in range(4):
            there = 4 * t + pp < pairs
            index = min(4 * t + pp, pairs - 1)
            wave = jnp.where(row == pp, waves[4 * t + pp], wave)
            last = jnp.where(row == pp, places - 1 if there else -1, last)
            stack.append(
                jnp.concatenate(
                    [
                        leg_ref[index, :, 0:whole],
                        jnp.broadcast_to(leg_ref[index, :, whole:places], (lats, span - whole)),
                    ],
                    axis=1,
                )
            )
        wave = jnp.concatenate([wave] * (span // LANES), axis=1)
        last = jnp.concatenate([last] * (span // LANES), axis=1)
        leg = dot(order, jnp.concatenate(stack, axis=0).astype(BF16))
        before = line <= cut_off - wave
        first = before & (line <= last)
        second = jnp.logical_not(before) & (line <= last)
        odd = ((line + jnp.where(before, 0, wave)) & 1) == 1
        signed = jnp.where(odd, -leg, leg)
        for r, rowset in enumerate((leg, signed)):
            near = jnp.where(first, rowset, 0.0)
            far = jnp.where(second, rowset, 0.0)
            for pp in range(4):
                at = 2 * eight * t + r * eight + 2 * pp * lats
                eh_ref[at:at + 2 * lats, :] = jnp.concatenate(
                    [near[pp * lats:(pp + 1) * lats], far[pp * lats:(pp + 1) * lats]], axis=0
                ).astype(BF16)
        part = pl.ds(2 * eight * t, 2 * eight)
        keeps.append(pltpu.make_async_copy(eh_ref.at[part], eh_hbm.at[part], out_sems.at[t]))
        keeps[-1].start()
    wait_all(keeps)


def solve_kernel(
    fields, rows, lats, eh_hbm, msg_ref, mix_ref, turn_ref, tau_ref, rate_ref,
    damped_hbm, out_ref, cs, eh_ref, damped_ref, in_sems, out_sems,
):
    eight = 8 * lats
    groups = eh_ref.shape[0] // (2 * eight)
    parts = [pl.ds(0, 2 * eight), pl.ds(2 * eight, 2 * eight * (groups - 1))]
    later = start_all(
        [eh_hbm.at[part] for part in parts], [eh_ref.at[part] for part in parts], in_sems
    )
    groups_f = msg_ref.shape[0] // eight
    wf = fields * 2
    unit = rows * wf
    span = eh_ref.shape[1]
    deep = 8 * KPAD
    lane = lane_iota((lats, LANES))
    tiles = [
        [msg_ref[pl.ds(8 * g + i8, lats, stride=8 * groups_f), :] for g in range(groups_f)]
        for i8 in range(8)
    ]
    tall = []
    for t in range(groups):
        here = [lanes_within(lane, unit * (t + g), unit) for g in range(groups_f)]
        for i8 in range(8):
            line = tiles[i8][0]
            for g in range(1, groups_f):
                line = jnp.where(here[g], tiles[i8][g], line)
            if t:
                line = pltpu.roll(line, LANES - unit * t, 1)
            tall.append(line)
    v_high, v_low = split(jnp.concatenate(tall, axis=0))
    mixed = dot_nt(mix_ref[...], jnp.concatenate([v_high, v_high, v_low], axis=1))

    rate = rate_ref[...]
    slot_pair = (lane_iota((2 * KPAD, 2 * eight)) % eight) // (2 * lats)
    blank = jnp.zeros((64 - 2 * KPAD, span), BF16)
    front = lane_iota((lats, LANES)) < 64

    lefts = []
    for t in range(groups):
        mine = mixed[:, eight * t:eight * (t + 1)]
        mine = jnp.concatenate([mine[0:2 * KPAD], mine[2 * KPAD:4 * KPAD]], axis=1)
        left = jnp.concatenate([jnp.where(slot_pair == pp, mine, 0.0) for pp in range(4)], axis=0)
        lefts.append(jnp.concatenate(split(left), axis=1))

    keeps = []
    for t in range(groups):
        left = lefts[t]
        legs = pl.ds(2 * eight * t, 2 * eight)
        if t < 2:
            later[t].wait()
        for start in range(0, span, 2 * LANES):
            size = min(2 * LANES, span - start)
            right = eh_ref[legs, start:start + size]
            modes = dot(left, jnp.concatenate([right, right], axis=0))
            damped = []
            for pp in range(4):
                tau = tau_ref[4 * t + pp:4 * t + pp + 1, start:start + size]
                below = 1.0 + tau * rate[:, 0:size]
                factor = pl.reciprocal(below, approx=True)
                factor = factor * (2.0 - below * factor)
                at = 2 * pp * KPAD
                damped.append(modes[at:at + KPAD] * factor)
                damped.append(modes[at + KPAD:at + 2 * KPAD] * factor)
            damped_ref[deep * t:deep * (t + 1), start:start + size] = jnp.concatenate(
                damped, axis=0
            ).astype(BF16)
        part = pl.ds(deep * t, deep)
        keeps.append(
            pltpu.make_async_copy(damped_ref.at[part], damped_hbm.at[part], out_sems.at[t])
        )
        keeps[-1].start()

    products = []
    for t in range(groups):
        legs = pl.ds(2 * eight * t, 2 * eight)
        pieces = []
        for pp in range(4):
            at = deep * t + 2 * KPAD * pp
            pieces += [damped_ref[at:at + 2 * KPAD, :], blank]
        products.append(dot_nt(eh_ref[legs, :], jnp.concatenate(pieces, axis=0)))

    highs, lows = [], []
    for sums in products:
        for r in range(rows):
            for i8 in range(8):
                at = (r * 8 + i8) * lats
                pp = i8 // 2
                tile = sums[at:at + lats, LANES * (pp // 2):LANES * (pp // 2 + 1)]
                if pp % 2:
                    tile = pltpu.roll(tile, 64, 1)
                high = tile.astype(BF16).astype(F32)
                low = pltpu.roll(tile - high, 64, 1)
                highs.append(jnp.where(front, high, low))
                lows.append(jnp.where(front, high, 0.0))
    own = jnp.concatenate(
        [jnp.concatenate(highs, axis=0), jnp.concatenate(lows, axis=0)], axis=1
    ).astype(BF16)
    cs[:, 0:FPAD] = dot_nt(own, turn_ref[...])

    lane = lane_iota((8, LANES))
    here = [
        lanes_within(lane, wf * u, wf) for u in range(rows * groups + groups_f - 1)
    ]
    for holder in range(lats):
        tiles = [jnp.zeros((8, LANES), F32) for _ in range(groups_f)]
        for u in range(rows * groups):
            piece = cs[pl.ds(u * eight + holder, 8, stride=lats), :]
            if u:
                piece = pltpu.roll(piece, wf * u, 1)
            for g in range(groups_f):
                tiles[g] = jnp.where(here[u + g], piece, tiles[g])
        for g in range(groups_f):
            at = (holder * groups_f + g) * 8
            out_ref[at:at + 8, :] = tiles[g]
    wait_all(keeps)


def output_kernel(damped_ref, back_ref, spec_ref, bk):
    everyone, quad, _, places = spec_ref.shape
    span = damped_ref.shape[1]

    @pl.when(pl.program_id(0) == 0)
    def _():
        shape = (FPAD, 8 * KPAD)
        pair_of = lane_iota(shape) // (2 * KPAD)
        for part in range(2):
            full = back_ref[part * FPAD:(part + 1) * FPAD, :].astype(F32)
            for pp in range(4):
                at = (4 * part + pp) * FPAD
                bk[at:at + FPAD, :] = jnp.where(pair_of == pp, full, 0.0).astype(BF16)

    for start in range(0, span, 2 * LANES):
        size = min(2 * LANES, span - start)
        spec = dot(bk[...], damped_ref[:, start:start + size])
        spec = spec[0:4 * FPAD] + spec[4 * FPAD:]
        kept = min(size, places - start)
        for pp in range(4):
            for f in range(everyone):
                at = pp * FPAD + 2 * f
                spec_ref[f, pp, :, start:start + kept] = spec[at:at + 2, 0:kept]


def per_device(grid, row_lengths, band_map, fold_map, legendre, to_modes, back_modes, mode_rates):
    fields, single, rows, width = grid.shape
    pairs, places, lats = legendre.shape
    cut_off = places - 2
    everyone = to_modes.shape[0]
    owners, per_owner = fold_map.shape
    groups = -(-per_owner // 8)
    slots = owners * groups * 8
    pieces = -(-(width // 4) // DEEP)
    turns = 4 * pieces
    span = -(-places // LANES) * LANES
    hbm = pl.BlockSpec(memory_space=pltpu.HBM)
    vmem = pl.BlockSpec(memory_space=pltpu.VMEM)
    room = pltpu.CompilerParams(vmem_limit_bytes=ROOM)
    message = pltpu.HBM((owners, 8, LANES), F32)
    holders = band_map.shape[0]
    groups_f = everyone // fields
    dma = pltpu.SemaphoreType.DMA
    row_lengths, band_map, fold_map, to_modes, back_modes, mode_rates, grid = (
        pltpu.with_memory_space_constraint(x, pltpu.HBM)
        for x in (row_lengths, band_map, fold_map, to_modes, back_modes, mode_rates, grid)
    )
    legendre = pltpu.with_memory_space_constraint(jnp.transpose(legendre, (0, 2, 1)), pltpu.HBM)

    sending, cos_table, sin_table, cos_turn, sin_turn = pl.pallas_call(
        functools.partial(forward_kernel, cut_off, groups),
        out_shape=(
            message,
            pltpu.VMEM((DEEP, slots), BF16),
            pltpu.VMEM((DEEP, slots), BF16),
            pltpu.VMEM((turns, slots), F32),
            pltpu.VMEM((turns, slots), F32),
        ),
        in_specs=[hbm] * 4,
        out_specs=(vmem,) * 5,
        scratch_shapes=[
            pltpu.SMEM(row_lengths.shape, jnp.int32),
            pltpu.SMEM(band_map.shape, jnp.int32),
            pltpu.VMEM(fold_map.shape, jnp.int32),
            pltpu.VMEM(grid.shape, BF16),
            dma((4,)),
            pltpu.VMEM((LANES, LANES), F32),
            pltpu.VMEM((8, slots), F32),
            pltpu.VMEM((16, 4 * DEEP * pieces), F32),
            pltpu.VMEM((16 * turns, DEEP), BF16),
            pltpu.VMEM((64, slots), BF16),
        ],
        compiler_params=room,
        name="forward_rows",
    )(row_lengths, band_map, fold_map, grid)
    tables = [
        pltpu.with_memory_space_constraint(x, pltpu.VMEM)
        for x in (cos_table, sin_table, cos_turn, sin_turn)
    ]
    arrived = lax.all_to_all(sending, ("lat", "fld"), split_axis=0, concat_axis=0, tiled=True)

    legs, mix, back, turn_back, tau, rate = pl.pallas_call(
        functools.partial(prepare_kernel, cut_off, pairs, fields, rows),
        out_shape=(
            pltpu.HBM((groups * 16 * lats, span), BF16),
            pltpu.VMEM((2 * rows * KPAD, 3 * LANES), BF16),
            pltpu.VMEM((2 * FPAD, 8 * KPAD), BF16),
            pltpu.VMEM((FPAD, 2 * LANES), BF16),
            pltpu.VMEM((-(-groups * 4 // 8) * 8, span), F32),
            pltpu.VMEM((KPAD, 2 * LANES), F32),
        ),
        in_specs=[hbm] * 6,
        out_specs=(hbm,) + (vmem,) * 5,
        scratch_shapes=[
            pltpu.SMEM(fold_map.shape, jnp.int32),
            pltpu.SMEM(band_map.shape, jnp.int32),
            pltpu.SMEM(mode_rates.shape, F32),
            pltpu.VMEM((pairs, lats, places), F32),
            pltpu.VMEM(to_modes.shape, F32),
            pltpu.VMEM(back_modes.shape, F32),
            dma((6,)),
            pltpu.VMEM((KPAD, LANES), F32),
            pltpu.VMEM((groups * 16 * lats, span), BF16),
            dma((groups,)),
        ],
        compiler_params=room,
        cost_estimate=pl.CostEstimate(flops=10**8, bytes_accessed=8 * 10**6, transcendentals=0),
        name="prepare",
    )(fold_map, band_map, mode_rates, legendre, to_modes, back_modes)
    legs = pltpu.with_memory_space_constraint(legs, pltpu.HBM)
    mix, back, turn_back, tau, rate = (
        pltpu.with_memory_space_constraint(x, pltpu.VMEM)
        for x in (mix, back, turn_back, tau, rate)
    )

    damped, leaving = pl.pallas_call(
        functools.partial(solve_kernel, fields, rows, lats),
        out_shape=(
            pltpu.HBM((groups * 8 * KPAD, span), BF16),
            pltpu.HBM((owners * 8, LANES), F32),
        ),
        in_specs=[hbm] + [vmem] * 5,
        out_specs=(hbm, vmem),
        scratch_shapes=[
            pltpu.VMEM((groups * 16 * lats, LANES), F32),
            pltpu.VMEM((groups * 16 * lats, span), BF16),
            pltpu.VMEM((groups * 8 * KPAD, span), BF16),
            dma((2,)),
            dma((groups,)),
        ],
        compiler_params=room,
        name="solve",
    )(legs, arrived.reshape(owners * 8, LANES), mix, turn_back, tau, rate)
    leaving = leaving.reshape(owners, 8, LANES)

    returned = lax.all_to_all(leaving, ("lat", "fld"), split_axis=0, concat_axis=0, tiled=True)

    damped = pltpu.with_memory_space_constraint(damped, pltpu.HBM)
    spectral = pl.pallas_call(
        output_kernel,
        grid=(groups,),
        out_shape=jax.ShapeDtypeStruct((everyone, pairs, 2, places), F32),
        in_specs=[
            pl.BlockSpec((8 * KPAD, span), lambda t: (t, 0)),
            pl.BlockSpec((2 * FPAD, 8 * KPAD), lambda t: (0, 0)),
        ],
        out_specs=pl.BlockSpec((everyone, 4, 2, places), lambda t: (0, t, 0, 0)),
        scratch_shapes=[pltpu.VMEM((8 * FPAD, 8 * KPAD), BF16)],
        compiler_params=pltpu.CompilerParams(
            dimension_semantics=("arbitrary",), vmem_limit_bytes=ROOM
        ),
        cost_estimate=pl.CostEstimate(flops=10**8, bytes_accessed=8 * 10**6, transcendentals=0),
        name="spectral_output",
    )(damped, back)

    grid_out = pl.pallas_call(
        functools.partial(inverse_kernel, groups),
        out_shape=jax.ShapeDtypeStruct(grid.shape, BF16),
        in_specs=[hbm] * 2 + [vmem] * 5,
        out_specs=vmem,
        scratch_shapes=[
            pltpu.SMEM(row_lengths.shape, jnp.int32),
            pltpu.SMEM(band_map.shape, jnp.int32),
            dma((2,)),
            pltpu.VMEM((32 * pieces, 4 * LANES), BF16),
        ],
        compiler_params=room,
        name="inverse_rows",
    )(row_lengths, band_map, *tables, returned)
    return (jnp.transpose(spectral, (0, 2, 1, 3)), grid_out)


def solution(mesh):
    placed = (
        P("fld", "lat", None, None),
        P(),
        P(),
        P(),
        P(("lat", "fld"), None, None),
        P(),
        P(),
        P(),
    )
    return jax.shard_map(
        per_device,
        mesh=mesh,
        in_specs=placed,
        out_specs=(P(None, None, ("lat", "fld"), None), P("fld", "lat", None, None)),
        check_vma=False,
    )
```

```python
import functools
import math

import jax
import jax.numpy as jnp
from jax import lax
from jax.experimental import pallas as pl
from jax.experimental.pallas import tpu as pltpu
from jax.sharding import PartitionSpec as P

LANES = 128
KPAD = 24
FPAD = 64
DEEP = 256
ROOM = 24 * 1024 * 1024
F32 = jnp.float32
BF16 = jnp.bfloat16
NT_DIMS = (((1,), (1,)), ((), ()))
SIN_POLY = (
    6.283185302447051,
    -41.34170038368319,
    81.60513023312113,
    -76.70299324464969,
    42.02573766814694,
    -14.899106966102595,
    3.237062655726421,
)
COS_POLY = (
    0.9999999889083757,
    -19.739204448887243,
    64.93911476570418,
    -85.45008785413638,
    60.167188450194914,
    -25.9658703083255,
    6.526145851512229,
)


def dot(a, b):
    return jnp.dot(a, b, preferred_element_type=F32)


def dot_nt(a, b):
    return lax.dot_general(a, b, NT_DIMS, preferred_element_type=F32)


def split(x):
    high = x.astype(BF16)
    return high, (x - high.astype(F32)).astype(BF16)


def horner(coefs, z):
    total = coefs[-1] * z + coefs[-2]
    for coef in coefs[-3::-1]:
        total = total * z + coef
    return total


def turn(steps, period, inverse):
    rest = steps - period * jnp.floor(steps * inverse + 0.5)
    part = rest * inverse
    z = part * part
    return horner(COS_POLY, z), part * horner(SIN_POLY, z)


def start_all(sources, targets, sems):
    copies = [
        pltpu.make_async_copy(source, target, sems.at[i])
        for i, (source, target) in enumerate(zip(sources, targets))
    ]
    for copy in copies:
        copy.start()
    return copies


def wait_all(copies):
    for copy in copies:
        copy.wait()


def lane_iota(shape):
    return lax.broadcasted_iota(jnp.int32, shape, len(shape) - 1)


def row_iota(shape):
    return lax.broadcasted_iota(jnp.int32, shape, len(shape) - 2)


def lanes_within(lane, start, size):
    start %= LANES
    if start + size <= LANES:
        return (lane >= start) & (lane < start + size)
    return (lane >= start) | (lane < start + size - LANES)


def spread_matrix():
    shape = (4 * LANES, LANES)
    picks = []
    for phase in range(4):
        picks.append(jnp.where(row_iota(shape) == 4 * lane_iota(shape) + phase, 1.0, 0.0))
    return jnp.concatenate(picks, axis=1).astype(BF16)


def phases_of(groups, wave, length, lanes):
    shape = (groups + 16, lanes)
    row = row_iota(shape)
    steps = jnp.where(row < groups, (row // 4) * (4 * DEEP) + row % 4, 4 * (row - groups))
    steps = jnp.where(row >= groups + 8, 32 << jnp.maximum(row - groups - 8, 0), steps)
    period = jnp.full(shape, length, jnp.int32).astype(F32)
    return turn(steps.astype(F32) * wave, period, 1.0 / period)


def forward_kernel(
    cut_off, groups, len_hbm, band_hbm, fold_hbm, grid_hbm,
    msg_ref, tc, ts, fc, fs,
    len_ref, band_ref, fold_ref, grid_ref, sems, fold_s, wave_s, xs, xq, xt,
):
    copies = start_all(
        (len_hbm, band_hbm, fold_hbm, grid_hbm), (len_ref, band_ref, fold_ref, grid_ref), sems
    )
    fields, _, rows, width = grid_ref.shape
    owners, per_owner = fold_ref.shape
    slots = tc.shape[1]
    pieces = xq.shape[0] // 64
    unit = rows * fields * 2
    spread_s = spread_matrix()
    shape = (owners * 8, fold_s.shape[0])
    repeat = jnp.where(row_iota(shape) // 8 == lane_iota(shape), 1.0, 0.0).astype(BF16)
    weigh = jnp.where(lane_iota((8, 2 * LANES)) < LANES, 8.0, 1.0).astype(BF16)
    shape = (LANES, 64 * groups)
    source = lane_iota(shape)
    vec = source % 16
    base = (vec % rows) * (fields * 2) + (vec // rows) * 2 + (source // 16) % 2
    target = (base + unit * (source // 64 + lax.axis_index("fld"))) % LANES
    packing = jnp.where((vec < rows * fields) & (row_iota(shape) == target), 1.0, 0.0).astype(BF16)
    fold_s[...] = jnp.full(fold_s.shape, -1.0, F32)
    xs[...] = jnp.zeros(xs.shape, F32)
    wait_all(copies)
    length = len_ref[band_ref[lax.axis_index("lat")]]
    top = jnp.minimum(cut_off, (length - 1) // 2)

    fold_s[0:owners, 0:per_owner] = fold_ref[...].astype(F32)
    eights = jnp.floor(fold_s[...] * 0.125)
    parts = jnp.concatenate([eights, fold_s[...] - 8.0 * eights], axis=1).astype(BF16)
    repeated = dot(repeat, parts)
    lane = lane_iota(repeated.shape)
    place = lane % LANES - row_iota(repeated.shape) % 8
    for t in range(groups):
        chosen = jnp.where(place == 8 * t, repeated, 0.0).astype(BF16)
        wave_s[:, owners * 8 * t:owners * 8 * (t + 1)] = dot_nt(weigh, chosen)

    for field in range(fields):
        xs[rows * field:rows * (field + 1), 0:width] = grid_ref[field, 0].astype(F32)
    stacked = jnp.concatenate(
        [xs[:, 4 * LANES * c:4 * LANES * (c + 1)] for c in range(2 * pieces)], axis=0
    ).astype(BF16)
    spread = dot(stacked, spread_s)
    across = (row_iota(spread.shape) // 16) * LANES + lane_iota(spread.shape) % LANES
    spread = jnp.where(across < length // 4, spread, 0.0).astype(BF16)
    for c in range(2 * pieces):
        for phase in range(4):
            at = (4 * (c // 2) + phase) * 16
            off = LANES * (c % 2)
            xq[at:at + 16, off:off + LANES] = spread[
                16 * c:16 * (c + 1), LANES * phase:LANES * (phase + 1)
            ]

    turns = 4 * pieces
    block = 2 * LANES
    values = xq[...]
    for i in range(slots // block):
        at = pl.ds(i * block, block)
        wave = wave_s[:, at]
        wave = jnp.concatenate([wave] * ((turns + 16) // 8), axis=0)
        co, si = phases_of(turns, wave, length, block)
        one = wave[0:1]
        weight = jnp.where(one == 0.0, 1.0, 2.0)
        weight = jnp.where((one >= 0.0) & (one <= jnp.full(one.shape, top, jnp.int32).astype(F32)), weight, 0.0)
        fc[:, at] = co[0:turns] * weight
        fs[:, at] = si[0:turns] * weight
        c_all = co[turns:turns + 8]
        s_all = si[turns:turns + 8]
        size, step = 8, turns + 8
        while size < DEEP:
            c1 = co[step:step + 1]
            s1 = si[step:step + 1]
            c_new = c_all * c1 - s_all * s1
            s_new = s_all * c1 + c_all * s1
            c_all = jnp.concatenate([c_all, c_new], axis=0)
            s_all = jnp.concatenate([s_all, s_new], axis=0)
            size, step = 2 * size, step + 1
        c_all = c_all.astype(BF16)
        s_all = s_all.astype(BF16)
        tc[:, at] = c_all
        ts[:, at] = s_all
        inner_c = dot(values, c_all)
        inner_s = dot(values, s_all)
        real = jnp.zeros((16, block), F32)
        imag = jnp.zeros((16, block), F32)
        for g in range(turns):
            c1 = fc[g:g + 1, at]
            s1 = fs[g:g + 1, at]
            part_c = inner_c[16 * g:16 * (g + 1)]
            part_s = inner_s[16 * g:16 * (g + 1)]
            real = real + (c1 * part_c - s1 * part_s)
            imag = imag - (c1 * part_s + s1 * part_c)
        both = jnp.concatenate([real, imag], axis=0) * jnp.where(one == 0.0, 1.0, 0.5)
        xt[:, at] = jnp.concatenate(split(both), axis=0)
    turned = jnp.concatenate(
        [xt[:, owners * 8 * t:owners * 8 * (t + 1)] for t in range(groups)], axis=0
    )
    total = dot(packing, turned)
    scale = 1.0 / jnp.sqrt(jnp.full(total.shape, length, jnp.int32).astype(F32))
    msg_ref[...] = jnp.transpose(total * scale).reshape(owners, 8, LANES)


def inverse_kernel(
    groups, len_hbm, band_hbm, tc, ts, fc, fs, msg_ref, grid_ref,
    len_ref, band_ref, sems, os,
):
    copies = start_all((len_hbm, band_hbm), (len_ref, band_ref), sems)
    spread_s = spread_matrix()
    fields, _, rows, width = grid_ref.shape
    owners = msg_ref.shape[0]
    slots = tc.shape[1]
    turns = fc.shape[0]
    unit = rows * fields * 2
    high, low = split(msg_ref[...].reshape(owners * 8, LANES))
    pieces = jnp.concatenate([high, low], axis=1)
    shape = (32 * groups, 2 * LANES)
    target = row_iota(shape) % 32
    vec = target % 16
    base = (vec % rows) * (fields * 2) + (vec // rows) * 2 + target // 16
    source = (base + unit * (row_iota(shape) // 32) + lax.axis_index("fld") * (fields * 2)) % LANES
    place = jnp.where(
        (vec < rows * fields) & (lane_iota(shape) % LANES == source), 1.0, 0.0
    ).astype(BF16)
    turned = dot_nt(place, pieces)
    block = 2 * LANES
    out = jnp.zeros((16 * turns, DEEP), F32)
    for i in range(slots // block):
        t, off = divmod(i * block, owners * 8)
        real = turned[32 * t:32 * t + 16, off:off + block]
        imag = turned[32 * t + 16:32 * t + 32, off:off + block]
        at = pl.ds(i * block, block)
        reals, imags = [], []
        for g in range(turns):
            c1 = fc[g:g + 1, at]
            s1 = fs[g:g + 1, at]
            reals.append(c1 * real - s1 * imag)
            imags.append(s1 * real + c1 * imag)
        reals = jnp.concatenate(reals, axis=0).astype(BF16)
        imags = jnp.concatenate(imags, axis=0).astype(BF16)
        out = out + (dot_nt(reals, tc[:, at]) - dot_nt(imags, ts[:, at]))
    wait_all(copies)
    length = len_ref[band_ref[lax.axis_index("lat")]]
    out = out * (1.0 / jnp.sqrt(jnp.full((16 * turns, DEEP), length, jnp.int32).astype(F32)))
    chunks = os.shape[0] // 16
    for c in range(chunks):
        for phase in range(4):
            at = (4 * (c // 2) + phase) * 16
            off = LANES * (c % 2)
            os[16 * c:16 * (c + 1), LANES * phase:LANES * (phase + 1)] = out[
                at:at + 16, off:off + LANES
            ].astype(BF16)
    merged = dot_nt(os[...], spread_s)
    for c in range(chunks):
        begin = 4 * LANES * c
        size = min(4 * LANES, width - begin)
        if size <= 0:
            continue
        inside = begin + lane_iota((16, size)) < length
        piece = jnp.where(inside, merged[16 * c:16 * (c + 1), 0:size], 0.0)
        for field in range(fields):
            grid_ref[field, 0, :, begin:begin + size] = piece[
                rows * field:rows * (field + 1)
            ].astype(BF16)


def prepare_kernel(
    cut_off, pairs, fields, rows, fold_hbm, band_hbm, rates_hbm, leg_hbm, tm_hbm, bm_hbm,
    eh_hbm, mix_ref, back_ref, turn_ref, tau_ref, rate_ref,
    fold_ref, band_ref, rates_ref, leg_ref, tm_ref, bm_ref, sems, pad_s, eh_ref, out_sems,
):
    copies = start_all(
        (fold_hbm, band_hbm, rates_hbm, tm_hbm, bm_hbm, leg_hbm),
        (fold_ref, band_ref, rates_ref, tm_ref, bm_ref, leg_ref),
        sems,
    )
    wait_all(copies[:-1])
    everyone = tm_ref.shape[0]
    _, lats, places = leg_ref.shape
    groups_f = everyone // fields
    wf = fields * 2
    unit = rows * wf
    span = eh_ref.shape[1]
    eight = 8 * lats
    groups = eh_ref.shape[0] // (2 * eight)
    owner = lax.axis_index("lat") * groups_f + lax.axis_index("fld")

    pad_s[...] = jnp.zeros(pad_s.shape, F32)
    pad_s[0:everyone, 0:everyone] = tm_ref[...]
    shape = (LANES, LANES)
    level = (lane_iota(shape) // unit) * fields + (lane_iota(shape) % wf) // 2
    pick = jnp.where(row_iota(shape) == level, 1.0, 0.0).astype(BF16)
    lane = lane_iota((KPAD, LANES))
    parts = []
    for piece in split(pad_s[...]):
        wide = dot(piece, pick)
        total = []
        for r in range(rows):
            for c in range(2):
                keep = ((lane % unit) // wf == r) & (lane % 2 == c) & (lane < unit * groups_f)
                total.append(jnp.where(keep, wide, 0.0))
        parts.append(jnp.concatenate(total, axis=0).astype(BF16))
    mix_ref[...] = jnp.concatenate([parts[0], parts[1], parts[0]], axis=1)

    pad_s[...] = jnp.zeros(pad_s.shape, F32)
    pad_s[0:everyone, 0:everyone] = bm_ref[...]
    shape = (FPAD, KPAD)
    expand = jnp.where(row_iota(shape) // 2 == lane_iota(shape), 1.0, 0.0).astype(BF16)
    shape = (LANES, 2 * LANES)
    repeat = jnp.where(row_iota(shape) == lane_iota(shape) % KPAD, 1.0, 0.0).astype(BF16)
    shape = (FPAD, 2 * LANES)
    same = row_iota(shape) % 2 == (lane_iota(shape) // KPAD) % 2
    half = lane_iota((FPAD, LANES)) < 64
    narrow = lane_iota((FPAD, LANES)) < 2 * KPAD
    fulls = []
    for part, piece in enumerate(split(pad_s[...])):
        full = jnp.where(same, dot(dot(expand, piece).astype(BF16), repeat), 0.0)
        back_ref[part * FPAD:(part + 1) * FPAD, :] = full[:, 0:8 * KPAD].astype(BF16)
        fulls.append(jnp.where(narrow, full[:, 0:LANES], 0.0))
    turn_ref[...] = jnp.concatenate(
        [jnp.where(half, fulls[0], pltpu.roll(fulls[0], 64, 1)), fulls[1]], axis=1
    ).astype(BF16)

    row = row_iota((KPAD, 2 * LANES))
    rate = jnp.zeros((KPAD, 2 * LANES), F32)
    for k in range(everyone):
        rate = jnp.where(row == k, rates_ref[k], rate)
    rate_ref[...] = rate
    paired = tau_ref.shape[0]
    row = row_iota((paired, LANES))
    waves = []
    wave = jnp.zeros((paired, LANES), jnp.int32)
    for pair in range(4 * groups):
        waves.append(fold_ref[owner, 2 * min(pair, pairs - 1)])
        wave = jnp.where(row == pair, waves[pair], wave)
    wave = jnp.concatenate([wave] * (span // LANES), axis=1)
    line = lane_iota((paired, span))
    degree = jnp.where(line > cut_off - wave, line - 1, line + wave)
    tau_ref[...] = (degree * (degree + 1)).astype(F32) * (1.0 / float(cut_off * (cut_off + 1)))

    quad_rows = 4 * lats
    shape = (quad_rows, quad_rows)
    band = jnp.zeros(shape, jnp.int32)
    for holder in range(lats):
        band = jnp.where(row_iota(shape) % lats == holder, band_ref[holder], band)
    order = jnp.where(
        (row_iota(shape) // lats == lane_iota(shape) // lats) & (lane_iota(shape) % lats == band),
        1.0,
        0.0,
    ).astype(BF16)

    whole = places // LANES * LANES
    line = lane_iota((quad_rows, span))
    row = row_iota((quad_rows, LANES)) // lats
    copies[-1].wait()
    keeps = []
    for t in range(groups):
        wave = jnp.zeros((quad_rows, LANES), jnp.int32)
        last = jnp.zeros((quad_rows, LANES), jnp.int32)
        stack = []
        for pp in range(4):
            there = 4 * t + pp < pairs
            index = min(4 * t + pp, pairs - 1)
            wave = jnp.where(row == pp, waves[4 * t + pp], wave)
            last = jnp.where(row == pp, places - 1 if there else -1, last)
            stack.append(
                jnp.concatenate(
                    [
                        leg_ref[index, :, 0:whole],
                        jnp.broadcast_to(leg_ref[index, :, whole:places], (lats, span - whole)),
                    ],
                    axis=1,
                )
            )
        wave = jnp.concatenate([wave] * (span // LANES), axis=1)
        last = jnp.concatenate([last] * (span // LANES), axis=1)
        leg = dot(order, jnp.concatenate(stack, axis=0).astype(BF16))
        before = line <= cut_off - wave
        first = before & (line <= last)
        second = jnp.logical_not(before) & (line <= last)
        odd = ((line + jnp.where(before, 0, wave)) & 1) == 1
        signed = jnp.where(odd, -leg, leg)
        for r, rowset in enumerate((leg, signed)):
            near = jnp.where(first, rowset, 0.0)
            far = jnp.where(second, rowset, 0.0)
            for pp in range(4):
                at = 2 * eight * t + r * eight + 2 * pp * lats
                eh_ref[at:at + 2 * lats, :] = jnp.concatenate(
                    [near[pp * lats:(pp + 1) * lats], far[pp * lats:(pp + 1) * lats]], axis=0
                ).astype(BF16)
        part = pl.ds(2 * eight * t, 2 * eight)
        keeps.append(pltpu.make_async_copy(eh_ref.at[part], eh_hbm.at[part], out_sems.at[t]))
        keeps[-1].start()
    wait_all(keeps)


def solve_kernel(
    fields, rows, lats, eh_hbm, msg_ref, mix_ref, turn_ref, tau_ref, rate_ref,
    near_ref, far_hbm, out_ref, cs, eh_ref, far_ref, in_sems, out_sems,
):
    eight = 8 * lats
    groups = eh_ref.shape[0] // (2 * eight)
    parts = [pl.ds(0, 2 * eight), pl.ds(2 * eight, 2 * eight * (groups - 1))]
    later = start_all(
        [eh_hbm.at[part] for part in parts], [eh_ref.at[part] for part in parts], in_sems
    )
    groups_f = msg_ref.shape[0] // eight
    wf = fields * 2
    unit = rows * wf
    span = eh_ref.shape[1]
    deep = 8 * KPAD
    near = near_ref.shape[0] // deep
    holds = [(near_ref, deep * t) for t in range(near)]
    holds += [(far_ref, deep * t) for t in range(groups - near)]
    lane = lane_iota((lats, LANES))
    tiles = [
        [msg_ref[pl.ds(8 * g + i8, lats, stride=8 * groups_f), :] for g in range(groups_f)]
        for i8 in range(8)
    ]
    tall = []
    for t in range(groups):
        here = [lanes_within(lane, unit * (t + g), unit) for g in range(groups_f)]
        for i8 in range(8):
            line = tiles[i8][0]
            for g in range(1, groups_f):
                line = jnp.where(here[g], tiles[i8][g], line)
            if t:
                line = pltpu.roll(line, LANES - unit * t, 1)
            tall.append(line)
    v_high, v_low = split(jnp.concatenate(tall, axis=0))
    mixed = dot_nt(mix_ref[...], jnp.concatenate([v_high, v_high, v_low], axis=1))

    rate = rate_ref[...]
    slot_pair = (lane_iota((2 * KPAD, 2 * eight)) % eight) // (2 * lats)
    blank = jnp.zeros((64 - 2 * KPAD, span), BF16)
    front = lane_iota((lats, LANES)) < 64

    lefts = []
    for t in range(groups):
        mine = mixed[:, eight * t:eight * (t + 1)]
        mine = jnp.concatenate([mine[0:2 * KPAD], mine[2 * KPAD:4 * KPAD]], axis=1)
        left = jnp.concatenate([jnp.where(slot_pair == pp, mine, 0.0) for pp in range(4)], axis=0)
        lefts.append(jnp.concatenate(split(left), axis=1))

    keeps = []
    for t in range(groups):
        left = lefts[t]
        legs = pl.ds(2 * eight * t, 2 * eight)
        if t < 2:
            later[t].wait()
        for start in range(0, span, 2 * LANES):
            size = min(2 * LANES, span - start)
            right = eh_ref[legs, start:start + size]
            modes = dot(left, jnp.concatenate([right, right], axis=0))
            damped = []
            for pp in range(4):
                tau = tau_ref[4 * t + pp:4 * t + pp + 1, start:start + size]
                below = 1.0 + tau * rate[:, 0:size]
                factor = pl.reciprocal(below, approx=True)
                factor = factor * (2.0 - below * factor)
                at = 2 * pp * KPAD
                damped.append(modes[at:at + KPAD] * factor)
                damped.append(modes[at + KPAD:at + 2 * KPAD] * factor)
            hold, at = holds[t]
            hold[at:at + deep, start:start + size] = jnp.concatenate(damped, axis=0).astype(BF16)
        if t >= near:
            part = pl.ds(deep * (t - near), deep)
            keeps.append(
                pltpu.make_async_copy(far_ref.at[part], far_hbm.at[part], out_sems.at[t - near])
            )
            keeps[-1].start()

    products = []
    for t in range(groups):
        legs = pl.ds(2 * eight * t, 2 * eight)
        pieces = []
        hold, base = holds[t]
        for pp in range(4):
            at = base + 2 * KPAD * pp
            pieces += [hold[at:at + 2 * KPAD, :], blank]
        products.append(dot_nt(eh_ref[legs, :], jnp.concatenate(pieces, axis=0)))

    highs, lows = [], []
    for sums in products:
        for r in range(rows):
            for i8 in range(8):
                at = (r * 8 + i8) * lats
                pp = i8 // 2
                tile = sums[at:at + lats, LANES * (pp // 2):LANES * (pp // 2 + 1)]
                if pp % 2:
                    tile = pltpu.roll(tile, 64, 1)
                high = tile.astype(BF16).astype(F32)
                low = pltpu.roll(tile - high, 64, 1)
                highs.append(jnp.where(front, high, low))
                lows.append(jnp.where(front, high, 0.0))
    own = jnp.concatenate(
        [jnp.concatenate(highs, axis=0), jnp.concatenate(lows, axis=0)], axis=1
    ).astype(BF16)
    cs[:, 0:FPAD] = dot_nt(own, turn_ref[...])

    lane = lane_iota((8, LANES))
    here = [
        lanes_within(lane, wf * u, wf) for u in range(rows * groups + groups_f - 1)
    ]
    for holder in range(lats):
        tiles = [jnp.zeros((8, LANES), F32) for _ in range(groups_f)]
        for u in range(rows * groups):
            piece = cs[pl.ds(u * eight + holder, 8, stride=lats), :]
            if u:
                piece = pltpu.roll(piece, wf * u, 1)
            for g in range(groups_f):
                tiles[g] = jnp.where(here[u + g], piece, tiles[g])
        for g in range(groups_f):
            at = (holder * groups_f + g) * 8
            out_ref[at:at + 8, :] = tiles[g]
    wait_all(keeps)


def output_kernel(near_ref, far_hbm, back_ref, spec_ref, bk, far_s, sems):
    everyone, quad, _, places = spec_ref.shape
    span = near_ref.shape[1]
    deep = 8 * KPAD
    near = near_ref.shape[0] // deep
    tall = 2 * everyone
    step = pl.program_id(0)

    def far_copy(t):
        part = pl.ds(pl.multiple_of(deep * t, deep), deep)
        return pltpu.make_async_copy(far_hbm.at[part], far_s.at[part], sems.at[t])

    @pl.when(step == 0)
    def _():
        for t in range(sems.shape[0]):
            far_copy(t).start()
        pair_of = lane_iota((tall, deep)) // (2 * KPAD)
        rows = []
        for part in range(2):
            full = back_ref[part * FPAD:part * FPAD + tall, :].astype(F32)
            for pp in range(4):
                rows.append(jnp.where(pair_of == pp, full, 0.0))
        bk[...] = jnp.concatenate(rows, axis=0).astype(BF16)

    def write(source, at):
        for start in range(0, span, 2 * LANES):
            size = min(2 * LANES, span - start)
            spec = dot(bk[...], source[pl.ds(at, deep), start:start + size])
            spec = spec[0:4 * tall] + spec[4 * tall:]
            kept = min(size, places - start)
            for pp in range(4):
                for f in range(everyone):
                    row = pp * tall + 2 * f
                    spec_ref[f, pp, :, start:start + kept] = spec[row:row + 2, 0:kept]

    @pl.when(step < near)
    def _():
        write(near_ref, pl.multiple_of(deep * step, deep))

    @pl.when(step >= near)
    def _():
        far_copy(step - near).wait()
        write(far_s, pl.multiple_of(deep * (step - near), deep))


def per_device(grid, row_lengths, band_map, fold_map, legendre, to_modes, back_modes, mode_rates):
    fields, single, rows, width = grid.shape
    pairs, places, lats = legendre.shape
    cut_off = places - 2
    everyone = to_modes.shape[0]
    owners, per_owner = fold_map.shape
    groups = -(-per_owner // 8)
    slots = owners * groups * 8
    pieces = -(-(width // 4) // DEEP)
    turns = 4 * pieces
    span = -(-places // LANES) * LANES
    hbm = pl.BlockSpec(memory_space=pltpu.HBM)
    vmem = pl.BlockSpec(memory_space=pltpu.VMEM)
    room = pltpu.CompilerParams(vmem_limit_bytes=ROOM)
    message = pltpu.HBM((owners, 8, LANES), F32)
    holders = band_map.shape[0]
    groups_f = everyone // fields
    dma = pltpu.SemaphoreType.DMA
    row_lengths, band_map, fold_map, to_modes, back_modes, mode_rates, grid = (
        pltpu.with_memory_space_constraint(x, pltpu.HBM)
        for x in (row_lengths, band_map, fold_map, to_modes, back_modes, mode_rates, grid)
    )
    legendre = pltpu.with_memory_space_constraint(jnp.transpose(legendre, (0, 2, 1)), pltpu.HBM)

    sending, cos_table, sin_table, cos_turn, sin_turn = pl.pallas_call(
        functools.partial(forward_kernel, cut_off, groups),
        out_shape=(
            message,
            pltpu.VMEM((DEEP, slots), BF16),
            pltpu.VMEM((DEEP, slots), BF16),
            pltpu.VMEM((turns, slots), F32),
            pltpu.VMEM((turns, slots), F32),
        ),
        in_specs=[hbm] * 4,
        out_specs=(vmem,) * 5,
        scratch_shapes=[
            pltpu.SMEM(row_lengths.shape, jnp.int32),
            pltpu.SMEM(band_map.shape, jnp.int32),
            pltpu.VMEM(fold_map.shape, jnp.int32),
            pltpu.VMEM(grid.shape, BF16),
            dma((4,)),
            pltpu.VMEM((LANES, LANES), F32),
            pltpu.VMEM((8, slots), F32),
            pltpu.VMEM((16, 4 * DEEP * pieces), F32),
            pltpu.VMEM((16 * turns, DEEP), BF16),
            pltpu.VMEM((64, slots), BF16),
        ],
        compiler_params=room,
        name="forward_rows",
    )(row_lengths, band_map, fold_map, grid)
    tables = [
        pltpu.with_memory_space_constraint(x, pltpu.VMEM)
        for x in (cos_table, sin_table, cos_turn, sin_turn)
    ]
    arrived = lax.all_to_all(sending, ("lat", "fld"), split_axis=0, concat_axis=0, tiled=True)

    legs, mix, back, turn_back, tau, rate = pl.pallas_call(
        functools.partial(prepare_kernel, cut_off, pairs, fields, rows),
        out_shape=(
            pltpu.HBM((groups * 16 * lats, span), BF16),
            pltpu.VMEM((2 * rows * KPAD, 3 * LANES), BF16),
            pltpu.VMEM((2 * FPAD, 8 * KPAD), BF16),
            pltpu.VMEM((FPAD, 2 * LANES), BF16),
            pltpu.VMEM((-(-groups * 4 // 8) * 8, span), F32),
            pltpu.VMEM((KPAD, 2 * LANES), F32),
        ),
        in_specs=[hbm] * 6,
        out_specs=(hbm,) + (vmem,) * 5,
        scratch_shapes=[
            pltpu.SMEM(fold_map.shape, jnp.int32),
            pltpu.SMEM(band_map.shape, jnp.int32),
            pltpu.SMEM(mode_rates.shape, F32),
            pltpu.VMEM((pairs, lats, places), F32),
            pltpu.VMEM(to_modes.shape, F32),
            pltpu.VMEM(back_modes.shape, F32),
            dma((6,)),
            pltpu.VMEM((KPAD, LANES), F32),
            pltpu.VMEM((groups * 16 * lats, span), BF16),
            dma((groups,)),
        ],
        compiler_params=room,
        cost_estimate=pl.CostEstimate(flops=10**8, bytes_accessed=8 * 10**6, transcendentals=0),
        name="prepare",
    )(fold_map, band_map, mode_rates, legendre, to_modes, back_modes)
    legs = pltpu.with_memory_space_constraint(legs, pltpu.HBM)
    mix, back, turn_back, tau, rate = (
        pltpu.with_memory_space_constraint(x, pltpu.VMEM)
        for x in (mix, back, turn_back, tau, rate)
    )

    near = groups // 2
    damped_near, damped_far, leaving = pl.pallas_call(
        functools.partial(solve_kernel, fields, rows, lats),
        out_shape=(
            pltpu.VMEM((near * 8 * KPAD, span), BF16),
            pltpu.HBM(((groups - near) * 8 * KPAD, span), BF16),
            pltpu.HBM((owners * 8, LANES), F32),
        ),
        in_specs=[hbm] + [vmem] * 5,
        out_specs=(vmem, hbm, vmem),
        scratch_shapes=[
            pltpu.VMEM((groups * 16 * lats, LANES), F32),
            pltpu.VMEM((groups * 16 * lats, span), BF16),
            pltpu.VMEM(((groups - near) * 8 * KPAD, span), BF16),
            dma((2,)),
            dma((groups - near,)),
        ],
        compiler_params=room,
        name="solve",
    )(legs, arrived.reshape(owners * 8, LANES), mix, turn_back, tau, rate)
    leaving = leaving.reshape(owners, 8, LANES)

    returned = lax.all_to_all(leaving, ("lat", "fld"), split_axis=0, concat_axis=0, tiled=True)

    damped_near = pltpu.with_memory_space_constraint(damped_near, pltpu.VMEM)
    damped_far = pltpu.with_memory_space_constraint(damped_far, pltpu.HBM)
    spectral = pl.pallas_call(
        output_kernel,
        grid=(groups,),
        out_shape=jax.ShapeDtypeStruct((everyone, pairs, 2, places), F32),
        in_specs=[
            pl.BlockSpec((near * 8 * KPAD, span), lambda t: (0, 0)),
            hbm,
            pl.BlockSpec((2 * FPAD, 8 * KPAD), lambda t: (0, 0)),
        ],
        out_specs=pl.BlockSpec((everyone, 4, 2, places), lambda t: (0, t, 0, 0)),
        scratch_shapes=[
            pltpu.VMEM((16 * everyone, 8 * KPAD), BF16),
            pltpu.VMEM(((groups - near) * 8 * KPAD, span), BF16),
            dma((groups - near,)),
        ],
        compiler_params=pltpu.CompilerParams(
            dimension_semantics=("arbitrary",), vmem_limit_bytes=ROOM
        ),
        cost_estimate=pl.CostEstimate(flops=10**8, bytes_accessed=8 * 10**6, transcendentals=0),
        name="spectral_output",
    )(damped_near, damped_far, back)

    grid_out = pl.pallas_call(
        functools.partial(inverse_kernel, groups),
        out_shape=jax.ShapeDtypeStruct(grid.shape, BF16),
        in_specs=[hbm] * 2 + [vmem] * 5,
        out_specs=vmem,
        scratch_shapes=[
            pltpu.SMEM(row_lengths.shape, jnp.int32),
            pltpu.SMEM(band_map.shape, jnp.int32),
            dma((2,)),
            pltpu.VMEM((32 * pieces, 4 * LANES), BF16),
        ],
        compiler_params=room,
        name="inverse_rows",
    )(row_lengths, band_map, *tables, returned)
    return (jnp.transpose(spectral, (0, 2, 1, 3)), grid_out)


def solution(mesh):
    placed = (
        P("fld", "lat", None, None),
        P(),
        P(),
        P(),
        P(("lat", "fld"), None, None),
        P(),
        P(),
        P(),
    )
    return jax.shard_map(
        per_device,
        mesh=mesh,
        in_specs=placed,
        out_specs=(P(None, None, ("lat", "fld"), None), P("fld", "lat", None, None)),
        check_vma=False,
    )
```

```python
import functools
import math

import jax
import jax.numpy as jnp
from jax import lax
from jax.experimental import pallas as pl
from jax.experimental.pallas import tpu as pltpu
from jax.sharding import PartitionSpec as P

LANES = 128
KPAD = 24
FPAD = 64
DEEP = 256
ROOM = 24 * 1024 * 1024
F32 = jnp.float32
BF16 = jnp.bfloat16
NT_DIMS = (((1,), (1,)), ((), ()))
SIN_POLY = (
    6.283185302447051,
    -41.34170038368319,
    81.60513023312113,
    -76.70299324464969,
    42.02573766814694,
    -14.899106966102595,
    3.237062655726421,
)
COS_POLY = (
    0.9999999889083757,
    -19.739204448887243,
    64.93911476570418,
    -85.45008785413638,
    60.167188450194914,
    -25.9658703083255,
    6.526145851512229,
)


def dot(a, b):
    return jnp.dot(a, b, preferred_element_type=F32)


def dot_nt(a, b):
    return lax.dot_general(a, b, NT_DIMS, preferred_element_type=F32)


def split(x):
    high = x.astype(BF16)
    return high, (x - high.astype(F32)).astype(BF16)


def horner(coefs, z):
    total = coefs[-1] * z + coefs[-2]
    for coef in coefs[-3::-1]:
        total = total * z + coef
    return total


def turn(steps, period, inverse):
    rest = steps - period * jnp.floor(steps * inverse + 0.5)
    part = rest * inverse
    z = part * part
    return horner(COS_POLY, z), part * horner(SIN_POLY, z)


def start_all(sources, targets, sems):
    copies = [
        pltpu.make_async_copy(source, target, sems.at[i])
        for i, (source, target) in enumerate(zip(sources, targets))
    ]
    for copy in copies:
        copy.start()
    return copies


def wait_all(copies):
    for copy in copies:
        copy.wait()


def lane_iota(shape):
    return lax.broadcasted_iota(jnp.int32, shape, len(shape) - 1)


def row_iota(shape):
    return lax.broadcasted_iota(jnp.int32, shape, len(shape) - 2)


def lanes_within(lane, start, size):
    start %= LANES
    if start + size <= LANES:
        return (lane >= start) & (lane < start + size)
    return (lane >= start) | (lane < start + size - LANES)


def spread_matrix():
    shape = (4 * LANES, LANES)
    picks = []
    for phase in range(4):
        picks.append(jnp.where(row_iota(shape) == 4 * lane_iota(shape) + phase, 1.0, 0.0))
    return jnp.concatenate(picks, axis=1).astype(BF16)


def phases_of(groups, wave, length, lanes):
    shape = (groups + 16, lanes)
    row = row_iota(shape)
    steps = jnp.where(row < groups, (row // 4) * (4 * DEEP) + row % 4, 4 * (row - groups))
    steps = jnp.where(row >= groups + 8, 32 << jnp.maximum(row - groups - 8, 0), steps)
    period = jnp.full(shape, length, jnp.int32).astype(F32)
    return turn(steps.astype(F32) * wave, period, 1.0 / period)


def forward_kernel(
    cut_off, groups, len_hbm, band_hbm, fold_hbm, grid_hbm,
    msg_ref, tc, ts, fc, fs,
    len_ref, band_ref, fold_ref, grid_ref, sems, fold_s, wave_s, xs, xq, xt,
):
    copies = start_all(
        (len_hbm, band_hbm, fold_hbm, grid_hbm), (len_ref, band_ref, fold_ref, grid_ref), sems
    )
    fields, _, rows, width = grid_ref.shape
    owners, per_owner = fold_ref.shape
    slots = tc.shape[1]
    pieces = xq.shape[0] // 64
    unit = rows * fields * 2
    spread_s = spread_matrix()
    shape = (owners * 8, fold_s.shape[0])
    repeat = jnp.where(row_iota(shape) // 8 == lane_iota(shape), 1.0, 0.0).astype(BF16)
    weigh = jnp.where(lane_iota((8, 2 * LANES)) < LANES, 8.0, 1.0).astype(BF16)
    shape = (LANES, 64 * groups)
    source = lane_iota(shape)
    vec = source % 16
    base = (vec % rows) * (fields * 2) + (vec // rows) * 2 + (source // 16) % 2
    target = (base + unit * (source // 64 + lax.axis_index("fld"))) % LANES
    packing = jnp.where((vec < rows * fields) & (row_iota(shape) == target), 1.0, 0.0).astype(BF16)
    fold_s[...] = jnp.full(fold_s.shape, -1.0, F32)
    xs[...] = jnp.zeros(xs.shape, F32)
    wait_all(copies)
    length = len_ref[band_ref[lax.axis_index("lat")]]
    top = jnp.minimum(cut_off, (length - 1) // 2)

    fold_s[0:owners, 0:per_owner] = fold_ref[...].astype(F32)
    eights = jnp.floor(fold_s[...] * 0.125)
    parts = jnp.concatenate([eights, fold_s[...] - 8.0 * eights], axis=1).astype(BF16)
    repeated = dot(repeat, parts)
    lane = lane_iota(repeated.shape)
    place = lane % LANES - row_iota(repeated.shape) % 8
    for t in range(groups):
        chosen = jnp.where(place == 8 * t, repeated, 0.0).astype(BF16)
        wave_s[:, owners * 8 * t:owners * 8 * (t + 1)] = dot_nt(weigh, chosen)

    for field in range(fields):
        xs[rows * field:rows * (field + 1), 0:width] = grid_ref[field, 0].astype(F32)
    stacked = jnp.concatenate(
        [xs[:, 4 * LANES * c:4 * LANES * (c + 1)] for c in range(2 * pieces)], axis=0
    ).astype(BF16)
    spread = dot(stacked, spread_s)
    across = (row_iota(spread.shape) // 16) * LANES + lane_iota(spread.shape) % LANES
    spread = jnp.where(across < length // 4, spread, 0.0).astype(BF16)
    for c in range(2 * pieces):
        for phase in range(4):
            at = (4 * (c // 2) + phase) * 16
            off = LANES * (c % 2)
            xq[at:at + 16, off:off + LANES] = spread[
                16 * c:16 * (c + 1), LANES * phase:LANES * (phase + 1)
            ]

    turns = 4 * pieces
    block = 2 * LANES
    values = xq[...]
    for i in range(slots // block):
        at = pl.ds(i * block, block)
        wave = wave_s[:, at]
        wave = jnp.concatenate([wave] * ((turns + 16) // 8), axis=0)
        co, si = phases_of(turns, wave, length, block)
        one = wave[0:1]
        weight = jnp.where(one == 0.0, 1.0, 2.0)
        weight = jnp.where((one >= 0.0) & (one <= jnp.full(one.shape, top, jnp.int32).astype(F32)), weight, 0.0)
        fc[:, at] = co[0:turns] * weight
        fs[:, at] = si[0:turns] * weight
        c_all = co[turns:turns + 8]
        s_all = si[turns:turns + 8]
        size, step = 8, turns + 8
        while size < DEEP:
            c1 = co[step:step + 1]
            s1 = si[step:step + 1]
            c_new = c_all * c1 - s_all * s1
            s_new = s_all * c1 + c_all * s1
            c_all = jnp.concatenate([c_all, c_new], axis=0)
            s_all = jnp.concatenate([s_all, s_new], axis=0)
            size, step = 2 * size, step + 1
        c_all = c_all.astype(BF16)
        s_all = s_all.astype(BF16)
        tc[:, at] = c_all
        ts[:, at] = s_all
        inner_c = dot(values, c_all)
        inner_s = dot(values, s_all)
        real = jnp.zeros((16, block), F32)
        imag = jnp.zeros((16, block), F32)
        for g in range(turns):
            c1 = fc[g:g + 1, at]
            s1 = fs[g:g + 1, at]
            part_c = inner_c[16 * g:16 * (g + 1)]
            part_s = inner_s[16 * g:16 * (g + 1)]
            real = real + (c1 * part_c - s1 * part_s)
            imag = imag - (c1 * part_s + s1 * part_c)
        both = jnp.concatenate([real, imag], axis=0) * jnp.where(one == 0.0, 1.0, 0.5)
        xt[:, at] = jnp.concatenate(split(both), axis=0)
    turned = jnp.concatenate(
        [xt[:, owners * 8 * t:owners * 8 * (t + 1)] for t in range(groups)], axis=0
    )
    total = dot(packing, turned)
    scale = 1.0 / jnp.sqrt(jnp.full(total.shape, length, jnp.int32).astype(F32))
    msg_ref[...] = jnp.transpose(total * scale).reshape(owners, 8, LANES)


def inverse_kernel(
    groups, len_hbm, band_hbm, tc, ts, fc, fs, msg_ref, grid_ref,
    len_ref, band_ref, sems, os,
):
    copies = start_all((len_hbm, band_hbm), (len_ref, band_ref), sems)
    spread_s = spread_matrix()
    fields, _, rows, width = grid_ref.shape
    owners = msg_ref.shape[0]
    slots = tc.shape[1]
    turns = fc.shape[0]
    unit = rows * fields * 2
    high, low = split(msg_ref[...].reshape(owners * 8, LANES))
    pieces = jnp.concatenate([high, low], axis=1)
    shape = (32 * groups, 2 * LANES)
    target = row_iota(shape) % 32
    vec = target % 16
    base = (vec % rows) * (fields * 2) + (vec // rows) * 2 + target // 16
    source = (base + unit * (row_iota(shape) // 32) + lax.axis_index("fld") * (fields * 2)) % LANES
    place = jnp.where(
        (vec < rows * fields) & (lane_iota(shape) % LANES == source), 1.0, 0.0
    ).astype(BF16)
    turned = dot_nt(place, pieces)
    block = 2 * LANES
    lefts, rights = [], []
    for i in range(slots // block):
        t, off = divmod(i * block, owners * 8)
        real = turned[32 * t:32 * t + 16, off:off + block]
        imag = turned[32 * t + 16:32 * t + 32, off:off + block]
        less_real = -real
        less_imag = -imag
        at = pl.ds(i * block, block)
        reals, imags = [], []
        for g in range(turns):
            c1 = fc[g:g + 1, at]
            s1 = fs[g:g + 1, at]
            reals.append(c1 * real + s1 * less_imag)
            imags.append(s1 * less_real + c1 * less_imag)
        lefts += [jnp.concatenate(reals, axis=0).astype(BF16), jnp.concatenate(imags, axis=0).astype(BF16)]
        rights += [tc[:, at], ts[:, at]]
    out = dot_nt(jnp.concatenate(lefts, axis=1), jnp.concatenate(rights, axis=1))
    wait_all(copies)
    length = len_ref[band_ref[lax.axis_index("lat")]]
    out = out * (1.0 / jnp.sqrt(jnp.full((16 * turns, DEEP), length, jnp.int32).astype(F32)))
    chunks = os.shape[0] // 16
    for c in range(chunks):
        for phase in range(4):
            at = (4 * (c // 2) + phase) * 16
            off = LANES * (c % 2)
            os[16 * c:16 * (c + 1), LANES * phase:LANES * (phase + 1)] = out[
                at:at + 16, off:off + LANES
            ].astype(BF16)
    merged = dot_nt(os[...], spread_s)
    for c in range(chunks):
        begin = 4 * LANES * c
        size = min(4 * LANES, width - begin)
        if size <= 0:
            continue
        inside = begin + lane_iota((16, size)) < length
        piece = jnp.where(inside, merged[16 * c:16 * (c + 1), 0:size], 0.0)
        for field in range(fields):
            grid_ref[field, 0, :, begin:begin + size] = piece[
                rows * field:rows * (field + 1)
            ].astype(BF16)


def prepare_kernel(
    cut_off, pairs, fields, rows, fold_hbm, band_hbm, rates_hbm, leg_hbm, tm_hbm, bm_hbm,
    eh_hbm, mix_ref, back_ref, turn_ref, tau_ref, rate_ref,
    fold_ref, band_ref, rates_ref, leg_ref, tm_ref, bm_ref, sems, pad_s, eh_ref, out_sems,
):
    copies = start_all(
        (fold_hbm, band_hbm, rates_hbm, tm_hbm, bm_hbm, leg_hbm),
        (fold_ref, band_ref, rates_ref, tm_ref, bm_ref, leg_ref),
        sems,
    )
    wait_all(copies[:-1])
    everyone = tm_ref.shape[0]
    _, lats, places = leg_ref.shape
    groups_f = everyone // fields
    wf = fields * 2
    unit = rows * wf
    span = eh_ref.shape[1]
    eight = 8 * lats
    groups = eh_ref.shape[0] // (2 * eight)
    owner = lax.axis_index("lat") * groups_f + lax.axis_index("fld")

    pad_s[...] = jnp.zeros(pad_s.shape, F32)
    pad_s[0:everyone, 0:everyone] = tm_ref[...]
    shape = (LANES, LANES)
    level = (lane_iota(shape) // unit) * fields + (lane_iota(shape) % wf) // 2
    pick = jnp.where(row_iota(shape) == level, 1.0, 0.0).astype(BF16)
    lane = lane_iota((KPAD, LANES))
    parts = []
    for piece in split(pad_s[...]):
        wide = dot(piece, pick)
        total = []
        for r in range(rows):
            for c in range(2):
                keep = ((lane % unit) // wf == r) & (lane % 2 == c) & (lane < unit * groups_f)
                total.append(jnp.where(keep, wide, 0.0))
        parts.append(jnp.concatenate(total, axis=0).astype(BF16))
    mix_ref[...] = jnp.concatenate([parts[0], parts[1], parts[0]], axis=1)

    pad_s[...] = jnp.zeros(pad_s.shape, F32)
    pad_s[0:everyone, 0:everyone] = bm_ref[...]
    shape = (FPAD, KPAD)
    expand = jnp.where(row_iota(shape) // 2 == lane_iota(shape), 1.0, 0.0).astype(BF16)
    shape = (LANES, 2 * LANES)
    repeat = jnp.where(row_iota(shape) == lane_iota(shape) % KPAD, 1.0, 0.0).astype(BF16)
    shape = (FPAD, 2 * LANES)
    same = row_iota(shape) % 2 == (lane_iota(shape) // KPAD) % 2
    fulls = []
    for part, piece in enumerate(split(pad_s[...])):
        full = jnp.where(same, dot(dot(expand, piece).astype(BF16), repeat), 0.0)
        back_ref[part * FPAD:(part + 1) * FPAD, :] = full[:, 0:8 * KPAD].astype(BF16)
        fulls.append(full)
    turn = jnp.where(lane_iota(shape) < 4 * KPAD, fulls[0], fulls[1])
    turn_ref[...] = turn[:, 0:6 * KPAD].astype(BF16)

    row = row_iota((KPAD, 2 * LANES))
    rate = jnp.zeros((KPAD, 2 * LANES), F32)
    for k in range(everyone):
        rate = jnp.where(row == k, rates_ref[k], rate)
    rate_ref[...] = rate
    paired = tau_ref.shape[0]
    row = row_iota((paired, LANES))
    waves = []
    wave = jnp.zeros((paired, LANES), jnp.int32)
    for pair in range(4 * groups):
        waves.append(fold_ref[owner, 2 * min(pair, pairs - 1)])
        wave = jnp.where(row == pair, waves[pair], wave)
    wave = jnp.concatenate([wave] * (span // LANES), axis=1)
    line = lane_iota((paired, span))
    degree = jnp.where(line > cut_off - wave, line - 1, line + wave)
    tau_ref[...] = (degree * (degree + 1)).astype(F32) * (1.0 / float(cut_off * (cut_off + 1)))

    quad_rows = 4 * lats
    shape = (quad_rows, quad_rows)
    band = jnp.zeros(shape, jnp.int32)
    for holder in range(lats):
        band = jnp.where(row_iota(shape) % lats == holder, band_ref[holder], band)
    order = jnp.where(
        (row_iota(shape) // lats == lane_iota(shape) // lats) & (lane_iota(shape) % lats == band),
        1.0,
        0.0,
    ).astype(BF16)

    whole = places // LANES * LANES
    line = lane_iota((quad_rows, span))
    row = row_iota((quad_rows, LANES)) // lats
    copies[-1].wait()
    keeps = []
    for t in range(groups):
        wave = jnp.zeros((quad_rows, LANES), jnp.int32)
        last = jnp.zeros((quad_rows, LANES), jnp.int32)
        stack = []
        for pp in range(4):
            there = 4 * t + pp < pairs
            index = min(4 * t + pp, pairs - 1)
            wave = jnp.where(row == pp, waves[4 * t + pp], wave)
            last = jnp.where(row == pp, places - 1 if there else -1, last)
            stack.append(
                jnp.concatenate(
                    [
                        leg_ref[index, :, 0:whole],
                        jnp.broadcast_to(leg_ref[index, :, whole:places], (lats, span - whole)),
                    ],
                    axis=1,
                )
            )
        wave = jnp.concatenate([wave] * (span // LANES), axis=1)
        last = jnp.concatenate([last] * (span // LANES), axis=1)
        leg = dot(order, jnp.concatenate(stack, axis=0).astype(BF16))
        before = line <= cut_off - wave
        first = before & (line <= last)
        second = jnp.logical_not(before) & (line <= last)
        odd = ((line + jnp.where(before, 0, wave)) & 1) == 1
        signed = jnp.where(odd, -leg, leg)
        for r, rowset in enumerate((leg, signed)):
            near = jnp.where(first, rowset, 0.0)
            far = jnp.where(second, rowset, 0.0)
            for pp in range(4):
                at = 2 * eight * t + r * eight + 2 * pp * lats
                eh_ref[at:at + 2 * lats, :] = jnp.concatenate(
                    [near[pp * lats:(pp + 1) * lats], far[pp * lats:(pp + 1) * lats]], axis=0
                ).astype(BF16)
        part = pl.ds(2 * eight * t, 2 * eight)
        keeps.append(pltpu.make_async_copy(eh_ref.at[part], eh_hbm.at[part], out_sems.at[t]))
        keeps[-1].start()
    wait_all(keeps)


def solve_kernel(
    fields, rows, lats, eh_hbm, msg_ref, mix_ref, turn_ref, tau_ref, rate_ref,
    near_ref, far_hbm, out_ref, cs, eh_ref, far_ref, in_sems, out_sems,
):
    eight = 8 * lats
    groups = eh_ref.shape[0] // (2 * eight)
    parts = [pl.ds(0, 2 * eight), pl.ds(2 * eight, 2 * eight * (groups - 1))]
    later = start_all(
        [eh_hbm.at[part] for part in parts], [eh_ref.at[part] for part in parts], in_sems
    )
    groups_f = msg_ref.shape[0] // eight
    wf = fields * 2
    unit = rows * wf
    span = eh_ref.shape[1]
    deep = 8 * KPAD
    near = near_ref.shape[0] // deep
    holds = [(near_ref, deep * t) for t in range(near)]
    holds += [(far_ref, deep * t) for t in range(groups - near)]
    lane = lane_iota((lats, LANES))
    tiles = [
        [msg_ref[pl.ds(8 * g + i8, lats, stride=8 * groups_f), :] for g in range(groups_f)]
        for i8 in range(8)
    ]
    tall = []
    for t in range(groups):
        here = [lanes_within(lane, unit * (t + g), unit) for g in range(groups_f)]
        for i8 in range(8):
            line = tiles[i8][0]
            for g in range(1, groups_f):
                line = jnp.where(here[g], tiles[i8][g], line)
            if t:
                line = pltpu.roll(line, LANES - unit * t, 1)
            tall.append(line)
    v_high, v_low = split(jnp.concatenate(tall, axis=0))
    mixed = dot_nt(mix_ref[...], jnp.concatenate([v_high, v_high, v_low], axis=1))

    rate = rate_ref[...]
    slot_pair = (lane_iota((2 * KPAD, 2 * eight)) % eight) // (2 * lats)
    lefts = []
    for t in range(groups):
        mine = mixed[:, eight * t:eight * (t + 1)]
        mine = jnp.concatenate([mine[0:2 * KPAD], mine[2 * KPAD:4 * KPAD]], axis=1)
        left = jnp.concatenate([jnp.where(slot_pair == pp, mine, 0.0) for pp in range(4)], axis=0)
        lefts.append(jnp.concatenate(split(left), axis=1))

    keeps = []
    for t in range(groups):
        left = lefts[t]
        legs = pl.ds(2 * eight * t, 2 * eight)
        if t < 2:
            later[t].wait()
        for start in range(0, span, 2 * LANES):
            size = min(2 * LANES, span - start)
            right = eh_ref[legs, start:start + size]
            modes = dot(left, jnp.concatenate([right, right], axis=0))
            damped = []
            for pp in range(4):
                tau = tau_ref[4 * t + pp:4 * t + pp + 1, start:start + size]
                below = 1.0 + tau * rate[:, 0:size]
                factor = pl.reciprocal(below, approx=True)
                factor = factor * (2.0 - below * factor)
                at = 2 * pp * KPAD
                damped.append(modes[at:at + KPAD] * factor)
                damped.append(modes[at + KPAD:at + 2 * KPAD] * factor)
            hold, at = holds[t]
            hold[at:at + deep, start:start + size] = jnp.concatenate(damped, axis=0).astype(BF16)
        if t >= near:
            part = pl.ds(deep * (t - near), deep)
            keeps.append(
                pltpu.make_async_copy(far_ref.at[part], far_hbm.at[part], out_sems.at[t - near])
            )
            keeps[-1].start()

    picks = []
    for t in range(groups):
        hold, at = holds[t]
        product = dot_nt(hold[at:at + deep, :], eh_ref[pl.ds(2 * eight * t, 2 * eight), :])
        pick = product[0:2 * KPAD]
        for pp in range(1, 4):
            pick = jnp.where(slot_pair == pp, product[2 * KPAD * pp:2 * KPAD * (pp + 1)], pick)
        picks.append(pick)
    high, low = split(jnp.concatenate(picks, axis=1))
    back = dot(turn_ref[...], jnp.concatenate([high, low, high], axis=0))
    back = jnp.concatenate([back, jnp.zeros((LANES - FPAD, back.shape[1]), F32)], axis=0)
    for at in range(0, back.shape[1], LANES):
        cs[at:at + LANES, :] = jnp.transpose(back[:, at:at + LANES])

    lane = lane_iota((8, LANES))
    here = [
        lanes_within(lane, wf * u, wf) for u in range(rows * groups + groups_f - 1)
    ]
    for holder in range(lats):
        tiles = [jnp.zeros((8, LANES), F32) for _ in range(groups_f)]
        for u in range(rows * groups):
            piece = cs[pl.ds(u * eight + holder, 8, stride=lats), :]
            if u:
                piece = pltpu.roll(piece, wf * u, 1)
            for g in range(groups_f):
                tiles[g] = jnp.where(here[u + g], piece, tiles[g])
        for g in range(groups_f):
            at = (holder * groups_f + g) * 8
            out_ref[at:at + 8, :] = tiles[g]
    wait_all(keeps)


def output_kernel(near_ref, far_hbm, back_ref, spec_ref, bk, far_s, sems):
    everyone, quad, _, places = spec_ref.shape
    span = near_ref.shape[1]
    deep = 8 * KPAD
    near = near_ref.shape[0] // deep
    tall = 2 * everyone
    step = pl.program_id(0)

    def far_copy(t):
        part = pl.ds(pl.multiple_of(deep * t, deep), deep)
        return pltpu.make_async_copy(far_hbm.at[part], far_s.at[part], sems.at[t])

    @pl.when(step == 0)
    def _():
        for t in range(sems.shape[0]):
            far_copy(t).start()
        pair_of = lane_iota((tall, deep)) // (2 * KPAD)
        rows = []
        for part in range(2):
            full = back_ref[part * FPAD:part * FPAD + tall, :].astype(F32)
            for pp in range(4):
                rows.append(jnp.where(pair_of == pp, full, 0.0))
        bk[...] = jnp.concatenate(rows, axis=0).astype(BF16)

    def write(source, at):
        for start in range(0, span, 2 * LANES):
            size = min(2 * LANES, span - start)
            spec = dot(bk[...], source[pl.ds(at, deep), start:start + size])
            spec = spec[0:4 * tall] + spec[4 * tall:]
            kept = min(size, places - start)
            for pp in range(4):
                for f in range(everyone):
                    row = pp * tall + 2 * f
                    spec_ref[f, pp, :, start:start + kept] = spec[row:row + 2, 0:kept]

    @pl.when(step < near)
    def _():
        write(near_ref, pl.multiple_of(deep * step, deep))

    @pl.when(step >= near)
    def _():
        far_copy(step - near).wait()
        write(far_s, pl.multiple_of(deep * (step - near), deep))


def per_device(grid, row_lengths, band_map, fold_map, legendre, to_modes, back_modes, mode_rates):
    fields, single, rows, width = grid.shape
    pairs, places, lats = legendre.shape
    cut_off = places - 2
    everyone = to_modes.shape[0]
    owners, per_owner = fold_map.shape
    groups = -(-per_owner // 8)
    slots = owners * groups * 8
    pieces = -(-(width // 4) // DEEP)
    turns = 4 * pieces
    span = -(-places // LANES) * LANES
    hbm = pl.BlockSpec(memory_space=pltpu.HBM)
    vmem = pl.BlockSpec(memory_space=pltpu.VMEM)
    room = pltpu.CompilerParams(vmem_limit_bytes=ROOM)
    message = pltpu.HBM((owners, 8, LANES), F32)
    holders = band_map.shape[0]
    groups_f = everyone // fields
    dma = pltpu.SemaphoreType.DMA
    row_lengths, band_map, fold_map, to_modes, back_modes, mode_rates, grid = (
        pltpu.with_memory_space_constraint(x, pltpu.HBM)
        for x in (row_lengths, band_map, fold_map, to_modes, back_modes, mode_rates, grid)
    )
    legendre = pltpu.with_memory_space_constraint(jnp.transpose(legendre, (0, 2, 1)), pltpu.HBM)

    sending, cos_table, sin_table, cos_turn, sin_turn = pl.pallas_call(
        functools.partial(forward_kernel, cut_off, groups),
        out_shape=(
            message,
            pltpu.VMEM((DEEP, slots), BF16),
            pltpu.VMEM((DEEP, slots), BF16),
            pltpu.VMEM((turns, slots), F32),
            pltpu.VMEM((turns, slots), F32),
        ),
        in_specs=[hbm] * 4,
        out_specs=(vmem,) * 5,
        scratch_shapes=[
            pltpu.SMEM(row_lengths.shape, jnp.int32),
            pltpu.SMEM(band_map.shape, jnp.int32),
            pltpu.VMEM(fold_map.shape, jnp.int32),
            pltpu.VMEM(grid.shape, BF16),
            dma((4,)),
            pltpu.VMEM((LANES, LANES), F32),
            pltpu.VMEM((8, slots), F32),
            pltpu.VMEM((16, 4 * DEEP * pieces), F32),
            pltpu.VMEM((16 * turns, DEEP), BF16),
            pltpu.VMEM((64, slots), BF16),
        ],
        compiler_params=room,
        name="forward_rows",
    )(row_lengths, band_map, fold_map, grid)
    tables = [
        pltpu.with_memory_space_constraint(x, pltpu.VMEM)
        for x in (cos_table, sin_table, cos_turn, sin_turn)
    ]
    arrived = lax.all_to_all(sending, ("lat", "fld"), split_axis=0, concat_axis=0, tiled=True)

    legs, mix, back, turn_back, tau, rate = pl.pallas_call(
        functools.partial(prepare_kernel, cut_off, pairs, fields, rows),
        out_shape=(
            pltpu.HBM((groups * 16 * lats, span), BF16),
            pltpu.VMEM((2 * rows * KPAD, 3 * LANES), BF16),
            pltpu.VMEM((2 * FPAD, 8 * KPAD), BF16),
            pltpu.VMEM((FPAD, 6 * KPAD), BF16),
            pltpu.VMEM((-(-groups * 4 // 8) * 8, span), F32),
            pltpu.VMEM((KPAD, 2 * LANES), F32),
        ),
        in_specs=[hbm] * 6,
        out_specs=(hbm,) + (vmem,) * 5,
        scratch_shapes=[
            pltpu.SMEM(fold_map.shape, jnp.int32),
            pltpu.SMEM(band_map.shape, jnp.int32),
            pltpu.SMEM(mode_rates.shape, F32),
            pltpu.VMEM((pairs, lats, places), F32),
            pltpu.VMEM(to_modes.shape, F32),
            pltpu.VMEM(back_modes.shape, F32),
            dma((6,)),
            pltpu.VMEM((KPAD, LANES), F32),
            pltpu.VMEM((groups * 16 * lats, span), BF16),
            dma((groups,)),
        ],
        compiler_params=room,
        cost_estimate=pl.CostEstimate(flops=10**8, bytes_accessed=8 * 10**6, transcendentals=0),
        name="prepare",
    )(fold_map, band_map, mode_rates, legendre, to_modes, back_modes)
    legs = pltpu.with_memory_space_constraint(legs, pltpu.HBM)
    mix, back, turn_back, tau, rate = (
        pltpu.with_memory_space_constraint(x, pltpu.VMEM)
        for x in (mix, back, turn_back, tau, rate)
    )

    near = groups // 2
    damped_near, damped_far, leaving = pl.pallas_call(
        functools.partial(solve_kernel, fields, rows, lats),
        out_shape=(
            pltpu.VMEM((near * 8 * KPAD, span), BF16),
            pltpu.HBM(((groups - near) * 8 * KPAD, span), BF16),
            pltpu.HBM((owners * 8, LANES), F32),
        ),
        in_specs=[hbm] + [vmem] * 5,
        out_specs=(vmem, hbm, vmem),
        scratch_shapes=[
            pltpu.VMEM((groups * 16 * lats, LANES), F32),
            pltpu.VMEM((groups * 16 * lats, span), BF16),
            pltpu.VMEM(((groups - near) * 8 * KPAD, span), BF16),
            dma((2,)),
            dma((groups - near,)),
        ],
        compiler_params=room,
        name="solve",
    )(legs, arrived.reshape(owners * 8, LANES), mix, turn_back, tau, rate)
    leaving = leaving.reshape(owners, 8, LANES)

    returned = lax.all_to_all(leaving, ("lat", "fld"), split_axis=0, concat_axis=0, tiled=True)

    damped_near = pltpu.with_memory_space_constraint(damped_near, pltpu.VMEM)
    damped_far = pltpu.with_memory_space_constraint(damped_far, pltpu.HBM)
    spectral = pl.pallas_call(
        output_kernel,
        grid=(groups,),
        out_shape=jax.ShapeDtypeStruct((everyone, pairs, 2, places), F32),
        in_specs=[
            pl.BlockSpec((near * 8 * KPAD, span), lambda t: (0, 0)),
            hbm,
            pl.BlockSpec((2 * FPAD, 8 * KPAD), lambda t: (0, 0)),
        ],
        out_specs=pl.BlockSpec((everyone, 4, 2, places), lambda t: (0, t, 0, 0)),
        scratch_shapes=[
            pltpu.VMEM((16 * everyone, 8 * KPAD), BF16),
            pltpu.VMEM(((groups - near) * 8 * KPAD, span), BF16),
            dma((groups - near,)),
        ],
        compiler_params=pltpu.CompilerParams(
            dimension_semantics=("arbitrary",), vmem_limit_bytes=ROOM
        ),
        cost_estimate=pl.CostEstimate(flops=10**8, bytes_accessed=8 * 10**6, transcendentals=0),
        name="spectral_output",
    )(damped_near, damped_far, back)

    grid_out = pl.pallas_call(
        functools.partial(inverse_kernel, groups),
        out_shape=jax.ShapeDtypeStruct(grid.shape, BF16),
        in_specs=[hbm] * 2 + [vmem] * 5,
        out_specs=vmem,
        scratch_shapes=[
            pltpu.SMEM(row_lengths.shape, jnp.int32),
            pltpu.SMEM(band_map.shape, jnp.int32),
            dma((2,)),
            pltpu.VMEM((32 * pieces, 4 * LANES), BF16),
        ],
        compiler_params=room,
        name="inverse_rows",
    )(row_lengths, band_map, *tables, returned)
    return (jnp.transpose(spectral, (0, 2, 1, 3)), grid_out)


def solution(mesh):
    placed = (
        P("fld", "lat", None, None),
        P(),
        P(),
        P(),
        P(("lat", "fld"), None, None),
        P(),
        P(),
        P(),
    )
    return jax.shard_map(
        per_device,
        mesh=mesh,
        in_specs=placed,
        out_specs=(P(None, None, ("lat", "fld"), None), P("fld", "lat", None, None)),
        check_vma=False,
    )
```

```python
import functools
import math

import jax
import jax.numpy as jnp
from jax import lax
from jax.experimental import pallas as pl
from jax.experimental.pallas import tpu as pltpu
from jax.sharding import PartitionSpec as P

LANES = 128
KPAD = 24
FPAD = 64
DEEP = 256
ROOM = 24 * 1024 * 1024
F32 = jnp.float32
BF16 = jnp.bfloat16
NT_DIMS = (((1,), (1,)), ((), ()))
SIN_POLY = (
    6.283185302447051,
    -41.34170038368319,
    81.60513023312113,
    -76.70299324464969,
    42.02573766814694,
    -14.899106966102595,
    3.237062655726421,
)
COS_POLY = (
    0.9999999889083757,
    -19.739204448887243,
    64.93911476570418,
    -85.45008785413638,
    60.167188450194914,
    -25.9658703083255,
    6.526145851512229,
)


def dot(a, b):
    return jnp.dot(a, b, preferred_element_type=F32)


def dot_nt(a, b):
    return lax.dot_general(a, b, NT_DIMS, preferred_element_type=F32)


def split(x):
    high = x.astype(BF16)
    return high, (x - high.astype(F32)).astype(BF16)


def horner(coefs, z):
    total = coefs[-1] * z + coefs[-2]
    for coef in coefs[-3::-1]:
        total = total * z + coef
    return total


def turn(steps, period, inverse):
    rest = steps - period * jnp.floor(steps * inverse + 0.5)
    part = rest * inverse
    z = part * part
    return horner(COS_POLY, z), part * horner(SIN_POLY, z)


def start_all(sources, targets, sems):
    copies = [
        pltpu.make_async_copy(source, target, sems.at[i])
        for i, (source, target) in enumerate(zip(sources, targets))
    ]
    for copy in copies:
        copy.start()
    return copies


def wait_all(copies):
    for copy in copies:
        copy.wait()


def lane_iota(shape):
    return lax.broadcasted_iota(jnp.int32, shape, len(shape) - 1)


def row_iota(shape):
    return lax.broadcasted_iota(jnp.int32, shape, len(shape) - 2)


def lanes_within(lane, start, size):
    start %= LANES
    if start + size <= LANES:
        return (lane >= start) & (lane < start + size)
    return (lane >= start) | (lane < start + size - LANES)


def spread_matrix():
    shape = (4 * LANES, LANES)
    picks = []
    for phase in range(4):
        picks.append(jnp.where(row_iota(shape) == 4 * lane_iota(shape) + phase, 1.0, 0.0))
    return jnp.concatenate(picks, axis=1).astype(BF16)


def phases_of(groups, wave, length, lanes):
    shape = (groups + 16, lanes)
    row = row_iota(shape)
    steps = jnp.where(row < groups, (row // 4) * (4 * DEEP) + row % 4, 4 * (row - groups))
    steps = jnp.where(row >= groups + 8, 32 << jnp.maximum(row - groups - 8, 0), steps)
    period = jnp.full(shape, length, jnp.int32).astype(F32)
    return turn(steps.astype(F32) * wave, period, 1.0 / period)


def forward_kernel(
    cut_off, groups, len_hbm, band_hbm, fold_hbm, grid_hbm,
    msg_ref, tc, ts, fc, fs,
    len_ref, band_ref, fold_ref, grid_ref, sems, fold_s, wave_s, xs, xq, xt,
):
    copies = start_all(
        (len_hbm, band_hbm, fold_hbm, grid_hbm), (len_ref, band_ref, fold_ref, grid_ref), sems
    )
    fields, _, rows, width = grid_ref.shape
    owners, per_owner = fold_ref.shape
    slots = tc.shape[1]
    pieces = xq.shape[0] // 64
    unit = rows * fields * 2
    spread_s = spread_matrix()
    shape = (owners * 8, fold_s.shape[0])
    repeat = jnp.where(row_iota(shape) // 8 == lane_iota(shape), 1.0, 0.0).astype(BF16)
    weigh = jnp.where(lane_iota((8, 2 * LANES)) < LANES, 8.0, 1.0).astype(BF16)
    shape = (LANES, 64 * groups)
    source = lane_iota(shape)
    vec = source % 16
    base = (vec % rows) * (fields * 2) + (vec // rows) * 2 + (source // 16) % 2
    target = (base + unit * (source // 64 + lax.axis_index("fld"))) % LANES
    packing = jnp.where((vec < rows * fields) & (row_iota(shape) == target), 1.0, 0.0).astype(BF16)
    fold_s[...] = jnp.full(fold_s.shape, -1.0, F32)
    xs[...] = jnp.zeros(xs.shape, F32)
    wait_all(copies)
    length = len_ref[band_ref[lax.axis_index("lat")]]
    top = jnp.minimum(cut_off, (length - 1) // 2)

    fold_s[0:owners, 0:per_owner] = fold_ref[...].astype(F32)
    eights = jnp.floor(fold_s[...] * 0.125)
    parts = jnp.concatenate([eights, fold_s[...] - 8.0 * eights], axis=1).astype(BF16)
    repeated = dot(repeat, parts)
    lane = lane_iota(repeated.shape)
    place = lane % LANES - row_iota(repeated.shape) % 8
    for t in range(groups):
        chosen = jnp.where(place == 8 * t, repeated, 0.0).astype(BF16)
        wave_s[:, owners * 8 * t:owners * 8 * (t + 1)] = dot_nt(weigh, chosen)

    for field in range(fields):
        xs[rows * field:rows * (field + 1), 0:width] = grid_ref[field, 0].astype(F32)
    stacked = jnp.concatenate(
        [xs[:, 4 * LANES * c:4 * LANES * (c + 1)] for c in range(2 * pieces)], axis=0
    ).astype(BF16)
    spread = dot(stacked, spread_s)
    across = (row_iota(spread.shape) // 16) * LANES + lane_iota(spread.shape) % LANES
    spread = jnp.where(across < length // 4, spread, 0.0).astype(BF16)
    for c in range(2 * pieces):
        for phase in range(4):
            at = (4 * (c // 2) + phase) * 16
            off = LANES * (c % 2)
            xq[at:at + 16, off:off + LANES] = spread[
                16 * c:16 * (c + 1), LANES * phase:LANES * (phase + 1)
            ]

    turns = 4 * pieces
    block = 2 * LANES
    values = xq[...]
    for i in range(slots // block):
        at = pl.ds(i * block, block)
        wave = wave_s[:, at]
        wave = jnp.concatenate([wave] * ((turns + 16) // 8), axis=0)
        co, si = phases_of(turns, wave, length, block)
        one = wave[0:1]
        weight = jnp.where(one == 0.0, 1.0, 2.0)
        weight = jnp.where((one >= 0.0) & (one <= jnp.full(one.shape, top, jnp.int32).astype(F32)), weight, 0.0)
        fc[:, at] = co[0:turns] * weight
        fs[:, at] = si[0:turns] * weight
        c_all = co[turns:turns + 8]
        s_all = si[turns:turns + 8]
        size, step = 8, turns + 8
        while size < DEEP:
            c1 = co[step:step + 1]
            s1 = si[step:step + 1]
            c_new = c_all * c1 - s_all * s1
            s_new = s_all * c1 + c_all * s1
            c_all = jnp.concatenate([c_all, c_new], axis=0)
            s_all = jnp.concatenate([s_all, s_new], axis=0)
            size, step = 2 * size, step + 1
        c_all = c_all.astype(BF16)
        s_all = s_all.astype(BF16)
        tc[:, at] = c_all
        ts[:, at] = s_all
        inner_c = dot(values, c_all)
        inner_s = dot(values, s_all)
        real = jnp.zeros((16, block), F32)
        imag = jnp.zeros((16, block), F32)
        for g in range(turns):
            c1 = fc[g:g + 1, at]
            s1 = fs[g:g + 1, at]
            part_c = inner_c[16 * g:16 * (g + 1)]
            part_s = inner_s[16 * g:16 * (g + 1)]
            real = real + (c1 * part_c - s1 * part_s)
            imag = imag - (c1 * part_s + s1 * part_c)
        both = jnp.concatenate([real, imag], axis=0) * jnp.where(one == 0.0, 1.0, 0.5)
        xt[:, at] = jnp.concatenate(split(both), axis=0)
    turned = jnp.concatenate(
        [xt[:, owners * 8 * t:owners * 8 * (t + 1)] for t in range(groups)], axis=0
    )
    total = dot(packing, turned)
    scale = 1.0 / jnp.sqrt(jnp.full(total.shape, length, jnp.int32).astype(F32))
    msg_ref[...] = jnp.transpose(total * scale).reshape(owners, 8, LANES)


def inverse_prepare_kernel(
    groups, fields, rows, tc, ts, after_hbm, right_ref, place_ref,
):
    del after_hbm
    unit = rows * fields * 2
    shape = place_ref.shape
    target = row_iota(shape) % 32
    vec = target % 16
    base = (vec % rows) * (fields * 2) + (vec // rows) * 2 + target // 16
    source = (base + unit * (row_iota(shape) // 32) + lax.axis_index("fld") * (fields * 2)) % LANES
    place_ref[...] = jnp.where(
        (vec < rows * fields) & (lane_iota(shape) % LANES == source), 1.0, 0.0
    ).astype(BF16)
    block = 2 * LANES
    for i in range(tc.shape[1] // block):
        at = pl.ds(i * block, block)
        for part, table in enumerate((tc, ts)):
            put = (2 * i + part) * block
            right_ref[put:put + block, :] = jnp.transpose(table[:, at].astype(F32)).astype(BF16)


def inverse_kernel(
    groups, len_hbm, band_hbm, right_ref, place_ref, fc, fs, msg_ref, grid_ref,
    len_ref, band_ref, sems, os,
):
    copies = start_all((len_hbm, band_hbm), (len_ref, band_ref), sems)
    spread_s = spread_matrix()
    fields, _, rows, width = grid_ref.shape
    owners = msg_ref.shape[0]
    slots, turns = fc.shape[1], fc.shape[0]
    high, low = split(msg_ref[...].reshape(owners * 8, LANES))
    turned = dot_nt(place_ref[...], jnp.concatenate([high, low], axis=1))
    block = 2 * LANES
    out = jnp.zeros((16 * turns, DEEP), F32)
    for i in range(slots // block):
        t, off = divmod(i * block, owners * 8)
        real = turned[32 * t:32 * t + 16, off:off + block]
        imag = turned[32 * t + 16:32 * t + 32, off:off + block]
        less_real = -real
        less_imag = -imag
        at = pl.ds(i * block, block)
        reals, imags = [], []
        for g in range(turns):
            c1 = fc[g:g + 1, at]
            s1 = fs[g:g + 1, at]
            reals.append(c1 * real + s1 * less_imag)
            imags.append(s1 * less_real + c1 * less_imag)
        left = jnp.concatenate(
            [
                jnp.concatenate(reals, axis=0).astype(BF16),
                jnp.concatenate(imags, axis=0).astype(BF16),
            ],
            axis=1,
        )
        out = out + dot(left, right_ref[2 * block * i:2 * block * (i + 1), :])
    wait_all(copies)
    length = len_ref[band_ref[lax.axis_index("lat")]]
    out = out * (1.0 / jnp.sqrt(jnp.full((16 * turns, DEEP), length, jnp.int32).astype(F32)))
    chunks = os.shape[0] // 16
    for c in range(chunks):
        for phase in range(4):
            at = (4 * (c // 2) + phase) * 16
            off = LANES * (c % 2)
            os[16 * c:16 * (c + 1), LANES * phase:LANES * (phase + 1)] = out[
                at:at + 16, off:off + LANES
            ].astype(BF16)
    merged = dot_nt(os[...], spread_s)
    for c in range(chunks):
        begin = 4 * LANES * c
        size = min(4 * LANES, width - begin)
        if size <= 0:
            continue
        inside = begin + lane_iota((16, size)) < length
        piece = jnp.where(inside, merged[16 * c:16 * (c + 1), 0:size], 0.0)
        for field in range(fields):
            grid_ref[field, 0, :, begin:begin + size] = piece[
                rows * field:rows * (field + 1)
            ].astype(BF16)


def prepare_kernel(
    cut_off, pairs, fields, rows, fold_hbm, band_hbm, rates_hbm, leg_hbm, tm_hbm, bm_hbm,
    eh_hbm, mix_ref, back_ref, turn_ref, tau_ref, rate_ref,
    fold_ref, band_ref, rates_ref, leg_ref, tm_ref, bm_ref, sems, pad_s, eh_ref, out_sems,
):
    copies = start_all(
        (fold_hbm, band_hbm, rates_hbm, tm_hbm, bm_hbm, leg_hbm),
        (fold_ref, band_ref, rates_ref, tm_ref, bm_ref, leg_ref),
        sems,
    )
    wait_all(copies[:-1])
    everyone = tm_ref.shape[0]
    _, lats, places = leg_ref.shape
    groups_f = everyone // fields
    wf = fields * 2
    unit = rows * wf
    span = eh_ref.shape[1]
    eight = 8 * lats
    groups = eh_ref.shape[0] // (2 * eight)
    owner = lax.axis_index("lat") * groups_f + lax.axis_index("fld")

    pad_s[...] = jnp.zeros(pad_s.shape, F32)
    pad_s[0:everyone, 0:everyone] = tm_ref[...]
    shape = (LANES, LANES)
    level = (lane_iota(shape) // unit) * fields + (lane_iota(shape) % wf) // 2
    pick = jnp.where(row_iota(shape) == level, 1.0, 0.0).astype(BF16)
    lane = lane_iota((KPAD, LANES))
    parts = []
    for piece in split(pad_s[...]):
        wide = dot(piece, pick)
        total = []
        for r in range(rows):
            for c in range(2):
                keep = ((lane % unit) // wf == r) & (lane % 2 == c) & (lane < unit * groups_f)
                total.append(jnp.where(keep, wide, 0.0))
        parts.append(jnp.concatenate(total, axis=0).astype(BF16))
    mix_ref[...] = jnp.concatenate([parts[0], parts[1], parts[0]], axis=1)

    pad_s[...] = jnp.zeros(pad_s.shape, F32)
    pad_s[0:everyone, 0:everyone] = bm_ref[...]
    shape = (FPAD, KPAD)
    expand = jnp.where(row_iota(shape) // 2 == lane_iota(shape), 1.0, 0.0).astype(BF16)
    shape = (LANES, 2 * LANES)
    repeat = jnp.where(row_iota(shape) == lane_iota(shape) % KPAD, 1.0, 0.0).astype(BF16)
    shape = (FPAD, 2 * LANES)
    same = row_iota(shape) % 2 == (lane_iota(shape) // KPAD) % 2
    fulls = []
    for part, piece in enumerate(split(pad_s[...])):
        full = jnp.where(same, dot(dot(expand, piece).astype(BF16), repeat), 0.0)
        back_ref[part * FPAD:(part + 1) * FPAD, :] = full[:, 0:8 * KPAD].astype(BF16)
        fulls.append(full)
    turn = jnp.where(lane_iota(shape) < 4 * KPAD, fulls[0], fulls[1])
    turn_ref[...] = turn[:, 0:6 * KPAD].astype(BF16)

    row = row_iota((KPAD, 2 * LANES))
    rate = jnp.zeros((KPAD, 2 * LANES), F32)
    for k in range(everyone):
        rate = jnp.where(row == k, rates_ref[k], rate)
    rate_ref[...] = rate
    paired = tau_ref.shape[0]
    row = row_iota((paired, LANES))
    waves = []
    wave = jnp.zeros((paired, LANES), jnp.int32)
    for pair in range(4 * groups):
        waves.append(fold_ref[owner, 2 * min(pair, pairs - 1)])
        wave = jnp.where(row == pair, waves[pair], wave)
    wave = jnp.concatenate([wave] * (span // LANES), axis=1)
    line = lane_iota((paired, span))
    degree = jnp.where(line > cut_off - wave, line - 1, line + wave)
    tau_ref[...] = (degree * (degree + 1)).astype(F32) * (1.0 / float(cut_off * (cut_off + 1)))

    quad_rows = 4 * lats
    shape = (quad_rows, quad_rows)
    band = jnp.zeros(shape, jnp.int32)
    for holder in range(lats):
        band = jnp.where(row_iota(shape) % lats == holder, band_ref[holder], band)
    order = jnp.where(
        (row_iota(shape) // lats == lane_iota(shape) // lats) & (lane_iota(shape) % lats == band),
        1.0,
        0.0,
    ).astype(BF16)

    whole = places // LANES * LANES
    line = lane_iota((quad_rows, span))
    row = row_iota((quad_rows, LANES)) // lats
    copies[-1].wait()
    keeps = []
    for t in range(groups):
        wave = jnp.zeros((quad_rows, LANES), jnp.int32)
        last = jnp.zeros((quad_rows, LANES), jnp.int32)
        stack = []
        for pp in range(4):
            there = 4 * t + pp < pairs
            index = min(4 * t + pp, pairs - 1)
            wave = jnp.where(row == pp, waves[4 * t + pp], wave)
            last = jnp.where(row == pp, places - 1 if there else -1, last)
            stack.append(
                jnp.concatenate(
                    [
                        leg_ref[index, :, 0:whole],
                        jnp.broadcast_to(leg_ref[index, :, whole:places], (lats, span - whole)),
                    ],
                    axis=1,
                )
            )
        wave = jnp.concatenate([wave] * (span // LANES), axis=1)
        last = jnp.concatenate([last] * (span // LANES), axis=1)
        leg = dot(order, jnp.concatenate(stack, axis=0).astype(BF16))
        before = line <= cut_off - wave
        first = before & (line <= last)
        second = jnp.logical_not(before) & (line <= last)
        odd = ((line + jnp.where(before, 0, wave)) & 1) == 1
        signed = jnp.where(odd, -leg, leg)
        for r, rowset in enumerate((leg, signed)):
            near = jnp.where(first, rowset, 0.0)
            far = jnp.where(second, rowset, 0.0)
            for pp in range(4):
                at = 2 * eight * t + r * eight + 2 * pp * lats
                eh_ref[at:at + 2 * lats, :] = jnp.concatenate(
                    [near[pp * lats:(pp + 1) * lats], far[pp * lats:(pp + 1) * lats]], axis=0
                ).astype(BF16)
        part = pl.ds(2 * eight * t, 2 * eight)
        keeps.append(pltpu.make_async_copy(eh_ref.at[part], eh_hbm.at[part], out_sems.at[t]))
        keeps[-1].start()
    wait_all(keeps)


def solve_kernel(
    fields, rows, lats, eh_hbm, msg_ref, mix_ref, turn_ref, tau_ref, rate_ref,
    damped_hbm, out_ref, cs, eh_ref, damped_ref, in_sems, out_sems,
):
    eight = 8 * lats
    groups = eh_ref.shape[0] // (2 * eight)
    parts = [pl.ds(0, 2 * eight), pl.ds(2 * eight, 2 * eight * (groups - 1))]
    later = start_all(
        [eh_hbm.at[part] for part in parts], [eh_ref.at[part] for part in parts], in_sems
    )
    groups_f = msg_ref.shape[0] // eight
    wf = fields * 2
    unit = rows * wf
    span = eh_ref.shape[1]
    deep = 8 * KPAD
    lane = lane_iota((lats, LANES))
    tiles = [
        [msg_ref[pl.ds(8 * g + i8, lats, stride=8 * groups_f), :] for g in range(groups_f)]
        for i8 in range(8)
    ]
    tall = []
    for t in range(groups):
        here = [lanes_within(lane, unit * (t + g), unit) for g in range(groups_f)]
        for i8 in range(8):
            line = tiles[i8][0]
            for g in range(1, groups_f):
                line = jnp.where(here[g], tiles[i8][g], line)
            if t:
                line = pltpu.roll(line, LANES - unit * t, 1)
            tall.append(line)
    v_high, v_low = split(jnp.concatenate(tall, axis=0))
    mixed = dot_nt(mix_ref[...], jnp.concatenate([v_high, v_high, v_low], axis=1))

    rate = rate_ref[...]
    slot_pair = (lane_iota((2 * KPAD, 2 * eight)) % eight) // (2 * lats)
    lefts = []
    for t in range(groups):
        mine = mixed[:, eight * t:eight * (t + 1)]
        mine = jnp.concatenate([mine[0:2 * KPAD], mine[2 * KPAD:4 * KPAD]], axis=1)
        left = jnp.concatenate([jnp.where(slot_pair == pp, mine, 0.0) for pp in range(4)], axis=0)
        lefts.append(jnp.concatenate(split(left), axis=1))

    keeps = []
    for t in range(groups):
        left = lefts[t]
        legs = pl.ds(2 * eight * t, 2 * eight)
        if t < 2:
            later[t].wait()
        for start in range(0, span, 2 * LANES):
            size = min(2 * LANES, span - start)
            right = eh_ref[legs, start:start + size]
            modes = dot(left, jnp.concatenate([right, right], axis=0))
            damped = []
            for pp in range(4):
                tau = tau_ref[4 * t + pp:4 * t + pp + 1, start:start + size]
                below = 1.0 + tau * rate[:, 0:size]
                factor = pl.reciprocal(below, approx=True)
                factor = factor * (2.0 - below * factor)
                at = 2 * pp * KPAD
                damped.append(modes[at:at + KPAD] * factor)
                damped.append(modes[at + KPAD:at + 2 * KPAD] * factor)
            damped_ref[deep * t:deep * (t + 1), start:start + size] = jnp.concatenate(
                damped, axis=0
            ).astype(BF16)
        part = pl.ds(deep * t, deep)
        keeps.append(
            pltpu.make_async_copy(damped_ref.at[part], damped_hbm.at[part], out_sems.at[t])
        )
        keeps[-1].start()

    picks = []
    for t in range(groups):
        product = dot_nt(damped_ref[deep * t:deep * (t + 1), :], eh_ref[pl.ds(2 * eight * t, 2 * eight), :])
        pick = product[0:2 * KPAD]
        for pp in range(1, 4):
            pick = jnp.where(slot_pair == pp, product[2 * KPAD * pp:2 * KPAD * (pp + 1)], pick)
        picks.append(pick)
    high, low = split(jnp.concatenate(picks, axis=1))
    back = dot(turn_ref[...], jnp.concatenate([high, low, high], axis=0))
    back = jnp.concatenate([back, jnp.zeros((LANES - FPAD, back.shape[1]), F32)], axis=0)
    for at in range(0, back.shape[1], LANES):
        cs[at:at + LANES, :] = jnp.transpose(back[:, at:at + LANES])

    lane = lane_iota((8, LANES))
    here = [
        lanes_within(lane, wf * u, wf) for u in range(rows * groups + groups_f - 1)
    ]
    for holder in range(lats):
        tiles = [jnp.zeros((8, LANES), F32) for _ in range(groups_f)]
        for u in range(rows * groups):
            piece = cs[pl.ds(u * eight + holder, 8, stride=lats), :]
            if u:
                piece = pltpu.roll(piece, wf * u, 1)
            for g in range(groups_f):
                tiles[g] = jnp.where(here[u + g], piece, tiles[g])
        for g in range(groups_f):
            at = (holder * groups_f + g) * 8
            out_ref[at:at + 8, :] = tiles[g]
    wait_all(keeps)


def output_kernel(damped_hbm, back_ref, spec_ref, bk, damped_s, sems):
    everyone, quad, _, places = spec_ref.shape
    span = damped_s.shape[1]
    deep = 8 * KPAD
    tall = 2 * everyone
    step = pl.program_id(0)

    def fetch(t):
        part = pl.ds(pl.multiple_of(deep * t, deep), deep)
        return pltpu.make_async_copy(damped_hbm.at[part], damped_s.at[part], sems.at[t])

    @pl.when(step == 0)
    def _():
        for t in range(sems.shape[0]):
            fetch(t).start()
        pair_of = lane_iota((tall, deep)) // (2 * KPAD)
        rows = []
        for part in range(2):
            full = back_ref[part * FPAD:part * FPAD + tall, :].astype(F32)
            for pp in range(4):
                rows.append(jnp.where(pair_of == pp, full, 0.0))
        bk[...] = jnp.concatenate(rows, axis=0).astype(BF16)

    fetch(step).wait()
    at = pl.multiple_of(deep * step, deep)
    for start in range(0, span, 2 * LANES):
        size = min(2 * LANES, span - start)
        spec = dot(bk[...], damped_s[pl.ds(at, deep), start:start + size])
        spec = spec[0:4 * tall] + spec[4 * tall:]
        kept = min(size, places - start)
        for pp in range(4):
            for f in range(everyone):
                row = pp * tall + 2 * f
                spec_ref[f, pp, :, start:start + kept] = spec[row:row + 2, 0:kept]


def per_device(grid, row_lengths, band_map, fold_map, legendre, to_modes, back_modes, mode_rates):
    fields, single, rows, width = grid.shape
    pairs, places, lats = legendre.shape
    cut_off = places - 2
    everyone = to_modes.shape[0]
    owners, per_owner = fold_map.shape
    groups = -(-per_owner // 8)
    slots = owners * groups * 8
    pieces = -(-(width // 4) // DEEP)
    turns = 4 * pieces
    span = -(-places // LANES) * LANES
    hbm = pl.BlockSpec(memory_space=pltpu.HBM)
    vmem = pl.BlockSpec(memory_space=pltpu.VMEM)
    room = pltpu.CompilerParams(vmem_limit_bytes=ROOM)
    message = pltpu.HBM((owners, 8, LANES), F32)
    holders = band_map.shape[0]
    groups_f = everyone // fields
    dma = pltpu.SemaphoreType.DMA
    row_lengths, band_map, fold_map, to_modes, back_modes, mode_rates, grid = (
        pltpu.with_memory_space_constraint(x, pltpu.HBM)
        for x in (row_lengths, band_map, fold_map, to_modes, back_modes, mode_rates, grid)
    )
    legendre = pltpu.with_memory_space_constraint(jnp.transpose(legendre, (0, 2, 1)), pltpu.HBM)

    sending, cos_table, sin_table, cos_turn, sin_turn = pl.pallas_call(
        functools.partial(forward_kernel, cut_off, groups),
        out_shape=(
            message,
            pltpu.VMEM((DEEP, slots), BF16),
            pltpu.VMEM((DEEP, slots), BF16),
            pltpu.VMEM((turns, slots), F32),
            pltpu.VMEM((turns, slots), F32),
        ),
        in_specs=[hbm] * 4,
        out_specs=(vmem,) * 5,
        scratch_shapes=[
            pltpu.SMEM(row_lengths.shape, jnp.int32),
            pltpu.SMEM(band_map.shape, jnp.int32),
            pltpu.VMEM(fold_map.shape, jnp.int32),
            pltpu.VMEM(grid.shape, BF16),
            dma((4,)),
            pltpu.VMEM((LANES, LANES), F32),
            pltpu.VMEM((8, slots), F32),
            pltpu.VMEM((16, 4 * DEEP * pieces), F32),
            pltpu.VMEM((16 * turns, DEEP), BF16),
            pltpu.VMEM((64, slots), BF16),
        ],
        compiler_params=room,
        name="forward_rows",
    )(row_lengths, band_map, fold_map, grid)
    tables = [
        pltpu.with_memory_space_constraint(x, pltpu.VMEM)
        for x in (cos_table, sin_table, cos_turn, sin_turn)
    ]
    arrived = lax.all_to_all(sending, ("lat", "fld"), split_axis=0, concat_axis=0, tiled=True)

    legs, mix, back, turn_back, tau, rate = pl.pallas_call(
        functools.partial(prepare_kernel, cut_off, pairs, fields, rows),
        out_shape=(
            pltpu.HBM((groups * 16 * lats, span), BF16),
            pltpu.VMEM((2 * rows * KPAD, 3 * LANES), BF16),
            pltpu.VMEM((2 * FPAD, 8 * KPAD), BF16),
            pltpu.VMEM((FPAD, 6 * KPAD), BF16),
            pltpu.VMEM((-(-groups * 4 // 8) * 8, span), F32),
            pltpu.VMEM((KPAD, 2 * LANES), F32),
        ),
        in_specs=[hbm] * 6,
        out_specs=(hbm,) + (vmem,) * 5,
        scratch_shapes=[
            pltpu.SMEM(fold_map.shape, jnp.int32),
            pltpu.SMEM(band_map.shape, jnp.int32),
            pltpu.SMEM(mode_rates.shape, F32),
            pltpu.VMEM((pairs, lats, places), F32),
            pltpu.VMEM(to_modes.shape, F32),
            pltpu.VMEM(back_modes.shape, F32),
            dma((6,)),
            pltpu.VMEM((KPAD, LANES), F32),
            pltpu.VMEM((groups * 16 * lats, span), BF16),
            dma((groups,)),
        ],
        compiler_params=room,
        cost_estimate=pl.CostEstimate(flops=10**8, bytes_accessed=8 * 10**6, transcendentals=0),
        name="prepare",
    )(fold_map, band_map, mode_rates, legendre, to_modes, back_modes)
    legs = pltpu.with_memory_space_constraint(legs, pltpu.HBM)
    mix, back, turn_back, tau, rate = (
        pltpu.with_memory_space_constraint(x, pltpu.VMEM)
        for x in (mix, back, turn_back, tau, rate)
    )

    damped, leaving = pl.pallas_call(
        functools.partial(solve_kernel, fields, rows, lats),
        out_shape=(
            pltpu.HBM((groups * 8 * KPAD, span), BF16),
            pltpu.HBM((owners * 8, LANES), F32),
        ),
        in_specs=[hbm] + [vmem] * 5,
        out_specs=(hbm, vmem),
        scratch_shapes=[
            pltpu.VMEM((groups * 16 * lats, LANES), F32),
            pltpu.VMEM((groups * 16 * lats, span), BF16),
            pltpu.VMEM((groups * 8 * KPAD, span), BF16),
            dma((2,)),
            dma((groups,)),
        ],
        compiler_params=room,
        name="solve",
    )(legs, arrived.reshape(owners * 8, LANES), mix, turn_back, tau, rate)
    leaving = leaving.reshape(owners, 8, LANES)

    returned = lax.all_to_all(leaving, ("lat", "fld"), split_axis=0, concat_axis=0, tiled=True)

    damped = pltpu.with_memory_space_constraint(damped, pltpu.HBM)
    spectral = pl.pallas_call(
        output_kernel,
        grid=(groups,),
        out_shape=jax.ShapeDtypeStruct((everyone, pairs, 2, places), F32),
        in_specs=[
            hbm,
            pl.BlockSpec((2 * FPAD, 8 * KPAD), lambda t: (0, 0)),
        ],
        out_specs=pl.BlockSpec((everyone, 4, 2, places), lambda t: (0, t, 0, 0)),
        scratch_shapes=[
            pltpu.VMEM((16 * everyone, 8 * KPAD), BF16),
            pltpu.VMEM((groups * 8 * KPAD, span), BF16),
            dma((groups,)),
        ],
        compiler_params=pltpu.CompilerParams(
            dimension_semantics=("arbitrary",), vmem_limit_bytes=ROOM
        ),
        cost_estimate=pl.CostEstimate(flops=10**8, bytes_accessed=8 * 10**6, transcendentals=0),
        name="spectral_output",
    )(damped, back)

    right, place = pl.pallas_call(
        functools.partial(inverse_prepare_kernel, groups, fields, rows),
        out_shape=(
            pltpu.VMEM((2 * slots, DEEP), BF16),
            pltpu.VMEM((32 * groups, 2 * LANES), BF16),
        ),
        in_specs=[vmem, vmem, hbm],
        out_specs=(vmem,) * 2,
        compiler_params=room,
        cost_estimate=pl.CostEstimate(flops=10**8, bytes_accessed=8 * 10**6, transcendentals=0),
        name="inverse_prepare",
    )(tables[0], tables[1], damped)
    right, place = (pltpu.with_memory_space_constraint(x, pltpu.VMEM) for x in (right, place))

    grid_out = pl.pallas_call(
        functools.partial(inverse_kernel, groups),
        out_shape=jax.ShapeDtypeStruct(grid.shape, BF16),
        in_specs=[hbm] * 2 + [vmem] * 5,
        out_specs=vmem,
        scratch_shapes=[
            pltpu.SMEM(row_lengths.shape, jnp.int32),
            pltpu.SMEM(band_map.shape, jnp.int32),
            dma((2,)),
            pltpu.VMEM((32 * pieces, 4 * LANES), BF16),
        ],
        compiler_params=room,
        name="inverse_rows",
    )(row_lengths, band_map, right, place, *tables[2:], returned)
    return (jnp.transpose(spectral, (0, 2, 1, 3)), grid_out)


def solution(mesh):
    placed = (
        P("fld", "lat", None, None),
        P(),
        P(),
        P(),
        P(("lat", "fld"), None, None),
        P(),
        P(),
        P(),
    )
    return jax.shard_map(
        per_device,
        mesh=mesh,
        in_specs=placed,
        out_specs=(P(None, None, ("lat", "fld"), None), P("fld", "lat", None, None)),
        check_vma=False,
    )
```

```python
import functools
import math

import jax
import jax.numpy as jnp
from jax import lax
from jax.experimental import pallas as pl
from jax.experimental.pallas import tpu as pltpu
from jax.sharding import PartitionSpec as P

LANES = 128
KPAD = 24
FPAD = 64
DEEP = 256
TWICE = 24
ROOM = 24 * 1024 * 1024
F32 = jnp.float32
BF16 = jnp.bfloat16
NT_DIMS = (((1,), (1,)), ((), ()))
SIN_POLY = (
    6.283185302447051,
    -41.34170038368319,
    81.60513023312113,
    -76.70299324464969,
    42.02573766814694,
    -14.899106966102595,
    3.237062655726421,
)
COS_POLY = (
    0.9999999889083757,
    -19.739204448887243,
    64.93911476570418,
    -85.45008785413638,
    60.167188450194914,
    -25.9658703083255,
    6.526145851512229,
)


def dot(a, b):
    return jnp.dot(a, b, preferred_element_type=F32)


def dot_nt(a, b):
    return lax.dot_general(a, b, NT_DIMS, preferred_element_type=F32)


def split(x):
    high = x.astype(BF16)
    return high, (x - high.astype(F32)).astype(BF16)


def horner(coefs, z):
    total = coefs[-1] * z + coefs[-2]
    for coef in coefs[-3::-1]:
        total = total * z + coef
    return total


def turn(steps, period, inverse):
    rest = steps - period * jnp.floor(steps * inverse + 0.5)
    part = rest * inverse
    z = part * part
    return horner(COS_POLY, z), part * horner(SIN_POLY, z)


def start_all(sources, targets, sems):
    copies = [
        pltpu.make_async_copy(source, target, sems.at[i])
        for i, (source, target) in enumerate(zip(sources, targets))
    ]
    for copy in copies:
        copy.start()
    return copies


def wait_all(copies):
    for copy in copies:
        copy.wait()


def lane_iota(shape):
    return lax.broadcasted_iota(jnp.int32, shape, len(shape) - 1)


def row_iota(shape):
    return lax.broadcasted_iota(jnp.int32, shape, len(shape) - 2)


def lanes_within(lane, start, size):
    start %= LANES
    if start + size <= LANES:
        return (lane >= start) & (lane < start + size)
    return (lane >= start) | (lane < start + size - LANES)


def spread_matrix():
    shape = (4 * LANES, LANES)
    picks = []
    for phase in range(4):
        picks.append(jnp.where(row_iota(shape) == 4 * lane_iota(shape) + phase, 1.0, 0.0))
    return jnp.concatenate(picks, axis=1).astype(BF16)


def phases_of(groups, wave, length, lanes):
    shape = (groups + 16, lanes)
    row = row_iota(shape)
    steps = jnp.where(row < groups, (row // 4) * (4 * DEEP) + row % 4, 4 * (row - groups))
    steps = jnp.where(row >= groups + 8, 32 << jnp.maximum(row - groups - 8, 0), steps)
    period = jnp.full(shape, length, jnp.int32).astype(F32)
    return turn(steps.astype(F32) * wave, period, 1.0 / period)


def two_phases(ref, g, at, used, block):
    first = ref[2 * g:2 * g + 1, at]
    second = ref[2 * g + 1:2 * g + 2, at]
    tiles = []
    for low in range(0, TWICE, 8):
        if low + 8 <= used:
            tiles.append(jnp.broadcast_to(first, (8, block)))
        elif low >= used:
            tiles.append(jnp.broadcast_to(second, (8, block)))
        else:
            tiles.append(jnp.where(low + row_iota((8, block)) < used, first, second))
    return jnp.concatenate(tiles, axis=0)


def forward_kernel(
    cut_off, groups, len_hbm, band_hbm, fold_hbm, grid_hbm,
    msg_ref, tc, ts, fc, fs,
    len_ref, band_ref, fold_ref, grid_ref, sems, fold_s, wave_s, xs, xt,
):
    copies = start_all(
        (len_hbm, band_hbm, fold_hbm, grid_hbm), (len_ref, band_ref, fold_ref, grid_ref), sems
    )
    fields, _, rows, width = grid_ref.shape
    owners, per_owner = fold_ref.shape
    slots = tc.shape[1]
    pieces = xs.shape[1] // (4 * DEEP)
    unit = rows * fields * 2
    used = rows * fields
    spread_s = spread_matrix()
    shape = (LANES, owners * 8)
    repeat = jnp.where(row_iota(shape) == lane_iota(shape) // 8, 1.0, 0.0).astype(BF16)
    shape = (8 * groups, 16 * groups)
    weigh = jnp.where(
        lane_iota(shape) % (8 * groups) // 8 == row_iota(shape) // 8,
        jnp.where(lane_iota(shape) < 8 * groups, 8.0, 1.0),
        0.0,
    ).astype(BF16)
    tall = 4 * TWICE
    shape = (LANES, tall * groups)
    source = lane_iota(shape)
    row = source % TWICE
    vec = row % used
    base = (vec % rows) * (fields * 2) + (vec // rows) * 2 + (source // TWICE) % 2
    target = (base + unit * (source // tall + lax.axis_index("fld"))) % LANES
    packing = jnp.where((row < 2 * used) & (row_iota(shape) == target), 1.0, 0.0).astype(BF16)
    fold_s[...] = jnp.full(fold_s.shape, -1.0, F32)
    xs[...] = jnp.zeros(xs.shape, F32)
    wait_all(copies)
    length = len_ref[band_ref[lax.axis_index("lat")]]
    top = jnp.minimum(cut_off, (length - 1) // 2)

    fold_s[0:owners, 0:per_owner] = fold_ref[...].astype(F32)
    turned = jnp.transpose(fold_s[...])[0:8 * groups]
    eights = jnp.floor(turned * 0.125)
    parts = jnp.concatenate([eights, turned - 8.0 * eights], axis=0).astype(BF16)
    repeated = dot(parts, repeat)
    own = lane_iota(repeated.shape) % 8 == row_iota(repeated.shape) % 8
    waves = dot(weigh, jnp.where(own, repeated, 0.0).astype(BF16))
    for t in range(groups):
        wave_s[:, owners * 8 * t:owners * 8 * (t + 1)] = waves[8 * t:8 * t + 8]

    for field in range(fields):
        points = grid_ref[field, 0].astype(F32)
        for copy in (0, used):
            at = copy + rows * field
            xs[at:at + rows, 0:width] = points
    stacked = jnp.concatenate(
        [xs[:, 4 * LANES * c:4 * LANES * (c + 1)] for c in range(2 * pieces)], axis=0
    ).astype(BF16)
    spread = dot(stacked, spread_s)
    shape = (TWICE, LANES)
    front = row_iota(shape) < used
    values = []
    for k in range(pieces):
        for pair in range(2):
            halves = []
            for half in range(2):
                c = 2 * k + half
                rows_c = spread[TWICE * c:TWICE * (c + 1)]
                off = 2 * LANES * pair
                both = jnp.where(
                    front, rows_c[:, off:off + LANES], rows_c[:, off + LANES:off + 2 * LANES]
                )
                inside = c * LANES + lane_iota(shape) < length // 4
                halves.append(jnp.where(inside, both, 0.0))
            values.append(jnp.concatenate(halves, axis=1))
    values = jnp.concatenate(values, axis=0).astype(BF16)

    turns = 4 * pieces
    block = 2 * LANES
    for i in range(slots // block):
        at = pl.ds(i * block, block)
        wave = wave_s[:, at]
        wave = jnp.concatenate([wave] * ((turns + 16) // 8), axis=0)
        co, si = phases_of(turns, wave, length, block)
        one = wave[0:1]
        weight = jnp.where(one == 0.0, 1.0, 2.0)
        weight = jnp.where((one >= 0.0) & (one <= jnp.full(one.shape, top, jnp.int32).astype(F32)), weight, 0.0)
        fc[:, at] = co[0:turns] * weight
        fs[:, at] = si[0:turns] * weight
        c_all = co[turns:turns + 8]
        s_all = si[turns:turns + 8]
        size, step = 8, turns + 8
        while size < DEEP:
            c1 = co[step:step + 1]
            s1 = si[step:step + 1]
            c_new = c_all * c1 - s_all * s1
            s_new = s_all * c1 + c_all * s1
            c_all = jnp.concatenate([c_all, c_new], axis=0)
            s_all = jnp.concatenate([s_all, s_new], axis=0)
            size, step = 2 * size, step + 1
        c_all = c_all.astype(BF16)
        s_all = s_all.astype(BF16)
        tc[:, at] = c_all
        ts[:, at] = s_all
        inner_c = dot(values, c_all)
        inner_s = dot(values, s_all)
        real = jnp.zeros((TWICE, block), F32)
        imag = jnp.zeros((TWICE, block), F32)
        for g in range(turns // 2):
            c1 = two_phases(fc, g, at, used, block)
            s1 = two_phases(fs, g, at, used, block)
            part_c = inner_c[TWICE * g:TWICE * (g + 1)]
            part_s = inner_s[TWICE * g:TWICE * (g + 1)]
            real = real + (c1 * part_c - s1 * part_s)
            imag = imag - (c1 * part_s + s1 * part_c)
        both = jnp.concatenate([real, imag], axis=0) * jnp.where(one == 0.0, 1.0, 0.5)
        xt[:, at] = jnp.concatenate(split(both), axis=0)

    turned = jnp.concatenate(
        [xt[:, owners * 8 * t:owners * 8 * (t + 1)] for t in range(groups)], axis=0
    )
    total = dot(packing, turned)
    scale = 1.0 / jnp.sqrt(jnp.full(total.shape, length, jnp.int32).astype(F32))
    msg_ref[...] = jnp.transpose(total * scale).reshape(owners, 8, LANES)


def inverse_kernel(
    groups, len_hbm, band_hbm, tc, ts, fc, fs, msg_ref, grid_ref,
    len_ref, band_ref, sems, os,
):
    copies = start_all((len_hbm, band_hbm), (len_ref, band_ref), sems)
    spread_s = spread_matrix()
    fields, _, rows, width = grid_ref.shape
    owners = msg_ref.shape[0]
    slots = tc.shape[1]
    turns = fc.shape[0]
    unit = rows * fields * 2
    high, low = split(msg_ref[...].reshape(owners * 8, LANES))
    pieces = jnp.concatenate([high, low], axis=1)
    used = rows * fields
    tall = 2 * TWICE
    shape = (tall * groups, 2 * LANES)
    target = row_iota(shape) % tall
    row = target % TWICE
    vec = row % used
    base = (vec % rows) * (fields * 2) + (vec // rows) * 2 + target // TWICE
    source = (base + unit * (row_iota(shape) // tall) + lax.axis_index("fld") * (fields * 2)) % LANES
    place = jnp.where(
        (row < 2 * used) & (lane_iota(shape) % LANES == source), 1.0, 0.0
    ).astype(BF16)
    turned = dot_nt(place, pieces)
    block = 2 * LANES
    out = jnp.zeros((TWICE * turns // 2, DEEP), F32)
    for i in range(slots // block):
        t, off = divmod(i * block, owners * 8)
        real = turned[tall * t:tall * t + TWICE, off:off + block]
        imag = turned[tall * t + TWICE:tall * (t + 1), off:off + block]
        at = pl.ds(i * block, block)
        reals, imags = [], []
        for g in range(turns // 2):
            c1 = two_phases(fc, g, at, used, block)
            s1 = two_phases(fs, g, at, used, block)
            reals.append(c1 * real - s1 * imag)
            imags.append(s1 * real + c1 * imag)
        reals = jnp.concatenate(reals, axis=0).astype(BF16)
        imags = jnp.concatenate(imags, axis=0).astype(BF16)
        out = out + (dot_nt(reals, tc[:, at]) - dot_nt(imags, ts[:, at]))
    wait_all(copies)
    length = len_ref[band_ref[lax.axis_index("lat")]]
    out = out * (1.0 / jnp.sqrt(jnp.full(out.shape, length, jnp.int32).astype(F32)))
    chunks = os.shape[0] // 16
    for c in range(chunks):
        off = LANES * (c % 2)
        for phase in range(4):
            at = (2 * (c // 2) + phase // 2) * TWICE
            piece = out[at:at + TWICE, off:off + LANES]
            if phase % 2:
                piece = pltpu.roll(piece, TWICE - used, 0)
            os[16 * c:16 * (c + 1), LANES * phase:LANES * (phase + 1)] = piece[0:16].astype(BF16)
    merged = dot_nt(os[...], spread_s)
    for c in range(chunks):
        begin = 4 * LANES * c
        size = min(4 * LANES, width - begin)
        if size <= 0:
            continue
        inside = begin + lane_iota((16, size)) < length
        piece = jnp.where(inside, merged[16 * c:16 * (c + 1), 0:size], 0.0)
        for field in range(fields):
            grid_ref[field, 0, :, begin:begin + size] = piece[
                rows * field:rows * (field + 1)
            ].astype(BF16)


def prepare_kernel(
    cut_off, pairs, fields, rows, fold_hbm, band_hbm, rates_hbm, leg_hbm, tm_hbm, bm_hbm,
    eh_hbm, mix_ref, back_ref, turn_ref, tau_ref, rate_ref,
    fold_ref, band_ref, rates_ref, leg_ref, tm_ref, bm_ref, sems, pad_s, eh_ref, out_sems,
):
    copies = start_all(
        (fold_hbm, band_hbm, rates_hbm, tm_hbm, bm_hbm, leg_hbm),
        (fold_ref, band_ref, rates_ref, tm_ref, bm_ref, leg_ref),
        sems,
    )
    wait_all(copies[:-1])
    everyone = tm_ref.shape[0]
    _, lats, places = leg_ref.shape
    groups_f = everyone // fields
    wf = fields * 2
    unit = rows * wf
    span = eh_ref.shape[1]
    eight = 8 * lats
    groups = eh_ref.shape[0] // (2 * eight)
    owner = lax.axis_index("lat") * groups_f + lax.axis_index("fld")

    pad_s[...] = jnp.zeros(pad_s.shape, F32)
    pad_s[0:everyone, 0:everyone] = tm_ref[...]
    shape = (LANES, LANES)
    level = (lane_iota(shape) // unit) * fields + (lane_iota(shape) % wf) // 2
    pick = jnp.where(row_iota(shape) == level, 1.0, 0.0).astype(BF16)
    lane = lane_iota((KPAD, LANES))
    parts = []
    for piece in split(pad_s[...]):
        wide = dot(piece, pick)
        total = []
        for r in range(rows):
            for c in range(2):
                keep = ((lane % unit) // wf == r) & (lane % 2 == c) & (lane < unit * groups_f)
                total.append(jnp.where(keep, wide, 0.0))
        parts.append(jnp.concatenate(total, axis=0).astype(BF16))
    mix_ref[...] = jnp.concatenate([parts[0], parts[1], parts[0]], axis=1)

    pad_s[...] = jnp.zeros(pad_s.shape, F32)
    pad_s[0:everyone, 0:everyone] = bm_ref[...]
    shape = (FPAD, KPAD)
    expand = jnp.where(row_iota(shape) // 2 == lane_iota(shape), 1.0, 0.0).astype(BF16)
    shape = (LANES, 2 * LANES)
    repeat = jnp.where(row_iota(shape) == lane_iota(shape) % KPAD, 1.0, 0.0).astype(BF16)
    shape = (FPAD, 2 * LANES)
    same = row_iota(shape) % 2 == (lane_iota(shape) // KPAD) % 2
    fulls = []
    for part, piece in enumerate(split(pad_s[...])):
        full = jnp.where(same, dot(dot(expand, piece).astype(BF16), repeat), 0.0)
        back_ref[part * FPAD:(part + 1) * FPAD, :] = full[:, 0:8 * KPAD].astype(BF16)
        fulls.append(full)
    turn = jnp.where(lane_iota(shape) < 4 * KPAD, fulls[0], fulls[1])
    turn_ref[...] = turn[:, 0:6 * KPAD].astype(BF16)

    row = row_iota((KPAD, 2 * LANES))
    rate = jnp.zeros((KPAD, 2 * LANES), F32)
    for k in range(everyone):
        rate = jnp.where(row == k, rates_ref[k], rate)
    rate_ref[...] = rate
    paired = tau_ref.shape[0]
    row = row_iota((paired, LANES))
    waves = []
    wave = jnp.zeros((paired, LANES), jnp.int32)
    for pair in range(4 * groups):
        waves.append(fold_ref[owner, 2 * min(pair, pairs - 1)])
        wave = jnp.where(row == pair, waves[pair], wave)
    wave = jnp.concatenate([wave] * (span // LANES), axis=1)
    line = lane_iota((paired, span))
    degree = jnp.where(line > cut_off - wave, line - 1, line + wave)
    tau_ref[...] = (degree * (degree + 1)).astype(F32) * (1.0 / float(cut_off * (cut_off + 1)))

    quad_rows = 4 * lats
    shape = (quad_rows, quad_rows)
    band = jnp.zeros(shape, jnp.int32)
    for holder in range(lats):
        band = jnp.where(row_iota(shape) % lats == holder, band_ref[holder], band)
    order = jnp.where(
        (row_iota(shape) // lats == lane_iota(shape) // lats) & (lane_iota(shape) % lats == band),
        1.0,
        0.0,
    ).astype(BF16)

    whole = places // LANES * LANES
    line = lane_iota((quad_rows, span))
    row = row_iota((quad_rows, LANES)) // lats
    copies[-1].wait()
    keeps = []
    for t in range(groups):
        wave = jnp.zeros((quad_rows, LANES), jnp.int32)
        last = jnp.zeros((quad_rows, LANES), jnp.int32)
        stack = []
        for pp in range(4):
            there = 4 * t + pp < pairs
            index = min(4 * t + pp, pairs - 1)
            wave = jnp.where(row == pp, waves[4 * t + pp], wave)
            last = jnp.where(row == pp, places - 1 if there else -1, last)
            stack.append(
                jnp.concatenate(
                    [
                        leg_ref[index, :, 0:whole],
                        jnp.broadcast_to(leg_ref[index, :, whole:places], (lats, span - whole)),
                    ],
                    axis=1,
                )
            )
        wave = jnp.concatenate([wave] * (span // LANES), axis=1)
        last = jnp.concatenate([last] * (span // LANES), axis=1)
        leg = dot(order, jnp.concatenate(stack, axis=0).astype(BF16))
        before = line <= cut_off - wave
        first = before & (line <= last)
        second = jnp.logical_not(before) & (line <= last)
        odd = ((line + jnp.where(before, 0, wave)) & 1) == 1
        signed = jnp.where(odd, -leg, leg)
        for r, rowset in enumerate((leg, signed)):
            near = jnp.where(first, rowset, 0.0)
            far = jnp.where(second, rowset, 0.0)
            for pp in range(4):
                at = 2 * eight * t + r * eight + 2 * pp * lats
                eh_ref[at:at + 2 * lats, :] = jnp.concatenate(
                    [near[pp * lats:(pp + 1) * lats], far[pp * lats:(pp + 1) * lats]], axis=0
                ).astype(BF16)
        part = pl.ds(2 * eight * t, 2 * eight)
        keeps.append(pltpu.make_async_copy(eh_ref.at[part], eh_hbm.at[part], out_sems.at[t]))
        keeps[-1].start()
    wait_all(keeps)


def solve_kernel(
    fields, rows, lats, eh_hbm, msg_ref, mix_ref, turn_ref, tau_ref, rate_ref,
    near_ref, far_hbm, out_ref, cs, eh_ref, far_ref, in_sems, out_sems,
):
    eight = 8 * lats
    groups = eh_ref.shape[0] // (2 * eight)
    parts = [pl.ds(0, 2 * eight), pl.ds(2 * eight, 2 * eight * (groups - 1))]
    later = start_all(
        [eh_hbm.at[part] for part in parts], [eh_ref.at[part] for part in parts], in_sems
    )
    groups_f = msg_ref.shape[0] // eight
    wf = fields * 2
    unit = rows * wf
    span = eh_ref.shape[1]
    deep = 8 * KPAD
    near = near_ref.shape[0] // deep
    holds = [(near_ref, deep * t) for t in range(near)]
    holds += [(far_ref, deep * t) for t in range(groups - near)]
    lane = lane_iota((lats, LANES))
    tiles = [
        [msg_ref[pl.ds(8 * g + i8, lats, stride=8 * groups_f), :] for g in range(groups_f)]
        for i8 in range(8)
    ]
    tall = []
    for t in range(groups):
        here = [lanes_within(lane, unit * (t + g), unit) for g in range(groups_f)]
        for i8 in range(8):
            line = tiles[i8][0]
            for g in range(1, groups_f):
                line = jnp.where(here[g], tiles[i8][g], line)
            if t:
                line = pltpu.roll(line, LANES - unit * t, 1)
            tall.append(line)
    v_high, v_low = split(jnp.concatenate(tall, axis=0))
    mixed = dot_nt(mix_ref[...], jnp.concatenate([v_high, v_high, v_low], axis=1))

    rate = rate_ref[...]
    slot_pair = (lane_iota((2 * KPAD, 2 * eight)) % eight) // (2 * lats)
    lefts = []
    for t in range(groups):
        mine = mixed[:, eight * t:eight * (t + 1)]
        mine = jnp.concatenate([mine[0:2 * KPAD], mine[2 * KPAD:4 * KPAD]], axis=1)
        left = jnp.concatenate([jnp.where(slot_pair == pp, mine, 0.0) for pp in range(4)], axis=0)
        lefts.append(jnp.concatenate(split(left), axis=1))

    keeps = []
    for t in range(groups):
        left = lefts[t]
        legs = pl.ds(2 * eight * t, 2 * eight)
        if t < 2:
            later[t].wait()
        for start in range(0, span, 2 * LANES):
            size = min(2 * LANES, span - start)
            right = eh_ref[legs, start:start + size]
            modes = dot(left, jnp.concatenate([right, right], axis=0))
            damped = []
            for pp in range(4):
                tau = tau_ref[4 * t + pp:4 * t + pp + 1, start:start + size]
                below = 1.0 + tau * rate[:, 0:size]
                factor = pl.reciprocal(below, approx=True)
                at = 2 * pp * KPAD
                damped.append(modes[at:at + KPAD] * factor)
                damped.append(modes[at + KPAD:at + 2 * KPAD] * factor)
            hold, at = holds[t]
            hold[at:at + deep, start:start + size] = jnp.concatenate(damped, axis=0).astype(BF16)
        if t >= near:
            part = pl.ds(deep * (t - near), deep)
            keeps.append(
                pltpu.make_async_copy(far_ref.at[part], far_hbm.at[part], out_sems.at[t - near])
            )
            keeps[-1].start()

    picks = []
    for t in range(groups):
        hold, at = holds[t]
        product = dot_nt(hold[at:at + deep, :], eh_ref[pl.ds(2 * eight * t, 2 * eight), :])
        pick = product[0:2 * KPAD]
        for pp in range(1, 4):
            pick = jnp.where(slot_pair == pp, product[2 * KPAD * pp:2 * KPAD * (pp + 1)], pick)
        picks.append(pick)
    high, low = split(jnp.concatenate(picks, axis=1))
    back = dot(turn_ref[...], jnp.concatenate([high, low, high], axis=0))
    back = jnp.concatenate([back, jnp.zeros((LANES - FPAD, back.shape[1]), F32)], axis=0)
    for at in range(0, back.shape[1], LANES):
        cs[at:at + LANES, :] = jnp.transpose(back[:, at:at + LANES])

    lane = lane_iota((8, LANES))
    here = [
        lanes_within(lane, wf * u, wf) for u in range(rows * groups + groups_f - 1)
    ]
    for holder in range(lats):
        tiles = [jnp.zeros((8, LANES), F32) for _ in range(groups_f)]
        for u in range(rows * groups):
            piece = cs[pl.ds(u * eight + holder, 8, stride=lats), :]
            if u:
                piece = pltpu.roll(piece, wf * u, 1)
            for g in range(groups_f):
                tiles[g] = jnp.where(here[u + g], piece, tiles[g])
        for g in range(groups_f):
            at = (holder * groups_f + g) * 8
            out_ref[at:at + 8, :] = tiles[g]
    wait_all(keeps)


def output_kernel(near_ref, far_hbm, back_ref, spec_ref, bk, far_s, sems):
    everyone, quad, _, places = spec_ref.shape
    span = near_ref.shape[1]
    deep = 8 * KPAD
    near = near_ref.shape[0] // deep
    tall = 2 * everyone
    step = pl.program_id(0)

    def far_copy(t):
        part = pl.ds(pl.multiple_of(deep * t, deep), deep)
        return pltpu.make_async_copy(far_hbm.at[part], far_s.at[part], sems.at[t])

    @pl.when(step == 0)
    def _():
        for t in range(sems.shape[0]):
            far_copy(t).start()
        pair_of = lane_iota((tall, deep)) // (2 * KPAD)
        rows = []
        for part in range(2):
            full = back_ref[part * FPAD:part * FPAD + tall, :].astype(F32)
            for pp in range(4):
                rows.append(jnp.where(pair_of == pp, full, 0.0))
        bk[...] = jnp.concatenate(rows, axis=0).astype(BF16)

    def write(source, at):
        for start in range(0, span, 2 * LANES):
            size = min(2 * LANES, span - start)
            spec = dot(bk[...], source[pl.ds(at, deep), start:start + size])
            spec = spec[0:4 * tall] + spec[4 * tall:]
            kept = min(size, places - start)
            for pp in range(4):
                for f in range(everyone):
                    row = pp * tall + 2 * f
                    spec_ref[f, pp, :, start:start + kept] = spec[row:row + 2, 0:kept]

    @pl.when(step < near)
    def _():
        write(near_ref, pl.multiple_of(deep * step, deep))

    @pl.when(step >= near)
    def _():
        far_copy(step - near).wait()
        write(far_s, pl.multiple_of(deep * (step - near), deep))


def per_device(grid, row_lengths, band_map, fold_map, legendre, to_modes, back_modes, mode_rates):
    fields, single, rows, width = grid.shape
    pairs, places, lats = legendre.shape
    cut_off = places - 2
    everyone = to_modes.shape[0]
    owners, per_owner = fold_map.shape
    groups = -(-per_owner // 8)
    slots = owners * groups * 8
    pieces = -(-(width // 4) // DEEP)
    turns = 4 * pieces
    span = -(-places // LANES) * LANES
    hbm = pl.BlockSpec(memory_space=pltpu.HBM)
    vmem = pl.BlockSpec(memory_space=pltpu.VMEM)
    room = pltpu.CompilerParams(vmem_limit_bytes=ROOM)
    message = pltpu.HBM((owners, 8, LANES), F32)
    holders = band_map.shape[0]
    groups_f = everyone // fields
    dma = pltpu.SemaphoreType.DMA
    row_lengths, band_map, fold_map, to_modes, back_modes, mode_rates, grid = (
        pltpu.with_memory_space_constraint(x, pltpu.HBM)
        for x in (row_lengths, band_map, fold_map, to_modes, back_modes, mode_rates, grid)
    )
    legendre = pltpu.with_memory_space_constraint(jnp.transpose(legendre, (0, 2, 1)), pltpu.HBM)

    sending, cos_table, sin_table, cos_turn, sin_turn = pl.pallas_call(
        functools.partial(forward_kernel, cut_off, groups),
        out_shape=(
            message,
            pltpu.VMEM((DEEP, slots), BF16),
            pltpu.VMEM((DEEP, slots), BF16),
            pltpu.VMEM((turns, slots), F32),
            pltpu.VMEM((turns, slots), F32),
        ),
        in_specs=[hbm] * 4,
        out_specs=(vmem,) * 5,
        scratch_shapes=[
            pltpu.SMEM(row_lengths.shape, jnp.int32),
            pltpu.SMEM(band_map.shape, jnp.int32),
            pltpu.VMEM(fold_map.shape, jnp.int32),
            pltpu.VMEM(grid.shape, BF16),
            dma((4,)),
            pltpu.VMEM((LANES, LANES), F32),
            pltpu.VMEM((8, slots), F32),
            pltpu.VMEM((TWICE, 4 * DEEP * pieces), F32),
            pltpu.VMEM((4 * TWICE, slots), BF16),
        ],
        compiler_params=room,
        name="forward_rows",
    )(row_lengths, band_map, fold_map, grid)
    tables = [
        pltpu.with_memory_space_constraint(x, pltpu.VMEM)
        for x in (cos_table, sin_table, cos_turn, sin_turn)
    ]
    arrived = lax.all_to_all(sending, ("lat", "fld"), split_axis=0, concat_axis=0, tiled=True)

    legs, mix, back, turn_back, tau, rate = pl.pallas_call(
        functools.partial(prepare_kernel, cut_off, pairs, fields, rows),
        out_shape=(
            pltpu.HBM((groups * 16 * lats, span), BF16),
            pltpu.VMEM((2 * rows * KPAD, 3 * LANES), BF16),
            pltpu.VMEM((2 * FPAD, 8 * KPAD), BF16),
            pltpu.VMEM((FPAD, 6 * KPAD), BF16),
            pltpu.VMEM((-(-groups * 4 // 8) * 8, span), F32),
            pltpu.VMEM((KPAD, 2 * LANES), F32),
        ),
        in_specs=[hbm] * 6,
        out_specs=(hbm,) + (vmem,) * 5,
        scratch_shapes=[
            pltpu.SMEM(fold_map.shape, jnp.int32),
            pltpu.SMEM(band_map.shape, jnp.int32),
            pltpu.SMEM(mode_rates.shape, F32),
            pltpu.VMEM((pairs, lats, places), F32),
            pltpu.VMEM(to_modes.shape, F32),
            pltpu.VMEM(back_modes.shape, F32),
            dma((6,)),
            pltpu.VMEM((KPAD, LANES), F32),
            pltpu.VMEM((groups * 16 * lats, span), BF16),
            dma((groups,)),
        ],
        compiler_params=room,
        cost_estimate=pl.CostEstimate(flops=10**8, bytes_accessed=8 * 10**6, transcendentals=0),
        name="prepare",
    )(fold_map, band_map, mode_rates, legendre, to_modes, back_modes)
    legs = pltpu.with_memory_space_constraint(legs, pltpu.HBM)
    mix, back, turn_back, tau, rate = (
        pltpu.with_memory_space_constraint(x, pltpu.VMEM)
        for x in (mix, back, turn_back, tau, rate)
    )

    near = groups // 2
    damped_near, damped_far, leaving = pl.pallas_call(
        functools.partial(solve_kernel, fields, rows, lats),
        out_shape=(
            pltpu.VMEM((near * 8 * KPAD, span), BF16),
            pltpu.HBM(((groups - near) * 8 * KPAD, span), BF16),
            pltpu.HBM((owners * 8, LANES), F32),
        ),
        in_specs=[hbm] + [vmem] * 5,
        out_specs=(vmem, hbm, vmem),
        scratch_shapes=[
            pltpu.VMEM((groups * 16 * lats, LANES), F32),
            pltpu.VMEM((groups * 16 * lats, span), BF16),
            pltpu.VMEM(((groups - near) * 8 * KPAD, span), BF16),
            dma((2,)),
            dma((groups - near,)),
        ],
        compiler_params=room,
        name="solve",
    )(legs, arrived.reshape(owners * 8, LANES), mix, turn_back, tau, rate)
    leaving = leaving.reshape(owners, 8, LANES)

    returned = lax.all_to_all(leaving, ("lat", "fld"), split_axis=0, concat_axis=0, tiled=True)

    damped_near = pltpu.with_memory_space_constraint(damped_near, pltpu.VMEM)
    damped_far = pltpu.with_memory_space_constraint(damped_far, pltpu.HBM)
    spectral = pl.pallas_call(
        output_kernel,
        grid=(groups,),
        out_shape=jax.ShapeDtypeStruct((everyone, pairs, 2, places), F32),
        in_specs=[
            pl.BlockSpec((near * 8 * KPAD, span), lambda t: (0, 0)),
            hbm,
            pl.BlockSpec((2 * FPAD, 8 * KPAD), lambda t: (0, 0)),
        ],
        out_specs=pl.BlockSpec((everyone, 4, 2, places), lambda t: (0, t, 0, 0)),
        scratch_shapes=[
            pltpu.VMEM((16 * everyone, 8 * KPAD), BF16),
            pltpu.VMEM(((groups - near) * 8 * KPAD, span), BF16),
            dma((groups - near,)),
        ],
        compiler_params=pltpu.CompilerParams(
            dimension_semantics=("arbitrary",), vmem_limit_bytes=ROOM
        ),
        cost_estimate=pl.CostEstimate(flops=10**8, bytes_accessed=8 * 10**6, transcendentals=0),
        name="spectral_output",
    )(damped_near, damped_far, back)

    grid_out = pl.pallas_call(
        functools.partial(inverse_kernel, groups),
        out_shape=jax.ShapeDtypeStruct(grid.shape, BF16),
        in_specs=[hbm] * 2 + [vmem] * 5,
        out_specs=vmem,
        scratch_shapes=[
            pltpu.SMEM(row_lengths.shape, jnp.int32),
            pltpu.SMEM(band_map.shape, jnp.int32),
            dma((2,)),
            pltpu.VMEM((32 * pieces, 4 * LANES), BF16),
        ],
        compiler_params=room,
        name="inverse_rows",
    )(row_lengths, band_map, *tables, returned)
    return (jnp.transpose(spectral, (0, 2, 1, 3)), grid_out)


def solution(mesh):
    placed = (
        P("fld", "lat", None, None),
        P(),
        P(),
        P(),
        P(("lat", "fld"), None, None),
        P(),
        P(),
        P(),
    )
    return jax.shard_map(
        per_device,
        mesh=mesh,
        in_specs=placed,
        out_specs=(P(None, None, ("lat", "fld"), None), P("fld", "lat", None, None)),
        check_vma=False,
    )
```

```python
import functools
import math

import jax
import jax.numpy as jnp
from jax import lax
from jax.experimental import pallas as pl
from jax.experimental.pallas import tpu as pltpu
from jax.sharding import PartitionSpec as P

LANES = 128
KPAD = 24
FPAD = 64
DEEP = 256
TWICE = 24
ROOM = 24 * 1024 * 1024
F32 = jnp.float32
BF16 = jnp.bfloat16
NT_DIMS = (((1,), (1,)), ((), ()))
SIN_POLY = (
    6.283185302447051,
    -41.34170038368319,
    81.60513023312113,
    -76.70299324464969,
    42.02573766814694,
    -14.899106966102595,
    3.237062655726421,
)
COS_POLY = (
    0.9999999889083757,
    -19.739204448887243,
    64.93911476570418,
    -85.45008785413638,
    60.167188450194914,
    -25.9658703083255,
    6.526145851512229,
)


def dot(a, b):
    return jnp.dot(a, b, preferred_element_type=F32)


def dot_nt(a, b):
    return lax.dot_general(a, b, NT_DIMS, preferred_element_type=F32)


def split(x):
    high = x.astype(BF16)
    return high, (x - high.astype(F32)).astype(BF16)


def horner(coefs, z):
    total = coefs[-1] * z + coefs[-2]
    for coef in coefs[-3::-1]:
        total = total * z + coef
    return total


def turn(steps, period, inverse):
    rest = steps - period * jnp.floor(steps * inverse + 0.5)
    part = rest * inverse
    z = part * part
    return horner(COS_POLY, z), part * horner(SIN_POLY, z)


def start_all(sources, targets, sems):
    copies = [
        pltpu.make_async_copy(source, target, sems.at[i])
        for i, (source, target) in enumerate(zip(sources, targets))
    ]
    for copy in copies:
        copy.start()
    return copies


def wait_all(copies):
    for copy in copies:
        copy.wait()


def lane_iota(shape):
    return lax.broadcasted_iota(jnp.int32, shape, len(shape) - 1)


def row_iota(shape):
    return lax.broadcasted_iota(jnp.int32, shape, len(shape) - 2)


def lanes_within(lane, start, size):
    start %= LANES
    if start + size <= LANES:
        return (lane >= start) & (lane < start + size)
    return (lane >= start) | (lane < start + size - LANES)


def spread_matrix():
    shape = (4 * LANES, LANES)
    picks = []
    for phase in range(4):
        picks.append(jnp.where(row_iota(shape) == 4 * lane_iota(shape) + phase, 1.0, 0.0))
    return jnp.concatenate(picks, axis=1).astype(BF16)


def phase_steps(groups, lanes):
    row = row_iota((groups + 16, lanes))
    steps = jnp.where(row < groups, (row >> 2) * (4 * DEEP) + (row & 3), 4 * (row - groups))
    steps = jnp.where(row >= groups + 8, 32 << jnp.maximum(row - groups - 8, 0), steps)
    return steps.astype(F32)


def slot_lane(index, fields, rows):
    used = rows * fields
    part = (index >= TWICE).astype(jnp.int32)
    row = index - TWICE * part
    vec = jnp.where(row >= used, row - used, row)
    lane = lax.rem(vec, rows) * (fields * 2) + lax.div(vec, rows) * 2 + part
    return jnp.where(row < 2 * used, lane, -LANES)


def two_phases(ref, g, at, used, block):
    first = ref[2 * g:2 * g + 1, at]
    second = ref[2 * g + 1:2 * g + 2, at]
    tiles = []
    for low in range(0, TWICE, 8):
        if low + 8 <= used:
            tiles.append(jnp.broadcast_to(first, (8, block)))
        elif low >= used:
            tiles.append(jnp.broadcast_to(second, (8, block)))
        else:
            tiles.append(jnp.where(low + row_iota((8, block)) < used, first, second))
    return jnp.concatenate(tiles, axis=0)


def forward_kernel(
    cut_off, groups, len_hbm, band_hbm, fold_hbm, grid_hbm,
    msg_ref, tc, ts, fc, fs,
    len_ref, band_ref, fold_ref, grid_ref, sems, fold_s, wave_s, xs, xt,
):
    copies = start_all(
        (len_hbm, band_hbm, fold_hbm, grid_hbm), (len_ref, band_ref, fold_ref, grid_ref), sems
    )
    fields, _, rows, width = grid_ref.shape
    owners, per_owner = fold_ref.shape
    slots = tc.shape[1]
    pieces = xs.shape[1] // (4 * DEEP)
    unit = rows * fields * 2
    used = rows * fields
    spread_s = spread_matrix()
    shape = (LANES, owners * 8)
    repeat = jnp.where(row_iota(shape) == lane_iota(shape) >> 3, 1.0, 0.0).astype(BF16)
    shape = (8 * groups, 16 * groups)
    weigh = jnp.where(
        jnp.where(lane_iota(shape) < 8 * groups, lane_iota(shape), lane_iota(shape) - 8 * groups) >> 3
        == row_iota(shape) >> 3,
        jnp.where(lane_iota(shape) < 8 * groups, 8.0, 1.0),
        0.0,
    ).astype(BF16)
    tall = 4 * TWICE
    shape = (LANES, tall * groups)
    one = (1, 2 * TWICE)
    base = slot_lane(lane_iota(one), fields, rows)
    targets = []
    for t in range(groups):
        target = base + unit * (t + lax.axis_index("fld"))
        target = jnp.where(base < 0, base, target & (LANES - 1))
        targets += [target, target]
    target = jnp.concatenate(targets, axis=1)
    packing = jnp.where(row_iota(shape) == target, 1.0, 0.0).astype(BF16)
    fold_s[...] = jnp.full(fold_s.shape, -1.0, F32)
    xs[...] = jnp.zeros(xs.shape, F32)
    wait_all(copies)
    length = len_ref[band_ref[lax.axis_index("lat")]]
    top = jnp.minimum(cut_off, (length - 1) // 2)

    fold_s[0:owners, 0:per_owner] = fold_ref[...].astype(F32)
    turned = jnp.transpose(fold_s[...])[0:8 * groups]
    eights = jnp.floor(turned * 0.125)
    parts = jnp.concatenate([eights, turned - 8.0 * eights], axis=0).astype(BF16)
    repeated = dot(parts, repeat)
    own = (lane_iota(repeated.shape) & 7) == (row_iota(repeated.shape) & 7)
    waves = dot(weigh, jnp.where(own, repeated, 0.0).astype(BF16))
    for t in range(groups):
        wave_s[:, owners * 8 * t:owners * 8 * (t + 1)] = waves[8 * t:8 * t + 8]

    for field in range(fields):
        points = grid_ref[field, 0].astype(F32)
        for copy in (0, used):
            at = copy + rows * field
            xs[at:at + rows, 0:width] = points
    stacked = jnp.concatenate(
        [xs[:, 4 * LANES * c:4 * LANES * (c + 1)] for c in range(2 * pieces)], axis=0
    ).astype(BF16)
    spread = dot(stacked, spread_s)
    shape = (TWICE, LANES)
    front = row_iota(shape) < used
    values = []
    for k in range(pieces):
        for pair in range(2):
            halves = []
            for half in range(2):
                c = 2 * k + half
                rows_c = spread[TWICE * c:TWICE * (c + 1)]
                off = 2 * LANES * pair
                both = jnp.where(
                    front, rows_c[:, off:off + LANES], rows_c[:, off + LANES:off + 2 * LANES]
                )
                inside = c * LANES + lane_iota(shape) < length // 4
                halves.append(jnp.where(inside, both, 0.0))
            values.append(jnp.concatenate(halves, axis=1))
    values = jnp.concatenate(values, axis=0).astype(BF16)

    turns = 4 * pieces
    block = 2 * LANES
    steps = phase_steps(turns, block)
    period = jnp.full(steps.shape, length, jnp.int32).astype(F32)
    inverse = 1.0 / period
    for i in range(slots // block):
        at = pl.ds(i * block, block)
        wave = wave_s[:, at]
        wave = jnp.concatenate([wave] * ((turns + 16) // 8), axis=0)
        co, si = turn(steps * wave, period, inverse)
        one = wave[0:1]
        weight = jnp.where(one == 0.0, 1.0, 2.0)
        weight = jnp.where((one >= 0.0) & (one <= jnp.full(one.shape, top, jnp.int32).astype(F32)), weight, 0.0)
        fc[:, at] = co[0:turns] * weight
        fs[:, at] = si[0:turns] * weight
        c_all = co[turns:turns + 8]
        s_all = si[turns:turns + 8]
        size, step = 8, turns + 8
        while size < DEEP:
            c1 = co[step:step + 1]
            s1 = si[step:step + 1]
            c_new = c_all * c1 - s_all * s1
            s_new = s_all * c1 + c_all * s1
            c_all = jnp.concatenate([c_all, c_new], axis=0)
            s_all = jnp.concatenate([s_all, s_new], axis=0)
            size, step = 2 * size, step + 1
        c_all = c_all.astype(BF16)
        s_all = s_all.astype(BF16)
        tc[:, at] = c_all
        ts[:, at] = s_all
        inner_c = dot(values, c_all)
        inner_s = dot(values, s_all)
        real = jnp.zeros((TWICE, block), F32)
        imag = jnp.zeros((TWICE, block), F32)
        for g in range(turns // 2):
            c1 = two_phases(fc, g, at, used, block)
            s1 = two_phases(fs, g, at, used, block)
            part_c = inner_c[TWICE * g:TWICE * (g + 1)]
            part_s = inner_s[TWICE * g:TWICE * (g + 1)]
            real = real + (c1 * part_c - s1 * part_s)
            imag = imag - (c1 * part_s + s1 * part_c)
        both = jnp.concatenate([real, imag], axis=0) * jnp.where(one == 0.0, 1.0, 0.5)
        xt[:, at] = jnp.concatenate(split(both), axis=0)

    turned = jnp.concatenate(
        [xt[:, owners * 8 * t:owners * 8 * (t + 1)] for t in range(groups)], axis=0
    )
    total = dot(packing, turned)
    scale = 1.0 / jnp.sqrt(jnp.full(total.shape, length, jnp.int32).astype(F32))
    msg_ref[...] = jnp.transpose(total * scale).reshape(owners, 8, LANES)


def inverse_kernel(
    groups, len_hbm, band_hbm, tc, ts, fc, fs, msg_ref, grid_ref,
    len_ref, band_ref, sems, os,
):
    copies = start_all((len_hbm, band_hbm), (len_ref, band_ref), sems)
    spread_s = spread_matrix()
    fields, _, rows, width = grid_ref.shape
    owners = msg_ref.shape[0]
    slots = tc.shape[1]
    turns = fc.shape[0]
    unit = rows * fields * 2
    high, low = split(msg_ref[...].reshape(owners * 8, LANES))
    pieces = jnp.concatenate([high, low], axis=1)
    used = rows * fields
    tall = 2 * TWICE
    shape = (tall, LANES)
    base = slot_lane(row_iota(shape), fields, rows)
    places = []
    for t in range(groups):
        source = (base + unit * t + lax.axis_index("fld") * (fields * 2)) & (LANES - 1)
        source = jnp.where(base < 0, base, source)
        places.append(jnp.where(lane_iota(shape) == source, 1.0, 0.0))
    place = jnp.concatenate(places, axis=0).astype(BF16)
    place = jnp.concatenate([place, place], axis=1)
    turned = dot_nt(place, pieces)
    block = 2 * LANES
    out = jnp.zeros((TWICE * turns // 2, DEEP), F32)
    for i in range(slots // block):
        t, off = divmod(i * block, owners * 8)
        real = turned[tall * t:tall * t + TWICE, off:off + block]
        imag = turned[tall * t + TWICE:tall * (t + 1), off:off + block]
        at = pl.ds(i * block, block)
        reals, imags = [], []
        for g in range(turns // 2):
            c1 = two_phases(fc, g, at, used, block)
            s1 = two_phases(fs, g, at, used, block)
            reals.append(c1 * real - s1 * imag)
            imags.append(s1 * real + c1 * imag)
        reals = jnp.concatenate(reals, axis=0).astype(BF16)
        imags = jnp.concatenate(imags, axis=0).astype(BF16)
        out = out + (dot_nt(reals, tc[:, at]) - dot_nt(imags, ts[:, at]))
    wait_all(copies)
    length = len_ref[band_ref[lax.axis_index("lat")]]
    out = out * (1.0 / jnp.sqrt(jnp.full(out.shape, length, jnp.int32).astype(F32)))
    chunks = os.shape[0] // 16
    for c in range(chunks):
        off = LANES * (c % 2)
        for phase in range(4):
            at = (2 * (c // 2) + phase // 2) * TWICE
            piece = out[at:at + TWICE, off:off + LANES]
            if phase % 2:
                piece = pltpu.roll(piece, TWICE - used, 0)
            os[16 * c:16 * (c + 1), LANES * phase:LANES * (phase + 1)] = piece[0:16].astype(BF16)
    merged = dot_nt(os[...], spread_s)
    for c in range(chunks):
        begin = 4 * LANES * c
        size = min(4 * LANES, width - begin)
        if size <= 0:
            continue
        inside = begin + lane_iota((16, size)) < length
        piece = jnp.where(inside, merged[16 * c:16 * (c + 1), 0:size], 0.0)
        for field in range(fields):
            grid_ref[field, 0, :, begin:begin + size] = piece[
                rows * field:rows * (field + 1)
            ].astype(BF16)


def prepare_kernel(
    cut_off, pairs, fields, rows, fold_hbm, band_hbm, rates_hbm, leg_hbm, tm_hbm, bm_hbm,
    eh_hbm, mix_ref, back_ref, turn_ref, tau_ref, rate_ref,
    fold_ref, band_ref, rates_ref, leg_ref, tm_ref, bm_ref, sems, pad_s, eh_ref, out_sems,
):
    copies = start_all(
        (fold_hbm, band_hbm, rates_hbm, tm_hbm, bm_hbm, leg_hbm),
        (fold_ref, band_ref, rates_ref, tm_ref, bm_ref, leg_ref),
        sems,
    )
    wait_all(copies[:-1])
    everyone = tm_ref.shape[0]
    _, lats, places = leg_ref.shape
    groups_f = everyone // fields
    wf = fields * 2
    unit = rows * wf
    span = eh_ref.shape[1]
    eight = 8 * lats
    groups = eh_ref.shape[0] // (2 * eight)
    owner = lax.axis_index("lat") * groups_f + lax.axis_index("fld")

    pad_s[...] = jnp.zeros(pad_s.shape, F32)
    pad_s[0:everyone, 0:everyone] = tm_ref[...]
    shape = (LANES, LANES)
    level = (lane_iota(shape) // unit) * fields + (lane_iota(shape) % wf) // 2
    pick = jnp.where(row_iota(shape) == level, 1.0, 0.0).astype(BF16)
    lane = lane_iota((KPAD, LANES))
    parts = []
    for piece in split(pad_s[...]):
        wide = dot(piece, pick)
        total = []
        for r in range(rows):
            for c in range(2):
                keep = ((lane % unit) // wf == r) & (lane % 2 == c) & (lane < unit * groups_f)
                total.append(jnp.where(keep, wide, 0.0))
        parts.append(jnp.concatenate(total, axis=0).astype(BF16))
    mix_ref[...] = jnp.concatenate([parts[0], parts[1], parts[0]], axis=1)

    pad_s[...] = jnp.zeros(pad_s.shape, F32)
    pad_s[0:everyone, 0:everyone] = bm_ref[...]
    shape = (FPAD, KPAD)
    expand = jnp.where(row_iota(shape) // 2 == lane_iota(shape), 1.0, 0.0).astype(BF16)
    shape = (LANES, 2 * LANES)
    repeat = jnp.where(row_iota(shape) == lane_iota(shape) % KPAD, 1.0, 0.0).astype(BF16)
    shape = (FPAD, 2 * LANES)
    same = row_iota(shape) % 2 == (lane_iota(shape) // KPAD) % 2
    fulls = []
    for part, piece in enumerate(split(pad_s[...])):
        full = jnp.where(same, dot(dot(expand, piece).astype(BF16), repeat), 0.0)
        back_ref[part * FPAD:(part + 1) * FPAD, :] = full[:, 0:8 * KPAD].astype(BF16)
        fulls.append(full)
    turn = jnp.where(lane_iota(shape) < 4 * KPAD, fulls[0], fulls[1])
    turn_ref[...] = turn[:, 0:6 * KPAD].astype(BF16)

    row = row_iota((KPAD, 2 * LANES))
    rate = jnp.zeros((KPAD, 2 * LANES), F32)
    for k in range(everyone):
        rate = jnp.where(row == k, rates_ref[k], rate)
    rate_ref[...] = rate
    paired = tau_ref.shape[0]
    row = row_iota((paired, LANES))
    waves = []
    wave = jnp.zeros((paired, LANES), jnp.int32)
    for pair in range(4 * groups):
        waves.append(fold_ref[owner, 2 * min(pair, pairs - 1)])
        wave = jnp.where(row == pair, waves[pair], wave)
    wave = jnp.concatenate([wave] * (span // LANES), axis=1)
    line = lane_iota((paired, span))
    degree = jnp.where(line > cut_off - wave, line - 1, line + wave)
    tau_ref[...] = (degree * (degree + 1)).astype(F32) * (1.0 / float(cut_off * (cut_off + 1)))

    quad_rows = 4 * lats
    shape = (quad_rows, quad_rows)
    band = jnp.zeros(shape, jnp.int32)
    for holder in range(lats):
        band = jnp.where(row_iota(shape) % lats == holder, band_ref[holder], band)
    order = jnp.where(
        (row_iota(shape) // lats == lane_iota(shape) // lats) & (lane_iota(shape) % lats == band),
        1.0,
        0.0,
    ).astype(BF16)

    whole = places // LANES * LANES
    line = lane_iota((quad_rows, span))
    row = row_iota((quad_rows, LANES)) // lats
    copies[-1].wait()
    keeps = []
    for t in range(groups):
        wave = jnp.zeros((quad_rows, LANES), jnp.int32)
        last = jnp.zeros((quad_rows, LANES), jnp.int32)
        stack = []
        for pp in range(4):
            there = 4 * t + pp < pairs
            index = min(4 * t + pp, pairs - 1)
            wave = jnp.where(row == pp, waves[4 * t + pp], wave)
            last = jnp.where(row == pp, places - 1 if there else -1, last)
            stack.append(
                jnp.concatenate(
                    [
                        leg_ref[index, :, 0:whole],
                        jnp.broadcast_to(leg_ref[index, :, whole:places], (lats, span - whole)),
                    ],
                    axis=1,
                )
            )
        wave = jnp.concatenate([wave] * (span // LANES), axis=1)
        last = jnp.concatenate([last] * (span // LANES), axis=1)
        leg = dot(order, jnp.concatenate(stack, axis=0).astype(BF16))
        before = line <= cut_off - wave
        first = before & (line <= last)
        second = jnp.logical_not(before) & (line <= last)
        odd = ((line + jnp.where(before, 0, wave)) & 1) == 1
        signed = jnp.where(odd, -leg, leg)
        for r, rowset in enumerate((leg, signed)):
            near = jnp.where(first, rowset, 0.0)
            far = jnp.where(second, rowset, 0.0)
            for pp in range(4):
                at = 2 * eight * t + r * eight + 2 * pp * lats
                eh_ref[at:at + 2 * lats, :] = jnp.concatenate(
                    [near[pp * lats:(pp + 1) * lats], far[pp * lats:(pp + 1) * lats]], axis=0
                ).astype(BF16)
        part = pl.ds(2 * eight * t, 2 * eight)
        keeps.append(pltpu.make_async_copy(eh_ref.at[part], eh_hbm.at[part], out_sems.at[t]))
        keeps[-1].start()
    wait_all(keeps)


def solve_kernel(
    fields, rows, lats, eh_hbm, msg_ref, mix_ref, turn_ref, tau_ref, rate_ref,
    near_ref, far_hbm, out_ref, cs, eh_ref, far_ref, in_sems, out_sems,
):
    eight = 8 * lats
    groups = eh_ref.shape[0] // (2 * eight)
    parts = [pl.ds(0, 2 * eight), pl.ds(2 * eight, 2 * eight * (groups - 1))]
    later = start_all(
        [eh_hbm.at[part] for part in parts], [eh_ref.at[part] for part in parts], in_sems
    )
    groups_f = msg_ref.shape[0] // eight
    wf = fields * 2
    unit = rows * wf
    span = eh_ref.shape[1]
    deep = 8 * KPAD
    near = near_ref.shape[0] // deep
    holds = [(near_ref, deep * t) for t in range(near)]
    holds += [(far_ref, deep * t) for t in range(groups - near)]
    lane = lane_iota((lats, LANES))
    tiles = [
        [msg_ref[pl.ds(8 * g + i8, lats, stride=8 * groups_f), :] for g in range(groups_f)]
        for i8 in range(8)
    ]
    tall = []
    for t in range(groups):
        here = [lanes_within(lane, unit * (t + g), unit) for g in range(groups_f)]
        for i8 in range(8):
            line = tiles[i8][0]
            for g in range(1, groups_f):
                line = jnp.where(here[g], tiles[i8][g], line)
            if t:
                line = pltpu.roll(line, LANES - unit * t, 1)
            tall.append(line)
    v_high, v_low = split(jnp.concatenate(tall, axis=0))
    mixed = dot_nt(mix_ref[...], jnp.concatenate([v_high, v_high, v_low], axis=1))

    rate = rate_ref[...]
    slot_pair = (lane_iota((2 * KPAD, 2 * eight)) % eight) // (2 * lats)
    lefts = []
    for t in range(groups):
        mine = mixed[:, eight * t:eight * (t + 1)]
        mine = jnp.concatenate([mine[0:2 * KPAD], mine[2 * KPAD:4 * KPAD]], axis=1)
        left = jnp.concatenate([jnp.where(slot_pair == pp, mine, 0.0) for pp in range(4)], axis=0)
        lefts.append(jnp.concatenate(split(left), axis=1))

    keeps = []
    for t in range(groups):
        left = lefts[t]
        legs = pl.ds(2 * eight * t, 2 * eight)
        if t < 2:
            later[t].wait()
        for start in range(0, span, 2 * LANES):
            size = min(2 * LANES, span - start)
            right = eh_ref[legs, start:start + size]
            modes = dot(left, jnp.concatenate([right, right], axis=0))
            damped = []
            for pp in range(4):
                tau = tau_ref[4 * t + pp:4 * t + pp + 1, start:start + size]
                below = 1.0 + tau * rate[:, 0:size]
                factor = pl.reciprocal(below, approx=True)
                at = 2 * pp * KPAD
                damped.append(modes[at:at + KPAD] * factor)
                damped.append(modes[at + KPAD:at + 2 * KPAD] * factor)
            hold, at = holds[t]
            hold[at:at + deep, start:start + size] = jnp.concatenate(damped, axis=0).astype(BF16)
        if t >= near:
            part = pl.ds(deep * (t - near), deep)
            keeps.append(
                pltpu.make_async_copy(far_ref.at[part], far_hbm.at[part], out_sems.at[t - near])
            )
            keeps[-1].start()

    picks = []
    for t in range(groups):
        hold, at = holds[t]
        product = dot_nt(hold[at:at + deep, :], eh_ref[pl.ds(2 * eight * t, 2 * eight), :])
        pick = product[0:2 * KPAD]
        for pp in range(1, 4):
            pick = jnp.where(slot_pair == pp, product[2 * KPAD * pp:2 * KPAD * (pp + 1)], pick)
        picks.append(pick)
    high, low = split(jnp.concatenate(picks, axis=1))
    back = dot(turn_ref[...], jnp.concatenate([high, low, high], axis=0))
    back = jnp.concatenate([back, jnp.zeros((LANES - FPAD, back.shape[1]), F32)], axis=0)
    for at in range(0, back.shape[1], LANES):
        cs[at:at + LANES, :] = jnp.transpose(back[:, at:at + LANES])

    lane = lane_iota((8, LANES))
    here = [
        lanes_within(lane, wf * u, wf) for u in range(rows * groups + groups_f - 1)
    ]
    for holder in range(lats):
        tiles = [jnp.zeros((8, LANES), F32) for _ in range(groups_f)]
        for u in range(rows * groups):
            piece = cs[pl.ds(u * eight + holder, 8, stride=lats), :]
            if u:
                piece = pltpu.roll(piece, wf * u, 1)
            for g in range(groups_f):
                tiles[g] = jnp.where(here[u + g], piece, tiles[g])
        for g in range(groups_f):
            at = (holder * groups_f + g) * 8
            out_ref[at:at + 8, :] = tiles[g]
    wait_all(keeps)


def output_kernel(near_ref, far_hbm, back_ref, spec_ref, bk, far_s, sems):
    everyone, quad, _, places = spec_ref.shape
    span = near_ref.shape[1]
    deep = 8 * KPAD
    near = near_ref.shape[0] // deep
    tall = 2 * everyone
    step = pl.program_id(0)

    def far_copy(t):
        part = pl.ds(pl.multiple_of(deep * t, deep), deep)
        return pltpu.make_async_copy(far_hbm.at[part], far_s.at[part], sems.at[t])

    @pl.when(step == 0)
    def _():
        for t in range(sems.shape[0]):
            far_copy(t).start()
        pair_of = lane_iota((tall, deep)) // (2 * KPAD)
        rows = []
        for part in range(2):
            full = back_ref[part * FPAD:part * FPAD + tall, :].astype(F32)
            for pp in range(4):
                rows.append(jnp.where(pair_of == pp, full, 0.0))
        bk[...] = jnp.concatenate(rows, axis=0).astype(BF16)

    def write(source, at):
        for start in range(0, span, 2 * LANES):
            size = min(2 * LANES, span - start)
            spec = dot(bk[...], source[pl.ds(at, deep), start:start + size])
            spec = spec[0:4 * tall] + spec[4 * tall:]
            kept = min(size, places - start)
            for pp in range(4):
                for f in range(everyone):
                    row = pp * tall + 2 * f
                    spec_ref[f, pp, :, start:start + kept] = spec[row:row + 2, 0:kept]

    @pl.when(step < near)
    def _():
        write(near_ref, pl.multiple_of(deep * step, deep))

    @pl.when(step >= near)
    def _():
        far_copy(step - near).wait()
        write(far_s, pl.multiple_of(deep * (step - near), deep))


def per_device(grid, row_lengths, band_map, fold_map, legendre, to_modes, back_modes, mode_rates):
    fields, single, rows, width = grid.shape
    pairs, places, lats = legendre.shape
    cut_off = places - 2
    everyone = to_modes.shape[0]
    owners, per_owner = fold_map.shape
    groups = -(-per_owner // 8)
    slots = owners * groups * 8
    pieces = -(-(width // 4) // DEEP)
    turns = 4 * pieces
    span = -(-places // LANES) * LANES
    hbm = pl.BlockSpec(memory_space=pltpu.HBM)
    vmem = pl.BlockSpec(memory_space=pltpu.VMEM)
    room = pltpu.CompilerParams(vmem_limit_bytes=ROOM)
    message = pltpu.HBM((owners, 8, LANES), F32)
    holders = band_map.shape[0]
    groups_f = everyone // fields
    dma = pltpu.SemaphoreType.DMA
    row_lengths, band_map, fold_map, to_modes, back_modes, mode_rates, grid = (
        pltpu.with_memory_space_constraint(x, pltpu.HBM)
        for x in (row_lengths, band_map, fold_map, to_modes, back_modes, mode_rates, grid)
    )
    legendre = pltpu.with_memory_space_constraint(jnp.transpose(legendre, (0, 2, 1)), pltpu.HBM)

    sending, cos_table, sin_table, cos_turn, sin_turn = pl.pallas_call(
        functools.partial(forward_kernel, cut_off, groups),
        out_shape=(
            message,
            pltpu.VMEM((DEEP, slots), BF16),
            pltpu.VMEM((DEEP, slots), BF16),
            pltpu.VMEM((turns, slots), F32),
            pltpu.VMEM((turns, slots), F32),
        ),
        in_specs=[hbm] * 4,
        out_specs=(vmem,) * 5,
        scratch_shapes=[
            pltpu.SMEM(row_lengths.shape, jnp.int32),
            pltpu.SMEM(band_map.shape, jnp.int32),
            pltpu.VMEM(fold_map.shape, jnp.int32),
            pltpu.VMEM(grid.shape, BF16),
            dma((4,)),
            pltpu.VMEM((LANES, LANES), F32),
            pltpu.VMEM((8, slots), F32),
            pltpu.VMEM((TWICE, 4 * DEEP * pieces), F32),
            pltpu.VMEM((4 * TWICE, slots), BF16),
        ],
        compiler_params=room,
        name="forward_rows",
    )(row_lengths, band_map, fold_map, grid)
    tables = [
        pltpu.with_memory_space_constraint(x, pltpu.VMEM)
        for x in (cos_table, sin_table, cos_turn, sin_turn)
    ]
    arrived = lax.all_to_all(sending, ("lat", "fld"), split_axis=0, concat_axis=0, tiled=True)

    legs, mix, back, turn_back, tau, rate = pl.pallas_call(
        functools.partial(prepare_kernel, cut_off, pairs, fields, rows),
        out_shape=(
            pltpu.HBM((groups * 16 * lats, span), BF16),
            pltpu.VMEM((2 * rows * KPAD, 3 * LANES), BF16),
            pltpu.VMEM((2 * FPAD, 8 * KPAD), BF16),
            pltpu.VMEM((FPAD, 6 * KPAD), BF16),
            pltpu.VMEM((-(-groups * 4 // 8) * 8, span), F32),
            pltpu.VMEM((KPAD, 2 * LANES), F32),
        ),
        in_specs=[hbm] * 6,
        out_specs=(hbm,) + (vmem,) * 5,
        scratch_shapes=[
            pltpu.SMEM(fold_map.shape, jnp.int32),
            pltpu.SMEM(band_map.shape, jnp.int32),
            pltpu.SMEM(mode_rates.shape, F32),
            pltpu.VMEM((pairs, lats, places), F32),
            pltpu.VMEM(to_modes.shape, F32),
            pltpu.VMEM(back_modes.shape, F32),
            dma((6,)),
            pltpu.VMEM((KPAD, LANES), F32),
            pltpu.VMEM((groups * 16 * lats, span), BF16),
            dma((groups,)),
        ],
        compiler_params=room,
        cost_estimate=pl.CostEstimate(flops=10**8, bytes_accessed=8 * 10**6, transcendentals=0),
        name="prepare",
    )(fold_map, band_map, mode_rates, legendre, to_modes, back_modes)
    legs = pltpu.with_memory_space_constraint(legs, pltpu.HBM)
    mix, back, turn_back, tau, rate = (
        pltpu.with_memory_space_constraint(x, pltpu.VMEM)
        for x in (mix, back, turn_back, tau, rate)
    )

    near = groups // 2
    damped_near, damped_far, leaving = pl.pallas_call(
        functools.partial(solve_kernel, fields, rows, lats),
        out_shape=(
            pltpu.VMEM((near * 8 * KPAD, span), BF16),
            pltpu.HBM(((groups - near) * 8 * KPAD, span), BF16),
            pltpu.HBM((owners * 8, LANES), F32),
        ),
        in_specs=[hbm] + [vmem] * 5,
        out_specs=(vmem, hbm, vmem),
        scratch_shapes=[
            pltpu.VMEM((groups * 16 * lats, LANES), F32),
            pltpu.VMEM((groups * 16 * lats, span), BF16),
            pltpu.VMEM(((groups - near) * 8 * KPAD, span), BF16),
            dma((2,)),
            dma((groups - near,)),
        ],
        compiler_params=room,
        name="solve",
    )(legs, arrived.reshape(owners * 8, LANES), mix, turn_back, tau, rate)
    leaving = leaving.reshape(owners, 8, LANES)

    returned = lax.all_to_all(leaving, ("lat", "fld"), split_axis=0, concat_axis=0, tiled=True)

    damped_near = pltpu.with_memory_space_constraint(damped_near, pltpu.VMEM)
    damped_far = pltpu.with_memory_space_constraint(damped_far, pltpu.HBM)
    spectral = pl.pallas_call(
        output_kernel,
        grid=(groups,),
        out_shape=jax.ShapeDtypeStruct((everyone, pairs, 2, places), F32),
        in_specs=[
            pl.BlockSpec((near * 8 * KPAD, span), lambda t: (0, 0)),
            hbm,
            pl.BlockSpec((2 * FPAD, 8 * KPAD), lambda t: (0, 0)),
        ],
        out_specs=pl.BlockSpec((everyone, 4, 2, places), lambda t: (0, t, 0, 0)),
        scratch_shapes=[
            pltpu.VMEM((16 * everyone, 8 * KPAD), BF16),
            pltpu.VMEM(((groups - near) * 8 * KPAD, span), BF16),
            dma((groups - near,)),
        ],
        compiler_params=pltpu.CompilerParams(
            dimension_semantics=("arbitrary",), vmem_limit_bytes=ROOM
        ),
        cost_estimate=pl.CostEstimate(flops=10**8, bytes_accessed=8 * 10**6, transcendentals=0),
        name="spectral_output",
    )(damped_near, damped_far, back)

    grid_out = pl.pallas_call(
        functools.partial(inverse_kernel, groups),
        out_shape=jax.ShapeDtypeStruct(grid.shape, BF16),
        in_specs=[hbm] * 2 + [vmem] * 5,
        out_specs=vmem,
        scratch_shapes=[
            pltpu.SMEM(row_lengths.shape, jnp.int32),
            pltpu.SMEM(band_map.shape, jnp.int32),
            dma((2,)),
            pltpu.VMEM((32 * pieces, 4 * LANES), BF16),
        ],
        compiler_params=room,
        name="inverse_rows",
    )(row_lengths, band_map, *tables, returned)
    return (jnp.transpose(spectral, (0, 2, 1, 3)), grid_out)


def solution(mesh):
    placed = (
        P("fld", "lat", None, None),
        P(),
        P(),
        P(),
        P(("lat", "fld"), None, None),
        P(),
        P(),
        P(),
    )
    return jax.shard_map(
        per_device,
        mesh=mesh,
        in_specs=placed,
        out_specs=(P(None, None, ("lat", "fld"), None), P("fld", "lat", None, None)),
        check_vma=False,
    )
```

```python
import functools
import math

import jax
import jax.numpy as jnp
from jax import lax
from jax.experimental import pallas as pl
from jax.experimental.pallas import tpu as pltpu
from jax.sharding import PartitionSpec as P

LANES = 128
KPAD = 24
FPAD = 64
DEEP = 256
TWICE = 24
ROOM = 24 * 1024 * 1024
F32 = jnp.float32
BF16 = jnp.bfloat16
NT_DIMS = (((1,), (1,)), ((), ()))
SIN_POLY = (
    6.283185302447051,
    -41.34170038368319,
    81.60513023312113,
    -76.70299324464969,
    42.02573766814694,
    -14.899106966102595,
    3.237062655726421,
)
COS_POLY = (
    0.9999999889083757,
    -19.739204448887243,
    64.93911476570418,
    -85.45008785413638,
    60.167188450194914,
    -25.9658703083255,
    6.526145851512229,
)


def dot(a, b):
    return jnp.dot(a, b, preferred_element_type=F32)


def dot_nt(a, b):
    return lax.dot_general(a, b, NT_DIMS, preferred_element_type=F32)


def split(x):
    high = x.astype(BF16)
    return high, (x - high.astype(F32)).astype(BF16)


def horner(coefs, z):
    total = coefs[-1] * z + coefs[-2]
    for coef in coefs[-3::-1]:
        total = total * z + coef
    return total


def turn(steps, period, inverse):
    rest = steps - period * jnp.floor(steps * inverse + 0.5)
    part = rest * inverse
    z = part * part
    return horner(COS_POLY, z), part * horner(SIN_POLY, z)


def start_all(sources, targets, sems):
    copies = [
        pltpu.make_async_copy(source, target, sems.at[i])
        for i, (source, target) in enumerate(zip(sources, targets))
    ]
    for copy in copies:
        copy.start()
    return copies


def wait_all(copies):
    for copy in copies:
        copy.wait()


def lane_iota(shape):
    return lax.broadcasted_iota(jnp.int32, shape, len(shape) - 1)


def row_iota(shape):
    return lax.broadcasted_iota(jnp.int32, shape, len(shape) - 2)


def lanes_within(lane, start, size):
    start %= LANES
    if start + size <= LANES:
        return (lane >= start) & (lane < start + size)
    return (lane >= start) | (lane < start + size - LANES)


def spread_matrix():
    shape = (4 * LANES, LANES)
    picks = []
    for phase in range(4):
        picks.append(jnp.where(row_iota(shape) == 4 * lane_iota(shape) + phase, 1.0, 0.0))
    return jnp.concatenate(picks, axis=1).astype(BF16)


def phase_steps(groups, lanes):
    row = row_iota((groups + 16, lanes))
    steps = jnp.where(row < groups, (row >> 2) * (4 * DEEP) + (row & 3), 4 * (row - groups))
    steps = jnp.where(row >= groups + 8, 32 << jnp.maximum(row - groups - 8, 0), steps)
    return steps.astype(F32)


def slot_lane(index, fields, rows):
    used = rows * fields
    part = (index >= TWICE).astype(jnp.int32)
    row = index - TWICE * part
    vec = jnp.where(row >= used, row - used, row)
    lane = lax.rem(vec, rows) * (fields * 2) + lax.div(vec, rows) * 2 + part
    return jnp.where(row < 2 * used, lane, -LANES)


def two_phases(ref, g, at, used, block):
    first = ref[2 * g:2 * g + 1, at]
    second = ref[2 * g + 1:2 * g + 2, at]
    tiles = []
    for low in range(0, TWICE, 8):
        if low + 8 <= used:
            tiles.append(jnp.broadcast_to(first, (8, block)))
        elif low >= used:
            tiles.append(jnp.broadcast_to(second, (8, block)))
        else:
            tiles.append(jnp.where(low + row_iota((8, block)) < used, first, second))
    return jnp.concatenate(tiles, axis=0)


def forward_kernel(
    cut_off, groups, len_hbm, band_hbm, fold_hbm, grid_hbm,
    msg_ref, tc, ts, fc, fs,
    len_ref, band_ref, fold_ref, grid_ref, sems, fold_s, wave_s, xs, xt,
):
    copies = start_all(
        (len_hbm, band_hbm, fold_hbm, grid_hbm), (len_ref, band_ref, fold_ref, grid_ref), sems
    )
    fields, _, rows, width = grid_ref.shape
    owners, per_owner = fold_ref.shape
    slots = tc.shape[1]
    pieces = xs.shape[1] // (4 * DEEP)
    unit = rows * fields * 2
    used = rows * fields
    spread_s = spread_matrix()
    shape = (LANES, owners * 8)
    repeat = jnp.where(row_iota(shape) == lane_iota(shape) >> 3, 1.0, 0.0).astype(BF16)
    shape = (8 * groups, 16 * groups)
    weigh = jnp.where(
        jnp.where(lane_iota(shape) < 8 * groups, lane_iota(shape), lane_iota(shape) - 8 * groups) >> 3
        == row_iota(shape) >> 3,
        jnp.where(lane_iota(shape) < 8 * groups, 8.0, 1.0),
        0.0,
    ).astype(BF16)
    tall = 4 * TWICE
    shape = (LANES, tall * groups)
    one = (1, 2 * TWICE)
    base = slot_lane(lane_iota(one), fields, rows)
    targets = []
    for t in range(groups):
        target = base + unit * (t + lax.axis_index("fld"))
        target = jnp.where(base < 0, base, target & (LANES - 1))
        targets += [target, target]
    target = jnp.concatenate(targets, axis=1)
    packing = jnp.where(row_iota(shape) == target, 1.0, 0.0).astype(BF16)
    fold_s[...] = jnp.full(fold_s.shape, -1.0, F32)
    xs[...] = jnp.zeros(xs.shape, F32)
    wait_all(copies)
    length = len_ref[band_ref[lax.axis_index("lat")]]
    top = jnp.minimum(cut_off, (length - 1) // 2)

    fold_s[0:owners, 0:per_owner] = fold_ref[...].astype(F32)
    turned = jnp.transpose(fold_s[...])[0:8 * groups]
    eights = jnp.floor(turned * 0.125)
    parts = jnp.concatenate([eights, turned - 8.0 * eights], axis=0).astype(BF16)
    repeated = dot(parts, repeat)
    own = (lane_iota(repeated.shape) & 7) == (row_iota(repeated.shape) & 7)
    waves = dot(weigh, jnp.where(own, repeated, 0.0).astype(BF16))
    for t in range(groups):
        wave_s[:, owners * 8 * t:owners * 8 * (t + 1)] = waves[8 * t:8 * t + 8]

    for field in range(fields):
        xs[rows * field:rows * (field + 1), 0:width] = grid_ref[field, 0].astype(F32)
    stacked = jnp.concatenate(
        [xs[:, 4 * LANES * c:4 * LANES * (c + 1)] for c in range(2 * pieces)], axis=0
    ).astype(BF16)
    spread = dot(stacked, spread_s)
    blank = jnp.zeros((TWICE - 16, LANES), F32)
    values = []
    for k in range(pieces):
        for pair in range(2):
            halves = []
            for half in range(2):
                c = 2 * k + half
                off = 2 * LANES * pair
                rows_c = spread[16 * c:16 * (c + 1)]
                inside = c * LANES + lane_iota((16, LANES)) < length // 4
                first, second = (
                    jnp.concatenate([jnp.where(inside, rows_c[:, o:o + LANES], 0.0), blank], axis=0)
                    for o in (off, off + LANES)
                )
                halves.append(first + pltpu.roll(second, used, 0))
            values.append(jnp.concatenate(halves, axis=1))
    values = jnp.concatenate(values, axis=0).astype(BF16)

    turns = 4 * pieces
    block = 2 * LANES
    steps = phase_steps(turns, block)
    period = jnp.full((1, block), length, jnp.int32).astype(F32)
    inverse = 1.0 / period
    for i in range(slots // block):
        at = pl.ds(i * block, block)
        wave = wave_s[:, at]
        wave = jnp.concatenate([wave] * ((turns + 16) // 8), axis=0)
        co, si = turn(steps * wave, period, inverse)
        one = wave[0:1]
        weight = jnp.where(one == 0.0, 1.0, 2.0)
        weight = jnp.where((one >= 0.0) & (one <= jnp.full(one.shape, top, jnp.int32).astype(F32)), weight, 0.0)
        fc[:, at] = co[0:turns] * weight
        fs[:, at] = si[0:turns] * weight
        c_all = co[turns:turns + 8]
        s_all = si[turns:turns + 8]
        size, step = 8, turns + 8
        while size < DEEP:
            c1 = co[step:step + 1]
            s1 = si[step:step + 1]
            c_new = c_all * c1 - s_all * s1
            s_new = s_all * c1 + c_all * s1
            c_all = jnp.concatenate([c_all, c_new], axis=0)
            s_all = jnp.concatenate([s_all, s_new], axis=0)
            size, step = 2 * size, step + 1
        c_all = c_all.astype(BF16)
        s_all = s_all.astype(BF16)
        tc[:, at] = c_all
        ts[:, at] = s_all
        inner_c = dot(values, c_all)
        inner_s = dot(values, s_all)
        real = jnp.zeros((TWICE, block), F32)
        imag = jnp.zeros((TWICE, block), F32)
        for g in range(turns // 2):
            c1 = two_phases(fc, g, at, used, block)
            s1 = two_phases(fs, g, at, used, block)
            part_c = inner_c[TWICE * g:TWICE * (g + 1)]
            part_s = inner_s[TWICE * g:TWICE * (g + 1)]
            real = real + (c1 * part_c - s1 * part_s)
            imag = imag - (c1 * part_s + s1 * part_c)
        both = jnp.concatenate([real, imag], axis=0) * jnp.where(one == 0.0, 1.0, 0.5)
        xt[:, at] = jnp.concatenate(split(both), axis=0)

    turned = jnp.concatenate(
        [xt[:, owners * 8 * t:owners * 8 * (t + 1)] for t in range(groups)], axis=0
    )
    total = dot(packing, turned)
    scale = 1.0 / jnp.sqrt(jnp.full(total.shape, length, jnp.int32).astype(F32))
    msg_ref[...] = jnp.transpose(total * scale).reshape(owners, 8, LANES)


def inverse_kernel(
    groups, len_hbm, band_hbm, tc, ts, fc, fs, msg_ref, grid_ref,
    len_ref, band_ref, sems, os,
):
    copies = start_all((len_hbm, band_hbm), (len_ref, band_ref), sems)
    spread_s = spread_matrix()
    fields, _, rows, width = grid_ref.shape
    owners = msg_ref.shape[0]
    slots = tc.shape[1]
    turns = fc.shape[0]
    unit = rows * fields * 2
    high, low = split(msg_ref[...].reshape(owners * 8, LANES))
    pieces = jnp.concatenate([high, low], axis=1)
    used = rows * fields
    tall = 2 * TWICE
    shape = (tall, LANES)
    base = slot_lane(row_iota(shape), fields, rows)
    places = []
    for t in range(groups):
        source = (base + unit * t + lax.axis_index("fld") * (fields * 2)) & (LANES - 1)
        source = jnp.where(base < 0, base, source)
        places.append(jnp.where(lane_iota(shape) == source, 1.0, 0.0))
    place = jnp.concatenate(places, axis=0).astype(BF16)
    place = jnp.concatenate([place, place], axis=1)
    turned = dot_nt(place, pieces)
    block = 2 * LANES
    out = jnp.zeros((TWICE * turns // 2, DEEP), F32)
    for i in range(slots // block):
        t, off = divmod(i * block, owners * 8)
        real = turned[tall * t:tall * t + TWICE, off:off + block]
        imag = turned[tall * t + TWICE:tall * (t + 1), off:off + block]
        at = pl.ds(i * block, block)
        reals, imags = [], []
        for g in range(turns // 2):
            c1 = two_phases(fc, g, at, used, block)
            s1 = two_phases(fs, g, at, used, block)
            reals.append(c1 * real - s1 * imag)
            imags.append(s1 * real + c1 * imag)
        reals = jnp.concatenate(reals, axis=0).astype(BF16)
        imags = jnp.concatenate(imags, axis=0).astype(BF16)
        out = out + (dot_nt(reals, tc[:, at]) - dot_nt(imags, ts[:, at]))
    wait_all(copies)
    length = len_ref[band_ref[lax.axis_index("lat")]]
    out = out * (1.0 / jnp.sqrt(jnp.full(out.shape, length, jnp.int32).astype(F32)))
    chunks = os.shape[0] // 16
    for c in range(chunks):
        off = LANES * (c % 2)
        for phase in range(4):
            at = (2 * (c // 2) + phase // 2) * TWICE
            piece = out[at:at + TWICE, off:off + LANES]
            if phase % 2:
                piece = pltpu.roll(piece, TWICE - used, 0)
            os[16 * c:16 * (c + 1), LANES * phase:LANES * (phase + 1)] = piece[0:16].astype(BF16)
    merged = dot_nt(os[...], spread_s)
    for c in range(chunks):
        begin = 4 * LANES * c
        size = min(4 * LANES, width - begin)
        if size <= 0:
            continue
        inside = begin + lane_iota((16, size)) < length
        piece = jnp.where(inside, merged[16 * c:16 * (c + 1), 0:size], 0.0)
        for field in range(fields):
            grid_ref[field, 0, :, begin:begin + size] = piece[
                rows * field:rows * (field + 1)
            ].astype(BF16)


def prepare_kernel(
    cut_off, pairs, fields, rows, fold_hbm, band_hbm, rates_hbm, leg_hbm, tm_hbm, bm_hbm,
    near_ref, far_hbm, mix_ref, back_ref, turn_ref, tau_ref, rate_ref,
    fold_ref, band_ref, rates_ref, leg_ref, tm_ref, bm_ref, sems, pad_s, far_ref, out_sems,
):
    copies = start_all(
        (fold_hbm, band_hbm, rates_hbm, tm_hbm, bm_hbm, leg_hbm),
        (fold_ref, band_ref, rates_ref, tm_ref, bm_ref, leg_ref),
        sems,
    )
    wait_all(copies[:-1])
    everyone = tm_ref.shape[0]
    _, lats, places = leg_ref.shape
    groups_f = everyone // fields
    wf = fields * 2
    unit = rows * wf
    span = near_ref.shape[1]
    eight = 8 * lats
    close = near_ref.shape[0] // (2 * eight)
    groups = close + far_ref.shape[0] // (2 * eight)
    owner = lax.axis_index("lat") * groups_f + lax.axis_index("fld")

    pad_s[...] = jnp.zeros(pad_s.shape, F32)
    pad_s[0:everyone, 0:everyone] = tm_ref[...]
    shape = (LANES, LANES)
    level = (lane_iota(shape) // unit) * fields + (lane_iota(shape) % wf) // 2
    pick = jnp.where(row_iota(shape) == level, 1.0, 0.0).astype(BF16)
    lane = lane_iota((KPAD, LANES))
    parts = []
    for piece in split(pad_s[...]):
        wide = dot(piece, pick)
        total = []
        for r in range(rows):
            for c in range(2):
                keep = ((lane % unit) // wf == r) & (lane % 2 == c) & (lane < unit * groups_f)
                total.append(jnp.where(keep, wide, 0.0))
        parts.append(jnp.concatenate(total, axis=0).astype(BF16))
    mix_ref[...] = jnp.concatenate([parts[0], parts[1], parts[0]], axis=1)

    pad_s[...] = jnp.zeros(pad_s.shape, F32)
    pad_s[0:everyone, 0:everyone] = bm_ref[...]
    shape = (FPAD, KPAD)
    expand = jnp.where(row_iota(shape) // 2 == lane_iota(shape), 1.0, 0.0).astype(BF16)
    shape = (LANES, 2 * LANES)
    repeat = jnp.where(row_iota(shape) == lane_iota(shape) % KPAD, 1.0, 0.0).astype(BF16)
    shape = (FPAD, 2 * LANES)
    same = row_iota(shape) % 2 == (lane_iota(shape) // KPAD) % 2
    fulls = []
    for part, piece in enumerate(split(pad_s[...])):
        full = jnp.where(same, dot(dot(expand, piece).astype(BF16), repeat), 0.0)
        back_ref[part * FPAD:(part + 1) * FPAD, :] = full[:, 0:8 * KPAD].astype(BF16)
        fulls.append(full)
    turn = jnp.where(lane_iota(shape) < 4 * KPAD, fulls[0], fulls[1])
    turn_ref[...] = turn[:, 0:6 * KPAD].astype(BF16)

    row = row_iota((KPAD, 2 * LANES))
    rate = jnp.zeros((KPAD, 2 * LANES), F32)
    for k in range(everyone):
        rate = jnp.where(row == k, rates_ref[k], rate)
    rate_ref[...] = rate
    paired = tau_ref.shape[0]
    row = row_iota((paired, LANES))
    waves = []
    wave = jnp.zeros((paired, LANES), jnp.int32)
    for pair in range(4 * groups):
        waves.append(fold_ref[owner, 2 * min(pair, pairs - 1)])
        wave = jnp.where(row == pair, waves[pair], wave)
    wave = jnp.concatenate([wave] * (span // LANES), axis=1)
    line = lane_iota((paired, span))
    degree = jnp.where(line > cut_off - wave, line - 1, line + wave)
    tau_ref[...] = (degree * (degree + 1)).astype(F32) * (1.0 / float(cut_off * (cut_off + 1)))

    quad_rows = 4 * lats
    shape = (quad_rows, quad_rows)
    band = jnp.zeros(shape, jnp.int32)
    for holder in range(lats):
        band = jnp.where(row_iota(shape) % lats == holder, band_ref[holder], band)
    order = jnp.where(
        (row_iota(shape) // lats == lane_iota(shape) // lats) & (lane_iota(shape) % lats == band),
        1.0,
        0.0,
    ).astype(BF16)

    whole = places // LANES * LANES
    line = lane_iota((quad_rows, span))
    row = row_iota((quad_rows, LANES)) // lats
    copies[-1].wait()
    keeps = []
    for t in range(groups):
        wave = jnp.zeros((quad_rows, LANES), jnp.int32)
        last = jnp.zeros((quad_rows, LANES), jnp.int32)
        stack = []
        for pp in range(4):
            there = 4 * t + pp < pairs
            index = min(4 * t + pp, pairs - 1)
            wave = jnp.where(row == pp, waves[4 * t + pp], wave)
            last = jnp.where(row == pp, places - 1 if there else -1, last)
            stack.append(
                jnp.concatenate(
                    [
                        leg_ref[index, :, 0:whole],
                        jnp.broadcast_to(leg_ref[index, :, whole:places], (lats, span - whole)),
                    ],
                    axis=1,
                )
            )
        wave = jnp.concatenate([wave] * (span // LANES), axis=1)
        last = jnp.concatenate([last] * (span // LANES), axis=1)
        leg = dot(order, jnp.concatenate(stack, axis=0).astype(BF16))
        before = line <= cut_off - wave
        first = before & (line <= last)
        second = jnp.logical_not(before) & (line <= last)
        odd = ((line + jnp.where(before, 0, wave)) & 1) == 1
        signed = jnp.where(odd, -leg, leg)
        for r, rowset in enumerate((leg, signed)):
            near = jnp.where(first, rowset, 0.0)
            far = jnp.where(second, rowset, 0.0)
            for pp in range(4):
                at = 2 * eight * (t if t < close else t - close) + r * eight + 2 * pp * lats
                hold = near_ref if t < close else far_ref
                hold[at:at + 2 * lats, :] = jnp.concatenate(
                    [near[pp * lats:(pp + 1) * lats], far[pp * lats:(pp + 1) * lats]], axis=0
                ).astype(BF16)
        if t >= close:
            part = pl.ds(2 * eight * (t - close), 2 * eight)
            keeps.append(
                pltpu.make_async_copy(far_ref.at[part], far_hbm.at[part], out_sems.at[t - close])
            )
            keeps[-1].start()
    wait_all(keeps)


def solve_kernel(
    fields, rows, lats, legs_hbm, legs_ref, msg_ref, mix_ref, turn_ref, tau_ref, rate_ref,
    near_ref, far_hbm, out_ref, cs, eh_ref, far_ref, in_sem, out_sems,
):
    eight = 8 * lats
    close = legs_ref.shape[0] // (2 * eight)
    groups = close + eh_ref.shape[0] // (2 * eight)
    fetch = pltpu.make_async_copy(legs_hbm, eh_ref, in_sem)
    fetch.start()
    quads = [legs_ref.at[pl.ds(2 * eight * t, 2 * eight)] for t in range(close)]
    quads += [eh_ref.at[pl.ds(2 * eight * t, 2 * eight)] for t in range(groups - close)]
    groups_f = msg_ref.shape[0] // eight
    wf = fields * 2
    unit = rows * wf
    span = legs_ref.shape[1]
    deep = 8 * KPAD
    near = near_ref.shape[0] // deep
    holds = [(near_ref, deep * t) for t in range(near)]
    holds += [(far_ref, deep * t) for t in range(groups - near)]
    lane = lane_iota((lats, LANES))
    tiles = [
        [msg_ref[pl.ds(8 * g + i8, lats, stride=8 * groups_f), :] for g in range(groups_f)]
        for i8 in range(8)
    ]
    tall = []
    for t in range(groups):
        here = [lanes_within(lane, unit * (t + g), unit) for g in range(groups_f)]
        for i8 in range(8):
            line = tiles[i8][0]
            for g in range(1, groups_f):
                line = jnp.where(here[g], tiles[i8][g], line)
            if t:
                line = pltpu.roll(line, LANES - unit * t, 1)
            tall.append(line)
    v_high, v_low = split(jnp.concatenate(tall, axis=0))
    mixed = dot_nt(mix_ref[...], jnp.concatenate([v_high, v_high, v_low], axis=1))

    rate = rate_ref[...]
    slot_pair = (lane_iota((2 * KPAD, 2 * eight)) % eight) // (2 * lats)
    lefts = []
    for t in range(groups):
        mine = mixed[:, eight * t:eight * (t + 1)]
        mine = jnp.concatenate([mine[0:2 * KPAD], mine[2 * KPAD:4 * KPAD]], axis=1)
        left = jnp.concatenate([jnp.where(slot_pair == pp, mine, 0.0) for pp in range(4)], axis=0)
        lefts.append(jnp.concatenate(split(left), axis=1))

    keeps = []
    for t in range(groups):
        left = lefts[t]
        if t == close:
            fetch.wait()
        for start in range(0, span, 2 * LANES):
            size = min(2 * LANES, span - start)
            right = quads[t][:, start:start + size]
            modes = dot(left, jnp.concatenate([right, right], axis=0))
            damped = []
            for pp in range(4):
                tau = tau_ref[4 * t + pp:4 * t + pp + 1, start:start + size]
                below = 1.0 + tau * rate[:, 0:size]
                factor = pl.reciprocal(below, approx=True)
                at = 2 * pp * KPAD
                damped.append(modes[at:at + KPAD] * factor)
                damped.append(modes[at + KPAD:at + 2 * KPAD] * factor)
            hold, at = holds[t]
            hold[at:at + deep, start:start + size] = jnp.concatenate(damped, axis=0).astype(BF16)
        if t >= near:
            part = pl.ds(deep * (t - near), deep)
            keeps.append(
                pltpu.make_async_copy(far_ref.at[part], far_hbm.at[part], out_sems.at[t - near])
            )
            keeps[-1].start()

    picks = []
    for t in range(groups):
        hold, at = holds[t]
        product = dot_nt(hold[at:at + deep, :], quads[t][...])
        pick = product[0:2 * KPAD]
        for pp in range(1, 4):
            pick = jnp.where(slot_pair == pp, product[2 * KPAD * pp:2 * KPAD * (pp + 1)], pick)
        picks.append(pick)
    high, low = split(jnp.concatenate(picks, axis=1))
    back = dot(turn_ref[...], jnp.concatenate([high, low, high], axis=0))
    back = jnp.concatenate([back, jnp.zeros((LANES - FPAD, back.shape[1]), F32)], axis=0)
    for at in range(0, back.shape[1], LANES):
        cs[at:at + LANES, :] = jnp.transpose(back[:, at:at + LANES])

    lane = lane_iota((8, LANES))
    here = [
        lanes_within(lane, wf * u, wf) for u in range(rows * groups + groups_f - 1)
    ]
    for holder in range(lats):
        tiles = [jnp.zeros((8, LANES), F32) for _ in range(groups_f)]
        for u in range(rows * groups):
            piece = cs[pl.ds(u * eight + holder, 8, stride=lats), :]
            if u:
                piece = pltpu.roll(piece, wf * u, 1)
            for g in range(groups_f):
                tiles[g] = jnp.where(here[u + g], piece, tiles[g])
        for g in range(groups_f):
            at = (holder * groups_f + g) * 8
            out_ref[at:at + 8, :] = tiles[g]
    wait_all(keeps)


def output_kernel(near_ref, far_hbm, back_ref, spec_ref, bk, far_s, sems):
    everyone, quad, _, places = spec_ref.shape
    span = near_ref.shape[1]
    deep = 8 * KPAD
    near = near_ref.shape[0] // deep
    tall = 2 * everyone
    step = pl.program_id(0)

    def far_copy(t):
        part = pl.ds(pl.multiple_of(deep * t, deep), deep)
        return pltpu.make_async_copy(far_hbm.at[part], far_s.at[part], sems.at[t])

    @pl.when(step == 0)
    def _():
        for t in range(sems.shape[0]):
            far_copy(t).start()
        pair_of = lane_iota((tall, deep)) // (2 * KPAD)
        rows = []
        for part in range(2):
            full = back_ref[part * FPAD:part * FPAD + tall, :].astype(F32)
            for pp in range(4):
                rows.append(jnp.where(pair_of == pp, full, 0.0))
        bk[...] = jnp.concatenate(rows, axis=0).astype(BF16)

    def write(source, at):
        for start in range(0, span, 2 * LANES):
            size = min(2 * LANES, span - start)
            spec = dot(bk[...], source[pl.ds(at, deep), start:start + size])
            spec = spec[0:4 * tall] + spec[4 * tall:]
            kept = min(size, places - start)
            for pp in range(4):
                for f in range(everyone):
                    row = pp * tall + 2 * f
                    spec_ref[f, pp, :, start:start + kept] = spec[row:row + 2, 0:kept]

    @pl.when(step < near)
    def _():
        write(near_ref, pl.multiple_of(deep * step, deep))

    @pl.when(step >= near)
    def _():
        far_copy(step - near).wait()
        write(far_s, pl.multiple_of(deep * (step - near), deep))


def per_device(grid, row_lengths, band_map, fold_map, legendre, to_modes, back_modes, mode_rates):
    fields, single, rows, width = grid.shape
    pairs, places, lats = legendre.shape
    cut_off = places - 2
    everyone = to_modes.shape[0]
    owners, per_owner = fold_map.shape
    groups = -(-per_owner // 8)
    slots = owners * groups * 8
    pieces = -(-(width // 4) // DEEP)
    turns = 4 * pieces
    span = -(-places // LANES) * LANES
    hbm = pl.BlockSpec(memory_space=pltpu.HBM)
    vmem = pl.BlockSpec(memory_space=pltpu.VMEM)
    room = pltpu.CompilerParams(vmem_limit_bytes=ROOM)
    message = pltpu.HBM((owners, 8, LANES), F32)
    holders = band_map.shape[0]
    groups_f = everyone // fields
    dma = pltpu.SemaphoreType.DMA
    row_lengths, band_map, fold_map, to_modes, back_modes, mode_rates, grid = (
        pltpu.with_memory_space_constraint(x, pltpu.HBM)
        for x in (row_lengths, band_map, fold_map, to_modes, back_modes, mode_rates, grid)
    )
    legendre = pltpu.with_memory_space_constraint(jnp.transpose(legendre, (0, 2, 1)), pltpu.HBM)

    sending, cos_table, sin_table, cos_turn, sin_turn = pl.pallas_call(
        functools.partial(forward_kernel, cut_off, groups),
        out_shape=(
            message,
            pltpu.VMEM((DEEP, slots), BF16),
            pltpu.VMEM((DEEP, slots), BF16),
            pltpu.VMEM((turns, slots), F32),
            pltpu.VMEM((turns, slots), F32),
        ),
        in_specs=[hbm] * 4,
        out_specs=(vmem,) * 5,
        scratch_shapes=[
            pltpu.SMEM(row_lengths.shape, jnp.int32),
            pltpu.SMEM(band_map.shape, jnp.int32),
            pltpu.VMEM(fold_map.shape, jnp.int32),
            pltpu.VMEM(grid.shape, BF16),
            dma((4,)),
            pltpu.VMEM((LANES, LANES), F32),
            pltpu.VMEM((8, slots), F32),
            pltpu.VMEM((16, 4 * DEEP * pieces), F32),
            pltpu.VMEM((4 * TWICE, slots), BF16),
        ],
        compiler_params=room,
        name="forward_rows",
    )(row_lengths, band_map, fold_map, grid)
    tables = [
        pltpu.with_memory_space_constraint(x, pltpu.VMEM)
        for x in (cos_table, sin_table, cos_turn, sin_turn)
    ]
    arrived = lax.all_to_all(sending, ("lat", "fld"), split_axis=0, concat_axis=0, tiled=True)

    close = 1
    legs, legs_far, mix, back, turn_back, tau, rate = pl.pallas_call(
        functools.partial(prepare_kernel, cut_off, pairs, fields, rows),
        out_shape=(
            pltpu.VMEM((close * 16 * lats, span), BF16),
            pltpu.HBM(((groups - close) * 16 * lats, span), BF16),
            pltpu.VMEM((2 * rows * KPAD, 3 * LANES), BF16),
            pltpu.VMEM((2 * FPAD, 8 * KPAD), BF16),
            pltpu.VMEM((FPAD, 6 * KPAD), BF16),
            pltpu.VMEM((-(-groups * 4 // 8) * 8, span), F32),
            pltpu.VMEM((KPAD, 2 * LANES), F32),
        ),
        in_specs=[hbm] * 6,
        out_specs=(vmem, hbm) + (vmem,) * 5,
        scratch_shapes=[
            pltpu.SMEM(fold_map.shape, jnp.int32),
            pltpu.SMEM(band_map.shape, jnp.int32),
            pltpu.SMEM(mode_rates.shape, F32),
            pltpu.VMEM((pairs, lats, places), F32),
            pltpu.VMEM(to_modes.shape, F32),
            pltpu.VMEM(back_modes.shape, F32),
            dma((6,)),
            pltpu.VMEM((KPAD, LANES), F32),
            pltpu.VMEM(((groups - close) * 16 * lats, span), BF16),
            dma((groups - close,)),
        ],
        compiler_params=room,
        cost_estimate=pl.CostEstimate(flops=10**8, bytes_accessed=8 * 10**6, transcendentals=0),
        name="prepare",
    )(fold_map, band_map, mode_rates, legendre, to_modes, back_modes)
    legs_far = pltpu.with_memory_space_constraint(legs_far, pltpu.HBM)
    legs, mix, back, turn_back, tau, rate = (
        pltpu.with_memory_space_constraint(x, pltpu.VMEM)
        for x in (legs, mix, back, turn_back, tau, rate)
    )

    near = groups // 2
    damped_near, damped_far, leaving = pl.pallas_call(
        functools.partial(solve_kernel, fields, rows, lats),
        out_shape=(
            pltpu.VMEM((near * 8 * KPAD, span), BF16),
            pltpu.HBM(((groups - near) * 8 * KPAD, span), BF16),
            pltpu.HBM((owners * 8, LANES), F32),
        ),
        in_specs=[hbm] + [vmem] * 6,
        out_specs=(vmem, hbm, vmem),
        scratch_shapes=[
            pltpu.VMEM((groups * 16 * lats, LANES), F32),
            pltpu.VMEM(((groups - close) * 16 * lats, span), BF16),
            pltpu.VMEM(((groups - near) * 8 * KPAD, span), BF16),
            dma,
            dma((groups - near,)),
        ],
        compiler_params=room,
        name="solve",
    )(legs_far, legs, arrived.reshape(owners * 8, LANES), mix, turn_back, tau, rate)
    leaving = leaving.reshape(owners, 8, LANES)

    returned = lax.all_to_all(leaving, ("lat", "fld"), split_axis=0, concat_axis=0, tiled=True)

    damped_near = pltpu.with_memory_space_constraint(damped_near, pltpu.VMEM)
    damped_far = pltpu.with_memory_space_constraint(damped_far, pltpu.HBM)
    spectral = pl.pallas_call(
        output_kernel,
        grid=(groups,),
        out_shape=jax.ShapeDtypeStruct((everyone, pairs, 2, places), F32),
        in_specs=[
            pl.BlockSpec((near * 8 * KPAD, span), lambda t: (0, 0)),
            hbm,
            pl.BlockSpec((2 * FPAD, 8 * KPAD), lambda t: (0, 0)),
        ],
        out_specs=pl.BlockSpec((everyone, 4, 2, places), lambda t: (0, t, 0, 0)),
        scratch_shapes=[
            pltpu.VMEM((16 * everyone, 8 * KPAD), BF16),
            pltpu.VMEM(((groups - near) * 8 * KPAD, span), BF16),
            dma((groups - near,)),
        ],
        compiler_params=pltpu.CompilerParams(
            dimension_semantics=("arbitrary",), vmem_limit_bytes=ROOM
        ),
        cost_estimate=pl.CostEstimate(flops=10**8, bytes_accessed=8 * 10**6, transcendentals=0),
        name="spectral_output",
    )(damped_near, damped_far, back)

    grid_out = pl.pallas_call(
        functools.partial(inverse_kernel, groups),
        out_shape=jax.ShapeDtypeStruct(grid.shape, BF16),
        in_specs=[hbm] * 2 + [vmem] * 5,
        out_specs=vmem,
        scratch_shapes=[
            pltpu.SMEM(row_lengths.shape, jnp.int32),
            pltpu.SMEM(band_map.shape, jnp.int32),
            dma((2,)),
            pltpu.VMEM((32 * pieces, 4 * LANES), BF16),
        ],
        compiler_params=room,
        name="inverse_rows",
    )(row_lengths, band_map, *tables, returned)
    return (jnp.transpose(spectral, (0, 2, 1, 3)), grid_out)


def solution(mesh):
    placed = (
        P("fld", "lat", None, None),
        P(),
        P(),
        P(),
        P(("lat", "fld"), None, None),
        P(),
        P(),
        P(),
    )
    return jax.shard_map(
        per_device,
        mesh=mesh,
        in_specs=placed,
        out_specs=(P(None, None, ("lat", "fld"), None), P("fld", "lat", None, None)),
        check_vma=False,
    )
```

```python
import functools
import math

import jax
import jax.numpy as jnp
from jax import lax
from jax.experimental import pallas as pl
from jax.experimental.pallas import tpu as pltpu
from jax.sharding import PartitionSpec as P

LANES = 128
KPAD = 24
FPAD = 64
DEEP = 256
TWICE = 24
ROOM = 24 * 1024 * 1024
F32 = jnp.float32
BF16 = jnp.bfloat16
NT_DIMS = (((1,), (1,)), ((), ()))
SIN_POLY = (
    6.283185302447051,
    -41.34170038368319,
    81.60513023312113,
    -76.70299324464969,
    42.02573766814694,
    -14.899106966102595,
    3.237062655726421,
)
COS_POLY = (
    0.9999999889083757,
    -19.739204448887243,
    64.93911476570418,
    -85.45008785413638,
    60.167188450194914,
    -25.9658703083255,
    6.526145851512229,
)


def dot(a, b):
    return jnp.dot(a, b, preferred_element_type=F32)


def dot_nt(a, b):
    return lax.dot_general(a, b, NT_DIMS, preferred_element_type=F32)


def split(x):
    high = x.astype(BF16)
    return high, (x - high.astype(F32)).astype(BF16)


def horner(coefs, z):
    total = coefs[-1] * z + coefs[-2]
    for coef in coefs[-3::-1]:
        total = total * z + coef
    return total


def turn(steps, period, inverse):
    rest = steps - period * jnp.floor(steps * inverse + 0.5)
    part = rest * inverse
    z = part * part
    return horner(COS_POLY, z), part * horner(SIN_POLY, z)


def start_all(sources, targets, sems):
    copies = [
        pltpu.make_async_copy(source, target, sems.at[i])
        for i, (source, target) in enumerate(zip(sources, targets))
    ]
    for copy in copies:
        copy.start()
    return copies


def wait_all(copies):
    for copy in copies:
        copy.wait()


def lane_iota(shape):
    return lax.broadcasted_iota(jnp.int32, shape, len(shape) - 1)


def row_iota(shape):
    return lax.broadcasted_iota(jnp.int32, shape, len(shape) - 2)


def lanes_within(lane, start, size):
    start %= LANES
    if start + size <= LANES:
        return (lane >= start) & (lane < start + size)
    return (lane >= start) | (lane < start + size - LANES)


def spread_matrix():
    shape = (4 * LANES, LANES)
    picks = []
    for phase in range(4):
        picks.append(jnp.where(row_iota(shape) == 4 * lane_iota(shape) + phase, 1.0, 0.0))
    return jnp.concatenate(picks, axis=1).astype(BF16)


def phase_steps(groups, lanes):
    row = row_iota((groups + 16, lanes))
    steps = jnp.where(row < groups, (row >> 2) * (4 * DEEP) + (row & 3), 4 * (row - groups))
    steps = jnp.where(row >= groups + 8, 32 << jnp.maximum(row - groups - 8, 0), steps)
    return steps.astype(F32)


def slot_lane(index, fields, rows):
    used = rows * fields
    part = (index >= TWICE).astype(jnp.int32)
    row = index - TWICE * part
    vec = jnp.where(row >= used, row - used, row)
    lane = lax.rem(vec, rows) * (fields * 2) + lax.div(vec, rows) * 2 + part
    return jnp.where(row < 2 * used, lane, -LANES)


def two_phases(ref, g, at, used, block):
    first = ref[2 * g:2 * g + 1, at]
    second = ref[2 * g + 1:2 * g + 2, at]
    tiles = []
    for low in range(0, TWICE, 8):
        if low + 8 <= used:
            tiles.append(jnp.broadcast_to(first, (8, block)))
        elif low >= used:
            tiles.append(jnp.broadcast_to(second, (8, block)))
        else:
            tiles.append(jnp.where(low + row_iota((8, block)) < used, first, second))
    return jnp.concatenate(tiles, axis=0)


def forward_kernel(
    cut_off, groups, len_hbm, band_hbm, fold_hbm, grid_hbm,
    msg_ref, tc, ts, fc, fs,
    len_ref, band_ref, fold_ref, grid_ref, sems, fold_s, wave_s, xs, xt,
):
    copies = start_all(
        (len_hbm, band_hbm, fold_hbm, grid_hbm), (len_ref, band_ref, fold_ref, grid_ref), sems
    )
    fields, _, rows, width = grid_ref.shape
    owners, per_owner = fold_ref.shape
    slots = tc.shape[1]
    pieces = xs.shape[1] // (4 * DEEP)
    unit = rows * fields * 2
    used = rows * fields
    spread_s = spread_matrix()
    shape = (LANES, owners * 8)
    repeat = jnp.where(row_iota(shape) == lane_iota(shape) >> 3, 1.0, 0.0).astype(BF16)
    shape = (8 * groups, 16 * groups)
    weigh = jnp.where(
        jnp.where(lane_iota(shape) < 8 * groups, lane_iota(shape), lane_iota(shape) - 8 * groups) >> 3
        == row_iota(shape) >> 3,
        jnp.where(lane_iota(shape) < 8 * groups, 8.0, 1.0),
        0.0,
    ).astype(BF16)
    tall = 4 * TWICE
    shape = (LANES, tall * groups)
    one = (1, 2 * TWICE)
    base = slot_lane(lane_iota(one), fields, rows)
    targets = []
    for t in range(groups):
        target = base + unit * (t + lax.axis_index("fld"))
        target = jnp.where(base < 0, base, target & (LANES - 1))
        targets += [target, target]
    target = jnp.concatenate(targets, axis=1)
    packing = jnp.where(row_iota(shape) == target, 1.0, 0.0).astype(BF16)
    fold_s[...] = jnp.full(fold_s.shape, -1.0, F32)
    xs[...] = jnp.zeros(xs.shape, F32)
    wait_all(copies)
    length = len_ref[band_ref[lax.axis_index("lat")]]
    top = jnp.minimum(cut_off, (length - 1) // 2)

    fold_s[0:owners, 0:per_owner] = fold_ref[...].astype(F32)
    turned = jnp.transpose(fold_s[...])[0:8 * groups]
    eights = jnp.floor(turned * 0.125)
    parts = jnp.concatenate([eights, turned - 8.0 * eights], axis=0).astype(BF16)
    repeated = dot(parts, repeat)
    own = (lane_iota(repeated.shape) & 7) == (row_iota(repeated.shape) & 7)
    waves = dot(weigh, jnp.where(own, repeated, 0.0).astype(BF16))
    for t in range(groups):
        wave_s[:, owners * 8 * t:owners * 8 * (t + 1)] = waves[8 * t:8 * t + 8]

    for field in range(fields):
        xs[rows * field:rows * (field + 1), 0:width] = grid_ref[field, 0].astype(F32)
    stacked = jnp.concatenate(
        [xs[:, 4 * LANES * c:4 * LANES * (c + 1)] for c in range(2 * pieces)], axis=0
    ).astype(BF16)
    spread = dot(stacked, spread_s)
    blank = jnp.zeros((TWICE - 16, LANES), F32)
    values = []
    for k in range(pieces):
        for pair in range(2):
            halves = []
            for half in range(2):
                c = 2 * k + half
                off = 2 * LANES * pair
                rows_c = spread[16 * c:16 * (c + 1)]
                inside = c * LANES + lane_iota((16, LANES)) < length // 4
                first, second = (
                    jnp.concatenate([jnp.where(inside, rows_c[:, o:o + LANES], 0.0), blank], axis=0)
                    for o in (off, off + LANES)
                )
                halves.append(first + pltpu.roll(second, used, 0))
            values.append(jnp.concatenate(halves, axis=1))
    values = jnp.concatenate(values, axis=0).astype(BF16)

    turns = 4 * pieces
    block = 2 * LANES
    steps = phase_steps(turns, block)
    period = jnp.full((1, block), length, jnp.int32).astype(F32)
    inverse = 1.0 / period
    def make_tables(i):
        at = pl.ds(i * block, block)
        wave = wave_s[:, at]
        wave = jnp.concatenate([wave] * ((turns + 16) // 8), axis=0)
        co, si = turn(steps * wave, period, inverse)
        one = wave[0:1]
        weight = jnp.where(one == 0.0, 1.0, 2.0)
        limit = jnp.full(one.shape, top, jnp.int32).astype(F32)
        weight = jnp.where((one >= 0.0) & (one <= limit), weight, 0.0)
        fc[:, at] = co[0:turns] * weight
        fs[:, at] = si[0:turns] * weight
        c_all = co[turns:turns + 8]
        s_all = si[turns:turns + 8]
        size, step = 8, turns + 8
        while size < DEEP:
            c1 = co[step:step + 1]
            s1 = si[step:step + 1]
            c_new = c_all * c1 - s_all * s1
            s_new = s_all * c1 + c_all * s1
            c_all = jnp.concatenate([c_all, c_new], axis=0)
            s_all = jnp.concatenate([s_all, s_new], axis=0)
            size, step = 2 * size, step + 1
        c_all = c_all.astype(BF16)
        s_all = s_all.astype(BF16)
        tc[:, at] = c_all
        ts[:, at] = s_all
        return c_all, s_all

    def finish(i, inner_c, inner_s):
        at = pl.ds(i * block, block)
        real = jnp.zeros((TWICE, block), F32)
        imag = jnp.zeros((TWICE, block), F32)
        for g in range(turns // 2):
            c1 = two_phases(fc, g, at, used, block)
            s1 = two_phases(fs, g, at, used, block)
            part_c = inner_c[TWICE * g:TWICE * (g + 1)]
            part_s = inner_s[TWICE * g:TWICE * (g + 1)]
            real = real + (c1 * part_c - s1 * part_s)
            imag = imag - (c1 * part_s + s1 * part_c)
        fix = jnp.where(wave_s[0:1, at] == 0.0, 1.0, 0.5)
        both = jnp.concatenate([real, imag], axis=0) * fix
        xt[:, at] = jnp.concatenate(split(both), axis=0)

    blocks = slots // block
    ready = make_tables(0)
    for i in range(blocks):
        inner_c = dot(values, ready[0])
        inner_s = dot(values, ready[1])
        if i + 1 < blocks:
            ready = make_tables(i + 1)
        finish(i, inner_c, inner_s)

    turned = jnp.concatenate(
        [xt[:, owners * 8 * t:owners * 8 * (t + 1)] for t in range(groups)], axis=0
    )
    total = dot(packing, turned)
    scale = 1.0 / jnp.sqrt(jnp.full(total.shape, length, jnp.int32).astype(F32))
    msg_ref[...] = jnp.transpose(total * scale).reshape(owners, 8, LANES)


def inverse_kernel(
    groups, len_hbm, band_hbm, tc, ts, fc, fs, msg_ref, grid_ref,
    len_ref, band_ref, sems, os,
):
    copies = start_all((len_hbm, band_hbm), (len_ref, band_ref), sems)
    spread_s = spread_matrix()
    fields, _, rows, width = grid_ref.shape
    owners = msg_ref.shape[0]
    slots = tc.shape[1]
    turns = fc.shape[0]
    unit = rows * fields * 2
    high, low = split(msg_ref[...].reshape(owners * 8, LANES))
    pieces = jnp.concatenate([high, low], axis=1)
    used = rows * fields
    tall = 2 * TWICE
    shape = (tall, LANES)
    base = slot_lane(row_iota(shape), fields, rows)
    places = []
    for t in range(groups):
        source = (base + unit * t + lax.axis_index("fld") * (fields * 2)) & (LANES - 1)
        source = jnp.where(base < 0, base, source)
        places.append(jnp.where(lane_iota(shape) == source, 1.0, 0.0))
    place = jnp.concatenate(places, axis=0).astype(BF16)
    place = jnp.concatenate([place, place], axis=1)
    turned = dot_nt(place, pieces)
    block = 2 * LANES
    out = jnp.zeros((TWICE * turns // 2, DEEP), F32)
    def twisted(i):
        t, off = divmod(i * block, owners * 8)
        real = turned[tall * t:tall * t + TWICE, off:off + block]
        imag = turned[tall * t + TWICE:tall * (t + 1), off:off + block]
        at = pl.ds(i * block, block)
        reals, imags = [], []
        for g in range(turns // 2):
            c1 = two_phases(fc, g, at, used, block)
            s1 = two_phases(fs, g, at, used, block)
            reals.append(c1 * real - s1 * imag)
            imags.append(s1 * real + c1 * imag)
        return (
            jnp.concatenate(reals, axis=0).astype(BF16),
            jnp.concatenate(imags, axis=0).astype(BF16),
        )

    blocks = slots // block
    ready = twisted(0)
    for i in range(blocks):
        at = pl.ds(i * block, block)
        part_r = dot_nt(ready[0], tc[:, at])
        part_i = dot_nt(ready[1], ts[:, at])
        if i + 1 < blocks:
            ready = twisted(i + 1)
        out = out + (part_r - part_i)
    wait_all(copies)
    length = len_ref[band_ref[lax.axis_index("lat")]]
    out = out * (1.0 / jnp.sqrt(jnp.full(out.shape, length, jnp.int32).astype(F32)))
    chunks = os.shape[0] // 16
    for c in range(chunks):
        off = LANES * (c % 2)
        for phase in range(4):
            at = (2 * (c // 2) + phase // 2) * TWICE
            piece = out[at:at + TWICE, off:off + LANES]
            if phase % 2:
                piece = pltpu.roll(piece, TWICE - used, 0)
            os[16 * c:16 * (c + 1), LANES * phase:LANES * (phase + 1)] = piece[0:16].astype(BF16)
    merged = dot_nt(os[...], spread_s)
    for c in range(chunks):
        begin = 4 * LANES * c
        size = min(4 * LANES, width - begin)
        if size <= 0:
            continue
        inside = begin + lane_iota((16, size)) < length
        piece = jnp.where(inside, merged[16 * c:16 * (c + 1), 0:size], 0.0)
        for field in range(fields):
            grid_ref[field, 0, :, begin:begin + size] = piece[
                rows * field:rows * (field + 1)
            ].astype(BF16)


def prepare_kernel(
    cut_off, pairs, fields, rows, fold_hbm, band_hbm, rates_hbm, leg_hbm, tm_hbm, bm_hbm,
    near_ref, far_hbm, mix_ref, back_ref, turn_ref, tau_ref, rate_ref,
    fold_ref, band_ref, rates_ref, leg_ref, tm_ref, bm_ref, sems, pad_s, far_ref, out_sems,
):
    copies = start_all(
        (fold_hbm, band_hbm, rates_hbm, tm_hbm, bm_hbm, leg_hbm),
        (fold_ref, band_ref, rates_ref, tm_ref, bm_ref, leg_ref),
        sems,
    )
    wait_all(copies[:-1])
    everyone = tm_ref.shape[0]
    _, lats, places = leg_ref.shape
    groups_f = everyone // fields
    wf = fields * 2
    unit = rows * wf
    span = near_ref.shape[1]
    eight = 8 * lats
    close = near_ref.shape[0] // (2 * eight)
    groups = close + far_ref.shape[0] // (2 * eight)
    owner = lax.axis_index("lat") * groups_f + lax.axis_index("fld")

    pad_s[...] = jnp.zeros(pad_s.shape, F32)
    pad_s[0:everyone, 0:everyone] = tm_ref[...]
    shape = (LANES, LANES)
    level = (lane_iota(shape) // unit) * fields + (lane_iota(shape) % wf) // 2
    pick = jnp.where(row_iota(shape) == level, 1.0, 0.0).astype(BF16)
    lane = lane_iota((KPAD, LANES))
    parts = []
    for piece in split(pad_s[...]):
        wide = dot(piece, pick)
        total = []
        for r in range(rows):
            for c in range(2):
                keep = ((lane % unit) // wf == r) & (lane % 2 == c) & (lane < unit * groups_f)
                total.append(jnp.where(keep, wide, 0.0))
        parts.append(jnp.concatenate(total, axis=0).astype(BF16))
    mix_ref[...] = jnp.concatenate([parts[0], parts[1], parts[0]], axis=1)

    pad_s[...] = jnp.zeros(pad_s.shape, F32)
    pad_s[0:everyone, 0:everyone] = bm_ref[...]
    shape = (FPAD, KPAD)
    expand = jnp.where(row_iota(shape) // 2 == lane_iota(shape), 1.0, 0.0).astype(BF16)
    shape = (LANES, 2 * LANES)
    repeat = jnp.where(row_iota(shape) == lane_iota(shape) % KPAD, 1.0, 0.0).astype(BF16)
    shape = (FPAD, 2 * LANES)
    same = row_iota(shape) % 2 == (lane_iota(shape) // KPAD) % 2
    fulls = []
    for part, piece in enumerate(split(pad_s[...])):
        full = jnp.where(same, dot(dot(expand, piece).astype(BF16), repeat), 0.0)
        back_ref[part * FPAD:(part + 1) * FPAD, :] = full[:, 0:8 * KPAD].astype(BF16)
        fulls.append(full)
    turn = jnp.where(lane_iota(shape) < 4 * KPAD, fulls[0], fulls[1])
    turn_ref[...] = turn[:, 0:6 * KPAD].astype(BF16)

    row = row_iota((KPAD, 2 * LANES))
    rate = jnp.zeros((KPAD, 2 * LANES), F32)
    for k in range(everyone):
        rate = jnp.where(row == k, rates_ref[k], rate)
    rate_ref[...] = rate
    paired = tau_ref.shape[0]
    row = row_iota((paired, LANES))
    waves = []
    wave = jnp.zeros((paired, LANES), jnp.int32)
    for pair in range(4 * groups):
        waves.append(fold_ref[owner, 2 * min(pair, pairs - 1)])
        wave = jnp.where(row == pair, waves[pair], wave)
    wave = jnp.concatenate([wave] * (span // LANES), axis=1)
    line = lane_iota((paired, span))
    degree = jnp.where(line > cut_off - wave, line - 1, line + wave)
    tau_ref[...] = (degree * (degree + 1)).astype(F32) * (1.0 / float(cut_off * (cut_off + 1)))

    quad_rows = 4 * lats
    shape = (quad_rows, quad_rows)
    band = jnp.zeros(shape, jnp.int32)
    for holder in range(lats):
        band = jnp.where(row_iota(shape) % lats == holder, band_ref[holder], band)
    order = jnp.where(
        (row_iota(shape) // lats == lane_iota(shape) // lats) & (lane_iota(shape) % lats == band),
        1.0,
        0.0,
    ).astype(BF16)

    whole = places // LANES * LANES
    line = lane_iota((quad_rows, span))
    row = row_iota((quad_rows, LANES)) // lats
    copies[-1].wait()
    keeps = []
    for t in range(groups):
        wave = jnp.zeros((quad_rows, LANES), jnp.int32)
        last = jnp.zeros((quad_rows, LANES), jnp.int32)
        stack = []
        for pp in range(4):
            there = 4 * t + pp < pairs
            index = min(4 * t + pp, pairs - 1)
            wave = jnp.where(row == pp, waves[4 * t + pp], wave)
            last = jnp.where(row == pp, places - 1 if there else -1, last)
            stack.append(
                jnp.concatenate(
                    [
                        leg_ref[index, :, 0:whole],
                        jnp.broadcast_to(leg_ref[index, :, whole:places], (lats, span - whole)),
                    ],
                    axis=1,
                )
            )
        wave = jnp.concatenate([wave] * (span // LANES), axis=1)
        last = jnp.concatenate([last] * (span // LANES), axis=1)
        leg = dot(order, jnp.concatenate(stack, axis=0).astype(BF16))
        before = line <= cut_off - wave
        first = before & (line <= last)
        second = jnp.logical_not(before) & (line <= last)
        odd = ((line + jnp.where(before, 0, wave)) & 1) == 1
        signed = jnp.where(odd, -leg, leg)
        for r, rowset in enumerate((leg, signed)):
            near = jnp.where(first, rowset, 0.0)
            far = jnp.where(second, rowset, 0.0)
            for pp in range(4):
                at = 2 * eight * (t if t < close else t - close) + r * eight + 2 * pp * lats
                hold = near_ref if t < close else far_ref
                hold[at:at + 2 * lats, :] = jnp.concatenate(
                    [near[pp * lats:(pp + 1) * lats], far[pp * lats:(pp + 1) * lats]], axis=0
                ).astype(BF16)
        if t >= close:
            part = pl.ds(2 * eight * (t - close), 2 * eight)
            keeps.append(
                pltpu.make_async_copy(far_ref.at[part], far_hbm.at[part], out_sems.at[t - close])
            )
            keeps[-1].start()
    wait_all(keeps)


def solve_kernel(
    fields, rows, lats, legs_hbm, legs_ref, msg_ref, mix_ref, turn_ref, tau_ref, rate_ref,
    near_ref, far_hbm, out_ref, cs, eh_ref, far_ref, in_sem, out_sems,
):
    eight = 8 * lats
    close = legs_ref.shape[0] // (2 * eight)
    groups = close + eh_ref.shape[0] // (2 * eight)
    fetch = pltpu.make_async_copy(legs_hbm, eh_ref, in_sem)
    fetch.start()
    quads = [legs_ref.at[pl.ds(2 * eight * t, 2 * eight)] for t in range(close)]
    quads += [eh_ref.at[pl.ds(2 * eight * t, 2 * eight)] for t in range(groups - close)]
    groups_f = msg_ref.shape[0] // eight
    wf = fields * 2
    unit = rows * wf
    span = legs_ref.shape[1]
    deep = 8 * KPAD
    near = near_ref.shape[0] // deep
    holds = [(near_ref, deep * t) for t in range(near)]
    holds += [(far_ref, deep * t) for t in range(groups - near)]
    lane = lane_iota((lats, LANES))
    tiles = [
        [msg_ref[pl.ds(8 * g + i8, lats, stride=8 * groups_f), :] for g in range(groups_f)]
        for i8 in range(8)
    ]
    tall = []
    for t in range(groups):
        here = [lanes_within(lane, unit * (t + g), unit) for g in range(groups_f)]
        for i8 in range(8):
            line = tiles[i8][0]
            for g in range(1, groups_f):
                line = jnp.where(here[g], tiles[i8][g], line)
            if t:
                line = pltpu.roll(line, LANES - unit * t, 1)
            tall.append(line)
    v_high, v_low = split(jnp.concatenate(tall, axis=0))
    mixed = dot_nt(mix_ref[...], jnp.concatenate([v_high, v_high, v_low], axis=1))

    rate = rate_ref[...]
    slot_pair = (lane_iota((2 * KPAD, 2 * eight)) % eight) // (2 * lats)
    lefts = []
    for t in range(groups):
        mine = mixed[:, eight * t:eight * (t + 1)]
        mine = jnp.concatenate([mine[0:2 * KPAD], mine[2 * KPAD:4 * KPAD]], axis=1)
        left = jnp.concatenate([jnp.where(slot_pair == pp, mine, 0.0) for pp in range(4)], axis=0)
        lefts.append(jnp.concatenate(split(left), axis=1))

    keeps = []

    def damp(t, start, modes):
        size = modes.shape[1]
        damped = []
        for pp in range(4):
            tau = tau_ref[4 * t + pp:4 * t + pp + 1, start:start + size]
            factor = pl.reciprocal(1.0 + tau * rate[:, 0:size], approx=True)
            at = 2 * pp * KPAD
            damped.append(modes[at:at + KPAD] * factor)
            damped.append(modes[at + KPAD:at + 2 * KPAD] * factor)
        hold, at = holds[t]
        hold[at:at + deep, start:start + size] = jnp.concatenate(damped, axis=0).astype(BF16)
        if t >= near and start + size == span:
            part = pl.ds(deep * (t - near), deep)
            keeps.append(
                pltpu.make_async_copy(far_ref.at[part], far_hbm.at[part], out_sems.at[t - near])
            )
            keeps[-1].start()

    waiting = None
    for t in range(groups):
        if t == close:
            fetch.wait()
        for start in range(0, span, 2 * LANES):
            size = min(2 * LANES, span - start)
            right = quads[t][:, start:start + size]
            modes = dot(lefts[t], jnp.concatenate([right, right], axis=0))
            if waiting is not None:
                damp(*waiting)
            waiting = (t, start, modes)
    damp(*waiting)

    def choose(product):
        pick = product[0:2 * KPAD]
        for pp in range(1, 4):
            pick = jnp.where(slot_pair == pp, product[2 * KPAD * pp:2 * KPAD * (pp + 1)], pick)
        return pick

    picks = []
    waiting = None
    for t in range(groups):
        hold, at = holds[t]
        product = dot_nt(hold[at:at + deep, :], quads[t][...])
        if waiting is not None:
            picks.append(choose(waiting))
        waiting = product
    picks.append(choose(waiting))
    high, low = split(jnp.concatenate(picks, axis=1))
    back = dot(turn_ref[...], jnp.concatenate([high, low, high], axis=0))
    back = jnp.concatenate([back, jnp.zeros((LANES - FPAD, back.shape[1]), F32)], axis=0)
    for at in range(0, back.shape[1], LANES):
        cs[at:at + LANES, :] = jnp.transpose(back[:, at:at + LANES])

    lane = lane_iota((8, LANES))
    here = [
        lanes_within(lane, wf * u, wf) for u in range(rows * groups + groups_f - 1)
    ]
    for holder in range(lats):
        tiles = [jnp.zeros((8, LANES), F32) for _ in range(groups_f)]
        for u in range(rows * groups):
            piece = cs[pl.ds(u * eight + holder, 8, stride=lats), :]
            if u:
                piece = pltpu.roll(piece, wf * u, 1)
            for g in range(groups_f):
                tiles[g] = jnp.where(here[u + g], piece, tiles[g])
        for g in range(groups_f):
            at = (holder * groups_f + g) * 8
            out_ref[at:at + 8, :] = tiles[g]
    wait_all(keeps)


def output_kernel(near_ref, far_hbm, back_ref, spec_ref, bk, far_s, sems):
    everyone, quad, _, places = spec_ref.shape
    span = near_ref.shape[1]
    deep = 8 * KPAD
    near = near_ref.shape[0] // deep
    tall = 2 * everyone
    step = pl.program_id(0)

    def far_copy(t):
        part = pl.ds(pl.multiple_of(deep * t, deep), deep)
        return pltpu.make_async_copy(far_hbm.at[part], far_s.at[part], sems.at[t])

    @pl.when(step == 0)
    def _():
        for t in range(sems.shape[0]):
            far_copy(t).start()
        pair_of = lane_iota((tall, deep)) // (2 * KPAD)
        rows = []
        for part in range(2):
            full = back_ref[part * FPAD:part * FPAD + tall, :].astype(F32)
            for pp in range(4):
                rows.append(jnp.where(pair_of == pp, full, 0.0))
        bk[...] = jnp.concatenate(rows, axis=0).astype(BF16)

    def write(source, at):
        for start in range(0, span, 2 * LANES):
            size = min(2 * LANES, span - start)
            spec = dot(bk[...], source[pl.ds(at, deep), start:start + size])
            spec = spec[0:4 * tall] + spec[4 * tall:]
            kept = min(size, places - start)
            for pp in range(4):
                for f in range(everyone):
                    row = pp * tall + 2 * f
                    spec_ref[f, pp, :, start:start + kept] = spec[row:row + 2, 0:kept]

    @pl.when(step < near)
    def _():
        write(near_ref, pl.multiple_of(deep * step, deep))

    @pl.when(step >= near)
    def _():
        far_copy(step - near).wait()
        write(far_s, pl.multiple_of(deep * (step - near), deep))


def per_device(grid, row_lengths, band_map, fold_map, legendre, to_modes, back_modes, mode_rates):
    fields, single, rows, width = grid.shape
    pairs, places, lats = legendre.shape
    cut_off = places - 2
    everyone = to_modes.shape[0]
    owners, per_owner = fold_map.shape
    groups = -(-per_owner // 8)
    slots = owners * groups * 8
    pieces = -(-(width // 4) // DEEP)
    turns = 4 * pieces
    span = -(-places // LANES) * LANES
    hbm = pl.BlockSpec(memory_space=pltpu.HBM)
    vmem = pl.BlockSpec(memory_space=pltpu.VMEM)
    room = pltpu.CompilerParams(vmem_limit_bytes=ROOM)
    message = pltpu.HBM((owners, 8, LANES), F32)
    holders = band_map.shape[0]
    groups_f = everyone // fields
    dma = pltpu.SemaphoreType.DMA
    row_lengths, band_map, fold_map, to_modes, back_modes, mode_rates, grid = (
        pltpu.with_memory_space_constraint(x, pltpu.HBM)
        for x in (row_lengths, band_map, fold_map, to_modes, back_modes, mode_rates, grid)
    )
    legendre = pltpu.with_memory_space_constraint(jnp.transpose(legendre, (0, 2, 1)), pltpu.HBM)

    sending, cos_table, sin_table, cos_turn, sin_turn = pl.pallas_call(
        functools.partial(forward_kernel, cut_off, groups),
        out_shape=(
            message,
            pltpu.VMEM((DEEP, slots), BF16),
            pltpu.VMEM((DEEP, slots), BF16),
            pltpu.VMEM((turns, slots), F32),
            pltpu.VMEM((turns, slots), F32),
        ),
        in_specs=[hbm] * 4,
        out_specs=(vmem,) * 5,
        scratch_shapes=[
            pltpu.SMEM(row_lengths.shape, jnp.int32),
            pltpu.SMEM(band_map.shape, jnp.int32),
            pltpu.VMEM(fold_map.shape, jnp.int32),
            pltpu.VMEM(grid.shape, BF16),
            dma((4,)),
            pltpu.VMEM((LANES, LANES), F32),
            pltpu.VMEM((8, slots), F32),
            pltpu.VMEM((16, 4 * DEEP * pieces), F32),
            pltpu.VMEM((4 * TWICE, slots), BF16),
        ],
        compiler_params=room,
        name="forward_rows",
    )(row_lengths, band_map, fold_map, grid)
    tables = [
        pltpu.with_memory_space_constraint(x, pltpu.VMEM)
        for x in (cos_table, sin_table, cos_turn, sin_turn)
    ]
    arrived = lax.all_to_all(sending, ("lat", "fld"), split_axis=0, concat_axis=0, tiled=True)

    close = 1
    legs, legs_far, mix, back, turn_back, tau, rate = pl.pallas_call(
        functools.partial(prepare_kernel, cut_off, pairs, fields, rows),
        out_shape=(
            pltpu.VMEM((close * 16 * lats, span), BF16),
            pltpu.HBM(((groups - close) * 16 * lats, span), BF16),
            pltpu.VMEM((2 * rows * KPAD, 3 * LANES), BF16),
            pltpu.VMEM((2 * FPAD, 8 * KPAD), BF16),
            pltpu.VMEM((FPAD, 6 * KPAD), BF16),
            pltpu.VMEM((-(-groups * 4 // 8) * 8, span), F32),
            pltpu.VMEM((KPAD, 2 * LANES), F32),
        ),
        in_specs=[hbm] * 6,
        out_specs=(vmem, hbm) + (vmem,) * 5,
        scratch_shapes=[
            pltpu.SMEM(fold_map.shape, jnp.int32),
            pltpu.SMEM(band_map.shape, jnp.int32),
            pltpu.SMEM(mode_rates.shape, F32),
            pltpu.VMEM((pairs, lats, places), F32),
            pltpu.VMEM(to_modes.shape, F32),
            pltpu.VMEM(back_modes.shape, F32),
            dma((6,)),
            pltpu.VMEM((KPAD, LANES), F32),
            pltpu.VMEM(((groups - close) * 16 * lats, span), BF16),
            dma((groups - close,)),
        ],
        compiler_params=room,
        cost_estimate=pl.CostEstimate(flops=10**8, bytes_accessed=8 * 10**6, transcendentals=0),
        name="prepare",
    )(fold_map, band_map, mode_rates, legendre, to_modes, back_modes)
    legs_far = pltpu.with_memory_space_constraint(legs_far, pltpu.HBM)
    legs, mix, back, turn_back, tau, rate = (
        pltpu.with_memory_space_constraint(x, pltpu.VMEM)
        for x in (legs, mix, back, turn_back, tau, rate)
    )

    near = groups // 2
    damped_near, damped_far, leaving = pl.pallas_call(
        functools.partial(solve_kernel, fields, rows, lats),
        out_shape=(
            pltpu.VMEM((near * 8 * KPAD, span), BF16),
            pltpu.HBM(((groups - near) * 8 * KPAD, span), BF16),
            pltpu.HBM((owners * 8, LANES), F32),
        ),
        in_specs=[hbm] + [vmem] * 6,
        out_specs=(vmem, hbm, vmem),
        scratch_shapes=[
            pltpu.VMEM((groups * 16 * lats, LANES), F32),
            pltpu.VMEM(((groups - close) * 16 * lats, span), BF16),
            pltpu.VMEM(((groups - near) * 8 * KPAD, span), BF16),
            dma,
            dma((groups - near,)),
        ],
        compiler_params=room,
        name="solve",
    )(legs_far, legs, arrived.reshape(owners * 8, LANES), mix, turn_back, tau, rate)
    leaving = leaving.reshape(owners, 8, LANES)

    returned = lax.all_to_all(leaving, ("lat", "fld"), split_axis=0, concat_axis=0, tiled=True)

    damped_near = pltpu.with_memory_space_constraint(damped_near, pltpu.VMEM)
    damped_far = pltpu.with_memory_space_constraint(damped_far, pltpu.HBM)
    spectral = pl.pallas_call(
        output_kernel,
        grid=(groups,),
        out_shape=jax.ShapeDtypeStruct((everyone, pairs, 2, places), F32),
        in_specs=[
            pl.BlockSpec((near * 8 * KPAD, span), lambda t: (0, 0)),
            hbm,
            pl.BlockSpec((2 * FPAD, 8 * KPAD), lambda t: (0, 0)),
        ],
        out_specs=pl.BlockSpec((everyone, 4, 2, places), lambda t: (0, t, 0, 0)),
        scratch_shapes=[
            pltpu.VMEM((16 * everyone, 8 * KPAD), BF16),
            pltpu.VMEM(((groups - near) * 8 * KPAD, span), BF16),
            dma((groups - near,)),
        ],
        compiler_params=pltpu.CompilerParams(
            dimension_semantics=("arbitrary",), vmem_limit_bytes=ROOM
        ),
        cost_estimate=pl.CostEstimate(flops=10**8, bytes_accessed=8 * 10**6, transcendentals=0),
        name="spectral_output",
    )(damped_near, damped_far, back)

    grid_out = pl.pallas_call(
        functools.partial(inverse_kernel, groups),
        out_shape=jax.ShapeDtypeStruct(grid.shape, BF16),
        in_specs=[hbm] * 2 + [vmem] * 5,
        out_specs=vmem,
        scratch_shapes=[
            pltpu.SMEM(row_lengths.shape, jnp.int32),
            pltpu.SMEM(band_map.shape, jnp.int32),
            dma((2,)),
            pltpu.VMEM((32 * pieces, 4 * LANES), BF16),
        ],
        compiler_params=room,
        name="inverse_rows",
    )(row_lengths, band_map, *tables, returned)
    return (jnp.transpose(spectral, (0, 2, 1, 3)), grid_out)


def solution(mesh):
    placed = (
        P("fld", "lat", None, None),
        P(),
        P(),
        P(),
        P(("lat", "fld"), None, None),
        P(),
        P(),
        P(),
    )
    return jax.shard_map(
        per_device,
        mesh=mesh,
        in_specs=placed,
        out_specs=(P(None, None, ("lat", "fld"), None), P("fld", "lat", None, None)),
        check_vma=False,
    )
```

```python
import functools
import math

import jax
import jax.numpy as jnp
from jax import lax
from jax.experimental import pallas as pl
from jax.experimental.pallas import tpu as pltpu
from jax.sharding import PartitionSpec as P

LANES = 128
KPAD = 24
FPAD = 64
DEEP = 256
TWICE = 24
ROOM = 24 * 1024 * 1024
F32 = jnp.float32
BF16 = jnp.bfloat16
NT_DIMS = (((1,), (1,)), ((), ()))
SIN_POLY = (
    6.283185302447051,
    -41.34170038368319,
    81.60513023312113,
    -76.70299324464969,
    42.02573766814694,
    -14.899106966102595,
    3.237062655726421,
)
COS_POLY = (
    0.9999999889083757,
    -19.739204448887243,
    64.93911476570418,
    -85.45008785413638,
    60.167188450194914,
    -25.9658703083255,
    6.526145851512229,
)


def dot(a, b):
    return jnp.dot(a, b, preferred_element_type=F32)


def dot_nt(a, b):
    return lax.dot_general(a, b, NT_DIMS, preferred_element_type=F32)


def split(x):
    high = x.astype(BF16)
    return high, (x - high.astype(F32)).astype(BF16)


def horner(coefs, z):
    total = coefs[-1] * z + coefs[-2]
    for coef in coefs[-3::-1]:
        total = total * z + coef
    return total


def turn(steps, period, inverse):
    rest = steps - period * jnp.floor(steps * inverse + 0.5)
    part = rest * inverse
    z = part * part
    return horner(COS_POLY, z), part * horner(SIN_POLY, z)


def start_all(sources, targets, sems):
    copies = [
        pltpu.make_async_copy(source, target, sems.at[i])
        for i, (source, target) in enumerate(zip(sources, targets))
    ]
    for copy in copies:
        copy.start()
    return copies


def wait_all(copies):
    for copy in copies:
        copy.wait()


def lane_iota(shape):
    return lax.broadcasted_iota(jnp.int32, shape, len(shape) - 1)


def row_iota(shape):
    return lax.broadcasted_iota(jnp.int32, shape, len(shape) - 2)


def lanes_within(lane, start, size):
    start %= LANES
    if start + size <= LANES:
        return (lane >= start) & (lane < start + size)
    return (lane >= start) | (lane < start + size - LANES)


def spread_matrix():
    shape = (4 * LANES, LANES)
    picks = []
    for phase in range(4):
        picks.append(jnp.where(row_iota(shape) == 4 * lane_iota(shape) + phase, 1.0, 0.0))
    return jnp.concatenate(picks, axis=1).astype(BF16)


def phase_steps(groups, lanes):
    row = row_iota((groups + 16, lanes))
    steps = jnp.where(row < groups, (row >> 2) * (4 * DEEP) + (row & 3), 4 * (row - groups))
    steps = jnp.where(row >= groups + 8, 32 << jnp.maximum(row - groups - 8, 0), steps)
    return steps.astype(F32)


def slot_lane(index, fields, rows):
    used = rows * fields
    part = (index >= TWICE).astype(jnp.int32)
    row = index - TWICE * part
    vec = jnp.where(row >= used, row - used, row)
    lane = lax.rem(vec, rows) * (fields * 2) + lax.div(vec, rows) * 2 + part
    return jnp.where(row < 2 * used, lane, -LANES)


def two_phases(ref, g, at, used, block):
    first = ref[2 * g:2 * g + 1, at]
    second = ref[2 * g + 1:2 * g + 2, at]
    tiles = []
    for low in range(0, TWICE, 8):
        if low + 8 <= used:
            tiles.append(jnp.broadcast_to(first, (8, block)))
        elif low >= used:
            tiles.append(jnp.broadcast_to(second, (8, block)))
        else:
            tiles.append(jnp.where(low + row_iota((8, block)) < used, first, second))
    return jnp.concatenate(tiles, axis=0)


def forward_kernel(
    cut_off, groups, len_hbm, band_hbm, fold_hbm, grid_hbm,
    msg_ref, tc, ts, fc, fs,
    len_ref, band_ref, fold_ref, grid_ref, sems, fold_s, wave_s, xs, xt,
):
    copies = start_all(
        (len_hbm, band_hbm, fold_hbm, grid_hbm), (len_ref, band_ref, fold_ref, grid_ref), sems
    )
    fields, _, rows, width = grid_ref.shape
    owners, per_owner = fold_ref.shape
    slots = tc.shape[1]
    pieces = xs.shape[1] // (4 * DEEP)
    unit = rows * fields * 2
    used = rows * fields
    spread_s = spread_matrix()
    shape = (LANES, owners * 8)
    repeat = jnp.where(row_iota(shape) == lane_iota(shape) >> 3, 1.0, 0.0).astype(BF16)
    shape = (8 * groups, 16 * groups)
    weigh = jnp.where(
        jnp.where(lane_iota(shape) < 8 * groups, lane_iota(shape), lane_iota(shape) - 8 * groups) >> 3
        == row_iota(shape) >> 3,
        jnp.where(lane_iota(shape) < 8 * groups, 8.0, 1.0),
        0.0,
    ).astype(BF16)
    tall = 4 * TWICE
    shape = (LANES, tall * groups)
    one = (1, 2 * TWICE)
    base = slot_lane(lane_iota(one), fields, rows)
    targets = []
    for t in range(groups):
        target = base + unit * (t + lax.axis_index("fld"))
        target = jnp.where(base < 0, base, target & (LANES - 1))
        targets += [target, target]
    target = jnp.concatenate(targets, axis=1)
    packing = jnp.where(row_iota(shape) == target, 1.0, 0.0).astype(BF16)
    fold_s[...] = jnp.full(fold_s.shape, -1.0, F32)
    xs[...] = jnp.zeros(xs.shape, F32)
    wait_all(copies)
    length = len_ref[band_ref[lax.axis_index("lat")]]
    top = jnp.minimum(cut_off, (length - 1) // 2)

    fold_s[0:owners, 0:per_owner] = fold_ref[...].astype(F32)
    turned = jnp.transpose(fold_s[...])[0:8 * groups]
    eights = jnp.floor(turned * 0.125)
    parts = jnp.concatenate([eights, turned - 8.0 * eights], axis=0).astype(BF16)
    repeated = dot(parts, repeat)
    own = (lane_iota(repeated.shape) & 7) == (row_iota(repeated.shape) & 7)
    waves = dot(weigh, jnp.where(own, repeated, 0.0).astype(BF16))
    for t in range(groups):
        wave_s[:, owners * 8 * t:owners * 8 * (t + 1)] = waves[8 * t:8 * t + 8]

    for field in range(fields):
        xs[rows * field:rows * (field + 1), 0:width] = grid_ref[field, 0].astype(F32)
    stacked = jnp.concatenate(
        [xs[:, 4 * LANES * c:4 * LANES * (c + 1)] for c in range(2 * pieces)], axis=0
    ).astype(BF16)
    spread = dot(stacked, spread_s)
    blank = jnp.zeros((TWICE - 16, LANES), F32)
    values = []
    for k in range(pieces):
        for pair in range(2):
            halves = []
            for half in range(2):
                c = 2 * k + half
                off = 2 * LANES * pair
                rows_c = spread[16 * c:16 * (c + 1)]
                inside = c * LANES + lane_iota((16, LANES)) < length // 4
                first, second = (
                    jnp.concatenate([jnp.where(inside, rows_c[:, o:o + LANES], 0.0), blank], axis=0)
                    for o in (off, off + LANES)
                )
                halves.append(first + pltpu.roll(second, used, 0))
            values.append(jnp.concatenate(halves, axis=1))
    values = jnp.concatenate(values, axis=0).astype(BF16)

    turns = 4 * pieces
    block = 2 * LANES
    steps = phase_steps(turns, block)
    period = jnp.full((1, block), length, jnp.int32).astype(F32)
    inverse = 1.0 / period
    def make_tables(i):
        at = pl.ds(i * block, block)
        wave = wave_s[:, at]
        wave = jnp.concatenate([wave] * ((turns + 16) // 8), axis=0)
        co, si = turn(steps * wave, period, inverse)
        one = wave[0:1]
        weight = jnp.where(one == 0.0, 1.0, 2.0)
        limit = jnp.full(one.shape, top, jnp.int32).astype(F32)
        weight = jnp.where((one >= 0.0) & (one <= limit), weight, 0.0)
        fc[:, at] = co[0:turns] * weight
        fs[:, at] = si[0:turns] * weight
        c_all = co[turns:turns + 8]
        s_all = si[turns:turns + 8]
        size, step = 8, turns + 8
        while size < DEEP:
            c1 = co[step:step + 1]
            s1 = si[step:step + 1]
            c_new = c_all * c1 - s_all * s1
            s_new = s_all * c1 + c_all * s1
            c_all = jnp.concatenate([c_all, c_new], axis=0)
            s_all = jnp.concatenate([s_all, s_new], axis=0)
            size, step = 2 * size, step + 1
        c_all = c_all.astype(BF16)
        s_all = s_all.astype(BF16)
        tc[:, at] = c_all
        ts[:, at] = s_all
        return c_all, s_all

    def finish(i, inner_c, inner_s):
        at = pl.ds(i * block, block)
        real = jnp.zeros((TWICE, block), F32)
        imag = jnp.zeros((TWICE, block), F32)
        for g in range(turns // 2):
            c1 = two_phases(fc, g, at, used, block)
            s1 = two_phases(fs, g, at, used, block)
            part_c = inner_c[TWICE * g:TWICE * (g + 1)]
            part_s = inner_s[TWICE * g:TWICE * (g + 1)]
            real = real + (c1 * part_c - s1 * part_s)
            imag = imag - (c1 * part_s + s1 * part_c)
        fix = jnp.where(wave_s[0:1, at] == 0.0, 1.0, 0.5)
        both = jnp.concatenate([real, imag], axis=0) * fix
        xt[:, at] = jnp.concatenate(split(both), axis=0)

    blocks = slots // block
    ready = make_tables(0)
    for i in range(blocks):
        inner_c = dot(values, ready[0])
        inner_s = dot(values, ready[1])
        if i + 1 < blocks:
            ready = make_tables(i + 1)
        finish(i, inner_c, inner_s)

    turned = jnp.concatenate(
        [xt[:, owners * 8 * t:owners * 8 * (t + 1)] for t in range(groups)], axis=0
    )
    total = dot(packing, turned)
    scale = 1.0 / jnp.sqrt(jnp.full(total.shape, length, jnp.int32).astype(F32))
    msg_ref[...] = jnp.transpose(total * scale).reshape(owners, 8, LANES)


def inverse_kernel(
    groups, len_hbm, band_hbm, tc, ts, fc, fs, msg_ref, grid_ref,
    len_ref, band_ref, sems, os,
):
    copies = start_all((len_hbm, band_hbm), (len_ref, band_ref), sems)
    spread_s = spread_matrix()
    fields, _, rows, width = grid_ref.shape
    owners = msg_ref.shape[0]
    slots = tc.shape[1]
    turns = fc.shape[0]
    unit = rows * fields * 2
    high, low = split(msg_ref[...].reshape(owners * 8, LANES))
    pieces = jnp.concatenate([high, low], axis=1)
    used = rows * fields
    tall = 2 * TWICE
    shape = (tall, LANES)
    base = slot_lane(row_iota(shape), fields, rows)
    places = []
    for t in range(groups):
        source = (base + unit * t + lax.axis_index("fld") * (fields * 2)) & (LANES - 1)
        source = jnp.where(base < 0, base, source)
        places.append(jnp.where(lane_iota(shape) == source, 1.0, 0.0))
    place = jnp.concatenate(places, axis=0).astype(BF16)
    place = jnp.concatenate([place, place], axis=1)
    turned = dot_nt(place, pieces)
    block = 2 * LANES
    out = jnp.zeros((TWICE * turns // 2, DEEP), F32)
    def twisted(i):
        t, off = divmod(i * block, owners * 8)
        real = turned[tall * t:tall * t + TWICE, off:off + block]
        imag = turned[tall * t + TWICE:tall * (t + 1), off:off + block]
        at = pl.ds(i * block, block)
        reals, imags = [], []
        for g in range(turns // 2):
            c1 = two_phases(fc, g, at, used, block)
            s1 = two_phases(fs, g, at, used, block)
            reals.append(c1 * real - s1 * imag)
            imags.append(s1 * real + c1 * imag)
        return (
            jnp.concatenate(reals, axis=0).astype(BF16),
            jnp.concatenate(imags, axis=0).astype(BF16),
        )

    blocks = slots // block
    ready = twisted(0)
    for i in range(blocks):
        at = pl.ds(i * block, block)
        part_r = dot_nt(ready[0], tc[:, at])
        part_i = dot_nt(ready[1], ts[:, at])
        if i + 1 < blocks:
            ready = twisted(i + 1)
        out = out + (part_r - part_i)
    wait_all(copies)
    length = len_ref[band_ref[lax.axis_index("lat")]]
    out = out * (1.0 / jnp.sqrt(jnp.full(out.shape, length, jnp.int32).astype(F32)))
    chunks = os.shape[0] // 16
    for c in range(chunks):
        off = LANES * (c % 2)
        for phase in range(4):
            at = (2 * (c // 2) + phase // 2) * TWICE
            piece = out[at:at + TWICE, off:off + LANES]
            if phase % 2:
                piece = pltpu.roll(piece, TWICE - used, 0)
            os[16 * c:16 * (c + 1), LANES * phase:LANES * (phase + 1)] = piece[0:16].astype(BF16)
    merged = dot_nt(os[...], spread_s)
    for c in range(chunks):
        begin = 4 * LANES * c
        size = min(4 * LANES, width - begin)
        if size <= 0:
            continue
        inside = begin + lane_iota((16, size)) < length
        piece = jnp.where(inside, merged[16 * c:16 * (c + 1), 0:size], 0.0)
        for field in range(fields):
            grid_ref[field, 0, :, begin:begin + size] = piece[
                rows * field:rows * (field + 1)
            ].astype(BF16)


def prepare_kernel(
    cut_off, pairs, fields, rows, fold_hbm, band_hbm, rates_hbm, leg_hbm, tm_hbm, bm_hbm,
    eh_hbm, round_ref, mix_ref, back_ref, turn_ref, tau_ref, rate_ref,
    fold_ref, band_ref, rates_ref, leg_ref, tm_ref, bm_ref, sems, pad_s, eh_ref, out_sems,
):
    copies = start_all(
        (fold_hbm, band_hbm, rates_hbm, tm_hbm, bm_hbm, leg_hbm),
        (fold_ref, band_ref, rates_ref, tm_ref, bm_ref, leg_ref),
        sems,
    )
    wait_all(copies[:-1])
    everyone = tm_ref.shape[0]
    _, lats, places = leg_ref.shape
    groups_f = everyone // fields
    wf = fields * 2
    unit = rows * wf
    span = eh_ref.shape[1]
    eight = 8 * lats
    groups = eh_ref.shape[0] // (2 * eight)
    owner = lax.axis_index("lat") * groups_f + lax.axis_index("fld")

    pad_s[...] = jnp.zeros(pad_s.shape, F32)
    pad_s[0:everyone, 0:everyone] = tm_ref[...]
    shape = (LANES, LANES)
    level = (lane_iota(shape) // unit) * fields + (lane_iota(shape) % wf) // 2
    pick = jnp.where(row_iota(shape) == level, 1.0, 0.0).astype(BF16)
    lane = lane_iota((KPAD, LANES))
    parts = []
    for piece in split(pad_s[...]):
        wide = dot(piece, pick)
        total = []
        for parity in range(2):
            for c in range(2):
                keep = (lane % 2 == c) & (lane < unit * groups_f)
                flip = (lane % unit) // wf >= 1 if parity else lane < 0
                total.append(jnp.where(keep, jnp.where(flip, -wide, wide), 0.0))
        total.append(jnp.zeros((LANES - 4 * KPAD, LANES), F32))
        parts.append(jnp.concatenate(total, axis=0).astype(BF16))
    mix_ref[...] = jnp.concatenate([parts[0], parts[1], parts[0]], axis=1)

    pad_s[...] = jnp.zeros(pad_s.shape, F32)
    pad_s[0:everyone, 0:everyone] = bm_ref[...]
    shape = (FPAD, KPAD)
    expand = jnp.where(row_iota(shape) // 2 == lane_iota(shape), 1.0, 0.0).astype(BF16)
    shape = (LANES, 2 * LANES)
    repeat = jnp.where(row_iota(shape) == lane_iota(shape) % KPAD, 1.0, 0.0).astype(BF16)
    shape = (FPAD, 2 * LANES)
    same = row_iota(shape) % 2 == (lane_iota(shape) // KPAD) % 2
    for part, piece in enumerate(split(pad_s[...])):
        full = jnp.where(same, dot(dot(expand, piece).astype(BF16), repeat), 0.0)
        back_ref[part * FPAD:(part + 1) * FPAD, :] = full[:, 0:8 * KPAD].astype(BF16)
    shape = (LANES, LANES)
    row, lane = row_iota(shape), lane_iota(shape)
    width = 2 * everyone
    south = lane >= width
    level = jnp.where(south, lane - width, lane)
    pick = jnp.where(row == (level >> 1), 1.0, 0.0).astype(BF16)
    part = lax.div(row, KPAD)
    keep = ((part & 1) == (level & 1)) & (part < 4) & (lane < 2 * width)
    flip = south & (part >= 2)
    wide = []
    for piece in split(jnp.transpose(jnp.concatenate([pad_s[...], jnp.zeros((LANES - KPAD, LANES), F32)], axis=0))):
        small = dot(piece, pick)[0:KPAD]
        tall = jnp.concatenate([small] * 5 + [jnp.zeros((LANES - 5 * KPAD, LANES), F32)], axis=0)
        wide.append(jnp.where(keep, jnp.where(flip, -tall, tall), 0.0).astype(BF16))
    turn_ref[...] = jnp.concatenate([wide[0], wide[0], wide[1]], axis=0)

    row = row_iota((KPAD, 2 * LANES))
    rate = jnp.zeros((KPAD, 2 * LANES), F32)
    for k in range(everyone):
        rate = jnp.where(row == k, rates_ref[k], rate)
    rate_ref[...] = rate
    wide_rate = jnp.concatenate([rate[:, 0:LANES]] * (span // LANES), axis=1)
    paired = tau_ref.shape[0]
    row = row_iota((paired, LANES))
    waves = []
    wave = jnp.zeros((paired, LANES), jnp.int32)
    for pair in range(4 * groups):
        waves.append(fold_ref[owner, 2 * min(pair, pairs - 1)])
        wave = jnp.where(row == 8 * (pair // 4) + pair % 4, waves[pair], wave)
    wave = jnp.concatenate([wave] * (span // LANES), axis=1)
    line = lane_iota((paired, span))
    degree = jnp.where(line > cut_off - wave, line - 1, line + wave)
    tau_ref[...] = (degree * (degree + 1)).astype(F32) * (1.0 / float(cut_off * (cut_off + 1)))

    quad_rows = 4 * lats
    shape = (quad_rows, quad_rows)
    band = jnp.zeros(shape, jnp.int32)
    for holder in range(lats):
        band = jnp.where(row_iota(shape) % lats == holder, band_ref[holder], band)
    order = jnp.where(
        (row_iota(shape) // lats == lane_iota(shape) // lats) & (lane_iota(shape) % lats == band),
        1.0,
        0.0,
    ).astype(BF16)

    whole = places // LANES * LANES
    line = lane_iota((quad_rows, span))
    row = row_iota((quad_rows, LANES)) // lats
    copies[-1].wait()
    keeps = []
    for t in range(groups):
        wave = jnp.zeros((quad_rows, LANES), jnp.int32)
        last = jnp.zeros((quad_rows, LANES), jnp.int32)
        stack = []
        for pp in range(4):
            there = 4 * t + pp < pairs
            index = min(4 * t + pp, pairs - 1)
            wave = jnp.where(row == pp, waves[4 * t + pp], wave)
            last = jnp.where(row == pp, places - 1 if there else -1, last)
            stack.append(
                jnp.concatenate(
                    [
                        leg_ref[index, :, 0:whole],
                        jnp.broadcast_to(leg_ref[index, :, whole:places], (lats, span - whole)),
                    ],
                    axis=1,
                )
            )
        wave = jnp.concatenate([wave] * (span // LANES), axis=1)
        last = jnp.concatenate([last] * (span // LANES), axis=1)
        leg = dot(order, jnp.concatenate(stack, axis=0).astype(BF16))
        before = line <= cut_off - wave
        first = before & (line <= last)
        second = jnp.logical_not(before) & (line <= last)
        odd = ((line + jnp.where(before, 0, wave)) & 1) == 1
        masks = [
            [jnp.where(side & odd, 1.0, 0.0) if par else jnp.where(odd, 0.0, jnp.where(side, 1.0, 0.0)) for par in range(2)]
            for side in (first, second)
        ]
        for par in range(2):
            near = leg * masks[0][par]
            far = leg * masks[1][par]
            for pp in range(4):
                at = 2 * eight * t + par * eight + 2 * pp * lats
                eh_ref[at:at + 2 * lats, :] = jnp.concatenate(
                    [near[pp * lats:(pp + 1) * lats], far[pp * lats:(pp + 1) * lats]], axis=0
                ).astype(BF16)
        part = pl.ds(2 * eight * t, 2 * eight)
        keeps.append(pltpu.make_async_copy(eh_ref.at[part], eh_hbm.at[part], out_sems.at[t]))
        keeps[-1].start()

        for pp in range(4):
            own = leg[pp * lats:(pp + 1) * lats]
            pairs_of = jnp.concatenate([own * own[j:j + 1] for j in range(lats)], axis=0)
            pair = 4 * t + pp
            factor = pl.reciprocal(1.0 + tau_ref[8 * t + pp:8 * t + pp + 1, :] * wide_rate, approx=True)
            damp = []
            for side in range(2):
                for par in range(2):
                    mask = masks[side][par][pp * lats:pp * lats + 8]
                    part = (factor * jnp.concatenate([mask] * (KPAD // 8), axis=0)).astype(BF16)
                    damp += [part, part]
                damp.append(jnp.zeros((LANES - 4 * KPAD, span), BF16))
            both = dot_nt(pairs_of.astype(BF16), jnp.concatenate([jnp.concatenate(damp[0:2], axis=0), jnp.concatenate(damp[2:4], axis=0), damp[4], jnp.concatenate(damp[5:7], axis=0), jnp.concatenate(damp[7:9], axis=0), damp[9]], axis=0))
            for side in range(2):
                at = (2 * pair + side) * lats * lats
                round_ref[at:at + lats * lats, :] = both[:, LANES * side:LANES * (side + 1)]
    wait_all(keeps)


def solve_kernel(
    fields, rows, lats, msg_ref, round_ref, mix_ref, turn_ref, mixed_ref, out_ref, cs,
):
    eight = 8 * lats
    groups = mixed_ref.shape[0] // eight
    groups_f = msg_ref.shape[0] // eight
    wf = fields * 2
    unit = rows * wf
    lane = lane_iota((lats, LANES))
    tiles = [
        [msg_ref[pl.ds(8 * g + i8, lats, stride=8 * groups_f), :] for g in range(groups_f)]
        for i8 in range(8)
    ]
    tall = []
    for t in range(groups):
        here = [lanes_within(lane, unit * (t + g), unit) for g in range(groups_f)]
        for i8 in range(8):
            line = tiles[i8][0]
            for g in range(1, groups_f):
                line = jnp.where(here[g], tiles[i8][g], line)
            if t:
                line = pltpu.roll(line, LANES - unit * t, 1)
            tall.append(line)
    v_high, v_low = split(jnp.concatenate(tall, axis=0))
    mixed_ref[...] = dot_nt(jnp.concatenate([v_high, v_high, v_low], axis=1), mix_ref[...])

    sums = []
    for slot in range(8 * groups):
        mine = mixed_ref[slot * lats:(slot + 1) * lats, :]
        total = jnp.zeros((lats, LANES), F32)
        for j in range(lats):
            at = (slot * lats + j) * lats
            total = total + mine[j:j + 1] * round_ref[at:at + lats, :]
        sums.append(total)
    high, low = split(jnp.concatenate(sums, axis=0))
    cs[...] = dot(jnp.concatenate([high, low, high], axis=1), turn_ref[...])

    lane = lane_iota((8, LANES))
    here = [
        lanes_within(lane, wf * u, wf) for u in range(rows * groups + groups_f - 1)
    ]
    for holder in range(lats):
        tiles = [jnp.zeros((8, LANES), F32) for _ in range(groups_f)]
        for t in range(groups):
            piece = cs[pl.ds(t * eight + holder, 8, stride=lats), :]
            for r in range(rows):
                u = rows * t + r
                moved = pltpu.roll(piece, (wf * u - wf * groups_f * r) % LANES, 1)
                for g in range(groups_f):
                    tiles[g] = jnp.where(here[u + g], moved, tiles[g])
        for g in range(groups_f):
            at = (holder * groups_f + g) * 8
            out_ref[at:at + 8, :] = tiles[g]


def output_kernel(
    lats, eh_hbm, mixed_ref, tau_ref, rate_ref, back_ref, spec_ref, bk, eh_s, sems,
):
    everyone, quad, _, places = spec_ref.shape
    span = eh_s.shape[1]
    eight = 8 * lats
    tall = 2 * everyone
    step = pl.program_id(0)

    def fetch(t):
        part = pl.ds(pl.multiple_of(2 * eight * t, 16), 2 * eight)
        return pltpu.make_async_copy(eh_hbm.at[part], eh_s.at[part], sems.at[t])

    @pl.when(step == 0)
    def _():
        for t in range(sems.shape[0]):
            fetch(t).start()
        pair_of = lane_iota((tall, 8 * KPAD)) // (2 * KPAD)
        parts = []
        for part in range(2):
            full = back_ref[part * FPAD:part * FPAD + tall, :].astype(F32)
            for pp in range(4):
                parts.append(jnp.where(pair_of == pp, full, 0.0))
        bk[...] = jnp.concatenate(parts, axis=0).astype(BF16)

    rate = rate_ref[...]
    taus = tau_ref[pl.ds(pl.multiple_of(8 * step, 8), 8), :]
    mine = mixed_ref[pl.ds(pl.multiple_of(eight * step, 8), eight), :]
    if eight < LANES:
        mine = jnp.concatenate([mine, jnp.zeros((LANES - eight, LANES), F32)], axis=0)
    mine = [
        jnp.transpose(mine[at:at + LANES])[:, 0:min(eight, LANES)] for at in range(0, eight, LANES)
    ]
    mine = jnp.concatenate(mine, axis=1) if len(mine) > 1 else mine[0]
    mine = jnp.concatenate([mine[0:2 * KPAD], mine[2 * KPAD:4 * KPAD]], axis=1)
    slot_pair = (lane_iota((2 * KPAD, 2 * eight)) & (eight - 1)) // (2 * lats)
    left = jnp.concatenate([jnp.where(slot_pair == pp, mine, 0.0) for pp in range(4)], axis=0)
    left = jnp.concatenate(split(left), axis=1)
    fetch(step).wait()
    legs = pl.ds(pl.multiple_of(2 * eight * step, 16), 2 * eight)
    for start in range(0, span, 2 * LANES):
        size = min(2 * LANES, span - start)
        right = eh_s[legs, start:start + size]
        modes = dot(left, jnp.concatenate([right, right], axis=0))
        damped = []
        for pp in range(4):
            tau = taus[pp:pp + 1, start:start + size]
            factor = pl.reciprocal(1.0 + tau * rate[:, 0:size], approx=True)
            at = 2 * pp * KPAD
            damped.append(modes[at:at + KPAD] * factor)
            damped.append(modes[at + KPAD:at + 2 * KPAD] * factor)
        spec = dot(bk[...], jnp.concatenate(damped, axis=0).astype(BF16))
        spec = spec[0:4 * tall] + spec[4 * tall:]
        kept = min(size, places - start)
        for pp in range(4):
            for f in range(everyone):
                row = pp * tall + 2 * f
                spec_ref[f, pp, :, start:start + kept] = spec[row:row + 2, 0:kept]


def per_device(grid, row_lengths, band_map, fold_map, legendre, to_modes, back_modes, mode_rates):
    fields, single, rows, width = grid.shape
    pairs, places, lats = legendre.shape
    cut_off = places - 2
    everyone = to_modes.shape[0]
    owners, per_owner = fold_map.shape
    groups = -(-per_owner // 8)
    slots = owners * groups * 8
    pieces = -(-(width // 4) // DEEP)
    turns = 4 * pieces
    span = -(-places // LANES) * LANES
    hbm = pl.BlockSpec(memory_space=pltpu.HBM)
    vmem = pl.BlockSpec(memory_space=pltpu.VMEM)
    room = pltpu.CompilerParams(vmem_limit_bytes=ROOM)
    message = pltpu.HBM((owners, 8, LANES), F32)
    holders = band_map.shape[0]
    groups_f = everyone // fields
    dma = pltpu.SemaphoreType.DMA
    row_lengths, band_map, fold_map, to_modes, back_modes, mode_rates, grid = (
        pltpu.with_memory_space_constraint(x, pltpu.HBM)
        for x in (row_lengths, band_map, fold_map, to_modes, back_modes, mode_rates, grid)
    )
    legendre = pltpu.with_memory_space_constraint(jnp.transpose(legendre, (0, 2, 1)), pltpu.HBM)

    sending, cos_table, sin_table, cos_turn, sin_turn = pl.pallas_call(
        functools.partial(forward_kernel, cut_off, groups),
        out_shape=(
            message,
            pltpu.VMEM((DEEP, slots), BF16),
            pltpu.VMEM((DEEP, slots), BF16),
            pltpu.VMEM((turns, slots), F32),
            pltpu.VMEM((turns, slots), F32),
        ),
        in_specs=[hbm] * 4,
        out_specs=(vmem,) * 5,
        scratch_shapes=[
            pltpu.SMEM(row_lengths.shape, jnp.int32),
            pltpu.SMEM(band_map.shape, jnp.int32),
            pltpu.VMEM(fold_map.shape, jnp.int32),
            pltpu.VMEM(grid.shape, BF16),
            dma((4,)),
            pltpu.VMEM((LANES, LANES), F32),
            pltpu.VMEM((8, slots), F32),
            pltpu.VMEM((16, 4 * DEEP * pieces), F32),
            pltpu.VMEM((4 * TWICE, slots), BF16),
        ],
        compiler_params=room,
        name="forward_rows",
    )(row_lengths, band_map, fold_map, grid)
    tables = [
        pltpu.with_memory_space_constraint(x, pltpu.VMEM)
        for x in (cos_table, sin_table, cos_turn, sin_turn)
    ]
    arrived = lax.all_to_all(sending, ("lat", "fld"), split_axis=0, concat_axis=0, tiled=True)

    legs, rounds, mix, back, turn_back, tau, rate = pl.pallas_call(
        functools.partial(prepare_kernel, cut_off, pairs, fields, rows),
        out_shape=(
            pltpu.HBM((groups * 16 * lats, span), BF16),
            pltpu.VMEM((groups * 8 * lats * lats, LANES), F32),
            pltpu.VMEM((LANES, 3 * LANES), BF16),
            pltpu.HBM((2 * FPAD, 8 * KPAD), BF16),
            pltpu.VMEM((3 * LANES, LANES), BF16),
            pltpu.HBM((8 * groups, span), F32),
            pltpu.HBM((KPAD, 2 * LANES), F32),
        ),
        in_specs=[hbm] * 6,
        out_specs=(hbm,) + (vmem,) * 6,
        scratch_shapes=[
            pltpu.SMEM(fold_map.shape, jnp.int32),
            pltpu.SMEM(band_map.shape, jnp.int32),
            pltpu.SMEM(mode_rates.shape, F32),
            pltpu.VMEM((pairs, lats, places), F32),
            pltpu.VMEM(to_modes.shape, F32),
            pltpu.VMEM(back_modes.shape, F32),
            dma((6,)),
            pltpu.VMEM((KPAD, LANES), F32),
            pltpu.VMEM((groups * 16 * lats, span), BF16),
            dma((groups,)),
        ],
        compiler_params=room,
        cost_estimate=pl.CostEstimate(flops=10**8, bytes_accessed=8 * 10**6, transcendentals=0),
        name="prepare",
    )(fold_map, band_map, mode_rates, legendre, to_modes, back_modes)
    legs, back, tau, rate = (
        pltpu.with_memory_space_constraint(x, pltpu.HBM) for x in (legs, back, tau, rate)
    )
    rounds, mix, turn_back = (
        pltpu.with_memory_space_constraint(x, pltpu.VMEM) for x in (rounds, mix, turn_back)
    )

    mixed, leaving = pl.pallas_call(
        functools.partial(solve_kernel, fields, rows, lats),
        out_shape=(
            pltpu.VMEM((groups * 8 * lats, LANES), F32),
            pltpu.HBM((owners * 8, LANES), F32),
        ),
        in_specs=[vmem] * 4,
        out_specs=(vmem,) * 2,
        scratch_shapes=[pltpu.VMEM((groups * 8 * lats, LANES), F32)],
        compiler_params=room,
        name="solve",
    )(arrived.reshape(owners * 8, LANES), rounds, mix, turn_back)
    leaving = leaving.reshape(owners, 8, LANES)

    returned = lax.all_to_all(leaving, ("lat", "fld"), split_axis=0, concat_axis=0, tiled=True)

    mixed = pltpu.with_memory_space_constraint(mixed, pltpu.VMEM)
    spectral = pl.pallas_call(
        functools.partial(output_kernel, lats),
        grid=(groups,),
        out_shape=jax.ShapeDtypeStruct((everyone, pairs, 2, places), F32),
        in_specs=[
            hbm,
            vmem,
            vmem,
            vmem,
            vmem,
        ],
        out_specs=pl.BlockSpec((everyone, 4, 2, places), lambda t: (0, t, 0, 0)),
        scratch_shapes=[
            pltpu.VMEM((16 * everyone, 8 * KPAD), BF16),
            pltpu.VMEM((groups * 16 * lats, span), BF16),
            dma((groups,)),
        ],
        compiler_params=pltpu.CompilerParams(
            dimension_semantics=("arbitrary",), vmem_limit_bytes=ROOM
        ),
        cost_estimate=pl.CostEstimate(flops=10**8, bytes_accessed=8 * 10**6, transcendentals=0),
        name="spectral_output",
    )(legs, mixed, tau, rate, back)

    grid_out = pl.pallas_call(
        functools.partial(inverse_kernel, groups),
        out_shape=jax.ShapeDtypeStruct(grid.shape, BF16),
        in_specs=[hbm] * 2 + [vmem] * 5,
        out_specs=vmem,
        scratch_shapes=[
            pltpu.SMEM(row_lengths.shape, jnp.int32),
            pltpu.SMEM(band_map.shape, jnp.int32),
            dma((2,)),
            pltpu.VMEM((32 * pieces, 4 * LANES), BF16),
        ],
        compiler_params=room,
        name="inverse_rows",
    )(row_lengths, band_map, *tables, returned)
    return (jnp.transpose(spectral, (0, 2, 1, 3)), grid_out)


def solution(mesh):
    placed = (
        P("fld", "lat", None, None),
        P(),
        P(),
        P(),
        P(("lat", "fld"), None, None),
        P(),
        P(),
        P(),
    )
    return jax.shard_map(
        per_device,
        mesh=mesh,
        in_specs=placed,
        out_specs=(P(None, None, ("lat", "fld"), None), P("fld", "lat", None, None)),
        check_vma=False,
    )
```

```python
import functools
import math

import jax
import jax.numpy as jnp
from jax import lax
from jax.experimental import pallas as pl
from jax.experimental.pallas import tpu as pltpu
from jax.sharding import PartitionSpec as P

LANES = 128
KPAD = 24
FPAD = 64
DEEP = 256
TWICE = 24
ROOM = 24 * 1024 * 1024
F32 = jnp.float32
BF16 = jnp.bfloat16
NT_DIMS = (((1,), (1,)), ((), ()))
SIN_POLY = (
    6.283185302447051,
    -41.34170038368319,
    81.60513023312113,
    -76.70299324464969,
    42.02573766814694,
    -14.899106966102595,
    3.237062655726421,
)
COS_POLY = (
    0.9999999889083757,
    -19.739204448887243,
    64.93911476570418,
    -85.45008785413638,
    60.167188450194914,
    -25.9658703083255,
    6.526145851512229,
)


def dot(a, b):
    return jnp.dot(a, b, preferred_element_type=F32)


def dot_nt(a, b):
    return lax.dot_general(a, b, NT_DIMS, preferred_element_type=F32)


def split(x):
    high = x.astype(BF16)
    return high, (x - high.astype(F32)).astype(BF16)


def horner(coefs, z):
    total = coefs[-1] * z + coefs[-2]
    for coef in coefs[-3::-1]:
        total = total * z + coef
    return total


def turn(steps, period, inverse):
    rest = steps - period * jnp.floor(steps * inverse + 0.5)
    part = rest * inverse
    z = part * part
    return horner(COS_POLY, z), part * horner(SIN_POLY, z)


def start_all(sources, targets, sems):
    copies = [
        pltpu.make_async_copy(source, target, sems.at[i])
        for i, (source, target) in enumerate(zip(sources, targets))
    ]
    for copy in copies:
        copy.start()
    return copies


def wait_all(copies):
    for copy in copies:
        copy.wait()


def lane_iota(shape):
    return lax.broadcasted_iota(jnp.int32, shape, len(shape) - 1)


def row_iota(shape):
    return lax.broadcasted_iota(jnp.int32, shape, len(shape) - 2)


def lanes_within(lane, start, size):
    start %= LANES
    if start + size <= LANES:
        return (lane >= start) & (lane < start + size)
    return (lane >= start) | (lane < start + size - LANES)


def spread_matrix():
    shape = (4 * LANES, LANES)
    picks = []
    for phase in range(4):
        picks.append(jnp.where(row_iota(shape) == 4 * lane_iota(shape) + phase, 1.0, 0.0))
    return jnp.concatenate(picks, axis=1).astype(BF16)


def phase_steps(groups, lanes):
    row = row_iota((groups + 16, lanes))
    steps = jnp.where(row < groups, (row >> 2) * (4 * DEEP) + (row & 3), 4 * (row - groups))
    steps = jnp.where(row >= groups + 8, 32 << jnp.maximum(row - groups - 8, 0), steps)
    return steps.astype(F32)


def slot_lane(index, fields, rows):
    used = rows * fields
    part = (index >= TWICE).astype(jnp.int32)
    row = index - TWICE * part
    vec = jnp.where(row >= used, row - used, row)
    lane = lax.rem(vec, rows) * (fields * 2) + lax.div(vec, rows) * 2 + part
    return jnp.where(row < 2 * used, lane, -LANES)


def two_phases(ref, g, at, used, block):
    first = ref[2 * g:2 * g + 1, at]
    second = ref[2 * g + 1:2 * g + 2, at]
    tiles = []
    for low in range(0, TWICE, 8):
        if low + 8 <= used:
            tiles.append(jnp.broadcast_to(first, (8, block)))
        elif low >= used:
            tiles.append(jnp.broadcast_to(second, (8, block)))
        else:
            tiles.append(jnp.where(low + row_iota((8, block)) < used, first, second))
    return jnp.concatenate(tiles, axis=0)


def forward_kernel(
    cut_off, groups, len_hbm, band_hbm, fold_hbm, grid_hbm,
    msg_ref, tc, ts, fc, fs,
    len_ref, band_ref, fold_ref, grid_ref, sems, fold_s, wave_s, xs, xt,
):
    copies = start_all(
        (len_hbm, band_hbm, fold_hbm, grid_hbm), (len_ref, band_ref, fold_ref, grid_ref), sems
    )
    fields, _, rows, width = grid_ref.shape
    owners, per_owner = fold_ref.shape
    slots = tc.shape[1]
    pieces = xs.shape[1] // (4 * DEEP)
    unit = rows * fields * 2
    used = rows * fields
    spread_s = spread_matrix()
    shape = (LANES, owners * 8)
    repeat = jnp.where(row_iota(shape) == lane_iota(shape) >> 3, 1.0, 0.0).astype(BF16)
    shape = (8 * groups, 16 * groups)
    weigh = jnp.where(
        jnp.where(lane_iota(shape) < 8 * groups, lane_iota(shape), lane_iota(shape) - 8 * groups) >> 3
        == row_iota(shape) >> 3,
        jnp.where(lane_iota(shape) < 8 * groups, 8.0, 1.0),
        0.0,
    ).astype(BF16)
    tall = 4 * TWICE
    shape = (LANES, tall * groups)
    one = (1, 2 * TWICE)
    base = slot_lane(lane_iota(one), fields, rows)
    targets = []
    for t in range(groups):
        target = base + unit * (t + lax.axis_index("fld"))
        target = jnp.where(base < 0, base, target & (LANES - 1))
        targets += [target, target]
    target = jnp.concatenate(targets, axis=1)
    packing = jnp.where(row_iota(shape) == target, 1.0, 0.0).astype(BF16)
    fold_s[...] = jnp.full(fold_s.shape, -1.0, F32)
    xs[...] = jnp.zeros(xs.shape, F32)
    wait_all(copies)
    length = len_ref[band_ref[lax.axis_index("lat")]]
    top = jnp.minimum(cut_off, (length - 1) // 2)

    fold_s[0:owners, 0:per_owner] = fold_ref[...].astype(F32)
    turned = jnp.transpose(fold_s[...])[0:8 * groups]
    eights = jnp.floor(turned * 0.125)
    parts = jnp.concatenate([eights, turned - 8.0 * eights], axis=0).astype(BF16)
    repeated = dot(parts, repeat)
    own = (lane_iota(repeated.shape) & 7) == (row_iota(repeated.shape) & 7)
    waves = dot(weigh, jnp.where(own, repeated, 0.0).astype(BF16))
    for t in range(groups):
        wave_s[:, owners * 8 * t:owners * 8 * (t + 1)] = waves[8 * t:8 * t + 8]

    for field in range(fields):
        xs[rows * field:rows * (field + 1), 0:width] = grid_ref[field, 0].astype(F32)
    stacked = jnp.concatenate(
        [xs[:, 4 * LANES * c:4 * LANES * (c + 1)] for c in range(2 * pieces)], axis=0
    ).astype(BF16)
    spread = dot(stacked, spread_s)
    blank = jnp.zeros((TWICE - 16, LANES), F32)
    values = []
    for k in range(pieces):
        for pair in range(2):
            halves = []
            for half in range(2):
                c = 2 * k + half
                off = 2 * LANES * pair
                rows_c = spread[16 * c:16 * (c + 1)]
                inside = c * LANES + lane_iota((16, LANES)) < length // 4
                first, second = (
                    jnp.concatenate([jnp.where(inside, rows_c[:, o:o + LANES], 0.0), blank], axis=0)
                    for o in (off, off + LANES)
                )
                halves.append(first + pltpu.roll(second, used, 0))
            values.append(jnp.concatenate(halves, axis=1))
    values = jnp.concatenate(values, axis=0).astype(BF16)

    turns = 4 * pieces
    block = 2 * LANES
    steps = phase_steps(turns, block)
    period = jnp.full((1, block), length, jnp.int32).astype(F32)
    inverse = 1.0 / period
    def make_tables(i):
        at = pl.ds(i * block, block)
        wave = wave_s[:, at]
        wave = jnp.concatenate([wave] * ((turns + 16) // 8), axis=0)
        co, si = turn(steps * wave, period, inverse)
        one = wave[0:1]
        weight = jnp.where(one == 0.0, 1.0, 2.0)
        limit = jnp.full(one.shape, top, jnp.int32).astype(F32)
        weight = jnp.where((one >= 0.0) & (one <= limit), weight, 0.0)
        fc[:, at] = co[0:turns] * weight
        fs[:, at] = si[0:turns] * weight
        c_all = co[turns:turns + 8]
        s_all = si[turns:turns + 8]
        size, step = 8, turns + 8
        while size < DEEP:
            c1 = co[step:step + 1]
            s1 = si[step:step + 1]
            c_new = c_all * c1 - s_all * s1
            s_new = s_all * c1 + c_all * s1
            c_all = jnp.concatenate([c_all, c_new], axis=0)
            s_all = jnp.concatenate([s_all, s_new], axis=0)
            size, step = 2 * size, step + 1
        c_all = c_all.astype(BF16)
        s_all = s_all.astype(BF16)
        tc[:, at] = c_all
        ts[:, at] = s_all
        return c_all, s_all

    def finish(i, inner_c, inner_s):
        at = pl.ds(i * block, block)
        real = jnp.zeros((TWICE, block), F32)
        imag = jnp.zeros((TWICE, block), F32)
        for g in range(turns // 2):
            c1 = two_phases(fc, g, at, used, block)
            s1 = two_phases(fs, g, at, used, block)
            part_c = inner_c[TWICE * g:TWICE * (g + 1)]
            part_s = inner_s[TWICE * g:TWICE * (g + 1)]
            real = real + (c1 * part_c - s1 * part_s)
            imag = imag - (c1 * part_s + s1 * part_c)
        fix = jnp.where(wave_s[0:1, at] == 0.0, 1.0, 0.5)
        both = jnp.concatenate([real, imag], axis=0) * fix
        xt[:, at] = jnp.concatenate(split(both), axis=0)

    blocks = slots // block
    ready = make_tables(0)
    for i in range(blocks):
        inner_c = dot(values, ready[0])
        inner_s = dot(values, ready[1])
        if i + 1 < blocks:
            ready = make_tables(i + 1)
        finish(i, inner_c, inner_s)

    turned = jnp.concatenate(
        [xt[:, owners * 8 * t:owners * 8 * (t + 1)] for t in range(groups)], axis=0
    )
    total = dot(packing, turned)
    scale = 1.0 / jnp.sqrt(jnp.full(total.shape, length, jnp.int32).astype(F32))
    msg_ref[...] = jnp.transpose(total * scale).reshape(owners, 8, LANES)


def inverse_kernel(
    groups, len_hbm, band_hbm, tc, ts, fc, fs, msg_ref, grid_ref,
    len_ref, band_ref, sems, os,
):
    copies = start_all((len_hbm, band_hbm), (len_ref, band_ref), sems)
    spread_s = spread_matrix()
    fields, _, rows, width = grid_ref.shape
    owners = msg_ref.shape[0]
    slots = tc.shape[1]
    turns = fc.shape[0]
    unit = rows * fields * 2
    high, low = split(msg_ref[...].reshape(owners * 8, LANES))
    pieces = jnp.concatenate([high, low], axis=1)
    used = rows * fields
    tall = 2 * TWICE
    shape = (tall, LANES)
    base = slot_lane(row_iota(shape), fields, rows)
    places = []
    for t in range(groups):
        source = (base + unit * t + lax.axis_index("fld") * (fields * 2)) & (LANES - 1)
        source = jnp.where(base < 0, base, source)
        places.append(jnp.where(lane_iota(shape) == source, 1.0, 0.0))
    place = jnp.concatenate(places, axis=0).astype(BF16)
    place = jnp.concatenate([place, place], axis=1)
    turned = dot_nt(place, pieces)
    block = 2 * LANES
    out = jnp.zeros((TWICE * turns // 2, DEEP), F32)
    def twisted(i):
        t, off = divmod(i * block, owners * 8)
        real = turned[tall * t:tall * t + TWICE, off:off + block]
        imag = turned[tall * t + TWICE:tall * (t + 1), off:off + block]
        at = pl.ds(i * block, block)
        reals, imags = [], []
        for g in range(turns // 2):
            c1 = two_phases(fc, g, at, used, block)
            s1 = two_phases(fs, g, at, used, block)
            reals.append(c1 * real - s1 * imag)
            imags.append(s1 * real + c1 * imag)
        return (
            jnp.concatenate(reals, axis=0).astype(BF16),
            jnp.concatenate(imags, axis=0).astype(BF16),
        )

    blocks = slots // block
    ready = twisted(0)
    for i in range(blocks):
        at = pl.ds(i * block, block)
        part_r = dot_nt(ready[0], tc[:, at])
        part_i = dot_nt(ready[1], ts[:, at])
        if i + 1 < blocks:
            ready = twisted(i + 1)
        out = out + (part_r - part_i)
    wait_all(copies)
    length = len_ref[band_ref[lax.axis_index("lat")]]
    out = out * (1.0 / jnp.sqrt(jnp.full(out.shape, length, jnp.int32).astype(F32)))
    chunks = os.shape[0] // 16
    for c in range(chunks):
        off = LANES * (c % 2)
        for phase in range(4):
            at = (2 * (c // 2) + phase // 2) * TWICE
            piece = out[at:at + TWICE, off:off + LANES]
            if phase % 2:
                piece = pltpu.roll(piece, TWICE - used, 0)
            os[16 * c:16 * (c + 1), LANES * phase:LANES * (phase + 1)] = piece[0:16].astype(BF16)
    merged = dot_nt(os[...], spread_s)
    for c in range(chunks):
        begin = 4 * LANES * c
        size = min(4 * LANES, width - begin)
        if size <= 0:
            continue
        inside = begin + lane_iota((16, size)) < length
        piece = jnp.where(inside, merged[16 * c:16 * (c + 1), 0:size], 0.0)
        for field in range(fields):
            grid_ref[field, 0, :, begin:begin + size] = piece[
                rows * field:rows * (field + 1)
            ].astype(BF16)


def prepare_kernel(
    cut_off, pairs, fields, rows, fold_hbm, band_hbm, rates_hbm, leg_hbm, tm_hbm, bm_hbm,
    eh_hbm, round_ref, mix_ref, back_ref, turn_ref, tau_ref, rate_ref,
    fold_ref, band_ref, rates_ref, leg_ref, tm_ref, bm_ref, sems, pad_s, eh_ref, out_sems,
):
    copies = start_all(
        (fold_hbm, band_hbm, rates_hbm, tm_hbm, bm_hbm, leg_hbm),
        (fold_ref, band_ref, rates_ref, tm_ref, bm_ref, leg_ref),
        sems,
    )
    wait_all(copies[:-1])
    everyone = tm_ref.shape[0]
    _, lats, places = leg_ref.shape
    groups_f = everyone // fields
    wf = fields * 2
    unit = rows * wf
    span = eh_ref.shape[1]
    eight = 8 * lats
    groups = eh_ref.shape[0] // (2 * eight)
    owner = lax.axis_index("lat") * groups_f + lax.axis_index("fld")

    pad_s[...] = jnp.zeros(pad_s.shape, F32)
    pad_s[0:everyone, 0:everyone] = tm_ref[...]
    shape = (LANES, LANES)
    level = (lane_iota(shape) // unit) * fields + (lane_iota(shape) % wf) // 2
    pick = jnp.where(row_iota(shape) == level, 1.0, 0.0).astype(BF16)
    lane = lane_iota((KPAD, LANES))
    parts = []
    for piece in split(pad_s[...]):
        wide = dot(piece, pick)
        total = []
        for c in range(2):
            for parity in range(2):
                keep = (lane % 2 == c) & (lane < unit * groups_f)
                flip = (lane % unit) // wf >= 1 if parity else lane < 0
                total.append(jnp.where(keep, jnp.where(flip, -wide, wide), 0.0))
        total.append(jnp.zeros((LANES - 4 * KPAD, LANES), F32))
        parts.append(jnp.concatenate(total, axis=0).astype(BF16))
    mix_ref[...] = jnp.concatenate([parts[0], parts[1], parts[0]], axis=1)

    pad_s[...] = jnp.zeros(pad_s.shape, F32)
    pad_s[0:everyone, 0:everyone] = bm_ref[...]
    shape = (FPAD, KPAD)
    expand = jnp.where(row_iota(shape) // 2 == lane_iota(shape), 1.0, 0.0).astype(BF16)
    shape = (LANES, 2 * LANES)
    repeat = jnp.where(row_iota(shape) == lane_iota(shape) % KPAD, 1.0, 0.0).astype(BF16)
    shape = (FPAD, 2 * LANES)
    same = row_iota(shape) % 2 == (lane_iota(shape) // KPAD) % 2
    for part, piece in enumerate(split(pad_s[...])):
        full = jnp.where(same, dot(dot(expand, piece).astype(BF16), repeat), 0.0)
        back_ref[part * FPAD:(part + 1) * FPAD, :] = full[:, 0:8 * KPAD].astype(BF16)
    shape = (LANES, LANES)
    row, lane = row_iota(shape), lane_iota(shape)
    width = 2 * everyone
    south = lane >= width
    level = jnp.where(south, lane - width, lane)
    pick = jnp.where(row == (level >> 1), 1.0, 0.0).astype(BF16)
    part = lax.div(row, KPAD)
    keep = ((part >> 1) == (level & 1)) & (part < 4) & (lane < 2 * width)
    flip = south & ((part & 1) == 1)
    wide = []
    for piece in split(jnp.transpose(jnp.concatenate([pad_s[...], jnp.zeros((LANES - KPAD, LANES), F32)], axis=0))):
        small = dot(piece, pick)[0:KPAD]
        tall = jnp.concatenate([small] * 5 + [jnp.zeros((LANES - 5 * KPAD, LANES), F32)], axis=0)
        wide.append(jnp.where(keep, jnp.where(flip, -tall, tall), 0.0).astype(BF16))
    turn_ref[...] = jnp.concatenate([wide[0], wide[0], wide[1]], axis=0)

    row = row_iota((KPAD, 2 * LANES))
    rate = jnp.zeros((KPAD, 2 * LANES), F32)
    for k in range(everyone):
        rate = jnp.where(row == k, rates_ref[k], rate)
    rate_ref[...] = rate
    wide_rate = jnp.concatenate([rate[:, 0:LANES]] * (span // LANES), axis=1)
    paired = tau_ref.shape[0]
    row = row_iota((paired, LANES))
    waves = []
    wave = jnp.zeros((paired, LANES), jnp.int32)
    for pair in range(4 * groups):
        waves.append(fold_ref[owner, 2 * min(pair, pairs - 1)])
        wave = jnp.where(row == 8 * (pair // 4) + pair % 4, waves[pair], wave)
    wave = jnp.concatenate([wave] * (span // LANES), axis=1)
    line = lane_iota((paired, span))
    degree = jnp.where(line > cut_off - wave, line - 1, line + wave)
    tau_ref[...] = (degree * (degree + 1)).astype(F32) * (1.0 / float(cut_off * (cut_off + 1)))

    quad_rows = 4 * lats
    shape = (quad_rows, quad_rows)
    band = jnp.zeros(shape, jnp.int32)
    for holder in range(lats):
        band = jnp.where(row_iota(shape) % lats == holder, band_ref[holder], band)
    order = jnp.where(
        (row_iota(shape) // lats == lane_iota(shape) // lats) & (lane_iota(shape) % lats == band),
        1.0,
        0.0,
    ).astype(BF16)

    whole = places // LANES * LANES
    line = lane_iota((quad_rows, span))
    row = row_iota((quad_rows, LANES)) // lats
    copies[-1].wait()
    keeps = []
    todo = []
    for t in range(groups):
        wave = jnp.zeros((quad_rows, LANES), jnp.int32)
        last = jnp.zeros((quad_rows, LANES), jnp.int32)
        stack = []
        for pp in range(4):
            there = 4 * t + pp < pairs
            index = min(4 * t + pp, pairs - 1)
            wave = jnp.where(row == pp, waves[4 * t + pp], wave)
            last = jnp.where(row == pp, places - 1 if there else -1, last)
            stack.append(
                jnp.concatenate(
                    [
                        leg_ref[index, :, 0:whole],
                        jnp.broadcast_to(leg_ref[index, :, whole:places], (lats, span - whole)),
                    ],
                    axis=1,
                )
            )
        wave = jnp.concatenate([wave] * (span // LANES), axis=1)
        last = jnp.concatenate([last] * (span // LANES), axis=1)
        leg = dot(order, jnp.concatenate(stack, axis=0).astype(BF16))
        before = line <= cut_off - wave
        first = before & (line <= last)
        second = jnp.logical_not(before) & (line <= last)
        odd = ((line + jnp.where(before, 0, wave)) & 1) == 1
        masks = [
            [jnp.where(side & odd, 1.0, 0.0) if par else jnp.where(odd, 0.0, jnp.where(side, 1.0, 0.0)) for par in range(2)]
            for side in (first, second)
        ]
        for par in range(2):
            near = leg * masks[0][par]
            far = leg * masks[1][par]
            for pp in range(4):
                at = 2 * eight * t + par * eight + 2 * pp * lats
                eh_ref[at:at + 2 * lats, :] = jnp.concatenate(
                    [near[pp * lats:(pp + 1) * lats], far[pp * lats:(pp + 1) * lats]], axis=0
                ).astype(BF16)
        part = pl.ds(2 * eight * t, 2 * eight)
        keeps.append(pltpu.make_async_copy(eh_ref.at[part], eh_hbm.at[part], out_sems.at[t]))
        keeps[-1].start()

        todo.append((leg, masks))

    rest = jnp.zeros((LANES - 4 * KPAD, span), F32)
    for t, (leg, masks) in enumerate(todo):
        for pp in range(4):
            own = leg[pp * lats:(pp + 1) * lats]
            pairs_of = jnp.concatenate([own * own[j:j + 1] for j in range(lats)], axis=0)
            pair = 4 * t + pp
            factor = pl.reciprocal(1.0 + tau_ref[8 * t + pp:8 * t + pp + 1, :] * wide_rate, approx=True)
            damp = []
            for side in range(2):
                for par in range(2):
                    mask = masks[side][par][pp * lats:pp * lats + 8]
                    damp.append(factor * jnp.concatenate([mask] * (KPAD // 8), axis=0))
            damp = jnp.concatenate(damp + [rest], axis=0).astype(BF16)
            at = pair * lats * lats
            round_ref[at:at + lats * lats, :] = dot_nt(pairs_of.astype(BF16), damp)
    wait_all(keeps)


def solve_kernel(
    fields, rows, lats, msg_ref, round_ref, mix_ref, turn_ref, mixed_ref, out_ref, cs,
):
    eight = 8 * lats
    groups = mixed_ref.shape[0] // eight
    groups_f = msg_ref.shape[0] // eight
    wf = fields * 2
    unit = rows * wf
    lane = lane_iota((lats, LANES))
    tiles = [
        [msg_ref[pl.ds(8 * g + i8, lats, stride=8 * groups_f), :] for g in range(groups_f)]
        for i8 in range(8)
    ]
    tall = []
    for t in range(groups):
        here = [lanes_within(lane, unit * (t + g), unit) for g in range(groups_f)]
        for i8 in range(8):
            line = tiles[i8][0]
            for g in range(1, groups_f):
                line = jnp.where(here[g], tiles[i8][g], line)
            if t:
                line = pltpu.roll(line, LANES - unit * t, 1)
            tall.append(line)
    v_high, v_low = split(jnp.concatenate(tall, axis=0))
    mixed_ref[...] = dot_nt(jnp.concatenate([v_high, v_high, v_low], axis=1), mix_ref[...])

    lane = lane_iota((lats, LANES))
    front = lane < 2 * KPAD
    sums = []
    for pair in range(4 * groups):
        one = mixed_ref[2 * pair * lats:(2 * pair + 1) * lats, :]
        two = mixed_ref[(2 * pair + 1) * lats:(2 * pair + 2) * lats, :]
        parts = (
            jnp.where(front, one, pltpu.roll(two, 2 * KPAD, 1)),
            jnp.where(front, pltpu.roll(one, LANES - 2 * KPAD, 1), two),
        )
        totals = [jnp.zeros((lats, LANES), F32) for _ in parts]
        for j in range(lats):
            at = (pair * lats + j) * lats
            matrix = round_ref[at:at + lats, :]
            totals = [
                total + part[j:j + 1] * matrix for total, part in zip(totals, parts)
            ]
        sums.append(jnp.where(front, totals[0], pltpu.roll(totals[1], 2 * KPAD, 1)))
        sums.append(jnp.where(front, pltpu.roll(totals[0], LANES - 2 * KPAD, 1), totals[1]))
    high, low = split(jnp.concatenate(sums, axis=0))
    cs[...] = dot(jnp.concatenate([high, low, high], axis=1), turn_ref[...])

    lane = lane_iota((8, LANES))
    here = [
        lanes_within(lane, wf * u, wf) for u in range(rows * groups + groups_f - 1)
    ]
    for holder in range(lats):
        tiles = [jnp.zeros((8, LANES), F32) for _ in range(groups_f)]
        for t in range(groups):
            piece = cs[pl.ds(t * eight + holder, 8, stride=lats), :]
            for r in range(rows):
                u = rows * t + r
                moved = pltpu.roll(piece, (wf * u - wf * groups_f * r) % LANES, 1)
                for g in range(groups_f):
                    tiles[g] = jnp.where(here[u + g], moved, tiles[g])
        for g in range(groups_f):
            at = (holder * groups_f + g) * 8
            out_ref[at:at + 8, :] = tiles[g]


def output_kernel(
    lats, eh_hbm, mixed_ref, tau_ref, rate_ref, back_ref, spec_ref, bk, eh_s, sems,
):
    everyone, quad, _, places = spec_ref.shape
    span = eh_s.shape[1]
    eight = 8 * lats
    tall = 2 * everyone
    step = pl.program_id(0)

    def fetch(t):
        part = pl.ds(pl.multiple_of(2 * eight * t, 16), 2 * eight)
        return pltpu.make_async_copy(eh_hbm.at[part], eh_s.at[part], sems.at[t])

    @pl.when(step == 0)
    def _():
        for t in range(sems.shape[0]):
            fetch(t).start()
        pair_of = lane_iota((tall, 8 * KPAD)) // (2 * KPAD)
        parts = []
        for part in range(2):
            full = back_ref[part * FPAD:part * FPAD + tall, :].astype(F32)
            for pp in range(4):
                parts.append(jnp.where(pair_of == pp, full, 0.0))
        bk[...] = jnp.concatenate(parts, axis=0).astype(BF16)

    rate = rate_ref[...]
    taus = tau_ref[pl.ds(pl.multiple_of(8 * step, 8), 8), :]
    mine = mixed_ref[pl.ds(pl.multiple_of(eight * step, 8), eight), :]
    if eight < LANES:
        mine = jnp.concatenate([mine, jnp.zeros((LANES - eight, LANES), F32)], axis=0)
    mine = [
        jnp.transpose(mine[at:at + LANES])[:, 0:min(eight, LANES)] for at in range(0, eight, LANES)
    ]
    mine = jnp.concatenate(mine, axis=1) if len(mine) > 1 else mine[0]
    mine = jnp.concatenate(
        [
            jnp.concatenate(
                [mine[par * KPAD:(par + 1) * KPAD], mine[(par + 2) * KPAD:(par + 3) * KPAD]], axis=0
            )
            for par in range(2)
        ],
        axis=1,
    )
    slot_pair = (lane_iota((2 * KPAD, 2 * eight)) & (eight - 1)) // (2 * lats)
    left = jnp.concatenate([jnp.where(slot_pair == pp, mine, 0.0) for pp in range(4)], axis=0)
    left = jnp.concatenate(split(left), axis=1)
    fetch(step).wait()
    legs = pl.ds(pl.multiple_of(2 * eight * step, 16), 2 * eight)
    for start in range(0, span, 2 * LANES):
        size = min(2 * LANES, span - start)
        right = eh_s[legs, start:start + size]
        modes = dot(left, jnp.concatenate([right, right], axis=0))
        damped = []
        for pp in range(4):
            tau = taus[pp:pp + 1, start:start + size]
            factor = pl.reciprocal(1.0 + tau * rate[:, 0:size], approx=True)
            at = 2 * pp * KPAD
            damped.append(modes[at:at + KPAD] * factor)
            damped.append(modes[at + KPAD:at + 2 * KPAD] * factor)
        spec = dot(bk[...], jnp.concatenate(damped, axis=0).astype(BF16))
        spec = spec[0:4 * tall] + spec[4 * tall:]
        kept = min(size, places - start)
        for pp in range(4):
            for f in range(everyone):
                row = pp * tall + 2 * f
                spec_ref[f, pp, :, start:start + kept] = spec[row:row + 2, 0:kept]


def per_device(grid, row_lengths, band_map, fold_map, legendre, to_modes, back_modes, mode_rates):
    fields, single, rows, width = grid.shape
    pairs, places, lats = legendre.shape
    cut_off = places - 2
    everyone = to_modes.shape[0]
    owners, per_owner = fold_map.shape
    groups = -(-per_owner // 8)
    slots = owners * groups * 8
    pieces = -(-(width // 4) // DEEP)
    turns = 4 * pieces
    span = -(-places // LANES) * LANES
    hbm = pl.BlockSpec(memory_space=pltpu.HBM)
    vmem = pl.BlockSpec(memory_space=pltpu.VMEM)
    room = pltpu.CompilerParams(vmem_limit_bytes=ROOM)
    message = pltpu.HBM((owners, 8, LANES), F32)
    holders = band_map.shape[0]
    groups_f = everyone // fields
    dma = pltpu.SemaphoreType.DMA
    row_lengths, band_map, fold_map, to_modes, back_modes, mode_rates, grid = (
        pltpu.with_memory_space_constraint(x, pltpu.HBM)
        for x in (row_lengths, band_map, fold_map, to_modes, back_modes, mode_rates, grid)
    )
    legendre = pltpu.with_memory_space_constraint(jnp.transpose(legendre, (0, 2, 1)), pltpu.HBM)

    sending, cos_table, sin_table, cos_turn, sin_turn = pl.pallas_call(
        functools.partial(forward_kernel, cut_off, groups),
        out_shape=(
            message,
            pltpu.VMEM((DEEP, slots), BF16),
            pltpu.VMEM((DEEP, slots), BF16),
            pltpu.VMEM((turns, slots), F32),
            pltpu.VMEM((turns, slots), F32),
        ),
        in_specs=[hbm] * 4,
        out_specs=(vmem,) * 5,
        scratch_shapes=[
            pltpu.SMEM(row_lengths.shape, jnp.int32),
            pltpu.SMEM(band_map.shape, jnp.int32),
            pltpu.VMEM(fold_map.shape, jnp.int32),
            pltpu.VMEM(grid.shape, BF16),
            dma((4,)),
            pltpu.VMEM((LANES, LANES), F32),
            pltpu.VMEM((8, slots), F32),
            pltpu.VMEM((16, 4 * DEEP * pieces), F32),
            pltpu.VMEM((4 * TWICE, slots), BF16),
        ],
        compiler_params=room,
        name="forward_rows",
    )(row_lengths, band_map, fold_map, grid)
    tables = [
        pltpu.with_memory_space_constraint(x, pltpu.VMEM)
        for x in (cos_table, sin_table, cos_turn, sin_turn)
    ]
    arrived = lax.all_to_all(sending, ("lat", "fld"), split_axis=0, concat_axis=0, tiled=True)

    legs, rounds, mix, back, turn_back, tau, rate = pl.pallas_call(
        functools.partial(prepare_kernel, cut_off, pairs, fields, rows),
        out_shape=(
            pltpu.HBM((groups * 16 * lats, span), BF16),
            pltpu.VMEM((groups * 4 * lats * lats, LANES), F32),
            pltpu.VMEM((LANES, 3 * LANES), BF16),
            pltpu.HBM((2 * FPAD, 8 * KPAD), BF16),
            pltpu.VMEM((3 * LANES, LANES), BF16),
            pltpu.HBM((8 * groups, span), F32),
            pltpu.HBM((KPAD, 2 * LANES), F32),
        ),
        in_specs=[hbm] * 6,
        out_specs=(hbm,) + (vmem,) * 6,
        scratch_shapes=[
            pltpu.SMEM(fold_map.shape, jnp.int32),
            pltpu.SMEM(band_map.shape, jnp.int32),
            pltpu.SMEM(mode_rates.shape, F32),
            pltpu.VMEM((pairs, lats, places), F32),
            pltpu.VMEM(to_modes.shape, F32),
            pltpu.VMEM(back_modes.shape, F32),
            dma((6,)),
            pltpu.VMEM((KPAD, LANES), F32),
            pltpu.VMEM((groups * 16 * lats, span), BF16),
            dma((groups,)),
        ],
        compiler_params=pltpu.CompilerParams(vmem_limit_bytes=2 * ROOM),
        cost_estimate=pl.CostEstimate(flops=10**8, bytes_accessed=8 * 10**6, transcendentals=0),
        name="prepare",
    )(fold_map, band_map, mode_rates, legendre, to_modes, back_modes)
    legs, back, tau, rate = (
        pltpu.with_memory_space_constraint(x, pltpu.HBM) for x in (legs, back, tau, rate)
    )
    rounds, mix, turn_back = (
        pltpu.with_memory_space_constraint(x, pltpu.VMEM) for x in (rounds, mix, turn_back)
    )

    mixed, leaving = pl.pallas_call(
        functools.partial(solve_kernel, fields, rows, lats),
        out_shape=(
            pltpu.VMEM((groups * 8 * lats, LANES), F32),
            pltpu.HBM((owners * 8, LANES), F32),
        ),
        in_specs=[vmem] * 4,
        out_specs=(vmem,) * 2,
        scratch_shapes=[pltpu.VMEM((groups * 8 * lats, LANES), F32)],
        compiler_params=room,
        name="solve",
    )(arrived.reshape(owners * 8, LANES), rounds, mix, turn_back)
    leaving = leaving.reshape(owners, 8, LANES)

    returned = lax.all_to_all(leaving, ("lat", "fld"), split_axis=0, concat_axis=0, tiled=True)

    mixed = pltpu.with_memory_space_constraint(mixed, pltpu.VMEM)
    spectral = pl.pallas_call(
        functools.partial(output_kernel, lats),
        grid=(groups,),
        out_shape=jax.ShapeDtypeStruct((everyone, pairs, 2, places), F32),
        in_specs=[
            hbm,
            vmem,
            vmem,
            vmem,
            vmem,
        ],
        out_specs=pl.BlockSpec((everyone, 4, 2, places), lambda t: (0, t, 0, 0)),
        scratch_shapes=[
            pltpu.VMEM((16 * everyone, 8 * KPAD), BF16),
            pltpu.VMEM((groups * 16 * lats, span), BF16),
            dma((groups,)),
        ],
        compiler_params=pltpu.CompilerParams(
            dimension_semantics=("arbitrary",), vmem_limit_bytes=ROOM
        ),
        cost_estimate=pl.CostEstimate(flops=10**8, bytes_accessed=8 * 10**6, transcendentals=0),
        name="spectral_output",
    )(legs, mixed, tau, rate, back)

    grid_out = pl.pallas_call(
        functools.partial(inverse_kernel, groups),
        out_shape=jax.ShapeDtypeStruct(grid.shape, BF16),
        in_specs=[hbm] * 2 + [vmem] * 5,
        out_specs=vmem,
        scratch_shapes=[
            pltpu.SMEM(row_lengths.shape, jnp.int32),
            pltpu.SMEM(band_map.shape, jnp.int32),
            dma((2,)),
            pltpu.VMEM((32 * pieces, 4 * LANES), BF16),
        ],
        compiler_params=room,
        name="inverse_rows",
    )(row_lengths, band_map, *tables, returned)
    return (jnp.transpose(spectral, (0, 2, 1, 3)), grid_out)


def solution(mesh):
    placed = (
        P("fld", "lat", None, None),
        P(),
        P(),
        P(),
        P(("lat", "fld"), None, None),
        P(),
        P(),
        P(),
    )
    return jax.shard_map(
        per_device,
        mesh=mesh,
        in_specs=placed,
        out_specs=(P(None, None, ("lat", "fld"), None), P("fld", "lat", None, None)),
        check_vma=False,
    )
```

```python
import functools
import math

import jax
import jax.numpy as jnp
from jax import lax
from jax.experimental import pallas as pl
from jax.experimental.pallas import tpu as pltpu
from jax.sharding import PartitionSpec as P

LANES = 128
KPAD = 24
FPAD = 64
DEEP = 256
TWICE = 24
ROOM = 24 * 1024 * 1024
F32 = jnp.float32
BF16 = jnp.bfloat16
NT_DIMS = (((1,), (1,)), ((), ()))
SIN_POLY = (
    6.283185302447051,
    -41.34170038368319,
    81.60513023312113,
    -76.70299324464969,
    42.02573766814694,
    -14.899106966102595,
    3.237062655726421,
)
COS_POLY = (
    0.9999999889083757,
    -19.739204448887243,
    64.93911476570418,
    -85.45008785413638,
    60.167188450194914,
    -25.9658703083255,
    6.526145851512229,
)


def dot(a, b):
    return jnp.dot(a, b, preferred_element_type=F32)


def dot_nt(a, b):
    return lax.dot_general(a, b, NT_DIMS, preferred_element_type=F32)


def split(x):
    high = x.astype(BF16)
    return high, (x - high.astype(F32)).astype(BF16)


def horner(coefs, z):
    total = coefs[-1] * z + coefs[-2]
    for coef in coefs[-3::-1]:
        total = total * z + coef
    return total


def turn(steps, period, inverse):
    rest = steps - period * jnp.floor(steps * inverse + 0.5)
    part = rest * inverse
    z = part * part
    return horner(COS_POLY, z), part * horner(SIN_POLY, z)


def start_all(sources, targets, sems):
    copies = [
        pltpu.make_async_copy(source, target, sems.at[i])
        for i, (source, target) in enumerate(zip(sources, targets))
    ]
    for copy in copies:
        copy.start()
    return copies


def wait_all(copies):
    for copy in copies:
        copy.wait()


def lane_iota(shape):
    return lax.broadcasted_iota(jnp.int32, shape, len(shape) - 1)


def row_iota(shape):
    return lax.broadcasted_iota(jnp.int32, shape, len(shape) - 2)


def lanes_within(lane, start, size):
    start %= LANES
    if start + size <= LANES:
        return (lane >= start) & (lane < start + size)
    return (lane >= start) | (lane < start + size - LANES)


def spread_matrix():
    shape = (4 * LANES, LANES)
    picks = []
    for phase in range(4):
        picks.append(jnp.where(row_iota(shape) == 4 * lane_iota(shape) + phase, 1.0, 0.0))
    return jnp.concatenate(picks, axis=1).astype(BF16)


def phase_steps(groups, lanes):
    row = row_iota((groups + 16, lanes))
    steps = jnp.where(row < groups, (row >> 2) * (4 * DEEP) + (row & 3), 4 * (row - groups))
    steps = jnp.where(row >= groups + 8, 32 << jnp.maximum(row - groups - 8, 0), steps)
    return steps.astype(F32)


def slot_lane(index, fields, rows):
    used = rows * fields
    part = (index >= TWICE).astype(jnp.int32)
    row = index - TWICE * part
    vec = jnp.where(row >= used, row - used, row)
    lane = lax.rem(vec, rows) * (fields * 2) + lax.div(vec, rows) * 2 + part
    return jnp.where(row < 2 * used, lane, -LANES)


def two_phases(ref, g, at, used, block):
    first = ref[2 * g:2 * g + 1, at]
    second = ref[2 * g + 1:2 * g + 2, at]
    tiles = []
    for low in range(0, TWICE, 8):
        if low + 8 <= used:
            tiles.append(jnp.broadcast_to(first, (8, block)))
        elif low >= used:
            tiles.append(jnp.broadcast_to(second, (8, block)))
        else:
            tiles.append(jnp.where(low + row_iota((8, block)) < used, first, second))
    return jnp.concatenate(tiles, axis=0)


def forward_kernel(
    cut_off, groups, len_hbm, band_hbm, fold_hbm, grid_hbm,
    msg_ref, tc, ts, fc, fs,
    len_ref, band_ref, fold_ref, grid_ref, sems, fold_s, wave_s, xs, xt,
):
    copies = start_all(
        (len_hbm, band_hbm, fold_hbm, grid_hbm), (len_ref, band_ref, fold_ref, grid_ref), sems
    )
    fields, _, rows, width = grid_ref.shape
    owners, per_owner = fold_ref.shape
    slots = tc.shape[1]
    pieces = xs.shape[1] // (4 * DEEP)
    unit = rows * fields * 2
    used = rows * fields
    spread_s = spread_matrix()
    shape = (LANES, owners * 8)
    repeat = jnp.where(row_iota(shape) == lane_iota(shape) >> 3, 1.0, 0.0).astype(BF16)
    shape = (8 * groups, 16 * groups)
    weigh = jnp.where(
        jnp.where(lane_iota(shape) < 8 * groups, lane_iota(shape), lane_iota(shape) - 8 * groups) >> 3
        == row_iota(shape) >> 3,
        jnp.where(lane_iota(shape) < 8 * groups, 8.0, 1.0),
        0.0,
    ).astype(BF16)
    tall = 4 * TWICE
    shape = (LANES, tall * groups)
    one = (1, 2 * TWICE)
    base = slot_lane(lane_iota(one), fields, rows)
    targets = []
    for t in range(groups):
        target = base + unit * (t + lax.axis_index("fld"))
        target = jnp.where(base < 0, base, target & (LANES - 1))
        targets += [target, target]
    target = jnp.concatenate(targets, axis=1)
    packing = jnp.where(row_iota(shape) == target, 1.0, 0.0).astype(BF16)
    fold_s[...] = jnp.full(fold_s.shape, -1.0, F32)
    xs[...] = jnp.zeros(xs.shape, F32)
    wait_all(copies)
    length = len_ref[band_ref[lax.axis_index("lat")]]
    top = jnp.minimum(cut_off, (length - 1) // 2)

    fold_s[0:owners, 0:per_owner] = fold_ref[...].astype(F32)
    turned = jnp.transpose(fold_s[...])[0:8 * groups]
    eights = jnp.floor(turned * 0.125)
    parts = jnp.concatenate([eights, turned - 8.0 * eights], axis=0).astype(BF16)
    repeated = dot(parts, repeat)
    own = (lane_iota(repeated.shape) & 7) == (row_iota(repeated.shape) & 7)
    waves = dot(weigh, jnp.where(own, repeated, 0.0).astype(BF16))
    for t in range(groups):
        wave_s[:, owners * 8 * t:owners * 8 * (t + 1)] = waves[8 * t:8 * t + 8]

    for field in range(fields):
        xs[rows * field:rows * (field + 1), 0:width] = grid_ref[field, 0].astype(F32)
    stacked = jnp.concatenate(
        [xs[:, 4 * LANES * c:4 * LANES * (c + 1)] for c in range(2 * pieces)], axis=0
    ).astype(BF16)
    spread = dot(stacked, spread_s)
    blank = jnp.zeros((TWICE - 16, LANES), F32)
    values = []
    for k in range(pieces):
        for pair in range(2):
            halves = []
            for half in range(2):
                c = 2 * k + half
                off = 2 * LANES * pair
                rows_c = spread[16 * c:16 * (c + 1)]
                inside = c * LANES + lane_iota((16, LANES)) < length // 4
                first, second = (
                    jnp.concatenate([jnp.where(inside, rows_c[:, o:o + LANES], 0.0), blank], axis=0)
                    for o in (off, off + LANES)
                )
                halves.append(first + pltpu.roll(second, used, 0))
            values.append(jnp.concatenate(halves, axis=1))
    values = jnp.concatenate(values, axis=0).astype(BF16)

    turns = 4 * pieces
    block = 2 * LANES
    steps = phase_steps(turns, block)
    period = jnp.full((1, block), length, jnp.int32).astype(F32)
    inverse = 1.0 / period
    def make_tables(i):
        at = pl.ds(i * block, block)
        wave = wave_s[:, at]
        wave = jnp.concatenate([wave] * ((turns + 16) // 8), axis=0)
        co, si = turn(steps * wave, period, inverse)
        one = wave[0:1]
        weight = jnp.where(one == 0.0, 1.0, 2.0)
        limit = jnp.full(one.shape, top, jnp.int32).astype(F32)
        weight = jnp.where((one >= 0.0) & (one <= limit), weight, 0.0)
        fc[:, at] = co[0:turns] * weight
        fs[:, at] = si[0:turns] * weight
        c_all = co[turns:turns + 8]
        s_all = si[turns:turns + 8]
        size, step = 8, turns + 8
        while size < DEEP:
            c1 = co[step:step + 1]
            s1 = si[step:step + 1]
            c_new = c_all * c1 - s_all * s1
            s_new = s_all * c1 + c_all * s1
            c_all = jnp.concatenate([c_all, c_new], axis=0)
            s_all = jnp.concatenate([s_all, s_new], axis=0)
            size, step = 2 * size, step + 1
        c_all = c_all.astype(BF16)
        s_all = s_all.astype(BF16)
        tc[:, at] = c_all
        ts[:, at] = s_all
        return c_all, s_all

    def finish(i, inner_c, inner_s):
        at = pl.ds(i * block, block)
        real = jnp.zeros((TWICE, block), F32)
        imag = jnp.zeros((TWICE, block), F32)
        for g in range(turns // 2):
            c1 = two_phases(fc, g, at, used, block)
            s1 = two_phases(fs, g, at, used, block)
            part_c = inner_c[TWICE * g:TWICE * (g + 1)]
            part_s = inner_s[TWICE * g:TWICE * (g + 1)]
            real = real + (c1 * part_c - s1 * part_s)
            imag = imag - (c1 * part_s + s1 * part_c)
        fix = jnp.where(wave_s[0:1, at] == 0.0, 1.0, 0.5)
        both = jnp.concatenate([real, imag], axis=0) * fix
        xt[:, at] = jnp.concatenate(split(both), axis=0)

    blocks = slots // block
    ready = make_tables(0)
    for i in range(blocks):
        inner_c = dot(values, ready[0])
        inner_s = dot(values, ready[1])
        if i + 1 < blocks:
            ready = make_tables(i + 1)
        finish(i, inner_c, inner_s)

    turned = jnp.concatenate(
        [xt[:, owners * 8 * t:owners * 8 * (t + 1)] for t in range(groups)], axis=0
    )
    total = dot(packing, turned)
    scale = 1.0 / jnp.sqrt(jnp.full(total.shape, length, jnp.int32).astype(F32))
    msg_ref[...] = jnp.transpose(total * scale).reshape(owners, 8, LANES)


def inverse_kernel(
    groups, len_hbm, band_hbm, tc, ts, fc, fs, msg_ref, grid_ref,
    len_ref, band_ref, sems, os,
):
    copies = start_all((len_hbm, band_hbm), (len_ref, band_ref), sems)
    spread_s = spread_matrix()
    fields, _, rows, width = grid_ref.shape
    owners = msg_ref.shape[0]
    slots = tc.shape[1]
    turns = fc.shape[0]
    unit = rows * fields * 2
    high, low = split(msg_ref[...].reshape(owners * 8, LANES))
    pieces = jnp.concatenate([high, low], axis=1)
    used = rows * fields
    tall = 2 * TWICE
    shape = (tall, LANES)
    base = slot_lane(row_iota(shape), fields, rows)
    places = []
    for t in range(groups):
        source = (base + unit * t + lax.axis_index("fld") * (fields * 2)) & (LANES - 1)
        source = jnp.where(base < 0, base, source)
        places.append(jnp.where(lane_iota(shape) == source, 1.0, 0.0))
    place = jnp.concatenate(places, axis=0).astype(BF16)
    place = jnp.concatenate([place, place], axis=1)
    turned = dot_nt(place, pieces)
    block = 2 * LANES
    out = jnp.zeros((TWICE * turns // 2, DEEP), F32)
    def twisted(i):
        t, off = divmod(i * block, owners * 8)
        real = turned[tall * t:tall * t + TWICE, off:off + block]
        imag = turned[tall * t + TWICE:tall * (t + 1), off:off + block]
        at = pl.ds(i * block, block)
        reals, imags = [], []
        for g in range(turns // 2):
            c1 = two_phases(fc, g, at, used, block)
            s1 = two_phases(fs, g, at, used, block)
            reals.append(c1 * real - s1 * imag)
            imags.append(s1 * real + c1 * imag)
        return (
            jnp.concatenate(reals, axis=0).astype(BF16),
            jnp.concatenate(imags, axis=0).astype(BF16),
        )

    blocks = slots // block
    ready = twisted(0)
    for i in range(blocks):
        at = pl.ds(i * block, block)
        part_r = dot_nt(ready[0], tc[:, at])
        part_i = dot_nt(ready[1], ts[:, at])
        if i + 1 < blocks:
            ready = twisted(i + 1)
        out = out + (part_r - part_i)
    wait_all(copies)
    length = len_ref[band_ref[lax.axis_index("lat")]]
    out = out * (1.0 / jnp.sqrt(jnp.full(out.shape, length, jnp.int32).astype(F32)))
    chunks = os.shape[0] // 16
    for c in range(chunks):
        off = LANES * (c % 2)
        for phase in range(4):
            at = (2 * (c // 2) + phase // 2) * TWICE
            piece = out[at:at + TWICE, off:off + LANES]
            if phase % 2:
                piece = pltpu.roll(piece, TWICE - used, 0)
            os[16 * c:16 * (c + 1), LANES * phase:LANES * (phase + 1)] = piece[0:16].astype(BF16)
    merged = dot_nt(os[...], spread_s)
    for c in range(chunks):
        begin = 4 * LANES * c
        size = min(4 * LANES, width - begin)
        if size <= 0:
            continue
        inside = begin + lane_iota((16, size)) < length
        piece = jnp.where(inside, merged[16 * c:16 * (c + 1), 0:size], 0.0)
        for field in range(fields):
            grid_ref[field, 0, :, begin:begin + size] = piece[
                rows * field:rows * (field + 1)
            ].astype(BF16)


def prepare_kernel(
    cut_off, pairs, fields, rows, fold_hbm, band_hbm, rates_hbm, leg_hbm, tm_hbm, bm_hbm,
    eh_hbm, round_ref, mix_ref, back_hbm, turn_ref, tau_hbm, rate_hbm,
    fold_ref, band_ref, rates_ref, leg_ref, tm_ref, bm_ref, sems, pad_s, eh_ref, out_sems,
    back_ref, tau_ref, rate_ref, small_sems,
):
    copies = start_all(
        (fold_hbm, band_hbm, rates_hbm, tm_hbm, bm_hbm, leg_hbm),
        (fold_ref, band_ref, rates_ref, tm_ref, bm_ref, leg_ref),
        sems,
    )
    wait_all(copies[:-1])
    everyone = tm_ref.shape[0]
    _, lats, places = leg_ref.shape
    groups_f = everyone // fields
    wf = fields * 2
    unit = rows * wf
    span = eh_ref.shape[1]
    eight = 8 * lats
    groups = eh_ref.shape[0] // (2 * eight)
    owner = lax.axis_index("lat") * groups_f + lax.axis_index("fld")

    pad_s[...] = jnp.zeros(pad_s.shape, F32)
    pad_s[0:everyone, 0:everyone] = tm_ref[...]
    shape = (LANES, LANES)
    level = (lane_iota(shape) // unit) * fields + (lane_iota(shape) % wf) // 2
    pick = jnp.where(row_iota(shape) == level, 1.0, 0.0).astype(BF16)
    lane = lane_iota((KPAD, LANES))
    parts = []
    for piece in split(pad_s[...]):
        wide = dot(piece, pick)
        total = []
        for c in range(2):
            for parity in range(2):
                keep = (lane % 2 == c) & (lane < unit * groups_f)
                flip = (lane % unit) // wf >= 1 if parity else lane < 0
                total.append(jnp.where(keep, jnp.where(flip, -wide, wide), 0.0))
        total.append(jnp.zeros((LANES - 4 * KPAD, LANES), F32))
        parts.append(jnp.concatenate(total, axis=0).astype(BF16))
    mix_ref[...] = jnp.concatenate([parts[0], parts[1], parts[0]], axis=1)

    pad_s[...] = jnp.zeros(pad_s.shape, F32)
    pad_s[0:everyone, 0:everyone] = bm_ref[...]
    shape = (FPAD, KPAD)
    expand = jnp.where(row_iota(shape) // 2 == lane_iota(shape), 1.0, 0.0).astype(BF16)
    shape = (LANES, 2 * LANES)
    repeat = jnp.where(row_iota(shape) == lane_iota(shape) % KPAD, 1.0, 0.0).astype(BF16)
    shape = (FPAD, 2 * LANES)
    same = row_iota(shape) % 2 == (lane_iota(shape) // KPAD) % 2
    for part, piece in enumerate(split(pad_s[...])):
        full = jnp.where(same, dot(dot(expand, piece).astype(BF16), repeat), 0.0)
        back_ref[part * FPAD:(part + 1) * FPAD, :] = full[:, 0:8 * KPAD].astype(BF16)
    shape = (LANES, LANES)
    row, lane = row_iota(shape), lane_iota(shape)
    width = 2 * everyone
    south = lane >= width
    level = jnp.where(south, lane - width, lane)
    pick = jnp.where(row == (level >> 1), 1.0, 0.0).astype(BF16)
    part = lax.div(row, KPAD)
    keep = ((part >> 1) == (level & 1)) & (part < 4) & (lane < 2 * width)
    flip = south & ((part & 1) == 1)
    wide = []
    for piece in split(jnp.transpose(jnp.concatenate([pad_s[...], jnp.zeros((LANES - KPAD, LANES), F32)], axis=0))):
        small = dot(piece, pick)[0:KPAD]
        tall = jnp.concatenate([small] * 5 + [jnp.zeros((LANES - 5 * KPAD, LANES), F32)], axis=0)
        wide.append(jnp.where(keep, jnp.where(flip, -tall, tall), 0.0).astype(BF16))
    turn_ref[...] = jnp.concatenate([wide[0], wide[0], wide[1]], axis=0)

    row = row_iota((KPAD, 2 * LANES))
    rate = jnp.zeros((KPAD, 2 * LANES), F32)
    for k in range(everyone):
        rate = jnp.where(row == k, rates_ref[k], rate)
    rate_ref[...] = rate
    wide_rate = jnp.concatenate([rate[:, 0:LANES]] * (span // LANES), axis=1)
    paired = tau_ref.shape[0]
    row = row_iota((paired, LANES))
    waves = []
    wave = jnp.zeros((paired, LANES), jnp.int32)
    for pair in range(4 * groups):
        waves.append(fold_ref[owner, 2 * min(pair, pairs - 1)])
        wave = jnp.where(row == 8 * (pair // 4) + pair % 4, waves[pair], wave)
    wave = jnp.concatenate([wave] * (span // LANES), axis=1)
    line = lane_iota((paired, span))
    degree = jnp.where(line > cut_off - wave, line - 1, line + wave)
    tau_ref[...] = (degree * (degree + 1)).astype(F32) * (1.0 / float(cut_off * (cut_off + 1)))

    quad_rows = 4 * lats
    shape = (quad_rows, quad_rows)
    band = jnp.zeros(shape, jnp.int32)
    for holder in range(lats):
        band = jnp.where(row_iota(shape) % lats == holder, band_ref[holder], band)
    order = jnp.where(
        (row_iota(shape) // lats == lane_iota(shape) // lats) & (lane_iota(shape) % lats == band),
        1.0,
        0.0,
    ).astype(BF16)

    whole = places // LANES * LANES
    line = lane_iota((quad_rows, span))
    row = row_iota((quad_rows, LANES)) // lats
    copies[-1].wait()
    keeps = start_all((back_ref, tau_ref, rate_ref), (back_hbm, tau_hbm, rate_hbm), small_sems)
    todo = []
    for t in range(groups):
        wave = jnp.zeros((quad_rows, LANES), jnp.int32)
        last = jnp.zeros((quad_rows, LANES), jnp.int32)
        stack = []
        for pp in range(4):
            there = 4 * t + pp < pairs
            index = min(4 * t + pp, pairs - 1)
            wave = jnp.where(row == pp, waves[4 * t + pp], wave)
            last = jnp.where(row == pp, places - 1 if there else -1, last)
            stack.append(
                jnp.concatenate(
                    [
                        leg_ref[index, :, 0:whole],
                        jnp.broadcast_to(leg_ref[index, :, whole:places], (lats, span - whole)),
                    ],
                    axis=1,
                )
            )
        wave = jnp.concatenate([wave] * (span // LANES), axis=1)
        last = jnp.concatenate([last] * (span // LANES), axis=1)
        leg = dot(order, jnp.concatenate(stack, axis=0).astype(BF16))
        before = line <= cut_off - wave
        first = before & (line <= last)
        second = jnp.logical_not(before) & (line <= last)
        odd = ((line + jnp.where(before, 0, wave)) & 1) == 1
        masks = [
            [jnp.where(side & odd, 1.0, 0.0) if par else jnp.where(odd, 0.0, jnp.where(side, 1.0, 0.0)) for par in range(2)]
            for side in (first, second)
        ]
        for par in range(2):
            near = leg * masks[0][par]
            far = leg * masks[1][par]
            for pp in range(4):
                at = 2 * eight * t + par * eight + 2 * pp * lats
                eh_ref[at:at + 2 * lats, :] = jnp.concatenate(
                    [near[pp * lats:(pp + 1) * lats], far[pp * lats:(pp + 1) * lats]], axis=0
                ).astype(BF16)
        part = pl.ds(2 * eight * t, 2 * eight)
        keeps.append(pltpu.make_async_copy(eh_ref.at[part], eh_hbm.at[part], out_sems.at[t]))
        keeps[-1].start()

        todo.append((leg, masks))

    rest = jnp.zeros((LANES - 4 * KPAD, span), F32)
    for t, (leg, masks) in enumerate(todo):
        for pp in range(4):
            own = leg[pp * lats:(pp + 1) * lats]
            pairs_of = jnp.concatenate([own * own[j:j + 1] for j in range(lats)], axis=0)
            pair = 4 * t + pp
            factor = pl.reciprocal(1.0 + tau_ref[8 * t + pp:8 * t + pp + 1, :] * wide_rate, approx=True)
            damp = []
            for side in range(2):
                for par in range(2):
                    mask = masks[side][par][pp * lats:pp * lats + 8]
                    damp.append(factor * jnp.concatenate([mask] * (KPAD // 8), axis=0))
            damp = jnp.concatenate(damp + [rest], axis=0).astype(BF16)
            at = pair * lats * lats
            round_ref[at:at + lats * lats, :] = dot_nt(pairs_of.astype(BF16), damp)
    wait_all(keeps)


def solve_kernel(
    fields, rows, lats, msg_ref, round_ref, mix_ref, turn_ref, mixed_ref, out_ref, cs,
):
    eight = 8 * lats
    groups = mixed_ref.shape[0] // eight
    groups_f = msg_ref.shape[0] // eight
    wf = fields * 2
    unit = rows * wf
    lane = lane_iota((lats, LANES))
    tiles = [
        [msg_ref[pl.ds(8 * g + i8, lats, stride=8 * groups_f), :] for g in range(groups_f)]
        for i8 in range(8)
    ]
    tall = []
    for t in range(groups):
        here = [lanes_within(lane, unit * (t + g), unit) for g in range(groups_f)]
        for i8 in range(8):
            line = tiles[i8][0]
            for g in range(1, groups_f):
                line = jnp.where(here[g], tiles[i8][g], line)
            if t:
                line = pltpu.roll(line, LANES - unit * t, 1)
            tall.append(line)
    v_high, v_low = split(jnp.concatenate(tall, axis=0))
    mixed_ref[...] = dot_nt(jnp.concatenate([v_high, v_high, v_low], axis=1), mix_ref[...])

    lane = lane_iota((lats, LANES))
    front = lane < 2 * KPAD
    sums = []
    for pair in range(4 * groups):
        one = mixed_ref[2 * pair * lats:(2 * pair + 1) * lats, :]
        two = mixed_ref[(2 * pair + 1) * lats:(2 * pair + 2) * lats, :]
        parts = (
            jnp.where(front, one, pltpu.roll(two, 2 * KPAD, 1)),
            jnp.where(front, pltpu.roll(one, LANES - 2 * KPAD, 1), two),
        )
        totals = [jnp.zeros((lats, LANES), F32) for _ in parts]
        for j in range(lats):
            at = (pair * lats + j) * lats
            matrix = round_ref[at:at + lats, :]
            totals = [
                total + part[j:j + 1] * matrix for total, part in zip(totals, parts)
            ]
        sums.append(jnp.where(front, totals[0], pltpu.roll(totals[1], 2 * KPAD, 1)))
        sums.append(jnp.where(front, pltpu.roll(totals[0], LANES - 2 * KPAD, 1), totals[1]))
    high, low = split(jnp.concatenate(sums, axis=0))
    cs[...] = dot(jnp.concatenate([high, low, high], axis=1), turn_ref[...])

    lane = lane_iota((8, LANES))
    here = [
        lanes_within(lane, wf * u, wf) for u in range(rows * groups + groups_f - 1)
    ]
    for holder in range(lats):
        tiles = [jnp.zeros((8, LANES), F32) for _ in range(groups_f)]
        for t in range(groups):
            piece = cs[pl.ds(t * eight + holder, 8, stride=lats), :]
            for r in range(rows):
                u = rows * t + r
                moved = pltpu.roll(piece, (wf * u - wf * groups_f * r) % LANES, 1)
                for g in range(groups_f):
                    tiles[g] = jnp.where(here[u + g], moved, tiles[g])
        for g in range(groups_f):
            at = (holder * groups_f + g) * 8
            out_ref[at:at + 8, :] = tiles[g]


def output_kernel(
    lats, eh_hbm, tau_hbm, rate_hbm, back_hbm, mixed_ref, spec_ref,
    bk, eh_s, sems, tau_ref, rate_ref, back_ref, small_sems,
):
    everyone, quad, _, places = spec_ref.shape
    span = eh_s.shape[1]
    eight = 8 * lats
    tall = 2 * everyone
    step = pl.program_id(0)

    def fetch(t):
        part = pl.ds(pl.multiple_of(2 * eight * t, 16), 2 * eight)
        return pltpu.make_async_copy(eh_hbm.at[part], eh_s.at[part], sems.at[t])

    @pl.when(step == 0)
    def _():
        small = start_all((back_hbm, tau_hbm, rate_hbm), (back_ref, tau_ref, rate_ref), small_sems)
        for t in range(sems.shape[0]):
            fetch(t).start()
        wait_all(small)
        pair_of = lane_iota((tall, 8 * KPAD)) // (2 * KPAD)
        full = back_ref[0:tall, :].astype(F32)
        parts = [jnp.where(pair_of == pp, full, 0.0) for pp in range(4)]
        bk[...] = jnp.concatenate(parts, axis=0).astype(BF16)

    rate = rate_ref[...]
    taus = tau_ref[pl.ds(pl.multiple_of(8 * step, 8), 8), :]
    mine = mixed_ref[pl.ds(pl.multiple_of(eight * step, 8), eight), :]
    if eight < LANES:
        mine = jnp.concatenate([mine, jnp.zeros((LANES - eight, LANES), F32)], axis=0)
    mine = [
        jnp.transpose(mine[at:at + LANES])[:, 0:min(eight, LANES)] for at in range(0, eight, LANES)
    ]
    mine = jnp.concatenate(mine, axis=1) if len(mine) > 1 else mine[0]
    mine = jnp.concatenate(
        [
            jnp.concatenate(
                [mine[par * KPAD:(par + 1) * KPAD], mine[(par + 2) * KPAD:(par + 3) * KPAD]], axis=0
            )
            for par in range(2)
        ],
        axis=1,
    )
    slot_pair = (lane_iota((2 * KPAD, 2 * eight)) & (eight - 1)) // (2 * lats)
    left = jnp.concatenate([jnp.where(slot_pair == pp, mine, 0.0) for pp in range(4)], axis=0)
    left = left.astype(BF16)
    fetch(step).wait()
    legs = pl.ds(pl.multiple_of(2 * eight * step, 16), 2 * eight)
    for start in range(0, span, 2 * LANES):
        size = min(2 * LANES, span - start)
        modes = dot(left, eh_s[legs, start:start + size])
        damped = []
        for pp in range(4):
            tau = taus[pp:pp + 1, start:start + size]
            factor = pl.reciprocal(1.0 + tau * rate[:, 0:size], approx=True)
            at = 2 * pp * KPAD
            damped.append(modes[at:at + KPAD] * factor)
            damped.append(modes[at + KPAD:at + 2 * KPAD] * factor)
        spec = dot(bk[...], jnp.concatenate(damped, axis=0).astype(BF16))
        kept = min(size, places - start)
        for pp in range(4):
            for f in range(everyone):
                row = pp * tall + 2 * f
                spec_ref[f, pp, :, start:start + kept] = spec[row:row + 2, 0:kept]


def per_device(grid, row_lengths, band_map, fold_map, legendre, to_modes, back_modes, mode_rates):
    fields, single, rows, width = grid.shape
    pairs, places, lats = legendre.shape
    cut_off = places - 2
    everyone = to_modes.shape[0]
    owners, per_owner = fold_map.shape
    groups = -(-per_owner // 8)
    slots = owners * groups * 8
    pieces = -(-(width // 4) // DEEP)
    turns = 4 * pieces
    span = -(-places // LANES) * LANES
    hbm = pl.BlockSpec(memory_space=pltpu.HBM)
    vmem = pl.BlockSpec(memory_space=pltpu.VMEM)
    room = pltpu.CompilerParams(vmem_limit_bytes=ROOM)
    message = pltpu.HBM((owners, 8, LANES), F32)
    holders = band_map.shape[0]
    groups_f = everyone // fields
    dma = pltpu.SemaphoreType.DMA
    row_lengths, band_map, fold_map, to_modes, back_modes, mode_rates, grid = (
        pltpu.with_memory_space_constraint(x, pltpu.HBM)
        for x in (row_lengths, band_map, fold_map, to_modes, back_modes, mode_rates, grid)
    )
    legendre = pltpu.with_memory_space_constraint(jnp.transpose(legendre, (0, 2, 1)), pltpu.HBM)

    sending, cos_table, sin_table, cos_turn, sin_turn = pl.pallas_call(
        functools.partial(forward_kernel, cut_off, groups),
        out_shape=(
            message,
            pltpu.VMEM((DEEP, slots), BF16),
            pltpu.VMEM((DEEP, slots), BF16),
            pltpu.VMEM((turns, slots), F32),
            pltpu.VMEM((turns, slots), F32),
        ),
        in_specs=[hbm] * 4,
        out_specs=(vmem,) * 5,
        scratch_shapes=[
            pltpu.SMEM(row_lengths.shape, jnp.int32),
            pltpu.SMEM(band_map.shape, jnp.int32),
            pltpu.VMEM(fold_map.shape, jnp.int32),
            pltpu.VMEM(grid.shape, BF16),
            dma((4,)),
            pltpu.VMEM((LANES, LANES), F32),
            pltpu.VMEM((8, slots), F32),
            pltpu.VMEM((16, 4 * DEEP * pieces), F32),
            pltpu.VMEM((4 * TWICE, slots), BF16),
        ],
        compiler_params=room,
        name="forward_rows",
    )(row_lengths, band_map, fold_map, grid)
    tables = [
        pltpu.with_memory_space_constraint(x, pltpu.VMEM)
        for x in (cos_table, sin_table, cos_turn, sin_turn)
    ]
    arrived = lax.all_to_all(sending, ("lat", "fld"), split_axis=0, concat_axis=0, tiled=True)

    legs, rounds, mix, back, turn_back, tau, rate = pl.pallas_call(
        functools.partial(prepare_kernel, cut_off, pairs, fields, rows),
        out_shape=(
            pltpu.HBM((groups * 16 * lats, span), BF16),
            pltpu.VMEM((groups * 4 * lats * lats, LANES), F32),
            pltpu.VMEM((LANES, 3 * LANES), BF16),
            pltpu.HBM((2 * FPAD, 8 * KPAD), BF16),
            pltpu.VMEM((3 * LANES, LANES), BF16),
            pltpu.HBM((8 * groups, span), F32),
            pltpu.HBM((KPAD, 2 * LANES), F32),
        ),
        in_specs=[hbm] * 6,
        out_specs=(hbm, vmem, vmem, hbm, vmem, hbm, hbm),
        scratch_shapes=[
            pltpu.SMEM(fold_map.shape, jnp.int32),
            pltpu.SMEM(band_map.shape, jnp.int32),
            pltpu.SMEM(mode_rates.shape, F32),
            pltpu.VMEM((pairs, lats, places), F32),
            pltpu.VMEM(to_modes.shape, F32),
            pltpu.VMEM(back_modes.shape, F32),
            dma((6,)),
            pltpu.VMEM((KPAD, LANES), F32),
            pltpu.VMEM((groups * 16 * lats, span), BF16),
            dma((groups,)),
            pltpu.VMEM((2 * FPAD, 8 * KPAD), BF16),
            pltpu.VMEM((8 * groups, span), F32),
            pltpu.VMEM((KPAD, 2 * LANES), F32),
            dma((3,)),
        ],
        compiler_params=pltpu.CompilerParams(vmem_limit_bytes=2 * ROOM),
        cost_estimate=pl.CostEstimate(flops=10**8, bytes_accessed=8 * 10**6, transcendentals=0),
        name="prepare",
    )(fold_map, band_map, mode_rates, legendre, to_modes, back_modes)
    legs, back, tau, rate = (
        pltpu.with_memory_space_constraint(x, pltpu.HBM) for x in (legs, back, tau, rate)
    )
    rounds, mix, turn_back = (
        pltpu.with_memory_space_constraint(x, pltpu.VMEM) for x in (rounds, mix, turn_back)
    )

    mixed, leaving = pl.pallas_call(
        functools.partial(solve_kernel, fields, rows, lats),
        out_shape=(
            pltpu.VMEM((groups * 8 * lats, LANES), F32),
            pltpu.HBM((owners * 8, LANES), F32),
        ),
        in_specs=[vmem] * 4,
        out_specs=(vmem,) * 2,
        scratch_shapes=[pltpu.VMEM((groups * 8 * lats, LANES), F32)],
        compiler_params=room,
        name="solve",
    )(arrived.reshape(owners * 8, LANES), rounds, mix, turn_back)
    leaving = leaving.reshape(owners, 8, LANES)

    returned = lax.all_to_all(leaving, ("lat", "fld"), split_axis=0, concat_axis=0, tiled=True)

    mixed = pltpu.with_memory_space_constraint(mixed, pltpu.VMEM)
    spectral = pl.pallas_call(
        functools.partial(output_kernel, lats),
        grid=(groups,),
        out_shape=jax.ShapeDtypeStruct((everyone, pairs, 2, places), F32),
        in_specs=[
            hbm,
            hbm,
            hbm,
            hbm,
            vmem,
        ],
        out_specs=pl.BlockSpec((everyone, 4, 2, places), lambda t: (0, t, 0, 0)),
        scratch_shapes=[
            pltpu.VMEM((8 * everyone, 8 * KPAD), BF16),
            pltpu.VMEM((groups * 16 * lats, span), BF16),
            dma((groups,)),
            pltpu.VMEM((8 * groups, span), F32),
            pltpu.VMEM((KPAD, 2 * LANES), F32),
            pltpu.VMEM((2 * FPAD, 8 * KPAD), BF16),
            dma((3,)),
        ],
        compiler_params=pltpu.CompilerParams(
            dimension_semantics=("arbitrary",), vmem_limit_bytes=ROOM
        ),
        cost_estimate=pl.CostEstimate(flops=10**8, bytes_accessed=8 * 10**6, transcendentals=0),
        name="spectral_output",
    )(legs, tau, rate, back, mixed)

    grid_out = pl.pallas_call(
        functools.partial(inverse_kernel, groups),
        out_shape=jax.ShapeDtypeStruct(grid.shape, BF16),
        in_specs=[hbm] * 2 + [vmem] * 5,
        out_specs=vmem,
        scratch_shapes=[
            pltpu.SMEM(row_lengths.shape, jnp.int32),
            pltpu.SMEM(band_map.shape, jnp.int32),
            dma((2,)),
            pltpu.VMEM((32 * pieces, 4 * LANES), BF16),
        ],
        compiler_params=room,
        name="inverse_rows",
    )(row_lengths, band_map, *tables, returned)
    return (jnp.transpose(spectral, (0, 2, 1, 3)), grid_out)


def solution(mesh):
    placed = (
        P("fld", "lat", None, None),
        P(),
        P(),
        P(),
        P(("lat", "fld"), None, None),
        P(),
        P(),
        P(),
    )
    return jax.shard_map(
        per_device,
        mesh=mesh,
        in_specs=placed,
        out_specs=(P(None, None, ("lat", "fld"), None), P("fld", "lat", None, None)),
        check_vma=False,
    )
```

```python
import functools
import math

import jax
import jax.numpy as jnp
from jax import lax
from jax.experimental import pallas as pl
from jax.experimental.pallas import tpu as pltpu
from jax.sharding import PartitionSpec as P

LANES = 128
KPAD = 24
FPAD = 64
DEEP = 256
TWICE = 24
ROOM = 24 * 1024 * 1024
F32 = jnp.float32
BF16 = jnp.bfloat16
NT_DIMS = (((1,), (1,)), ((), ()))
SIN_POLY = (
    6.283185302447051,
    -41.34170038368319,
    81.60513023312113,
    -76.70299324464969,
    42.02573766814694,
    -14.899106966102595,
    3.237062655726421,
)
COS_POLY = (
    0.9999999889083757,
    -19.739204448887243,
    64.93911476570418,
    -85.45008785413638,
    60.167188450194914,
    -25.9658703083255,
    6.526145851512229,
)


def dot(a, b):
    return jnp.dot(a, b, preferred_element_type=F32)


def dot_nt(a, b):
    return lax.dot_general(a, b, NT_DIMS, preferred_element_type=F32)


def split(x):
    high = x.astype(BF16)
    return high, (x - high.astype(F32)).astype(BF16)


def horner(coefs, z):
    total = coefs[-1] * z + coefs[-2]
    for coef in coefs[-3::-1]:
        total = total * z + coef
    return total


def turn(steps, period, inverse):
    rest = steps - period * jnp.floor(steps * inverse + 0.5)
    part = rest * inverse
    z = part * part
    return horner(COS_POLY, z), part * horner(SIN_POLY, z)


def start_all(sources, targets, sems):
    copies = [
        pltpu.make_async_copy(source, target, sems.at[i])
        for i, (source, target) in enumerate(zip(sources, targets))
    ]
    for copy in copies:
        copy.start()
    return copies


def wait_all(copies):
    for copy in copies:
        copy.wait()


def lane_iota(shape):
    return lax.broadcasted_iota(jnp.int32, shape, len(shape) - 1)


def row_iota(shape):
    return lax.broadcasted_iota(jnp.int32, shape, len(shape) - 2)


def lanes_within(lane, start, size):
    start %= LANES
    if start + size <= LANES:
        return (lane >= start) & (lane < start + size)
    return (lane >= start) | (lane < start + size - LANES)


def spread_matrix():
    shape = (4 * LANES, LANES)
    picks = []
    for phase in range(4):
        picks.append(jnp.where(row_iota(shape) == 4 * lane_iota(shape) + phase, 1.0, 0.0))
    return jnp.concatenate(picks, axis=1).astype(BF16)


def phase_steps(groups, lanes):
    row = row_iota((groups + 16, lanes))
    steps = jnp.where(row < groups, (row >> 2) * (4 * DEEP) + (row & 3), 4 * (row - groups))
    steps = jnp.where(row >= groups + 8, 32 << jnp.maximum(row - groups - 8, 0), steps)
    return steps.astype(F32)


def slot_lane(index, fields, rows):
    used = rows * fields
    part = (index >= TWICE).astype(jnp.int32)
    row = index - TWICE * part
    vec = jnp.where(row >= used, row - used, row)
    lane = lax.rem(vec, rows) * (fields * 2) + lax.div(vec, rows) * 2 + part
    return jnp.where(row < 2 * used, lane, -LANES)


def two_phases(ref, g, at, used, block):
    first = ref[2 * g:2 * g + 1, at]
    second = ref[2 * g + 1:2 * g + 2, at]
    tiles = []
    for low in range(0, TWICE, 8):
        if low + 8 <= used:
            tiles.append(jnp.broadcast_to(first, (8, block)))
        elif low >= used:
            tiles.append(jnp.broadcast_to(second, (8, block)))
        else:
            tiles.append(jnp.where(low + row_iota((8, block)) < used, first, second))
    return jnp.concatenate(tiles, axis=0)


def forward_kernel(
    cut_off, groups, len_hbm, band_hbm, fold_hbm, grid_hbm,
    msg_ref, tc, ts, fc, fs,
    len_ref, band_ref, fold_ref, grid_ref, sems, fold_s, wave_s, xs, xt,
):
    copies = start_all(
        (len_hbm, band_hbm, fold_hbm, grid_hbm), (len_ref, band_ref, fold_ref, grid_ref), sems
    )
    fields, _, rows, width = grid_ref.shape
    owners, per_owner = fold_ref.shape
    slots = tc.shape[1]
    pieces = xs.shape[1] // (4 * DEEP)
    unit = rows * fields * 2
    used = rows * fields
    spread_s = spread_matrix()
    shape = (LANES, owners * 8)
    repeat = jnp.where(row_iota(shape) == lane_iota(shape) >> 3, 1.0, 0.0).astype(BF16)
    shape = (8 * groups, 16 * groups)
    weigh = jnp.where(
        jnp.where(lane_iota(shape) < 8 * groups, lane_iota(shape), lane_iota(shape) - 8 * groups) >> 3
        == row_iota(shape) >> 3,
        jnp.where(lane_iota(shape) < 8 * groups, 8.0, 1.0),
        0.0,
    ).astype(BF16)
    tall = 4 * TWICE
    shape = (LANES, tall * groups)
    one = (1, 2 * TWICE)
    base = slot_lane(lane_iota(one), fields, rows)
    targets = []
    for t in range(groups):
        target = base + unit * (t + lax.axis_index("fld"))
        target = jnp.where(base < 0, base, target & (LANES - 1))
        targets += [target, target]
    target = jnp.concatenate(targets, axis=1)
    packing = jnp.where(row_iota(shape) == target, 1.0, 0.0).astype(BF16)
    fold_s[...] = jnp.full(fold_s.shape, -1.0, F32)
    xs[...] = jnp.zeros(xs.shape, F32)
    wait_all(copies)
    length = len_ref[band_ref[lax.axis_index("lat")]]
    top = jnp.minimum(cut_off, (length - 1) // 2)

    fold_s[0:owners, 0:per_owner] = fold_ref[...].astype(F32)
    turned = jnp.transpose(fold_s[...])[0:8 * groups]
    eights = jnp.floor(turned * 0.125)
    parts = jnp.concatenate([eights, turned - 8.0 * eights], axis=0).astype(BF16)
    repeated = dot(parts, repeat)
    own = (lane_iota(repeated.shape) & 7) == (row_iota(repeated.shape) & 7)
    waves = dot(weigh, jnp.where(own, repeated, 0.0).astype(BF16))
    for t in range(groups):
        wave_s[:, owners * 8 * t:owners * 8 * (t + 1)] = waves[8 * t:8 * t + 8]

    for field in range(fields):
        xs[rows * field:rows * (field + 1), 0:width] = grid_ref[field, 0].astype(F32)
    stacked = jnp.concatenate(
        [xs[:, 4 * LANES * c:4 * LANES * (c + 1)] for c in range(2 * pieces)], axis=0
    ).astype(BF16)
    spread = dot(stacked, spread_s)
    blank = jnp.zeros((TWICE - 16, LANES), F32)
    values = []
    for k in range(pieces):
        for pair in range(2):
            halves = []
            for half in range(2):
                c = 2 * k + half
                off = 2 * LANES * pair
                rows_c = spread[16 * c:16 * (c + 1)]
                inside = c * LANES + lane_iota((16, LANES)) < length // 4
                first, second = (
                    jnp.concatenate([jnp.where(inside, rows_c[:, o:o + LANES], 0.0), blank], axis=0)
                    for o in (off, off + LANES)
                )
                halves.append(first + pltpu.roll(second, used, 0))
            values.append(jnp.concatenate(halves, axis=1))
    values = jnp.concatenate(values, axis=0).astype(BF16)

    turns = 4 * pieces
    block = 2 * LANES
    steps = phase_steps(turns, block)
    period = jnp.full((1, block), length, jnp.int32).astype(F32)
    inverse = 1.0 / period
    def make_tables(i):
        at = pl.ds(i * block, block)
        wave = wave_s[:, at]
        wave = jnp.concatenate([wave] * ((turns + 16) // 8), axis=0)
        co, si = turn(steps * wave, period, inverse)
        one = wave[0:1]
        weight = jnp.where(one == 0.0, 1.0, 2.0)
        limit = jnp.full(one.shape, top, jnp.int32).astype(F32)
        weight = jnp.where((one >= 0.0) & (one <= limit), weight, 0.0)
        fc[:, at] = co[0:turns] * weight
        fs[:, at] = si[0:turns] * weight
        c_all = co[turns:turns + 8]
        s_all = si[turns:turns + 8]
        size, step = 8, turns + 8
        while size < DEEP:
            c1 = co[step:step + 1]
            s1 = si[step:step + 1]
            c_new = c_all * c1 - s_all * s1
            s_new = s_all * c1 + c_all * s1
            c_all = jnp.concatenate([c_all, c_new], axis=0)
            s_all = jnp.concatenate([s_all, s_new], axis=0)
            size, step = 2 * size, step + 1
        c_all = c_all.astype(BF16)
        s_all = s_all.astype(BF16)
        tc[:, at] = c_all
        ts[:, at] = s_all
        return c_all, s_all

    def finish(i, inner_c, inner_s):
        at = pl.ds(i * block, block)
        real = jnp.zeros((TWICE, block), F32)
        imag = jnp.zeros((TWICE, block), F32)
        for g in range(turns // 2):
            c1 = two_phases(fc, g, at, used, block)
            s1 = two_phases(fs, g, at, used, block)
            part_c = inner_c[TWICE * g:TWICE * (g + 1)]
            part_s = inner_s[TWICE * g:TWICE * (g + 1)]
            real = real + (c1 * part_c - s1 * part_s)
            imag = imag - (c1 * part_s + s1 * part_c)
        fix = jnp.where(wave_s[0:1, at] == 0.0, 1.0, 0.5)
        both = jnp.concatenate([real, imag], axis=0) * fix
        xt[:, at] = jnp.concatenate(split(both), axis=0)

    blocks = slots // block
    ready = make_tables(0)
    for i in range(blocks):
        inner_c = dot(values, ready[0])
        inner_s = dot(values, ready[1])
        if i + 1 < blocks:
            ready = make_tables(i + 1)
        finish(i, inner_c, inner_s)

    turned = jnp.concatenate(
        [xt[:, owners * 8 * t:owners * 8 * (t + 1)] for t in range(groups)], axis=0
    )
    total = dot(packing, turned)
    scale = 1.0 / jnp.sqrt(jnp.full(total.shape, length, jnp.int32).astype(F32))
    msg_ref[...] = jnp.transpose(total * scale).reshape(owners, 8, LANES)


def inverse_kernel(
    groups, len_hbm, band_hbm, tc, ts, fc, fs, msg_ref, grid_ref,
    len_ref, band_ref, sems, os,
):
    copies = start_all((len_hbm, band_hbm), (len_ref, band_ref), sems)
    spread_s = spread_matrix()
    fields, _, rows, width = grid_ref.shape
    owners = msg_ref.shape[0]
    slots = tc.shape[1]
    turns = fc.shape[0]
    unit = rows * fields * 2
    high, low = split(msg_ref[...].reshape(owners * 8, LANES))
    pieces = jnp.concatenate([high, low], axis=1)
    used = rows * fields
    tall = 2 * TWICE
    shape = (tall, LANES)
    base = slot_lane(row_iota(shape), fields, rows)
    places = []
    for t in range(groups):
        source = (base + unit * t + lax.axis_index("fld") * (fields * 2)) & (LANES - 1)
        source = jnp.where(base < 0, base, source)
        places.append(jnp.where(lane_iota(shape) == source, 1.0, 0.0))
    place = jnp.concatenate(places, axis=0).astype(BF16)
    place = jnp.concatenate([place, place], axis=1)
    turned = dot_nt(place, pieces)
    block = 2 * LANES
    out = jnp.zeros((TWICE * turns // 2, DEEP), F32)
    def twisted(i):
        t, off = divmod(i * block, owners * 8)
        real = turned[tall * t:tall * t + TWICE, off:off + block]
        imag = turned[tall * t + TWICE:tall * (t + 1), off:off + block]
        at = pl.ds(i * block, block)
        reals, imags = [], []
        for g in range(turns // 2):
            c1 = two_phases(fc, g, at, used, block)
            s1 = two_phases(fs, g, at, used, block)
            reals.append(c1 * real - s1 * imag)
            imags.append(s1 * real + c1 * imag)
        return (
            jnp.concatenate(reals, axis=0).astype(BF16),
            jnp.concatenate(imags, axis=0).astype(BF16),
        )

    blocks = slots // block
    ready = twisted(0)
    for i in range(blocks):
        at = pl.ds(i * block, block)
        part_r = dot_nt(ready[0], tc[:, at])
        part_i = dot_nt(ready[1], ts[:, at])
        if i + 1 < blocks:
            ready = twisted(i + 1)
        out = out + (part_r - part_i)
    wait_all(copies)
    length = len_ref[band_ref[lax.axis_index("lat")]]
    out = out * (1.0 / jnp.sqrt(jnp.full(out.shape, length, jnp.int32).astype(F32)))
    chunks = os.shape[0] // 16
    for c in range(chunks):
        off = LANES * (c % 2)
        for phase in range(4):
            at = (2 * (c // 2) + phase // 2) * TWICE
            piece = out[at:at + TWICE, off:off + LANES]
            if phase % 2:
                piece = pltpu.roll(piece, TWICE - used, 0)
            os[16 * c:16 * (c + 1), LANES * phase:LANES * (phase + 1)] = piece[0:16].astype(BF16)
    merged = dot_nt(os[...], spread_s)
    for c in range(chunks):
        begin = 4 * LANES * c
        size = min(4 * LANES, width - begin)
        if size <= 0:
            continue
        inside = begin + lane_iota((16, size)) < length
        piece = jnp.where(inside, merged[16 * c:16 * (c + 1), 0:size], 0.0)
        for field in range(fields):
            grid_ref[field, 0, :, begin:begin + size] = piece[
                rows * field:rows * (field + 1)
            ].astype(BF16)


def prepare_kernel(
    cut_off, pairs, fields, rows, fold_hbm, band_hbm, rates_hbm, leg_hbm, tm_hbm, bm_hbm,
    eh_hbm, round_ref, mix_ref, back_hbm, turn_ref, tau_hbm, rate_hbm,
    fold_ref, band_ref, rates_ref, leg_ref, tm_ref, bm_ref, sems, pad_s, eh_ref, out_sems,
    back_ref, tau_ref, rate_ref, small_sems,
):
    copies = start_all(
        (fold_hbm, band_hbm, rates_hbm, tm_hbm, bm_hbm, leg_hbm),
        (fold_ref, band_ref, rates_ref, tm_ref, bm_ref, leg_ref),
        sems,
    )
    wait_all(copies[:-1])
    everyone = tm_ref.shape[0]
    _, lats, places = leg_ref.shape
    groups_f = everyone // fields
    wf = fields * 2
    unit = rows * wf
    span = eh_ref.shape[1]
    eight = 8 * lats
    groups = eh_ref.shape[0] // (2 * eight)
    owner = lax.axis_index("lat") * groups_f + lax.axis_index("fld")

    pad_s[...] = jnp.zeros(pad_s.shape, F32)
    pad_s[0:everyone, 0:everyone] = tm_ref[...]
    shape = (LANES, LANES)
    level = (lane_iota(shape) // unit) * fields + (lane_iota(shape) % wf) // 2
    pick = jnp.where(row_iota(shape) == level, 1.0, 0.0).astype(BF16)
    lane = lane_iota((KPAD, LANES))
    parts = []
    for piece in split(pad_s[...]):
        wide = dot(piece, pick)
        total = []
        for c in range(2):
            for parity in range(2):
                keep = (lane % 2 == c) & (lane < unit * groups_f)
                flip = (lane % unit) // wf >= 1 if parity else lane < 0
                total.append(jnp.where(keep, jnp.where(flip, -wide, wide), 0.0))
        total.append(jnp.zeros((LANES - 4 * KPAD, LANES), F32))
        parts.append(jnp.concatenate(total, axis=0).astype(BF16))
    mix_ref[...] = jnp.concatenate([parts[0], parts[1], parts[0]], axis=1)

    pad_s[...] = jnp.zeros(pad_s.shape, F32)
    pad_s[0:everyone, 0:everyone] = bm_ref[...]
    shape = (FPAD, KPAD)
    expand = jnp.where(row_iota(shape) // 2 == lane_iota(shape), 1.0, 0.0).astype(BF16)
    shape = (LANES, 2 * LANES)
    repeat = jnp.where(row_iota(shape) == lane_iota(shape) % KPAD, 1.0, 0.0).astype(BF16)
    shape = (FPAD, 2 * LANES)
    same = row_iota(shape) % 2 == (lane_iota(shape) // KPAD) % 2
    for part, piece in enumerate(split(pad_s[...])):
        full = jnp.where(same, dot(dot(expand, piece).astype(BF16), repeat), 0.0)
        back_ref[part * FPAD:(part + 1) * FPAD, :] = full[:, 0:8 * KPAD].astype(BF16)
    shape = (LANES, LANES)
    row, lane = row_iota(shape), lane_iota(shape)
    width = 2 * everyone
    south = lane >= width
    level = jnp.where(south, lane - width, lane)
    pick = jnp.where(row == (level >> 1), 1.0, 0.0).astype(BF16)
    part = lax.div(row, KPAD)
    keep = ((part >> 1) == (level & 1)) & (part < 4) & (lane < 2 * width)
    flip = south & ((part & 1) == 1)
    wide = []
    for piece in split(jnp.transpose(jnp.concatenate([pad_s[...], jnp.zeros((LANES - KPAD, LANES), F32)], axis=0))):
        small = dot(piece, pick)[0:KPAD]
        tall = jnp.concatenate([small] * 5 + [jnp.zeros((LANES - 5 * KPAD, LANES), F32)], axis=0)
        wide.append(jnp.where(keep, jnp.where(flip, -tall, tall), 0.0).astype(BF16))
    turn_ref[...] = jnp.concatenate([wide[0], wide[0], wide[1]], axis=0)

    row = row_iota((KPAD, 2 * LANES))
    rate = jnp.zeros((KPAD, 2 * LANES), F32)
    for k in range(everyone):
        rate = jnp.where(row == k, rates_ref[k], rate)
    rate_ref[...] = rate
    wide_rate = jnp.concatenate([rate[:, 0:LANES]] * (span // LANES), axis=1)
    paired = tau_ref.shape[0]
    row = row_iota((paired, LANES))
    waves = []
    wave = jnp.zeros((paired, LANES), jnp.int32)
    for pair in range(4 * groups):
        waves.append(fold_ref[owner, 2 * min(pair, pairs - 1)])
        wave = jnp.where(row == 8 * (pair // 4) + pair % 4, waves[pair], wave)
    wave = jnp.concatenate([wave] * (span // LANES), axis=1)
    line = lane_iota((paired, span))
    degree = jnp.where(line > cut_off - wave, line - 1, line + wave)
    tau_ref[...] = (degree * (degree + 1)).astype(F32) * (1.0 / float(cut_off * (cut_off + 1)))

    quad_rows = 4 * lats
    shape = (quad_rows, quad_rows)
    band = jnp.zeros(shape, jnp.int32)
    for holder in range(lats):
        band = jnp.where(row_iota(shape) % lats == holder, band_ref[holder], band)
    order = jnp.where(
        (row_iota(shape) // lats == lane_iota(shape) // lats) & (lane_iota(shape) % lats == band),
        1.0,
        0.0,
    ).astype(BF16)

    whole = places // LANES * LANES
    line = lane_iota((quad_rows, span))
    row = row_iota((quad_rows, LANES)) // lats
    copies[-1].wait()
    keeps = start_all((back_ref, tau_ref, rate_ref), (back_hbm, tau_hbm, rate_hbm), small_sems)
    todo = []
    for t in range(groups):
        wave = jnp.zeros((quad_rows, LANES), jnp.int32)
        last = jnp.zeros((quad_rows, LANES), jnp.int32)
        stack = []
        for pp in range(4):
            there = 4 * t + pp < pairs
            index = min(4 * t + pp, pairs - 1)
            wave = jnp.where(row == pp, waves[4 * t + pp], wave)
            last = jnp.where(row == pp, places - 1 if there else -1, last)
            stack.append(
                jnp.concatenate(
                    [
                        leg_ref[index, :, 0:whole],
                        jnp.broadcast_to(leg_ref[index, :, whole:places], (lats, span - whole)),
                    ],
                    axis=1,
                )
            )
        wave = jnp.concatenate([wave] * (span // LANES), axis=1)
        last = jnp.concatenate([last] * (span // LANES), axis=1)
        leg = dot(order, jnp.concatenate(stack, axis=0).astype(BF16))
        before = line <= cut_off - wave
        first = before & (line <= last)
        second = jnp.logical_not(before) & (line <= last)
        odd = ((line + jnp.where(before, 0, wave)) & 1) == 1
        masks = [
            [jnp.where(side & odd, 1.0, 0.0) if par else jnp.where(odd, 0.0, jnp.where(side, 1.0, 0.0)) for par in range(2)]
            for side in (first, second)
        ]
        for par in range(2):
            near = leg * masks[0][par]
            far = leg * masks[1][par]
            for pp in range(4):
                at = 2 * eight * t + par * eight + 2 * pp * lats
                eh_ref[at:at + 2 * lats, :] = jnp.concatenate(
                    [near[pp * lats:(pp + 1) * lats], far[pp * lats:(pp + 1) * lats]], axis=0
                ).astype(BF16)
        part = pl.ds(2 * eight * t, 2 * eight)
        keeps.append(pltpu.make_async_copy(eh_ref.at[part], eh_hbm.at[part], out_sems.at[t]))
        keeps[-1].start()

        todo.append((leg, masks))

    rest = jnp.zeros((LANES - 4 * KPAD, span), F32)
    for t, (leg, masks) in enumerate(todo):
        for pp in range(4):
            own = leg[pp * lats:(pp + 1) * lats]
            pairs_of = jnp.concatenate([own * own[j:j + 1] for j in range(lats)], axis=0)
            pair = 4 * t + pp
            factor = pl.reciprocal(1.0 + tau_ref[8 * t + pp:8 * t + pp + 1, :] * wide_rate, approx=True)
            damp = []
            for side in range(2):
                for par in range(2):
                    mask = masks[side][par][pp * lats:pp * lats + 8]
                    damp.append(factor * jnp.concatenate([mask] * (KPAD // 8), axis=0))
            damp = jnp.concatenate(damp + [rest], axis=0).astype(BF16)
            at = pair * lats * lats
            round_ref[at:at + lats * lats, :] = dot_nt(pairs_of.astype(BF16), damp)
    wait_all(keeps)


def solve_kernel(
    fields, rows, lats, msg_ref, round_ref, mix_ref, turn_ref, mixed_ref, out_ref, cs,
):
    eight = 8 * lats
    groups = mixed_ref.shape[0] // eight
    groups_f = msg_ref.shape[0] // eight
    wf = fields * 2
    unit = rows * wf
    lane = lane_iota((lats, LANES))
    tiles = [
        [msg_ref[pl.ds(8 * g + i8, lats, stride=8 * groups_f), :] for g in range(groups_f)]
        for i8 in range(8)
    ]
    tall = []
    for t in range(groups):
        here = [lanes_within(lane, unit * (t + g), unit) for g in range(groups_f)]
        for i8 in range(8):
            line = tiles[i8][0]
            for g in range(1, groups_f):
                line = jnp.where(here[g], tiles[i8][g], line)
            if t:
                line = pltpu.roll(line, LANES - unit * t, 1)
            tall.append(line)
    v_high, v_low = split(jnp.concatenate(tall, axis=0))
    mixed_ref[...] = dot_nt(jnp.concatenate([v_high, v_high, v_low], axis=1), mix_ref[...])

    lane = lane_iota((lats, LANES))
    front = lane < 2 * KPAD
    sums = []
    for pair in range(4 * groups):
        one = mixed_ref[2 * pair * lats:(2 * pair + 1) * lats, :]
        two = mixed_ref[(2 * pair + 1) * lats:(2 * pair + 2) * lats, :]
        parts = (
            jnp.where(front, one, pltpu.roll(two, 2 * KPAD, 1)),
            jnp.where(front, pltpu.roll(one, LANES - 2 * KPAD, 1), two),
        )
        totals = [jnp.zeros((lats, LANES), F32) for _ in parts]
        for j in range(lats):
            at = (pair * lats + j) * lats
            matrix = round_ref[at:at + lats, :]
            totals = [
                total + part[j:j + 1] * matrix for total, part in zip(totals, parts)
            ]
        sums.append(jnp.where(front, totals[0], pltpu.roll(totals[1], 2 * KPAD, 1)))
        sums.append(jnp.where(front, pltpu.roll(totals[0], LANES - 2 * KPAD, 1), totals[1]))
    high, low = split(jnp.concatenate(sums, axis=0))
    cs[...] = dot(jnp.concatenate([high, low, high], axis=1), turn_ref[...])

    lane = lane_iota((8, LANES))
    here = [
        lanes_within(lane, wf * u, wf) for u in range(rows * groups + groups_f - 1)
    ]
    for holder in range(lats):
        tiles = [jnp.zeros((8, LANES), F32) for _ in range(groups_f)]
        for t in range(groups):
            piece = cs[pl.ds(t * eight + holder, 8, stride=lats), :]
            for r in range(rows):
                u = rows * t + r
                moved = pltpu.roll(piece, (wf * u - wf * groups_f * r) % LANES, 1)
                for g in range(groups_f):
                    tiles[g] = jnp.where(here[u + g], moved, tiles[g])
        for g in range(groups_f):
            at = (holder * groups_f + g) * 8
            out_ref[at:at + 8, :] = tiles[g]


def modes_kernel(
    lats, everyone, legs_hbm, tau_hbm, rate_hbm, back_hbm, mixed_ref, damped_ref, bk_ref,
    legs_ref, tau_ref, rate_ref, back_ref, sems, small_sems,
):
    small = start_all((back_hbm, tau_hbm, rate_hbm), (back_ref, tau_ref, rate_ref), small_sems)
    span = legs_ref.shape[1]
    eight = 8 * lats
    deep = 8 * KPAD
    groups = legs_ref.shape[0] // (2 * eight)
    parts = [pl.ds(0, 2 * eight), pl.ds(2 * eight, 2 * eight * (groups - 1))]
    fetches = start_all(
        [legs_hbm.at[part] for part in parts], [legs_ref.at[part] for part in parts], sems
    )
    slot_pair = (lane_iota((2 * KPAD, 2 * eight)) & (eight - 1)) // (2 * lats)
    lefts = []
    for t in range(groups):
        mine = mixed_ref[eight * t:eight * (t + 1), :]
        if eight < LANES:
            mine = jnp.concatenate([mine, jnp.zeros((LANES - eight, LANES), F32)], axis=0)
        mine = [
            jnp.transpose(mine[at:at + LANES])[:, 0:min(eight, LANES)]
            for at in range(0, eight, LANES)
        ]
        mine = jnp.concatenate(mine, axis=1) if len(mine) > 1 else mine[0]
        mine = jnp.concatenate(
            [
                jnp.concatenate(
                    [mine[par * KPAD:(par + 1) * KPAD], mine[(par + 2) * KPAD:(par + 3) * KPAD]],
                    axis=0,
                )
                for par in range(2)
            ],
            axis=1,
        )
        left = jnp.concatenate([jnp.where(slot_pair == pp, mine, 0.0) for pp in range(4)], axis=0)
        lefts.append(jnp.concatenate(split(left), axis=1))
    wait_all(small)
    tall = 2 * everyone
    pair_of = lane_iota((tall, deep)) // (2 * KPAD)
    blocks = []
    for part in range(2):
        full = back_ref[part * FPAD:part * FPAD + tall, :].astype(F32)
        blocks += [jnp.where(pair_of == pp, full, 0.0) for pp in range(4)]
    bk_ref[...] = jnp.concatenate(blocks, axis=0).astype(BF16)
    rate = rate_ref[...]
    for t in range(groups):
        if t < 2:
            fetches[t].wait()
        for start in range(0, span, 2 * LANES):
            size = min(2 * LANES, span - start)
            right = legs_ref[2 * eight * t:2 * eight * (t + 1), start:start + size]
            modes = dot(lefts[t], jnp.concatenate([right, right], axis=0))
            damped = []
            for pp in range(4):
                tau = tau_ref[8 * t + pp:8 * t + pp + 1, start:start + size]
                factor = pl.reciprocal(1.0 + tau * rate[:, 0:size], approx=True)
                at = 2 * pp * KPAD
                damped.append(modes[at:at + KPAD] * factor)
                damped.append(modes[at + KPAD:at + 2 * KPAD] * factor)
            damped_ref[deep * t:deep * (t + 1), start:start + size] = jnp.concatenate(
                damped, axis=0
            ).astype(BF16)


def output_kernel(damped_ref, bk_ref, spec_ref):
    everyone, quad, _, places = spec_ref.shape
    span = damped_ref.shape[1]
    deep = 8 * KPAD
    tall = 2 * everyone
    at = pl.multiple_of(deep * pl.program_id(0), deep)
    for start in range(0, span, 2 * LANES):
        size = min(2 * LANES, span - start)
        spec = dot(bk_ref[...], damped_ref[pl.ds(at, deep), start:start + size])
        spec = spec[0:4 * tall] + spec[4 * tall:]
        kept = min(size, places - start)
        for pp in range(4):
            for f in range(everyone):
                row = pp * tall + 2 * f
                spec_ref[f, pp, :, start:start + kept] = spec[row:row + 2, 0:kept]


def per_device(grid, row_lengths, band_map, fold_map, legendre, to_modes, back_modes, mode_rates):
    fields, single, rows, width = grid.shape
    pairs, places, lats = legendre.shape
    cut_off = places - 2
    everyone = to_modes.shape[0]
    owners, per_owner = fold_map.shape
    groups = -(-per_owner // 8)
    slots = owners * groups * 8
    pieces = -(-(width // 4) // DEEP)
    turns = 4 * pieces
    span = -(-places // LANES) * LANES
    hbm = pl.BlockSpec(memory_space=pltpu.HBM)
    vmem = pl.BlockSpec(memory_space=pltpu.VMEM)
    room = pltpu.CompilerParams(vmem_limit_bytes=ROOM)
    message = pltpu.HBM((owners, 8, LANES), F32)
    holders = band_map.shape[0]
    groups_f = everyone // fields
    dma = pltpu.SemaphoreType.DMA
    row_lengths, band_map, fold_map, to_modes, back_modes, mode_rates, grid = (
        pltpu.with_memory_space_constraint(x, pltpu.HBM)
        for x in (row_lengths, band_map, fold_map, to_modes, back_modes, mode_rates, grid)
    )
    legendre = pltpu.with_memory_space_constraint(jnp.transpose(legendre, (0, 2, 1)), pltpu.HBM)

    sending, cos_table, sin_table, cos_turn, sin_turn = pl.pallas_call(
        functools.partial(forward_kernel, cut_off, groups),
        out_shape=(
            message,
            pltpu.VMEM((DEEP, slots), BF16),
            pltpu.VMEM((DEEP, slots), BF16),
            pltpu.VMEM((turns, slots), F32),
            pltpu.VMEM((turns, slots), F32),
        ),
        in_specs=[hbm] * 4,
        out_specs=(vmem,) * 5,
        scratch_shapes=[
            pltpu.SMEM(row_lengths.shape, jnp.int32),
            pltpu.SMEM(band_map.shape, jnp.int32),
            pltpu.VMEM(fold_map.shape, jnp.int32),
            pltpu.VMEM(grid.shape, BF16),
            dma((4,)),
            pltpu.VMEM((LANES, LANES), F32),
            pltpu.VMEM((8, slots), F32),
            pltpu.VMEM((16, 4 * DEEP * pieces), F32),
            pltpu.VMEM((4 * TWICE, slots), BF16),
        ],
        compiler_params=room,
        name="forward_rows",
    )(row_lengths, band_map, fold_map, grid)
    tables = [
        pltpu.with_memory_space_constraint(x, pltpu.VMEM)
        for x in (cos_table, sin_table, cos_turn, sin_turn)
    ]
    arrived = lax.all_to_all(sending, ("lat", "fld"), split_axis=0, concat_axis=0, tiled=True)

    legs, rounds, mix, back, turn_back, tau, rate = pl.pallas_call(
        functools.partial(prepare_kernel, cut_off, pairs, fields, rows),
        out_shape=(
            pltpu.HBM((groups * 16 * lats, span), BF16),
            pltpu.VMEM((groups * 4 * lats * lats, LANES), F32),
            pltpu.VMEM((LANES, 3 * LANES), BF16),
            pltpu.HBM((2 * FPAD, 8 * KPAD), BF16),
            pltpu.VMEM((3 * LANES, LANES), BF16),
            pltpu.HBM((8 * groups, span), F32),
            pltpu.HBM((KPAD, 2 * LANES), F32),
        ),
        in_specs=[hbm] * 6,
        out_specs=(hbm, vmem, vmem, hbm, vmem, hbm, hbm),
        scratch_shapes=[
            pltpu.SMEM(fold_map.shape, jnp.int32),
            pltpu.SMEM(band_map.shape, jnp.int32),
            pltpu.SMEM(mode_rates.shape, F32),
            pltpu.VMEM((pairs, lats, places), F32),
            pltpu.VMEM(to_modes.shape, F32),
            pltpu.VMEM(back_modes.shape, F32),
            dma((6,)),
            pltpu.VMEM((KPAD, LANES), F32),
            pltpu.VMEM((groups * 16 * lats, span), BF16),
            dma((groups,)),
            pltpu.VMEM((2 * FPAD, 8 * KPAD), BF16),
            pltpu.VMEM((8 * groups, span), F32),
            pltpu.VMEM((KPAD, 2 * LANES), F32),
            dma((3,)),
        ],
        compiler_params=pltpu.CompilerParams(vmem_limit_bytes=2 * ROOM),
        cost_estimate=pl.CostEstimate(flops=10**8, bytes_accessed=8 * 10**6, transcendentals=0),
        name="prepare",
    )(fold_map, band_map, mode_rates, legendre, to_modes, back_modes)
    legs, back, tau, rate = (
        pltpu.with_memory_space_constraint(x, pltpu.HBM) for x in (legs, back, tau, rate)
    )
    rounds, mix, turn_back = (
        pltpu.with_memory_space_constraint(x, pltpu.VMEM) for x in (rounds, mix, turn_back)
    )

    mixed, leaving = pl.pallas_call(
        functools.partial(solve_kernel, fields, rows, lats),
        out_shape=(
            pltpu.VMEM((groups * 8 * lats, LANES), F32),
            pltpu.HBM((owners * 8, LANES), F32),
        ),
        in_specs=[vmem] * 4,
        out_specs=(vmem,) * 2,
        scratch_shapes=[pltpu.VMEM((groups * 8 * lats, LANES), F32)],
        compiler_params=room,
        name="solve",
    )(arrived.reshape(owners * 8, LANES), rounds, mix, turn_back)
    leaving = leaving.reshape(owners, 8, LANES)

    returned = lax.all_to_all(leaving, ("lat", "fld"), split_axis=0, concat_axis=0, tiled=True)

    mixed = pltpu.with_memory_space_constraint(mixed, pltpu.VMEM)
    cost = pl.CostEstimate(flops=10**8, bytes_accessed=8 * 10**6, transcendentals=0)
    damped, spread_back = pl.pallas_call(
        functools.partial(modes_kernel, lats, everyone),
        out_shape=(
            pltpu.VMEM((groups * 8 * KPAD, span), BF16),
            pltpu.VMEM((16 * everyone, 8 * KPAD), BF16),
        ),
        in_specs=[hbm] * 4 + [vmem],
        out_specs=(vmem,) * 2,
        scratch_shapes=[
            pltpu.VMEM((groups * 16 * lats, span), BF16),
            pltpu.VMEM((8 * groups, span), F32),
            pltpu.VMEM((KPAD, 2 * LANES), F32),
            pltpu.VMEM((2 * FPAD, 8 * KPAD), BF16),
            dma((2,)),
            dma((3,)),
        ],
        compiler_params=room,
        cost_estimate=cost,
        name="modes",
    )(legs, tau, rate, back, mixed)
    damped, spread_back = (
        pltpu.with_memory_space_constraint(x, pltpu.VMEM) for x in (damped, spread_back)
    )
    spectral = pl.pallas_call(
        output_kernel,
        grid=(groups,),
        out_shape=jax.ShapeDtypeStruct((everyone, pairs, 2, places), F32),
        in_specs=[vmem, vmem],
        out_specs=pl.BlockSpec((everyone, 4, 2, places), lambda t: (0, t, 0, 0)),
        compiler_params=pltpu.CompilerParams(
            dimension_semantics=("arbitrary",), vmem_limit_bytes=ROOM
        ),
        cost_estimate=cost,
        name="spectral_output",
    )(damped, spread_back)

    grid_out = pl.pallas_call(
        functools.partial(inverse_kernel, groups),
        out_shape=jax.ShapeDtypeStruct(grid.shape, BF16),
        in_specs=[hbm] * 2 + [vmem] * 5,
        out_specs=vmem,
        scratch_shapes=[
            pltpu.SMEM(row_lengths.shape, jnp.int32),
            pltpu.SMEM(band_map.shape, jnp.int32),
            dma((2,)),
            pltpu.VMEM((32 * pieces, 4 * LANES), BF16),
        ],
        compiler_params=room,
        name="inverse_rows",
    )(row_lengths, band_map, *tables, returned)
    return (jnp.transpose(spectral, (0, 2, 1, 3)), grid_out)


def solution(mesh):
    placed = (
        P("fld", "lat", None, None),
        P(),
        P(),
        P(),
        P(("lat", "fld"), None, None),
        P(),
        P(),
        P(),
    )
    return jax.shard_map(
        per_device,
        mesh=mesh,
        in_specs=placed,
        out_specs=(P(None, None, ("lat", "fld"), None), P("fld", "lat", None, None)),
        check_vma=False,
    )
```

```python
import functools
import math

import jax
import jax.numpy as jnp
from jax import lax
from jax.experimental import pallas as pl
from jax.experimental.pallas import tpu as pltpu
from jax.sharding import PartitionSpec as P

LANES = 128
KPAD = 24
FPAD = 64
DEEP = 256
TWICE = 24
ROOM = 24 * 1024 * 1024
F32 = jnp.float32
BF16 = jnp.bfloat16
NT_DIMS = (((1,), (1,)), ((), ()))
SIN_POLY = (
    6.283185302447051,
    -41.34170038368319,
    81.60513023312113,
    -76.70299324464969,
    42.02573766814694,
    -14.899106966102595,
    3.237062655726421,
)
COS_POLY = (
    0.9999999889083757,
    -19.739204448887243,
    64.93911476570418,
    -85.45008785413638,
    60.167188450194914,
    -25.9658703083255,
    6.526145851512229,
)


def dot(a, b):
    return jnp.dot(a, b, preferred_element_type=F32)


def dot_nt(a, b):
    return lax.dot_general(a, b, NT_DIMS, preferred_element_type=F32)


def split(x):
    high = x.astype(BF16)
    return high, (x - high.astype(F32)).astype(BF16)


def horner(coefs, z):
    total = coefs[-1] * z + coefs[-2]
    for coef in coefs[-3::-1]:
        total = total * z + coef
    return total


def turn(steps, period, inverse):
    rest = steps - period * jnp.floor(steps * inverse + 0.5)
    part = rest * inverse
    z = part * part
    return horner(COS_POLY, z), part * horner(SIN_POLY, z)


def start_all(sources, targets, sems):
    copies = [
        pltpu.make_async_copy(source, target, sems.at[i])
        for i, (source, target) in enumerate(zip(sources, targets))
    ]
    for copy in copies:
        copy.start()
    return copies


def wait_all(copies):
    for copy in copies:
        copy.wait()


def lane_iota(shape):
    return lax.broadcasted_iota(jnp.int32, shape, len(shape) - 1)


def row_iota(shape):
    return lax.broadcasted_iota(jnp.int32, shape, len(shape) - 2)


def lanes_within(lane, start, size):
    start %= LANES
    if start + size <= LANES:
        return (lane >= start) & (lane < start + size)
    return (lane >= start) | (lane < start + size - LANES)


def spread_matrix():
    shape = (4 * LANES, LANES)
    picks = []
    for phase in range(4):
        picks.append(jnp.where(row_iota(shape) == 4 * lane_iota(shape) + phase, 1.0, 0.0))
    return jnp.concatenate(picks, axis=1).astype(BF16)


def phase_steps(groups, lanes):
    row = row_iota((groups + 16, lanes))
    steps = jnp.where(row < groups, (row >> 2) * (4 * DEEP) + (row & 3), 4 * (row - groups))
    steps = jnp.where(row >= groups + 8, 32 << jnp.maximum(row - groups - 8, 0), steps)
    return steps.astype(F32)


def slot_lane(index, fields, rows):
    used = rows * fields
    part = (index >= TWICE).astype(jnp.int32)
    row = index - TWICE * part
    vec = jnp.where(row >= used, row - used, row)
    lane = lax.rem(vec, rows) * (fields * 2) + lax.div(vec, rows) * 2 + part
    return jnp.where(row < 2 * used, lane, -LANES)


def two_phases(ref, g, at, used, block):
    first = ref[2 * g:2 * g + 1, at]
    second = ref[2 * g + 1:2 * g + 2, at]
    tiles = []
    for low in range(0, TWICE, 8):
        if low + 8 <= used:
            tiles.append(jnp.broadcast_to(first, (8, block)))
        elif low >= used:
            tiles.append(jnp.broadcast_to(second, (8, block)))
        else:
            tiles.append(jnp.where(low + row_iota((8, block)) < used, first, second))
    return jnp.concatenate(tiles, axis=0)


def forward_kernel(
    cut_off, groups, len_hbm, band_hbm, fold_hbm, grid_hbm,
    msg_ref, tc, ts, fc, fs,
    len_ref, band_ref, fold_ref, grid_ref, sems, fold_s, wave_s, xs, xt,
):
    copies = start_all(
        (len_hbm, band_hbm, fold_hbm, grid_hbm), (len_ref, band_ref, fold_ref, grid_ref), sems
    )
    fields, _, rows, width = grid_ref.shape
    owners, per_owner = fold_ref.shape
    slots = tc.shape[1]
    pieces = xs.shape[1] // (4 * DEEP)
    unit = rows * fields * 2
    used = rows * fields
    spread_s = spread_matrix()
    shape = (LANES, owners * 8)
    repeat = jnp.where(row_iota(shape) == lane_iota(shape) >> 3, 1.0, 0.0).astype(BF16)
    shape = (8 * groups, 16 * groups)
    weigh = jnp.where(
        jnp.where(lane_iota(shape) < 8 * groups, lane_iota(shape), lane_iota(shape) - 8 * groups) >> 3
        == row_iota(shape) >> 3,
        jnp.where(lane_iota(shape) < 8 * groups, 8.0, 1.0),
        0.0,
    ).astype(BF16)
    tall = 4 * TWICE
    shape = (LANES, tall * groups)
    one = (1, 2 * TWICE)
    base = slot_lane(lane_iota(one), fields, rows)
    targets = []
    for t in range(groups):
        target = base + unit * (t + lax.axis_index("fld"))
        target = jnp.where(base < 0, base, target & (LANES - 1))
        targets += [target, target]
    target = jnp.concatenate(targets, axis=1)
    packing = jnp.where(row_iota(shape) == target, 1.0, 0.0).astype(BF16)
    fold_s[...] = jnp.full(fold_s.shape, -1.0, F32)
    xs[...] = jnp.zeros(xs.shape, F32)
    wait_all(copies)
    length = len_ref[band_ref[lax.axis_index("lat")]]
    top = jnp.minimum(cut_off, (length - 1) // 2)

    fold_s[0:owners, 0:per_owner] = fold_ref[...].astype(F32)
    turned = jnp.transpose(fold_s[...])[0:8 * groups]
    eights = jnp.floor(turned * 0.125)
    parts = jnp.concatenate([eights, turned - 8.0 * eights], axis=0).astype(BF16)
    repeated = dot(parts, repeat)
    own = (lane_iota(repeated.shape) & 7) == (row_iota(repeated.shape) & 7)
    waves = dot(weigh, jnp.where(own, repeated, 0.0).astype(BF16))
    for t in range(groups):
        wave_s[:, owners * 8 * t:owners * 8 * (t + 1)] = waves[8 * t:8 * t + 8]

    for field in range(fields):
        xs[rows * field:rows * (field + 1), 0:width] = grid_ref[field, 0].astype(F32)
    stacked = jnp.concatenate(
        [xs[:, 4 * LANES * c:4 * LANES * (c + 1)] for c in range(2 * pieces)], axis=0
    ).astype(BF16)
    spread = dot(stacked, spread_s)
    blank = jnp.zeros((TWICE - 16, LANES), F32)
    values = []
    for k in range(pieces):
        for pair in range(2):
            halves = []
            for half in range(2):
                c = 2 * k + half
                off = 2 * LANES * pair
                rows_c = spread[16 * c:16 * (c + 1)]
                inside = c * LANES + lane_iota((16, LANES)) < length // 4
                first, second = (
                    jnp.concatenate([jnp.where(inside, rows_c[:, o:o + LANES], 0.0), blank], axis=0)
                    for o in (off, off + LANES)
                )
                halves.append(first + pltpu.roll(second, used, 0))
            values.append(jnp.concatenate(halves, axis=1))
    values = jnp.concatenate(values, axis=0).astype(BF16)

    turns = 4 * pieces
    block = 2 * LANES
    steps = phase_steps(turns, block)
    period = jnp.full((1, block), length, jnp.int32).astype(F32)
    inverse = 1.0 / period
    def make_tables(i):
        at = pl.ds(i * block, block)
        wave = wave_s[:, at]
        wave = jnp.concatenate([wave] * ((turns + 16) // 8), axis=0)
        co, si = turn(steps * wave, period, inverse)
        one = wave[0:1]
        weight = jnp.where(one == 0.0, 1.0, 2.0)
        limit = jnp.full(one.shape, top, jnp.int32).astype(F32)
        weight = jnp.where((one >= 0.0) & (one <= limit), weight, 0.0)
        fc[:, at] = co[0:turns] * weight
        fs[:, at] = si[0:turns] * weight
        c_all = co[turns:turns + 8]
        s_all = si[turns:turns + 8]
        size, step = 8, turns + 8
        while size < DEEP:
            c1 = co[step:step + 1]
            s1 = si[step:step + 1]
            c_new = c_all * c1 - s_all * s1
            s_new = s_all * c1 + c_all * s1
            c_all = jnp.concatenate([c_all, c_new], axis=0)
            s_all = jnp.concatenate([s_all, s_new], axis=0)
            size, step = 2 * size, step + 1
        c_all = c_all.astype(BF16)
        s_all = s_all.astype(BF16)
        tc[:, at] = c_all
        ts[:, at] = s_all
        return c_all, s_all

    def finish(i, inner_c, inner_s):
        at = pl.ds(i * block, block)
        real = jnp.zeros((TWICE, block), F32)
        imag = jnp.zeros((TWICE, block), F32)
        for g in range(turns // 2):
            c1 = two_phases(fc, g, at, used, block)
            s1 = two_phases(fs, g, at, used, block)
            part_c = inner_c[TWICE * g:TWICE * (g + 1)]
            part_s = inner_s[TWICE * g:TWICE * (g + 1)]
            real = real + (c1 * part_c - s1 * part_s)
            imag = imag - (c1 * part_s + s1 * part_c)
        fix = jnp.where(wave_s[0:1, at] == 0.0, 1.0, 0.5)
        both = jnp.concatenate([real, imag], axis=0) * fix
        xt[:, at] = jnp.concatenate(split(both), axis=0)

    blocks = slots // block
    ready = make_tables(0)
    for i in range(blocks):
        inner_c = dot(values, ready[0])
        inner_s = dot(values, ready[1])
        if i + 1 < blocks:
            ready = make_tables(i + 1)
        finish(i, inner_c, inner_s)

    turned = jnp.concatenate(
        [xt[:, owners * 8 * t:owners * 8 * (t + 1)] for t in range(groups)], axis=0
    )
    total = dot(packing, turned)
    scale = 1.0 / jnp.sqrt(jnp.full(total.shape, length, jnp.int32).astype(F32))
    msg_ref[...] = jnp.transpose(total * scale).reshape(owners, 8, LANES)


def inverse_kernel(
    groups, len_hbm, band_hbm, tc, ts, fc, fs, place_ref, gather_ref, msg_ref, grid_ref,
    len_ref, band_ref, sems, os,
):
    copies = start_all((len_hbm, band_hbm), (len_ref, band_ref), sems)
    fields, _, rows, width = grid_ref.shape
    owners = msg_ref.shape[0]
    slots = tc.shape[1]
    turns = fc.shape[0]
    unit = rows * fields * 2
    high, low = split(msg_ref[...].reshape(owners * 8, LANES))
    pieces = jnp.concatenate([high, low], axis=1)
    used = rows * fields
    tall = 2 * TWICE
    turned = dot_nt(place_ref[...], pieces)
    block = 2 * LANES
    out = jnp.zeros((TWICE * turns // 2, DEEP), F32)
    def twisted(i):
        t, off = divmod(i * block, owners * 8)
        real = turned[tall * t:tall * t + TWICE, off:off + block]
        imag = turned[tall * t + TWICE:tall * (t + 1), off:off + block]
        at = pl.ds(i * block, block)
        reals, imags = [], []
        for g in range(turns // 2):
            c1 = two_phases(fc, g, at, used, block)
            s1 = two_phases(fs, g, at, used, block)
            reals.append(c1 * real - s1 * imag)
            imags.append(s1 * real + c1 * imag)
        return (
            jnp.concatenate(reals, axis=0).astype(BF16),
            jnp.concatenate(imags, axis=0).astype(BF16),
        )

    blocks = slots // block
    ready = twisted(0)
    for i in range(blocks):
        at = pl.ds(i * block, block)
        part_r = dot_nt(ready[0], tc[:, at])
        part_i = dot_nt(ready[1], ts[:, at])
        if i + 1 < blocks:
            ready = twisted(i + 1)
        out = out + (part_r - part_i)
    wait_all(copies)
    length = len_ref[band_ref[lax.axis_index("lat")]]
    out = out * (1.0 / jnp.sqrt(jnp.full(out.shape, length, jnp.int32).astype(F32)))
    chunks = os.shape[0] // 16
    for c in range(chunks):
        off = LANES * (c % 2)
        for phase in range(4):
            at = (2 * (c // 2) + phase // 2) * TWICE
            piece = out[at:at + TWICE, off:off + LANES]
            if phase % 2:
                piece = pltpu.roll(piece, TWICE - used, 0)
            os[16 * c:16 * (c + 1), LANES * phase:LANES * (phase + 1)] = piece[0:16].astype(BF16)
    merged = dot_nt(os[...], gather_ref[...])
    for c in range(chunks):
        begin = 4 * LANES * c
        size = min(4 * LANES, width - begin)
        if size <= 0:
            continue
        inside = begin + lane_iota((16, size)) < length
        piece = jnp.where(inside, merged[16 * c:16 * (c + 1), 0:size], 0.0)
        for field in range(fields):
            grid_ref[field, 0, :, begin:begin + size] = piece[
                rows * field:rows * (field + 1)
            ].astype(BF16)


def prepare_kernel(
    cut_off, pairs, fields, rows, fold_hbm, band_hbm, rates_hbm, leg_hbm, tm_hbm, bm_hbm,
    eh_hbm, round_ref, mix_ref, back_hbm, turn_ref, tau_hbm, rate_hbm,
    fold_ref, band_ref, rates_ref, leg_ref, tm_ref, bm_ref, sems, pad_s, eh_ref, out_sems,
    back_ref, tau_ref, rate_ref, small_sems,
):
    copies = start_all(
        (fold_hbm, band_hbm, rates_hbm, tm_hbm, bm_hbm, leg_hbm),
        (fold_ref, band_ref, rates_ref, tm_ref, bm_ref, leg_ref),
        sems,
    )
    wait_all(copies[:-1])
    everyone = tm_ref.shape[0]
    _, lats, places = leg_ref.shape
    groups_f = everyone // fields
    wf = fields * 2
    unit = rows * wf
    span = eh_ref.shape[1]
    eight = 8 * lats
    groups = eh_ref.shape[0] // (2 * eight)
    owner = lax.axis_index("lat") * groups_f + lax.axis_index("fld")

    pad_s[...] = jnp.zeros(pad_s.shape, F32)
    pad_s[0:everyone, 0:everyone] = tm_ref[...]
    shape = (LANES, LANES)
    level = (lane_iota(shape) // unit) * fields + (lane_iota(shape) % wf) // 2
    pick = jnp.where(row_iota(shape) == level, 1.0, 0.0).astype(BF16)
    lane = lane_iota((KPAD, LANES))
    parts = []
    for piece in split(pad_s[...]):
        wide = dot(piece, pick)
        total = []
        for c in range(2):
            for parity in range(2):
                keep = (lane % 2 == c) & (lane < unit * groups_f)
                flip = (lane % unit) // wf >= 1 if parity else lane < 0
                total.append(jnp.where(keep, jnp.where(flip, -wide, wide), 0.0))
        total.append(jnp.zeros((LANES - 4 * KPAD, LANES), F32))
        parts.append(jnp.concatenate(total, axis=0).astype(BF16))
    mix_ref[...] = jnp.concatenate([parts[0], parts[1], parts[0]], axis=1)

    pad_s[...] = jnp.zeros(pad_s.shape, F32)
    pad_s[0:everyone, 0:everyone] = bm_ref[...]
    shape = (FPAD, KPAD)
    expand = jnp.where(row_iota(shape) // 2 == lane_iota(shape), 1.0, 0.0).astype(BF16)
    shape = (LANES, 2 * LANES)
    repeat = jnp.where(row_iota(shape) == lane_iota(shape) % KPAD, 1.0, 0.0).astype(BF16)
    shape = (FPAD, 2 * LANES)
    same = row_iota(shape) % 2 == (lane_iota(shape) // KPAD) % 2
    for part, piece in enumerate(split(pad_s[...])):
        full = jnp.where(same, dot(dot(expand, piece).astype(BF16), repeat), 0.0)
        back_ref[part * FPAD:(part + 1) * FPAD, :] = full[:, 0:8 * KPAD].astype(BF16)
    shape = (LANES, LANES)
    row, lane = row_iota(shape), lane_iota(shape)
    width = 2 * everyone
    south = lane >= width
    level = jnp.where(south, lane - width, lane)
    pick = jnp.where(row == (level >> 1), 1.0, 0.0).astype(BF16)
    part = lax.div(row, KPAD)
    keep = ((part >> 1) == (level & 1)) & (part < 4) & (lane < 2 * width)
    flip = south & ((part & 1) == 1)
    wide = []
    for piece in split(jnp.transpose(jnp.concatenate([pad_s[...], jnp.zeros((LANES - KPAD, LANES), F32)], axis=0))):
        small = dot(piece, pick)[0:KPAD]
        tall = jnp.concatenate([small] * 5 + [jnp.zeros((LANES - 5 * KPAD, LANES), F32)], axis=0)
        wide.append(jnp.where(keep, jnp.where(flip, -tall, tall), 0.0).astype(BF16))
    turn_ref[...] = jnp.concatenate([wide[0], wide[0], wide[1]], axis=0)

    row = row_iota((KPAD, 2 * LANES))
    rate = jnp.zeros((KPAD, 2 * LANES), F32)
    for k in range(everyone):
        rate = jnp.where(row == k, rates_ref[k], rate)
    rate_ref[...] = rate
    wide_rate = jnp.concatenate([rate[:, 0:LANES]] * (span // LANES), axis=1)
    paired = tau_ref.shape[0]
    row = row_iota((paired, LANES))
    waves = []
    wave = jnp.zeros((paired, LANES), jnp.int32)
    for pair in range(4 * groups):
        waves.append(fold_ref[owner, 2 * min(pair, pairs - 1)])
        wave = jnp.where(row == 8 * (pair // 4) + pair % 4, waves[pair], wave)
    wave = jnp.concatenate([wave] * (span // LANES), axis=1)
    line = lane_iota((paired, span))
    degree = jnp.where(line > cut_off - wave, line - 1, line + wave)
    tau_ref[...] = (degree * (degree + 1)).astype(F32) * (1.0 / float(cut_off * (cut_off + 1)))

    quad_rows = 4 * lats
    shape = (quad_rows, quad_rows)
    band = jnp.zeros(shape, jnp.int32)
    for holder in range(lats):
        band = jnp.where(row_iota(shape) % lats == holder, band_ref[holder], band)
    order = jnp.where(
        (row_iota(shape) // lats == lane_iota(shape) // lats) & (lane_iota(shape) % lats == band),
        1.0,
        0.0,
    ).astype(BF16)

    whole = places // LANES * LANES
    line = lane_iota((quad_rows, span))
    row = row_iota((quad_rows, LANES)) // lats
    copies[-1].wait()
    keeps = start_all((back_ref, tau_ref, rate_ref), (back_hbm, tau_hbm, rate_hbm), small_sems)
    todo = []
    for t in range(groups):
        wave = jnp.zeros((quad_rows, LANES), jnp.int32)
        last = jnp.zeros((quad_rows, LANES), jnp.int32)
        stack = []
        for pp in range(4):
            there = 4 * t + pp < pairs
            index = min(4 * t + pp, pairs - 1)
            wave = jnp.where(row == pp, waves[4 * t + pp], wave)
            last = jnp.where(row == pp, places - 1 if there else -1, last)
            stack.append(
                jnp.concatenate(
                    [
                        leg_ref[index, :, 0:whole],
                        jnp.broadcast_to(leg_ref[index, :, whole:places], (lats, span - whole)),
                    ],
                    axis=1,
                )
            )
        wave = jnp.concatenate([wave] * (span // LANES), axis=1)
        last = jnp.concatenate([last] * (span // LANES), axis=1)
        leg = dot(order, jnp.concatenate(stack, axis=0).astype(BF16))
        before = line <= cut_off - wave
        first = before & (line <= last)
        second = jnp.logical_not(before) & (line <= last)
        odd = ((line + jnp.where(before, 0, wave)) & 1) == 1
        masks = [
            [jnp.where(side & odd, 1.0, 0.0) if par else jnp.where(odd, 0.0, jnp.where(side, 1.0, 0.0)) for par in range(2)]
            for side in (first, second)
        ]
        for par in range(2):
            near = leg * masks[0][par]
            far = leg * masks[1][par]
            for pp in range(4):
                at = 2 * eight * t + par * eight + 2 * pp * lats
                eh_ref[at:at + 2 * lats, :] = jnp.concatenate(
                    [near[pp * lats:(pp + 1) * lats], far[pp * lats:(pp + 1) * lats]], axis=0
                ).astype(BF16)
        part = pl.ds(2 * eight * t, 2 * eight)
        keeps.append(pltpu.make_async_copy(eh_ref.at[part], eh_hbm.at[part], out_sems.at[t]))
        keeps[-1].start()

        todo.append((leg, masks))

    rest = jnp.zeros((LANES - 4 * KPAD, span), F32)
    for t, (leg, masks) in enumerate(todo):
        for pp in range(4):
            own = leg[pp * lats:(pp + 1) * lats]
            pairs_of = jnp.concatenate([own * own[j:j + 1] for j in range(lats)], axis=0)
            pair = 4 * t + pp
            factor = pl.reciprocal(1.0 + tau_ref[8 * t + pp:8 * t + pp + 1, :] * wide_rate, approx=True)
            damp = []
            for side in range(2):
                for par in range(2):
                    mask = masks[side][par][pp * lats:pp * lats + 8]
                    damp.append(factor * jnp.concatenate([mask] * (KPAD // 8), axis=0))
            damp = jnp.concatenate(damp + [rest], axis=0).astype(BF16)
            at = pair * lats * lats
            round_ref[at:at + lats * lats, :] = dot_nt(pairs_of.astype(BF16), damp)
    wait_all(keeps)


def solve_kernel(
    fields, rows, lats, msg_ref, round_ref, mix_ref, turn_ref, mixed_ref, out_ref, cs,
):
    eight = 8 * lats
    groups = mixed_ref.shape[0] // eight
    groups_f = msg_ref.shape[0] // eight
    wf = fields * 2
    unit = rows * wf
    lane = lane_iota((lats, LANES))
    tiles = [
        [msg_ref[pl.ds(8 * g + i8, lats, stride=8 * groups_f), :] for g in range(groups_f)]
        for i8 in range(8)
    ]
    tall = []
    for t in range(groups):
        here = [lanes_within(lane, unit * (t + g), unit) for g in range(groups_f)]
        for i8 in range(8):
            line = tiles[i8][0]
            for g in range(1, groups_f):
                line = jnp.where(here[g], tiles[i8][g], line)
            if t:
                line = pltpu.roll(line, LANES - unit * t, 1)
            tall.append(line)
    v_high, v_low = split(jnp.concatenate(tall, axis=0))
    mixed_ref[...] = dot_nt(jnp.concatenate([v_high, v_high, v_low], axis=1), mix_ref[...])

    lane = lane_iota((lats, LANES))
    front = lane < 2 * KPAD
    sums = []
    for pair in range(4 * groups):
        one = mixed_ref[2 * pair * lats:(2 * pair + 1) * lats, :]
        two = mixed_ref[(2 * pair + 1) * lats:(2 * pair + 2) * lats, :]
        parts = (
            jnp.where(front, one, pltpu.roll(two, 2 * KPAD, 1)),
            jnp.where(front, pltpu.roll(one, LANES - 2 * KPAD, 1), two),
        )
        totals = [jnp.zeros((lats, LANES), F32) for _ in parts]
        for j in range(lats):
            at = (pair * lats + j) * lats
            matrix = round_ref[at:at + lats, :]
            totals = [
                total + part[j:j + 1] * matrix for total, part in zip(totals, parts)
            ]
        sums.append(jnp.where(front, totals[0], pltpu.roll(totals[1], 2 * KPAD, 1)))
        sums.append(jnp.where(front, pltpu.roll(totals[0], LANES - 2 * KPAD, 1), totals[1]))
    high, low = split(jnp.concatenate(sums, axis=0))
    cs[...] = dot(jnp.concatenate([high, low, high], axis=1), turn_ref[...])

    lane = lane_iota((8, LANES))
    here = [
        lanes_within(lane, wf * u, wf) for u in range(rows * groups + groups_f - 1)
    ]
    for holder in range(lats):
        tiles = [jnp.zeros((8, LANES), F32) for _ in range(groups_f)]
        for t in range(groups):
            piece = cs[pl.ds(t * eight + holder, 8, stride=lats), :]
            for r in range(rows):
                u = rows * t + r
                moved = pltpu.roll(piece, (wf * u - wf * groups_f * r) % LANES, 1)
                for g in range(groups_f):
                    tiles[g] = jnp.where(here[u + g], moved, tiles[g])
        for g in range(groups_f):
            at = (holder * groups_f + g) * 8
            out_ref[at:at + 8, :] = tiles[g]


def modes_kernel(
    lats, everyone, fields, rows, legs_hbm, tau_hbm, rate_hbm, back_hbm, mixed_ref,
    damped_ref, bk_ref, place_ref, gather_ref,
    legs_ref, tau_ref, rate_ref, back_ref, sems, small_sems,
):
    small = start_all((back_hbm, tau_hbm, rate_hbm), (back_ref, tau_ref, rate_ref), small_sems)
    span = legs_ref.shape[1]
    eight = 8 * lats
    deep = 8 * KPAD
    groups = legs_ref.shape[0] // (2 * eight)
    parts = [pl.ds(0, 2 * eight), pl.ds(2 * eight, 2 * eight * (groups - 1))]
    fetches = start_all(
        [legs_hbm.at[part] for part in parts], [legs_ref.at[part] for part in parts], sems
    )
    slot_pair = (lane_iota((2 * KPAD, 2 * eight)) & (eight - 1)) // (2 * lats)
    lefts = []
    for t in range(groups):
        mine = mixed_ref[eight * t:eight * (t + 1), :]
        if eight < LANES:
            mine = jnp.concatenate([mine, jnp.zeros((LANES - eight, LANES), F32)], axis=0)
        mine = [
            jnp.transpose(mine[at:at + LANES])[:, 0:min(eight, LANES)]
            for at in range(0, eight, LANES)
        ]
        mine = jnp.concatenate(mine, axis=1) if len(mine) > 1 else mine[0]
        mine = jnp.concatenate(
            [
                jnp.concatenate(
                    [mine[par * KPAD:(par + 1) * KPAD], mine[(par + 2) * KPAD:(par + 3) * KPAD]],
                    axis=0,
                )
                for par in range(2)
            ],
            axis=1,
        )
        left = jnp.concatenate([jnp.where(slot_pair == pp, mine, 0.0) for pp in range(4)], axis=0)
        lefts.append(jnp.concatenate(split(left), axis=1))
    gather_ref[...] = spread_matrix()
    unit = rows * fields * 2
    tall = 2 * TWICE
    shape = (tall, LANES)
    base = slot_lane(row_iota(shape), fields, rows)
    places = []
    for t in range(groups):
        source = (base + unit * t + lax.axis_index("fld") * (fields * 2)) & (LANES - 1)
        source = jnp.where(base < 0, base, source)
        places.append(jnp.where(lane_iota(shape) == source, 1.0, 0.0))
    place = jnp.concatenate(places, axis=0).astype(BF16)
    place_ref[...] = jnp.concatenate([place, place], axis=1)
    wait_all(small)
    tall = 2 * everyone
    pair_of = lane_iota((tall, deep)) // (2 * KPAD)
    blocks = []
    for part in range(2):
        full = back_ref[part * FPAD:part * FPAD + tall, :].astype(F32)
        blocks += [jnp.where(pair_of == pp, full, 0.0) for pp in range(4)]
    bk_ref[...] = jnp.concatenate(blocks, axis=0).astype(BF16)
    rate = rate_ref[...]
    for t in range(groups):
        if t < 2:
            fetches[t].wait()
        for start in range(0, span, 2 * LANES):
            size = min(2 * LANES, span - start)
            right = legs_ref[2 * eight * t:2 * eight * (t + 1), start:start + size]
            modes = dot(lefts[t], jnp.concatenate([right, right], axis=0))
            damped = []
            for pp in range(4):
                tau = tau_ref[8 * t + pp:8 * t + pp + 1, start:start + size]
                factor = pl.reciprocal(1.0 + tau * rate[:, 0:size], approx=True)
                at = 2 * pp * KPAD
                damped.append(modes[at:at + KPAD] * factor)
                damped.append(modes[at + KPAD:at + 2 * KPAD] * factor)
            damped_ref[deep * t:deep * (t + 1), start:start + size] = jnp.concatenate(
                damped, axis=0
            ).astype(BF16)


def output_kernel(damped_ref, bk_ref, spec_ref):
    everyone, quad, _, places = spec_ref.shape
    span = damped_ref.shape[1]
    deep = 8 * KPAD
    tall = 2 * everyone
    at = pl.multiple_of(deep * pl.program_id(0), deep)
    for start in range(0, span, 2 * LANES):
        size = min(2 * LANES, span - start)
        spec = dot(bk_ref[...], damped_ref[pl.ds(at, deep), start:start + size])
        spec = spec[0:4 * tall] + spec[4 * tall:]
        kept = min(size, places - start)
        for pp in range(4):
            for f in range(everyone):
                row = pp * tall + 2 * f
                spec_ref[f, pp, :, start:start + kept] = spec[row:row + 2, 0:kept]


def per_device(grid, row_lengths, band_map, fold_map, legendre, to_modes, back_modes, mode_rates):
    fields, single, rows, width = grid.shape
    pairs, places, lats = legendre.shape
    cut_off = places - 2
    everyone = to_modes.shape[0]
    owners, per_owner = fold_map.shape
    groups = -(-per_owner // 8)
    slots = owners * groups * 8
    pieces = -(-(width // 4) // DEEP)
    turns = 4 * pieces
    span = -(-places // LANES) * LANES
    hbm = pl.BlockSpec(memory_space=pltpu.HBM)
    vmem = pl.BlockSpec(memory_space=pltpu.VMEM)
    room = pltpu.CompilerParams(vmem_limit_bytes=ROOM)
    message = pltpu.HBM((owners, 8, LANES), F32)
    holders = band_map.shape[0]
    groups_f = everyone // fields
    dma = pltpu.SemaphoreType.DMA
    row_lengths, band_map, fold_map, to_modes, back_modes, mode_rates, grid = (
        pltpu.with_memory_space_constraint(x, pltpu.HBM)
        for x in (row_lengths, band_map, fold_map, to_modes, back_modes, mode_rates, grid)
    )
    legendre = pltpu.with_memory_space_constraint(jnp.transpose(legendre, (0, 2, 1)), pltpu.HBM)

    sending, cos_table, sin_table, cos_turn, sin_turn = pl.pallas_call(
        functools.partial(forward_kernel, cut_off, groups),
        out_shape=(
            message,
            pltpu.VMEM((DEEP, slots), BF16),
            pltpu.VMEM((DEEP, slots), BF16),
            pltpu.VMEM((turns, slots), F32),
            pltpu.VMEM((turns, slots), F32),
        ),
        in_specs=[hbm] * 4,
        out_specs=(vmem,) * 5,
        scratch_shapes=[
            pltpu.SMEM(row_lengths.shape, jnp.int32),
            pltpu.SMEM(band_map.shape, jnp.int32),
            pltpu.VMEM(fold_map.shape, jnp.int32),
            pltpu.VMEM(grid.shape, BF16),
            dma((4,)),
            pltpu.VMEM((LANES, LANES), F32),
            pltpu.VMEM((8, slots), F32),
            pltpu.VMEM((16, 4 * DEEP * pieces), F32),
            pltpu.VMEM((4 * TWICE, slots), BF16),
        ],
        compiler_params=room,
        name="forward_rows",
    )(row_lengths, band_map, fold_map, grid)
    tables = [
        pltpu.with_memory_space_constraint(x, pltpu.VMEM)
        for x in (cos_table, sin_table, cos_turn, sin_turn)
    ]
    arrived = lax.all_to_all(sending, ("lat", "fld"), split_axis=0, concat_axis=0, tiled=True)

    legs, rounds, mix, back, turn_back, tau, rate = pl.pallas_call(
        functools.partial(prepare_kernel, cut_off, pairs, fields, rows),
        out_shape=(
            pltpu.HBM((groups * 16 * lats, span), BF16),
            pltpu.VMEM((groups * 4 * lats * lats, LANES), F32),
            pltpu.VMEM((LANES, 3 * LANES), BF16),
            pltpu.HBM((2 * FPAD, 8 * KPAD), BF16),
            pltpu.VMEM((3 * LANES, LANES), BF16),
            pltpu.HBM((8 * groups, span), F32),
            pltpu.HBM((KPAD, 2 * LANES), F32),
        ),
        in_specs=[hbm] * 6,
        out_specs=(hbm, vmem, vmem, hbm, vmem, hbm, hbm),
        scratch_shapes=[
            pltpu.SMEM(fold_map.shape, jnp.int32),
            pltpu.SMEM(band_map.shape, jnp.int32),
            pltpu.SMEM(mode_rates.shape, F32),
            pltpu.VMEM((pairs, lats, places), F32),
            pltpu.VMEM(to_modes.shape, F32),
            pltpu.VMEM(back_modes.shape, F32),
            dma((6,)),
            pltpu.VMEM((KPAD, LANES), F32),
            pltpu.VMEM((groups * 16 * lats, span), BF16),
            dma((groups,)),
            pltpu.VMEM((2 * FPAD, 8 * KPAD), BF16),
            pltpu.VMEM((8 * groups, span), F32),
            pltpu.VMEM((KPAD, 2 * LANES), F32),
            dma((3,)),
        ],
        compiler_params=pltpu.CompilerParams(vmem_limit_bytes=2 * ROOM),
        cost_estimate=pl.CostEstimate(flops=10**8, bytes_accessed=8 * 10**6, transcendentals=0),
        name="prepare",
    )(fold_map, band_map, mode_rates, legendre, to_modes, back_modes)
    legs, back, tau, rate = (
        pltpu.with_memory_space_constraint(x, pltpu.HBM) for x in (legs, back, tau, rate)
    )
    rounds, mix, turn_back = (
        pltpu.with_memory_space_constraint(x, pltpu.VMEM) for x in (rounds, mix, turn_back)
    )

    mixed, leaving = pl.pallas_call(
        functools.partial(solve_kernel, fields, rows, lats),
        out_shape=(
            pltpu.VMEM((groups * 8 * lats, LANES), F32),
            pltpu.HBM((owners * 8, LANES), F32),
        ),
        in_specs=[vmem] * 4,
        out_specs=(vmem,) * 2,
        scratch_shapes=[pltpu.VMEM((groups * 8 * lats, LANES), F32)],
        compiler_params=room,
        name="solve",
    )(arrived.reshape(owners * 8, LANES), rounds, mix, turn_back)
    leaving = leaving.reshape(owners, 8, LANES)

    returned = lax.all_to_all(leaving, ("lat", "fld"), split_axis=0, concat_axis=0, tiled=True)

    mixed = pltpu.with_memory_space_constraint(mixed, pltpu.VMEM)
    cost = pl.CostEstimate(flops=10**8, bytes_accessed=8 * 10**6, transcendentals=0)
    damped, spread_back, place, gather = pl.pallas_call(
        functools.partial(modes_kernel, lats, everyone, fields, rows),
        out_shape=(
            pltpu.VMEM((groups * 8 * KPAD, span), BF16),
            pltpu.VMEM((16 * everyone, 8 * KPAD), BF16),
            pltpu.VMEM((2 * TWICE * groups, 2 * LANES), BF16),
            pltpu.VMEM((4 * LANES, 4 * LANES), BF16),
        ),
        in_specs=[hbm] * 4 + [vmem],
        out_specs=(vmem,) * 4,
        scratch_shapes=[
            pltpu.VMEM((groups * 16 * lats, span), BF16),
            pltpu.VMEM((8 * groups, span), F32),
            pltpu.VMEM((KPAD, 2 * LANES), F32),
            pltpu.VMEM((2 * FPAD, 8 * KPAD), BF16),
            dma((2,)),
            dma((3,)),
        ],
        compiler_params=room,
        cost_estimate=cost,
        name="modes",
    )(legs, tau, rate, back, mixed)
    damped, spread_back, place, gather = (
        pltpu.with_memory_space_constraint(x, pltpu.VMEM)
        for x in (damped, spread_back, place, gather)
    )
    spectral = pl.pallas_call(
        output_kernel,
        grid=(groups,),
        out_shape=jax.ShapeDtypeStruct((everyone, pairs, 2, places), F32),
        in_specs=[vmem, vmem],
        out_specs=pl.BlockSpec((everyone, 4, 2, places), lambda t: (0, t, 0, 0)),
        compiler_params=pltpu.CompilerParams(
            dimension_semantics=("arbitrary",), vmem_limit_bytes=ROOM
        ),
        cost_estimate=cost,
        name="spectral_output",
    )(damped, spread_back)

    grid_out = pl.pallas_call(
        functools.partial(inverse_kernel, groups),
        out_shape=jax.ShapeDtypeStruct(grid.shape, BF16),
        in_specs=[hbm] * 2 + [vmem] * 7,
        out_specs=vmem,
        scratch_shapes=[
            pltpu.SMEM(row_lengths.shape, jnp.int32),
            pltpu.SMEM(band_map.shape, jnp.int32),
            dma((2,)),
            pltpu.VMEM((32 * pieces, 4 * LANES), BF16),
        ],
        compiler_params=room,
        name="inverse_rows",
    )(row_lengths, band_map, *tables, place, gather, returned)
    return (jnp.transpose(spectral, (0, 2, 1, 3)), grid_out)


def solution(mesh):
    placed = (
        P("fld", "lat", None, None),
        P(),
        P(),
        P(),
        P(("lat", "fld"), None, None),
        P(),
        P(),
        P(),
    )
    return jax.shard_map(
        per_device,
        mesh=mesh,
        in_specs=placed,
        out_specs=(P(None, None, ("lat", "fld"), None), P("fld", "lat", None, None)),
        check_vma=False,
    )
```
